128 devices in a mesh: seq: 128 (over z, x, y, core).
Axes of the slice: x: 4, y: 4, z: 4, core: 2. Of those that a mesh axis runs over, the one named last changes fastest.
Arguments:
- block_input: float32 [16384, 2560], P('seq'), may hold values from -6 to 6
- cotangent: float32 [16384, 2560], P('seq'), may hold values from -6 to 6
- segments: int32 [16384], P('seq'), may hold values from 0 to 7, as said below
- adapter_index: int32 [8], replicated, may hold values from 0 to 7, each once
- norm_first: float32 [2560], replicated, may hold values from 0.5 to 1.5
- norm_second: float32 [2560], replicated, may hold values from 0.5 to 1.5
- conv_taps: float32 [4, 2560], replicated, may hold values from -3 to 3
- decay_rate: float32 [2560], replicated, may hold values from 7.6293945e-06 to 0.03
- gelu_proj: bfloat16 [2560, 2560], P('seq'), may hold values from -0.125 to 0.125
- input_proj: bfloat16 [2560, 2560], P('seq'), may hold values from -0.125 to 0.125
- inner_gate: bfloat16 [2560, 256], P('seq'), may hold values from -0.375 to 0.375
- decay_gate: bfloat16 [2560, 256], P('seq'), may hold values from -0.375 to 0.375
- output_proj: bfloat16 [2560, 2560], P('seq'), may hold values from -0.125 to 0.125
- widen_proj: bfloat16 [2560, 15360], P('seq'), may hold values from -0.125 to 0.125
- narrow_proj: bfloat16 [7680, 2560], P('seq'), may hold values from -0.0625 to 0.0625
- enter_square: bfloat16 [5, 2560, 128], replicated, may hold values from -0.125 to 0.125
- leave_square: bfloat16 [5, 128, 2560], replicated, may hold values from -1.5 to 1.5
- enter_widen: bfloat16 [2560, 128], replicated, may hold values from -0.125 to 0.125
- leave_widen: bfloat16 [128, 15360], replicated, may hold values from -1.5 to 1.5
- enter_narrow: bfloat16 [7680, 128], replicated, may hold values from -0.0625 to 0.0625
- leave_narrow: bfloat16 [128, 2560], replicated, may hold values from -1.5 to 1.5
Outputs:
- block_output: float32 [16384, 2560], P('seq')
- input_grad: float32 [16384, 2560], P('seq')
- grad_enter_square: float32 [5, 2560, 128], replicated
- grad_leave_square: float32 [5, 128, 2560], replicated
- grad_enter_widen: float32 [2560, 128], replicated
- grad_leave_widen: float32 [128, 15360], replicated
- grad_enter_narrow: float32 [7680, 128], replicated
- grad_leave_narrow: float32 [128, 2560], replicated
The draws below stay inside these ranges and needn't reach their ends.
Inputs may be any that keep to these rules, and one draw needn't show every extreme that they name: `segments`: document numbers never fall along the tokens and every number is used; documents 0 to 2 lie within the first 128 tokens, documents 4 to 7 within the last 128 tokens, and document 3 covers all tokens between. `adapter_index`: each document uses an adapter of its own.
All inputs are finite; a program needn't handle non-finite values.
Results may differ from the reference program's by a relative error of at most 0.017.
Values may be sent and summed in bfloat16 or wider, within the bound.
No kernel may reach another device: no remote copies, remote signals or barrier semaphores. Data moves between devices by JAX's collectives and lax.ppermute only.
A program may use at most 512 MiB of HBM per device.

```python
import math
import jax
import jax.numpy as jnp
from jax import lax

HEADS = 10
HD = 256
D = 2560
FF = 7680
TAPS = 4
RANK = 16
ADAPTERS = 8
TOK_DEV = 128
TOKENS = 16384


def draw_segments(key, part):
    key = jax.random.fold_in(key, 11)
    subkeys = jax.random.split(key, 2)
    upper = max(TOK_DEV // 4, 2)
    head_sizes = jax.random.randint(subkeys[0], (3,), 1, upper)
    tail_sizes = jax.random.randint(subkeys[1], (4,), 1, upper)
    middle = TOKENS - jnp.sum(head_sizes) - jnp.sum(tail_sizes)
    lengths = jnp.concatenate([head_sizes, middle[None], tail_sizes]).astype(jnp.int32)
    boundaries = jnp.cumsum(lengths)
    positions = jnp.arange(TOKENS, dtype=jnp.int32)
    return jnp.sum((positions[:, None] >= boundaries[None, :]).astype(jnp.int32), axis=1).astype(jnp.int32)


def block_scale(rng, shape, cuts, smallest, largest):
    factor_of, own = 1.0, jax.random.fold_in(rng, 6)
    for dim, blocks in cuts:
        steps = jnp.exp(jax.random.uniform(jax.random.fold_in(own, dim), (blocks,), jnp.float32, smallest / len(cuts), largest / len(cuts)))
        factor_of = factor_of * jnp.repeat(steps, shape[dim] // blocks).reshape([-1 if axis == dim else 1 for axis in range(len(shape))])
    return factor_of


def scatter_about(own_key, shape, width, reach, cuts=(), kind=jnp.bfloat16):
    entries = width * jax.random.normal(own_key, shape, jnp.float32)
    if cuts:
        entries = entries * block_scale(own_key, shape, cuts, -0.22, 0.18)
    return jnp.clip(entries, -reach, reach).astype(kind)


def setup_inputs(seed: int = 0) -> dict:
    keys = jax.random.split(jax.random.key(seed), 22)
    return {
        "block_input": scatter_about(keys[0], (TOKENS, D), 1.0, 6.0, ((0, 128),), jnp.float32),
        "cotangent": scatter_about(keys[1], (TOKENS, D), 1.0, 6.0, ((0, 128),), jnp.float32),
        "segments": draw_segments(jax.random.fold_in(keys[21], 71), 0),
        "adapter_index": jax.random.permutation(keys[3], ADAPTERS).astype(jnp.int32),
        "norm_first": jnp.clip(1.0 + 0.1 * jax.random.normal(keys[4], (D,), jnp.float32), 0.5, 1.5),
        "norm_second": jnp.clip(1.0 + 0.1 * jax.random.normal(keys[5], (D,), jnp.float32), 0.5, 1.5),
        "conv_taps": scatter_about(keys[6], (TAPS, D), 0.5, 3.0, (), jnp.float32),
        "decay_rate": jnp.clip(jnp.exp(jax.random.uniform(keys[7], (D,), jnp.float32, math.log(7.62939453125e-06), math.log(0.03))), 7.62939453125e-06, 0.03),
        "gelu_proj": scatter_about(keys[8], (D, D), D ** -0.5, 0.125, ((0, 128),)),
        "input_proj": scatter_about(keys[9], (D, D), D ** -0.5, 0.125, ((0, 128),)),
        "inner_gate": scatter_about(keys[10], (D, HD), HD ** -0.5, 0.375, ((0, 128),)),
        "decay_gate": scatter_about(keys[11], (D, HD), HD ** -0.5, 0.375, ((0, 128),)),
        "output_proj": scatter_about(keys[12], (D, D), D ** -0.5, 0.125, ((0, 128),)),
        "widen_proj": scatter_about(keys[13], (D, 2 * FF), D ** -0.5, 0.125, ((0, 128),)),
        "narrow_proj": scatter_about(keys[14], (FF, D), FF ** -0.5, 0.0625, ((0, 128),)),
        "enter_square": scatter_about(keys[15], (5, D, ADAPTERS * RANK), D ** -0.5, 0.125),
        "leave_square": scatter_about(keys[16], (5, ADAPTERS * RANK, D), RANK ** -0.5, 1.5),
        "enter_widen": scatter_about(keys[17], (D, ADAPTERS * RANK), D ** -0.5, 0.125),
        "leave_widen": scatter_about(keys[18], (ADAPTERS * RANK, 2 * FF), RANK ** -0.5, 1.5),
        "enter_narrow": scatter_about(keys[19], (FF, ADAPTERS * RANK), FF ** -0.5, 0.0625),
        "leave_narrow": scatter_about(keys[20], (ADAPTERS * RANK, D), RANK ** -0.5, 1.5),
    }


@jax.custom_vjp
def low(v):
    return lax.optimization_barrier(v.astype(jnp.bfloat16)).astype(jnp.float32)

@jax.custom_vjp
def low_back(v):
    return v

def low_keep(v):
    return (low(v), None)

def low_pass(kept, grad):
    return (grad,)

def back_keep(v):
    return (v, None)

def back_low(kept, grad):
    return (low(grad),)
low.defvjp(low_keep, low_pass)
low_back.defvjp(back_keep, back_low)
HIGH = lax.Precision.HIGHEST
eps_norm = 1e-06
floor_scale = 0.001

def matmul(left_side, right_side):
    return jnp.dot(left_side, right_side, precision=HIGH, preferred_element_type=jnp.float32)

def rms_scale(values, gain):
    return values * lax.rsqrt(lax.optimization_barrier(jnp.mean(values * values, axis=-1, keepdims=True)) + eps_norm) * gain

def blocked(values, weight):
    head_rows = values.reshape(values.shape[0], HEADS, -1)
    shaped = weight.reshape(HEADS, -1, weight.shape[1])
    return jnp.einsum('thi,hij->thj', head_rows, shaped, precision=HIGH).reshape(values.shape[0], -1)

def adapted(inputs, base_term, down_map, up_map, select):
    latent = low_back(matmul(inputs, down_map))
    picked = low(latent * select)
    return low_back(base_term + matmul(picked, up_map))

def linked(former, latter):
    return (former[0] * latter[0], latter[0] * former[1] + latter[1])

def convolve(filler, segments, conv_taps):
    combined = conv_taps[0] * filler
    for offset in range(1, conv_taps.shape[0]):
        moved = jnp.pad(filler, ((offset, 0), (0, 0)))[:-offset]
        earlier = jnp.pad(segments, (offset, 0), constant_values=-1)[:-offset]
        same_doc = (earlier == segments).astype(jnp.float32)[:, None]
        combined = combined + conv_taps[offset] * moved * same_doc
    return combined

def recur_inputs(inner_pre, decay_pre, convolved, retain, decay_rate):
    gate_in = jax.nn.sigmoid(inner_pre)
    log_decay = -8.0 * decay_rate * jax.nn.sigmoid(decay_pre)
    decays = jnp.exp(log_decay) * retain
    scale = jnp.where(retain > 0.5, jnp.sqrt(jnp.maximum(-jnp.expm1(2.0 * log_decay), floor_scale)), 1.0)
    return (decays, convolved * gate_in * scale)

def reference(block_input, cotangent, segments, adapter_index, norm_first, norm_second, conv_taps, decay_rate, gelu_proj, input_proj, inner_gate, decay_gate, output_proj, widen_proj, narrow_proj, enter_square, leave_square, enter_widen, leave_widen, enter_narrow, leave_narrow):
    weights = [v.astype(jnp.float32) for v in (gelu_proj, input_proj, inner_gate, decay_gate, output_proj, widen_proj, narrow_proj)]
    columns = enter_square.shape[-1]
    rank_size = columns // ADAPTERS
    owners = jnp.take(adapter_index, segments)
    select = (owners[:, None] == (jnp.arange(columns) // rank_size)[None, :]).astype(jnp.float32)
    earlier = jnp.concatenate([jnp.full((1,), -1, jnp.int32), segments[:-1].astype(jnp.int32)])
    retain = (segments == earlier).astype(jnp.float32)[:, None]
    hidden_ff = widen_proj.shape[1] // 2
    blocks = max(1, TOKENS // 2048)

    def forward(inputs, square_in, square_out, widen_in, widen_out, narrow_in, narrow_out):
        normed = low(rms_scale(inputs, norm_first))
        gelu_pre = adapted(normed, matmul(normed, weights[0]), square_in[0], square_out[0], select)
        branch = jax.nn.gelu(gelu_pre, approximate=True)
        filler = adapted(normed, matmul(normed, weights[1]), square_in[1], square_out[1], select)
        convolved = low(convolve(filler, segments, conv_taps))
        inner_pre = adapted(convolved, blocked(convolved, weights[2]), square_in[2], square_out[2], select)
        decay_pre = adapted(convolved, blocked(convolved, weights[3]), square_in[3], square_out[3], select)
        decays, pushed = recur_inputs(inner_pre, decay_pre, convolved, retain, decay_rate)
        states = lax.associative_scan(linked, (decays, pushed))[1]
        mixed_rows = low(branch * states)
        residual = inputs + adapted(mixed_rows, matmul(mixed_rows, weights[4]), square_in[4], square_out[4], select)

        def feed(pieces):
            row_block, chosen = pieces
            normed_two = low(rms_scale(row_block, norm_second))
            gate_up = adapted(normed_two, matmul(normed_two, weights[5]), widen_in, widen_out, chosen)
            hidden = low(jax.nn.gelu(gate_up[:, :hidden_ff], approximate=True) * gate_up[:, hidden_ff:])
            return row_block + adapted(hidden, matmul(hidden, weights[6]), narrow_in, narrow_out, chosen)
        result = lax.map(jax.checkpoint(feed), (residual.reshape(blocks, -1, residual.shape[1]), select.reshape(blocks, -1, columns)))
        return result.reshape(residual.shape)
    adapters_wide = tuple((v.astype(jnp.float32) for v in (enter_square, leave_square, enter_widen, leave_widen, enter_narrow, leave_narrow)))
    result, pullback = jax.vjp(forward, block_input, *adapters_wide)
    gradients = pullback(cotangent)
    return (result, gradients[0], gradients[1], gradients[2], gradients[3], gradients[4], gradients[5], gradients[6])
```

```python
import functools
import jax
import jax.numpy as jnp
from jax import lax
from jax.experimental import pallas as pl
from jax.experimental.pallas import tpu as pltpu
from jax.sharding import Mesh, PartitionSpec as P

HEADS = 10
ADAPTERS = 8
HALO = 16
MIDDLE = 3
AXES = ("z", "x", "v", "u", "c")
SIZES = (4, 4, 2, 2, 2)
YAX = ("v", "u")
RING = ("v", "u", "c")
PLANE = ("z", "x")

eps_norm = 1e-06
floor_scale = 0.001
bf16 = jnp.bfloat16
f32 = jnp.float32


def dot(a, b):
    return jnp.dot(a, b, preferred_element_type=f32)


def dot_nt(a, b):
    return lax.dot_general(a, b, (((1,), (1,)), ((), ())), preferred_element_type=f32)


def dot_tn(a, b):
    return lax.dot_general(a, b, (((0,), (0,)), ((), ())), preferred_element_type=f32)


def low(v):
    return lax.reduce_precision(v, 8, 7)


def norm_scale(values):
    return lax.rsqrt(jnp.mean(values * values, axis=-1, keepdims=True) + eps_norm)


def norm_apply(values, gain):
    return (values * norm_scale(values) * gain).astype(bf16)


def norm_back(values, gain, grad):
    s = norm_scale(values)
    gq = gain * grad
    return s * gq - values * (s * s * s) * jnp.mean(values * gq, axis=-1, keepdims=True)


def gelu_parts(a):
    k = 0.7978845608028654
    a2 = a * a
    th = jnp.tanh(k * (a + 0.044715 * a2 * a))
    value = 0.5 * a * (1.0 + th)
    slope = 0.5 * (1.0 + th) + 0.5 * a * (1.0 - th * th) * (k * (1.0 + 3.0 * 0.044715 * a2))
    return value, slope


def swap(v):
    return lax.ppermute(v, "c", [(0, 1), (1, 0)])


def shift4(v, axis, by):
    return lax.ppermute(v, axis, [(i, (i + by) % 4) for i in range(4)])


def chip_shift(v, by):
    chips = 64
    pairs = [
        (2 * p + c, 2 * (p + by) + c) for p in range(chips) for c in range(2) if 0 <= p + by < chips
    ]
    return lax.ppermute(v, AXES, pairs)


def both(own, other, c):
    rows = own.shape[0]
    three = jnp.concatenate([own, other, own], axis=0)
    return lax.dynamic_slice_in_dim(three, c * rows, 2 * rows, axis=0)


def half(v, c, axis):
    size = v.shape[axis] // 2
    return lax.dynamic_slice_in_dim(v, c * size, size, axis=axis)


def scan_kernel(d_ref, p_ref, s_ref, q_ref):
    rows, width = d_ref.shape
    row = lax.broadcasted_iota(jnp.int32, (8, width), 0)

    def tile(i, carry):
        state, product = carry
        at = pl.ds(pl.multiple_of(i * 8, 8), 8)
        a = d_ref[at, :]
        b = p_ref[at, :]
        for s in (1, 2, 4):
            b = a * jnp.where(row >= s, pltpu.roll(b, s, 0), 0.0) + b
            a = a * jnp.where(row >= s, pltpu.roll(a, s, 0), 1.0)
        value = b + a * state
        through = a * product
        s_ref[at, :] = value
        q_ref[at, :] = through
        return value[7:8, :], through[7:8, :]

    lax.fori_loop(
        0, rows // 8, tile, (jnp.zeros((1, width), f32), jnp.ones((1, width), f32))
    )


def scan_back_kernel(main, d_ref, g_ref, s_ref, q_ref):
    rows, width = d_ref.shape
    row = lax.broadcasted_iota(jnp.int32, (8, width), 0)

    def tile(i, carry):
        state, product, after = carry
        at = pl.ds(pl.multiple_of(i * 8, 8), 8)
        d = d_ref[at, :]
        b = g_ref[at, :]
        a = jnp.where(row < 7, pltpu.roll(d, 7, 0), after)
        for s in (1, 2, 4):
            b = a * jnp.where(row < 8 - s, pltpu.roll(b, 8 - s, 0), 0.0) + b
            a = a * jnp.where(row < 8 - s, pltpu.roll(a, 8 - s, 0), 1.0)
        value = b + a * state
        through = a * product
        s_ref[at, :] = value
        q_ref[at, :] = through
        return value[0:1, :], through[0:1, :], d[0:1, :]

    zero = jnp.zeros((1, width), f32)
    one = jnp.ones((1, width), f32)
    last = rows // 8 - 1
    lax.fori_loop(0, (rows - main) // 8, lambda k, t: tile(last - k, t), (zero, zero, one))
    lax.fori_loop(0, main // 8, lambda k, t: tile(main // 8 - 1 - k, t), (zero, one, one))


def scan_call(kernel, a, b):
    rows, cols = a.shape
    wide = 256 if cols % 256 == 0 else 128
    block = pl.BlockSpec((rows, wide), lambda i: (0, i))
    return pl.pallas_call(
        kernel,
        grid=(cols // wide,),
        in_specs=[block, block],
        out_specs=[block, block],
        out_shape=[jax.ShapeDtypeStruct((rows, cols), f32)] * 2,
        compiler_params=pltpu.CompilerParams(vmem_limit_bytes=32 * 2**20),
        cost_estimate=pl.CostEstimate(
            flops=20 * rows * cols, bytes_accessed=16 * rows * cols, transcendentals=0
        ),
    )(a, b)


def linked(former, latter):
    return (former[0] * latter[0], latter[0] * former[1] + latter[1])


def line_carry(value, axis, reverse):
    sign = -1 if reverse else 1
    here = lax.axis_index(axis)
    here = 3 - here if reverse else here
    came = {by: shift4(value, axis, sign * by) for by in (1, 2, 3)}
    unit = (jnp.ones_like(value[0]), jnp.zeros_like(value[0]))

    def take(so_far, by, valid):
        new = linked(so_far, (came[by][0], came[by][1]))
        return tuple(jnp.where(valid, a, b) for a, b in zip(new, so_far))

    enter = unit
    for by in (3, 2, 1):
        enter = take(enter, by, here >= by)
    total = linked(enter, (value[0], value[1]))
    for by in (3, 2, 1):
        total = take(total, by, here < by)
    return enter, jnp.stack(total)


def chips_carry(value, reverse):
    by_y, line = line_carry(value, YAX, reverse)
    by_x, plane = line_carry(line, "x", reverse)
    by_z, _ = line_carry(plane, "z", reverse)
    return linked(linked(by_z, by_x), by_y)[1]


def index_of(place):
    at = 0
    for i, n in zip(place, (4, 4, 4, 2)):
        at = at * n + i
    return at


def spread_rounds(order):
    reached = {0: {(0, 0, 0)}, 1: {(3, 3, 3)}}
    rounds = []
    for axis in order:
        for hop in (2, 1):
            pairs = []
            for c in (0, 1):
                new = set()
                for place in sorted(reached[c]):
                    to = list(place)
                    to[axis] = place[axis] ^ hop
                    new.add(tuple(to))
                    pairs.append((index_of((*place, c)), index_of((*to, c))))
                reached[c] |= new
            rounds.append(pairs)
    return rounds


def spread(payload):
    rows = payload.shape[0]
    cut = rows // 3 // 16 * 16
    bounds = [0, rows - 2 * cut, rows - cut, rows]
    parts = []
    for k, order in enumerate(((0, 1, 2), (1, 2, 0), (2, 0, 1))):
        part = payload[bounds[k] : bounds[k + 1]]
        for pairs in spread_rounds(order):
            part = part + lax.ppermute(part, AXES, pairs)
        parts.append(part)
    return jnp.concatenate(parts, axis=0)


def line_sum(v, axis):
    one, two, three = (shift4(v, axis, by).astype(f32) for by in (1, 2, 3))
    return (v.astype(f32) + two) + (one + three)


def to_low(v):
    return low(v).astype(bf16)


def ring_rows(own):
    parts = [own] + [shift4(own, YAX, by) for by in (1, 2, 3)]
    rows = []
    for part in parts:
        rows += [part, swap(part)]
    return rows


def ring_scatter(part, rows):
    mine = [part[(2 * k) * rows : (2 * k + 1) * rows] for k in range(4)]
    theirs = jnp.concatenate([part[(2 * k + 1) * rows : (2 * k + 2) * rows] for k in range(4)], axis=0)
    got = swap(theirs.astype(bf16)).astype(f32)
    mine = [m + got[k * rows : (k + 1) * rows] for k, m in enumerate(mine)]
    total = mine[0]
    for by in (1, 2, 3):
        total = total + shift4(mine[by].astype(bf16), YAX, -by).astype(f32)
    return total


def per_device(
    block_input,
    cotangent,
    segments,
    adapter_index,
    norm_first,
    norm_second,
    conv_taps,
    decay_rate,
    gelu_proj,
    input_proj,
    inner_gate,
    decay_gate,
    output_proj,
    widen_proj,
    narrow_proj,
    enter_square,
    leave_square,
    enter_widen,
    leave_widen,
    enter_narrow,
    leave_narrow,
):
    c = lax.axis_index("c")
    y = lax.axis_index(YAX)
    member = lax.axis_index(RING)
    plane = lax.axis_index(PLANE)
    chip = lax.axis_index(("z", "x", "v", "u"))
    place = lax.axis_index(AXES)
    toks, width = block_input.shape
    halfw = width // 2
    heads = HEADS // 2
    head = width // HEADS
    columns = enter_square.shape[-1]
    rank = columns // ADAPTERS
    main = 2 * toks
    extra = 2 * toks
    rows = main + extra
    per = gelu_proj.shape[0]
    gate_rows = per * head // width
    ff = widen_proj.shape[1] // 2
    slot = ff // 8
    slotp = slot * 16 // 15
    per_n = narrow_proj.shape[0]
    chunk = slotp // 16

    shard = jnp.concatenate(
        [
            gelu_proj,
            input_proj,
            output_proj,
            inner_gate.reshape(gate_rows, width),
            decay_gate.reshape(gate_rows, width),
        ],
        axis=0,
    )
    near = lax.all_gather(shard[None], AXES, axis=0, tiled=True)

    pieces = widen_proj.reshape(per, 2, 8, slot).transpose(2, 0, 1, 3)
    pieces = jnp.pad(pieces, ((0, 0), (0, 0), (0, 0), (0, slotp - slot)))
    pieces = lax.all_to_all(pieces.reshape(8 * per, 2 * slotp), RING, 0, 0, tiled=True)
    to_first = [(16 * m + p, 8 * p + m) for p in range(16) for m in range(8)]
    to_second = [(16 * m + p + 1, 8 * p + m) for p in range(16) for m in range(8) if 16 * m + p + 1 < 128]
    two = jnp.concatenate(
        [lax.ppermute(narrow_proj, AXES, to_first), lax.ppermute(narrow_proj, AXES, to_second)], axis=0
    )
    two = jnp.pad(two, ((0, 2 * chunk - 2 * per_n), (0, 0)))
    rows_n = lax.dynamic_slice_in_dim(two, jnp.minimum(plane, 14) * (chunk - per_n), chunk, axis=0)
    rows_n = jnp.where(plane < 15, rows_n, jnp.zeros_like(rows_n))
    far = lax.all_gather(
        jnp.concatenate([pieces, rows_n.reshape(-1, 2 * slotp)], axis=0)[None], PLANE, axis=0, tiled=True
    )

    middle_at = adapter_index[MIDDLE] * rank
    column_owner = jnp.arange(columns) // rank
    owner_of = jnp.arange(adapter_index.shape[0])

    def select_of(segs):
        owners = jnp.sum((segs[:, None] == owner_of[None, :]).astype(jnp.int32) * adapter_index[None, :], axis=1)
        return (owners[:, None] == column_owner[None, :]).astype(f32)

    def middle(v):
        return lax.dynamic_slice_in_dim(v, middle_at, rank, axis=1)

    grad_down_own = cotangent.astype(bf16)
    seg_row = jnp.pad(segments.astype(bf16)[None, :], ((0, 15), (0, width - toks)))
    payload = jnp.concatenate([block_input.astype(bf16), grad_down_own, seg_row], axis=0)
    source = (place == 0) | (place == 127)
    payload = spread(jnp.where(source, payload, jnp.zeros_like(payload)))
    paired = both(payload, swap(payload), c)
    count = payload.shape[0]
    x_extra = jnp.concatenate([paired[:toks], paired[count : count + toks]], axis=0).astype(f32)
    down_extra = jnp.concatenate([paired[toks : 2 * toks], paired[count + toks : count + 2 * toks]], axis=0)
    seg_first = paired[2 * toks, :toks].astype(jnp.int32)
    seg_last = paired[count + 2 * toks, :toks].astype(jnp.int32)
    seg_extra = jnp.concatenate([seg_first, seg_last])
    select_extra = select_of(seg_extra) * (seg_extra != MIDDLE).astype(f32)[:, None]

    normed_own = norm_apply(block_input, norm_first)
    normed_main = both(normed_own, swap(normed_own), c)
    normed_halo = chip_shift(normed_main[main - HALO :], 1)
    seg_main = both(segments, swap(segments), c)
    halo_seg = jnp.where(chip > 0, MIDDLE, -1)
    seg_all = jnp.concatenate(
        [jnp.broadcast_to(halo_seg, (HALO,)), seg_main, seg_first + 100, seg_last + 200]
    )
    select_main = select_of(seg_main)
    select = jnp.concatenate([select_main, select_extra], axis=0)
    select_halo = jnp.broadcast_to((column_owner == adapter_index[MIDDLE]).astype(f32)[None, :], (HALO, columns))
    select_long = jnp.concatenate([select_halo, select], axis=0)
    normed_extra = norm_apply(x_extra, norm_first)
    normed_long = jnp.concatenate([normed_halo, normed_main, normed_extra], axis=0)
    normed = normed_long[HALO:]

    ring_down = jnp.concatenate(ring_rows(grad_down_own) + [down_extra], axis=0)
    ring_seg = jnp.concatenate(ring_rows(segments))
    ring_select = jnp.concatenate([select_of(ring_seg), select_extra], axis=0)
    latent_grad_n = (dot_nt(ring_down, leave_narrow) * ring_select).astype(bf16)

    taps = half(conv_taps, c, 1)
    rate = half(decay_rate, c, 0)[None, :]
    enter_half = half(enter_square, c, 1)
    leave_half = half(leave_square, c, 2)

    w_gelu = lax.dynamic_slice(near, (0, 0, c * halfw), (128, per, halfw)).reshape(width, halfw)
    w_in = lax.dynamic_slice(near, (0, per, c * halfw), (128, per, halfw)).reshape(width, halfw)
    w_out = lax.dynamic_slice(near, (c * 64, 2 * per, 0), (64, per, width)).reshape(halfw, width)
    w_gates = lax.dynamic_slice(near, (c * 64, 3 * per, 0), (64, 2 * gate_rows, width))
    w_inner = w_gates[:, :gate_rows].reshape(heads, head, head)
    w_decay = w_gates[:, gate_rows:].reshape(heads, head, head)

    def block_apply(values, weight):
        return jnp.einsum(
            "thi,hij->thj", values.reshape(-1, heads, head), weight, preferred_element_type=f32
        ).reshape(-1, halfw)

    def block_back(grads, weight):
        return jnp.einsum(
            "thj,hij->thi", grads.reshape(-1, heads, head), weight, preferred_element_type=f32
        ).reshape(-1, halfw)

    picked_fill = (dot(normed_long, enter_square[1]) * select_long).astype(bf16)
    filler = dot(normed_long, w_in) + dot(picked_fill, leave_half[1])
    picked_fill = picked_fill[HALO:]
    same_docs = []
    combined = taps[0] * filler[HALO:]
    for k in range(1, conv_taps.shape[0]):
        same = (seg_all[HALO - k : -k] == seg_all[HALO:]).astype(f32)[:, None]
        same_docs.append(same)
        combined = combined + taps[k] * filler[HALO - k : -k] * same
    convolved = combined.astype(bf16)
    conv_wide = convolved.astype(f32)
    retain = same_docs[0]
    latent = jnp.concatenate([dot(convolved, enter_half[2]), dot(convolved, enter_half[3])], axis=1)
    latent = latent + swap(latent)
    picked_inner = (latent[:, :columns] * select).astype(bf16)
    picked_decay = (latent[:, columns:] * select).astype(bf16)
    inner_pre = block_apply(convolved, w_inner) + dot(picked_inner, leave_half[2])
    decay_pre = block_apply(convolved, w_decay) + dot(picked_decay, leave_half[3])
    sig_in = jax.nn.sigmoid(inner_pre)
    sig_decay = jax.nn.sigmoid(decay_pre)
    log_decay = -8.0 * rate * sig_decay
    raw_decay = jnp.exp(log_decay)
    decays = raw_decay * retain
    grown = -jnp.expm1(2.0 * log_decay)
    scale = jnp.where(retain > 0.5, jnp.sqrt(jnp.maximum(grown, floor_scale)), 1.0)
    pushed = conv_wide * sig_in * scale
    local_state, products = scan_call(scan_kernel, decays, pushed)
    entering = chips_carry(jnp.stack([products[main - 1], local_state[main - 1]]), False)
    picked_gelu = (dot(normed, enter_square[0]) * select).astype(bf16)
    gelu_pre = dot(normed, w_gelu) + dot(picked_gelu, leave_half[0])
    branch, gelu_slope = gelu_parts(gelu_pre)
    states = local_state + products * entering[None, :]
    mixed = (branch * states).astype(bf16)
    latent_out = dot(mixed, enter_half[4])
    out_part = dot(mixed, w_out) + dot((latent_out * select).astype(bf16), leave_square[4])
    picked_out = ((latent_out + swap(latent_out)) * select).astype(bf16)
    mine = lax.dynamic_slice_in_dim(out_part, c * toks, toks, axis=0)
    theirs = lax.dynamic_slice_in_dim(out_part, (1 - c) * toks, toks, axis=0)
    out_extra = to_low(out_part[main:])
    got = swap(jnp.concatenate([theirs.astype(bf16), out_extra], axis=0)).astype(f32)
    residual = block_input + mine + got[:toks]
    residual_extra = x_extra + (out_extra.astype(f32) + got[toks:])
    normed_two_own = norm_apply(residual, norm_second)
    normed_two_extra = norm_apply(residual_extra, norm_second)

    n2 = jnp.concatenate(ring_rows(normed_two_own) + [normed_two_extra], axis=0)
    ring_main = 8 * toks
    w_wide = far[:, : 8 * per].reshape(width, 2 * slotp)
    w_narrow = far[:, 8 * per :].reshape(slotp, width)
    pad_cols = ((0, 0), (0, slotp - slot))
    leave_a = jnp.pad(lax.dynamic_slice_in_dim(leave_widen, member * slot, slot, axis=1), pad_cols)
    leave_b = jnp.pad(lax.dynamic_slice_in_dim(leave_widen, ff + member * slot, slot, axis=1), pad_cols)
    leave_wide = jnp.concatenate([leave_a, leave_b], axis=1)
    enter_down = jnp.pad(
        lax.dynamic_slice_in_dim(enter_narrow, member * slot, slot, axis=0), ((0, slotp - slot), (0, 0))
    )
    picked_wide = (dot(n2, enter_widen) * ring_select).astype(bf16)
    gate_up = dot(n2, w_wide) + dot(picked_wide, leave_wide)
    grad_hidden = dot_nt(ring_down, w_narrow) + dot_nt(latent_grad_n, enter_down)
    act, act_slope = gelu_parts(gate_up[:, :slotp])
    up = gate_up[:, slotp:]
    hidden = (act * up).astype(bf16)
    grad_gate_up = jnp.concatenate([act_slope * up * grad_hidden, act * grad_hidden], axis=1).astype(bf16)
    latent_grad_w = (dot_nt(grad_gate_up, leave_wide) * ring_select).astype(bf16)
    n2_part = dot_nt(grad_gate_up, w_wide) + dot_nt(latent_grad_w, enter_widen)
    latent_n = dot(hidden, enter_down)
    picked_n = (latent_n * ring_select).astype(bf16)
    down_part = dot(hidden[:ring_main], w_narrow) + dot(picked_n[:ring_main], leave_narrow)

    wide_mid = dot_tn(middle(picked_wide[:ring_main]), grad_gate_up[:ring_main])
    down_mid = dot_tn(middle(latent_grad_n[:ring_main]), hidden[:ring_main])
    leave_n_mid = dot_tn(middle(picked_n[:ring_main]), ring_down[:ring_main])
    enter_w_mid = dot_tn(middle(latent_grad_w[:ring_main]), n2[:ring_main])
    ffn_mid = jnp.concatenate([wide_mid, down_mid, leave_n_mid, enter_w_mid], axis=1)
    ffn_mid = to_low(line_sum(to_low(line_sum(to_low(ffn_mid), "x")), "z"))
    wide_extra = dot_tn(picked_wide[ring_main:], grad_gate_up[ring_main:])
    down_extra_grad = dot_tn(latent_grad_n[ring_main:], hidden[ring_main:])
    leave_n_extra = dot_tn(picked_n[ring_main:], ring_down[ring_main:])
    enter_w_extra = dot_tn(latent_grad_w[ring_main:], n2[ring_main:])
    ffn_extra = jnp.concatenate([wide_extra, down_extra_grad, leave_n_extra, enter_w_extra], axis=1).astype(bf16)
    ffn_all = lax.all_gather(jnp.concatenate([ffn_mid, ffn_extra], axis=0), RING, axis=0)
    ffn_all = ffn_all.astype(f32)

    ffn_full = ffn_all[:, rank:] + jnp.tile(ffn_all[:, :rank], (1, ADAPTERS, 1)) * (
        column_owner == adapter_index[MIDDLE]
    ).astype(f32)[None, :, None]
    grad_leave_widen = jnp.concatenate(
        [ffn_full[m, :, s * slotp : s * slotp + slot] for s in (0, 1) for m in range(8)], axis=1
    )
    grad_enter_narrow = jnp.concatenate(
        [ffn_full[m, :, 2 * slotp : 2 * slotp + slot].T for m in range(8)], axis=0
    )
    ffn_sum = jnp.sum(ffn_full[:, :, 3 * slotp :], axis=0)
    grad_leave_narrow = ffn_sum[:, :width]
    grad_enter_widen = ffn_sum[:, width:].T

    quarter = extra // 8
    main_part = n2_part[:ring_main]
    mine_rows = [main_part[(2 * k) * toks : (2 * k + 1) * toks] for k in range(4)]
    their_rows = [main_part[(2 * k + 1) * toks : (2 * k + 2) * toks] for k in range(4)]
    extra_part = n2_part[ring_main:]
    mine_extra = half(extra_part, c, 0)
    their_extra = half(extra_part, 1 - c, 0)
    got = swap(jnp.concatenate(their_rows + [their_extra], axis=0).astype(bf16)).astype(f32)
    mine_extra = mine_extra + got[4 * toks :]
    mine_rows = [m + got[k * toks : (k + 1) * toks] for k, m in enumerate(mine_rows)]
    grad_normed_two = mine_rows[0]
    extra_sum = lax.dynamic_slice_in_dim(mine_extra, y * quarter, quarter, axis=0)
    for by in (1, 2, 3):
        at = jnp.remainder(y - by, 4)
        send = jnp.concatenate(
            [mine_rows[by], lax.dynamic_slice_in_dim(mine_extra, at * quarter, quarter, axis=0)], axis=0
        ).astype(bf16)
        came = shift4(send, YAX, -by).astype(f32)
        grad_normed_two = grad_normed_two + came[:toks]
        extra_sum = extra_sum + came[toks:]
    extra_sum = extra_sum.astype(bf16)
    quarters = [extra_sum] + [shift4(extra_sum, YAX, by) for by in (1, 2, 3)]
    ordered = jnp.concatenate(quarters[::-1] + quarters[::-1], axis=0)
    half_extra = lax.dynamic_slice_in_dim(ordered, (3 - y) * quarter, 4 * quarter, axis=0)
    grad_normed_two_extra = both(half_extra, swap(half_extra), c).astype(f32)
    down_own = ring_scatter(down_part, toks)
    block_output = residual + down_own

    grad_residual = cotangent + norm_back(residual, norm_second, grad_normed_two)
    grad_residual_extra = down_extra.astype(f32) + norm_back(residual_extra, norm_second, grad_normed_two_extra)
    grad_out_own = grad_residual.astype(bf16)
    grad_out = jnp.concatenate(
        [both(grad_out_own, swap(grad_out_own), c), grad_residual_extra.astype(bf16)], axis=0
    )
    lg_out = (dot_nt(grad_out, leave_square[4]) * select).astype(bf16)
    grad_mixed = dot_nt(grad_out, w_out) + dot_nt(lg_out, enter_half[4])
    grad_gelu = (gelu_slope * (grad_mixed * states)).astype(bf16)
    grad_states = grad_mixed * branch
    back_local, trailing = scan_call(functools.partial(scan_back_kernel, main), decays, grad_states)
    coming = chips_carry(jnp.stack([decays[0] * trailing[0], decays[0] * back_local[0]]), True)
    carried = back_local + trailing * coming[None, :]
    states_before = jnp.concatenate([entering[None, :], states[:-1]], axis=0)
    through_in = carried * conv_wide * scale
    grad_inner = (through_in * sig_in * (1.0 - sig_in)).astype(bf16)
    grad_grown = jnp.where(
        (grown > floor_scale) & (retain > 0.5), carried * conv_wide * sig_in * 0.5 / scale, 0.0
    )
    grad_log = carried * states_before * decays - 2.0 * raw_decay * raw_decay * grad_grown
    grad_decay = (grad_log * (-8.0 * rate) * sig_decay * (1.0 - sig_decay)).astype(bf16)
    latent = jnp.concatenate([dot_nt(grad_inner, leave_half[2]), dot_nt(grad_decay, leave_half[3])], axis=1)
    latent = latent + swap(latent)
    lg_inner = (latent[:, :columns] * select).astype(bf16)
    lg_decay = (latent[:, columns:] * select).astype(bf16)
    grad_conv = (
        carried * sig_in * scale
        + block_back(grad_inner, w_inner)
        + block_back(grad_decay, w_decay)
        + dot_nt(lg_inner, enter_half[2])
        + dot_nt(lg_decay, enter_half[3])
    )
    conv_halo = chip_shift(grad_conv[:HALO], -1)
    halo_on = jnp.ones((HALO, 1), f32)
    long_conv = jnp.concatenate([grad_conv[:main], conv_halo, grad_conv[main:], jnp.zeros((HALO, halfw), f32)], axis=0)
    grad_filler = taps[0] * long_conv[: rows + HALO]
    for k in range(1, conv_taps.shape[0]):
        same = same_docs[k - 1]
        long_same = jnp.concatenate([same[:main], halo_on, same[main:], jnp.zeros((HALO, 1), f32)], axis=0)
        grad_filler = grad_filler + taps[k] * (long_conv * long_same)[k : k + rows + HALO]
    grad_filler = jnp.concatenate([grad_filler[:main], grad_filler[main + HALO :]], axis=0).astype(bf16)
    latent = jnp.concatenate([dot_nt(grad_gelu, leave_half[0]), dot_nt(grad_filler, leave_half[1])], axis=1)
    two_select = jnp.concatenate([select, select], axis=1)
    own_lg = (latent[:main] * two_select[:main]).astype(bf16)
    grad_normed = (
        dot_nt(grad_gelu[:main], w_gelu)
        + dot_nt(grad_filler[:main], w_in)
        + dot_nt(own_lg[:, :columns], enter_square[0])
        + dot_nt(own_lg[:, columns:], enter_square[1])
    )
    mine = lax.dynamic_slice_in_dim(grad_normed, c * toks, toks, axis=0)
    theirs = lax.dynamic_slice_in_dim(grad_normed, (1 - c) * toks, toks, axis=0)
    grad_normed = mine + swap(theirs.astype(bf16)).astype(f32)
    input_grad = grad_residual + norm_back(block_input, norm_first, grad_normed)
    latent = latent + swap(latent)
    lg_two = (latent * two_select).astype(bf16)
    lg_gelu, lg_fill = lg_two[:, :columns], lg_two[:, columns:]

    normed_half = half(normed, c, 1)
    grad_out_half = half(grad_out, c, 1)
    enters = [
        (normed_half, lg_gelu),
        (normed_half, lg_fill),
        (convolved, lg_inner),
        (convolved, lg_decay),
        (mixed, lg_out),
    ]
    leaves = [
        (picked_gelu, grad_gelu),
        (picked_fill, grad_filler),
        (picked_inner, grad_inner),
        (picked_decay, grad_decay),
        (picked_out, grad_out_half),
    ]
    mid = [dot_tn(middle(lg[:main]), v[:main]) for v, lg in enters]
    mid += [dot_tn(middle(pick[:main]), g[:main]) for pick, g in leaves]
    mid = to_low(jnp.concatenate(mid, axis=0))
    for axis in (YAX, "x", "z"):
        mid = to_low(line_sum(mid, axis))
    enter_extra = jnp.stack([dot_tn(v[main:], lg[main:]) for v, lg in enters]).astype(bf16)
    leave_extra = jnp.stack([dot_tn(pick[main:], g[main:]) for pick, g in leaves]).astype(bf16)

    def halves(v, axis):
        other = swap(v)
        first = jnp.where(c == 0, v, other)
        second = jnp.where(c == 0, other, v)
        return jnp.concatenate([first, second], axis=axis).astype(f32)

    mid = halves(mid, 1).reshape(10, rank, width)
    mask = (column_owner == adapter_index[MIDDLE]).astype(f32)
    grad_leave_square = halves(leave_extra, 2) + jnp.tile(mid[5:], (1, ADAPTERS, 1)) * mask[None, :, None]
    grad_enter_square = (
        halves(enter_extra, 1) + jnp.tile(mid[:5].transpose(0, 2, 1), (1, 1, ADAPTERS)) * mask[None, None, :]
    )
    return (
        block_output,
        input_grad,
        grad_enter_square,
        grad_leave_square,
        grad_enter_widen,
        grad_leave_widen,
        grad_enter_narrow,
        grad_leave_narrow,
    )


def solution(mesh):
    split = Mesh(mesh.devices.reshape(SIZES), AXES)
    by_row = P(AXES, None)
    return jax.shard_map(
        per_device,
        mesh=split,
        in_specs=(by_row, by_row, P(AXES), P(), P(), P(), P(), P())
        + (by_row,) * 7
        + (P(),) * 6,
        out_specs=(by_row, by_row, P(), P(), P(), P(), P(), P()),
        check_vma=False,
    )
```

```python
import functools
import jax
import jax.numpy as jnp
from jax import lax
from jax.experimental import pallas as pl
from jax.experimental.pallas import tpu as pltpu
from jax.sharding import Mesh, PartitionSpec as P

HEADS = 10
ADAPTERS = 8
HALO = 16
MIDDLE = 3
AXES = ("z", "x", "v", "u", "c")
SIZES = (4, 4, 2, 2, 2)
YAX = ("v", "u")
RING = ("v", "u", "c")
PLANE = ("z", "x")
QUAD = ("u", "c")
CHIPS = ("z", "x", "v", "u")
VMEM = 56 * 2**20

eps_norm = 1e-06
floor_scale = 0.001
bf16 = jnp.bfloat16
f32 = jnp.float32


def dot(a, b):
    return jnp.dot(a, b, preferred_element_type=f32)


def dot_nt(a, b):
    return lax.dot_general(a, b, (((1,), (1,)), ((), ())), preferred_element_type=f32)


def dot_tn(a, b):
    return lax.dot_general(a, b, (((0,), (0,)), ((), ())), preferred_element_type=f32)


def low(v):
    return lax.reduce_precision(v, 8, 7)


def to_low(v):
    return low(v).astype(bf16)


def norm_scale(values):
    return lax.rsqrt(jnp.mean(values * values, axis=-1, keepdims=True) + eps_norm)


def norm_apply(values, gain):
    return (values * norm_scale(values) * gain).astype(bf16)


def norm_back(values, gain, grad):
    s = norm_scale(values)
    gq = gain * grad
    return s * gq - values * (s * s * s) * jnp.mean(values * gq, axis=-1, keepdims=True)


def sigmoid(v):
    return 1.0 / (1.0 + jnp.exp(-v))


def gelu_parts(a):
    k = 0.7978845608028654
    a2 = a * a
    th = jnp.tanh(k * (a + 0.044715 * a2 * a))
    value = 0.5 * a * (1.0 + th)
    slope = 0.5 * (1.0 + th) + 0.5 * a * (1.0 - th * th) * (k * (1.0 + 3.0 * 0.044715 * a2))
    return value, slope


def swap(v):
    return lax.ppermute(v, "c", [(0, 1), (1, 0)])


def shift4(v, axis, by):
    return lax.ppermute(v, axis, [(i, (i + by) % 4) for i in range(4)])


def chip_shift(v, by, cross=False):
    chips = 64
    pairs = [
        (2 * p + c, 2 * (p + by) + (1 - c if cross else c))
        for p in range(chips)
        for c in range(2)
        if 0 <= p + by < chips
    ]
    return lax.ppermute(v, AXES, pairs)


def both(own, other, c):
    rows = own.shape[0]
    three = jnp.concatenate([own, other, own], axis=0)
    return lax.dynamic_slice_in_dim(three, c * rows, 2 * rows, axis=0)


def half(v, c, axis):
    size = v.shape[axis] // 2
    return lax.dynamic_slice_in_dim(v, c * size, size, axis=axis)


def after(first, *values):
    held = lax.optimization_barrier((first, *values))[1:]
    return held[0] if len(held) == 1 else held


def tied(value, other):
    return value + other[(0,) * other.ndim].astype(f32) * 0.0


def line_order(parts, y):
    back = parts[::-1]
    twice = jnp.stack(back + back)
    return lax.dynamic_slice_in_dim(twice, 3 - y, 4, axis=0)


def call(kernel, grid, ins, outs, scratch, scalars, args, micros, waits=()):
    count = len(args)

    def body(s_ref, *refs):
        kernel(s_ref, *refs[:count], *refs[count + len(waits) :])

    ins = list(ins) + [pl.BlockSpec(memory_space=pl.ANY)] * len(waits)
    args = (*args, *waits)
    return pl.pallas_call(
        body,
        grid_spec=pltpu.PrefetchScalarGridSpec(
            num_scalar_prefetch=1,
            grid=grid,
            in_specs=ins,
            out_specs=[spec for spec, _ in outs],
            scratch_shapes=scratch,
        ),
        out_shape=[jax.ShapeDtypeStruct(*shape) for _, shape in outs],
        compiler_params=pltpu.CompilerParams(vmem_limit_bytes=VMEM),
        cost_estimate=pl.CostEstimate(flops=int(micros * 1e9), bytes_accessed=int(micros * 2e6), transcendentals=0),
    )(scalars, *args)


def fixed(shape):
    return pl.BlockSpec(shape, lambda *_: (0,) * len(shape), pipeline_mode=pl.Buffered(1))


def scan_rows(d_ref, p_ref, s_ref, q_ref):
    rows, width = d_ref.shape
    row = lax.broadcasted_iota(jnp.int32, (8, width), 0)

    def tile(i, carry):
        state, product = carry
        at = pl.ds(pl.multiple_of(i * 8, 8), 8)
        a = d_ref[at, :]
        b = p_ref[at, :]
        for s in (1, 2, 4):
            b = a * jnp.where(row >= s, pltpu.roll(b, s, 0), 0.0) + b
            a = a * jnp.where(row >= s, pltpu.roll(a, s, 0), 1.0)
        value = b + a * state
        through = a * product
        s_ref[at, :] = value
        q_ref[at, :] = through
        return value[7:8, :], through[7:8, :]

    lax.fori_loop(
        0, rows // 8, tile, (jnp.zeros((1, width), f32), jnp.ones((1, width), f32)), unroll=8
    )


def scan_rows_back(d_ref, g_ref, s_ref, q_ref, main):
    rows, width = d_ref.shape
    row = lax.broadcasted_iota(jnp.int32, (8, width), 0)

    def tile(i, carry):
        state, product, after_row = carry
        at = pl.ds(pl.multiple_of(i * 8, 8), 8)
        d = d_ref[at, :]
        b = g_ref[at, :]
        a = jnp.where(row < 7, pltpu.roll(d, 7, 0), after_row)
        for s in (1, 2, 4):
            b = a * jnp.where(row < 8 - s, pltpu.roll(b, 8 - s, 0), 0.0) + b
            a = a * jnp.where(row < 8 - s, pltpu.roll(a, 8 - s, 0), 1.0)
        value = b + a * state
        through = a * product
        s_ref[at, :] = value
        q_ref[at, :] = through
        return value[0:1, :], through[0:1, :], d[0:1, :]

    zero = jnp.zeros((1, width), f32)
    one = jnp.ones((1, width), f32)
    last, cut = rows // 8 - 1, main // 8
    lax.fori_loop(0, last + 1 - cut, lambda k, t: tile(last - k, t), (zero, zero, one), unroll=8)
    lax.fori_loop(0, cut, lambda k, t: tile(cut - 1 - k, t), (zero, one, one), unroll=8)


def tile_of(w, i):
    block = w[:, i]
    return block.reshape(block.shape[0] * block.shape[1], block.shape[2])


def ends_kernel(stretches, s_ref, near_ref, gain_ref, x_ref, normed_ref, down_ref, marks_ref, hold_ref):
    toks = x_ref.shape[0] // 2
    quarter = x_ref.shape[1] // 4
    reach = quarter + marks_ref.shape[1]
    size = 8 * stretches
    for core in range(2):
        for p in range(16):
            for h in range(stretches):
                row = p * size + h * 8
                for y in range(4):
                    block = near_ref[2 * p + y // 2, 2 * (y % 2) + core, :, h * reach : (h + 1) * reach].astype(f32)
                    cols = slice(y * quarter, (y + 1) * quarter)
                    if row < toks:
                        x_ref[core * toks + row : core * toks + row + 8, cols] = block[:, :quarter]
                        if y == 0:
                            marks_ref[core * toks + row : core * toks + row + 8, :] = block[:, quarter:]
                    else:
                        to = core * toks + row - toks
                        hold_ref[to : to + 8, cols] = block[:, :quarter]
    down_ref[...] = hold_ref[...].astype(bf16)
    x = x_ref[...]
    normed_ref[...] = norm_apply(x, gain_ref[...])


def pack_kernel(s_ref, exa_ref, exb_ref, exn_ref, pick_ref, lg_ref, down_ref, n2_ref, mid_ref, out_ref):
    cols, wide = exa_ref.shape
    rank = mid_ref.shape[0]
    lanes = out_ref.shape[1]
    share = down_ref.shape[1]
    for i, ref in enumerate((exa_ref, exb_ref, exn_ref)):
        out_ref[:cols, i * wide : (i + 1) * wide] = ref[...]
    at = 3 * wide
    out_ref[:cols, at : at + share] = dot_tn(pick_ref[...], down_ref[...]).astype(bf16)
    out_ref[:cols, at + share :] = dot_tn(lg_ref[...], n2_ref[...]).astype(bf16)
    total = mid_ref.shape[1]
    for i in range(3):
        lo, hi = i * lanes, min((i + 1) * lanes, total)
        rows = slice(cols + i * rank, cols + (i + 1) * rank)
        out_ref[rows, : hi - lo] = mid_ref[:, lo:hi]
        if hi - lo < lanes:
            out_ref[rows, hi - lo :] = jnp.zeros((rank, lanes - hi + lo), bf16)


def fill_kernel(c_ref, x_ref, w_ref, pick_ref, leave_ref, mask_ref, taps_ref, enter_ref, conv_ref, lat_ref, acc_ref):
    rows, width = conv_ref.shape
    acc_ref[...] = dot(x_ref[...], tile_of(w_ref, 0)) + dot(pick_ref[...], leave_ref[...])
    step = width // 5
    for j in range(5):
        at = slice(j * step, (j + 1) * step)
        total = taps_ref[0:1, at] * acc_ref[HALO : HALO + rows, at]
        for k in range(1, taps_ref.shape[0]):
            total = total + taps_ref[k : k + 1, at] * acc_ref[HALO - k : HALO - k + rows, at] * mask_ref[:, k - 1 : k]
        conv_ref[:, at] = total.astype(bf16)

    @pl.when(pl.program_id(0) == 0)
    def _():
        lat_ref[...] = jnp.zeros_like(lat_ref)

    lat_ref[...] += dot(conv_ref[...], enter_ref[...])


def gate_weights(w_ref, hold_ref):
    @pl.when(pl.program_id(0) == 0)
    def _():
        wide = w_ref.shape[3]
        for i in range(4):
            hold_ref[:, i * wide : (i + 1) * wide] = tile_of(w_ref, i)

    head = 2 * w_ref.shape[3]
    at = pl.ds(pl.multiple_of(pl.program_id(0) * head, head), head)
    return hold_ref[at, :head], hold_ref[at, head:]


def gates_kernel(
    c_ref, conv_ref, own_ref, other_ref, select_ref, w_ref, leave_in_ref, leave_de_ref, mask_ref, rate_ref,
    sin_ref, sde_ref, dec_ref, state_ref, prod_ref, pick_in_ref, pick_de_ref, push_ref, hold_ref,
):
    cols = select_ref.shape[1]
    inner, decay = gate_weights(w_ref, hold_ref)

    @pl.when(pl.program_id(0) == 0)
    def _():
        lat = own_ref[...] + other_ref[...]
        select = select_ref[...]
        pick_in_ref[...] = (lat[:, :cols] * select).astype(bf16)
        pick_de_ref[...] = (lat[:, cols:] * select).astype(bf16)

    retain = mask_ref[:, 0:1]
    conv = conv_ref[...]
    sig_in = sigmoid(dot(conv, inner) + dot(pick_in_ref[...], leave_in_ref[...]))
    sig_de = sigmoid(dot(conv, decay) + dot(pick_de_ref[...], leave_de_ref[...]))
    raw = jnp.exp(-8.0 * rate_ref[...] * sig_de)
    scale = jnp.where(retain > 0.5, jnp.sqrt(jnp.maximum(1.0 - raw * raw, floor_scale)), 1.0)
    sin_ref[...] = sig_in
    sde_ref[...] = sig_de
    dec_ref[...] = raw * retain
    push_ref[...] = conv.astype(f32) * sig_in * scale
    scan_rows(dec_ref, push_ref, state_ref, prod_ref)


def gelu_kernel(c_ref, x_ref, w_ref, pick_ref, leave_ref, value_ref, slope_ref):
    pre = dot(x_ref[...], tile_of(w_ref, 0)) + dot(pick_ref[...], leave_ref[...])
    value, slope = gelu_parts(pre)
    value_ref[...] = value
    slope_ref[...] = slope


def out_kernel(
    c_ref, state_ref, prod_ref, entering_ref, branch_ref, w_ref, enter_ref, leave_ref, select_ref,
    states_ref, mixed_ref, lat_ref, mine_ref, send_ref, extra_ref, acc_ref, hold_ref,
):
    b = pl.program_id(0)
    q = w_ref.shape[3]
    states = state_ref[...] + prod_ref[...] * entering_ref[...]
    states_ref[...] = states
    hold_ref[...] = (branch_ref[...] * states).astype(bf16)
    mixed_ref[...] = hold_ref[...]

    @pl.when(b == 0)
    def _():
        lat_ref[...] = jnp.zeros_like(lat_ref)
        acc_ref[...] = jnp.zeros_like(acc_ref)

    lat_ref[...] += dot(hold_ref[...], enter_ref[...])
    for i in range(4):
        acc_ref[:, i * q : (i + 1) * q] += dot(hold_ref[...], tile_of(w_ref, i))

    @pl.when(b == pl.num_programs(0) - 1)
    def _():
        acc_ref[...] += dot((lat_ref[...] * select_ref[...]).astype(bf16), leave_ref[...])
        rows = mine_ref.shape[0]
        at = pl.multiple_of(c_ref[0] * rows, rows)
        mine_ref[...] = acc_ref[pl.ds(at, rows), :]
        send_ref[:rows, :] = acc_ref[pl.ds(pl.multiple_of(rows - at, rows), rows), :].astype(bf16)
        extra = acc_ref[2 * rows :, :].astype(bf16)
        send_ref[rows:, :] = extra
        extra_ref[...] = extra


def narrow_block(far_ref, j, top):
    wide = far_ref.shape[2]
    tail = wide // 4
    low_rows = (far_ref.shape[1] - top) // 5
    planes = pl.ds(4 * j, 4)
    main = far_ref[planes, top : top + 4 * low_rows, :].reshape(16 * low_rows, wide)
    pieces = []
    for p in range(4):
        rows = far_ref[4 * j + p, top + 4 * low_rows :, :]
        pieces += [rows[:, k * tail : (k + 1) * tail] for k in range(4)]
    return main, jnp.concatenate(pieces, axis=0)


def fetch(refs, hold_ref, sems):
    size = refs[0].shape[0]
    return [pltpu.make_async_copy(r, hold_ref.at[pl.ds(i * size, size), :], sems.at[i]) for i, r in enumerate(refs)]


def ffn_kernel(count, s_ref, *refs):
    n2_refs, gd_refs = refs[: 2 * count], refs[2 * count : 4 * count]
    far_ref, la_ref, lb_ref, en_ref, ew_ref, ln_ref, select_ref = refs[4 * count : 4 * count + 7]
    mine_ref, theirs_ref, ga_ref, gb_ref, hid_ref, lgw_ref, pickn_ref, pickw_ref, lgn_ref = refs[4 * count + 7 : 4 * count + 16]
    n2_hold, gd_hold, n2_sems, gd_sems = refs[4 * count + 16 :]
    side, width = mine_ref.shape
    slotp = hid_ref.shape[1]
    step = slotp // 4
    wide = far_ref.shape[2]
    top = width // 16
    n2_copies = fetch(n2_refs, n2_hold, n2_sems)
    gd_copies = fetch(gd_refs, gd_hold, gd_sems)
    for copy in n2_copies + gd_copies:
        copy.start()
    for copy in n2_copies + gd_copies:
        copy.wait()
    select = select_ref[...]
    pickw_ref[...] = (dot(n2_hold[...], ew_ref[...]) * select).astype(bf16)
    lgn_ref[...] = (dot_nt(gd_hold[...], ln_ref[...]) * select).astype(bf16)

    def hidden(j, _):
        at = pl.ds(pl.multiple_of(j * step, step), step)
        at_b = pl.ds(pl.multiple_of(slotp + j * step, step), step)
        a = dot(n2_hold[...], far_ref[:, :top, at].reshape(width, step)) + dot(pickw_ref[...], la_ref[:, at])
        up = dot(n2_hold[...], far_ref[:, :top, at_b].reshape(width, step)) + dot(pickw_ref[...], lb_ref[:, at])
        main, last = narrow_block(far_ref, j, top)
        grad = dot_nt(gd_hold[:, :wide], main) + dot_nt(gd_hold[:, wide:], last) + dot_nt(lgn_ref[...], en_ref[at, :])
        act, slope = gelu_parts(a)
        hid_ref[:, at] = (act * up).astype(bf16)
        ga_ref[:, at] = (slope * up * grad).astype(bf16)
        gb_ref[:, at] = (act * grad).astype(bf16)
        return 0

    lax.fori_loop(0, 4, hidden, 0)
    lgw_ref[...] = ((dot_nt(ga_ref[...], la_ref[...]) + dot_nt(gb_ref[...], lb_ref[...])) * select).astype(bf16)
    pickn_ref[...] = (dot(hid_ref[...], en_ref[...]) * select).astype(bf16)
    part = width // 4

    def back(q, _):
        at = pl.ds(pl.multiple_of(q * part, part), part)
        planes = pl.ds(4 * q, 4)
        total = dot_nt(ga_ref[...], far_ref[planes, :top, :slotp].reshape(part, slotp))
        total += dot_nt(gb_ref[...], far_ref[planes, :top, slotp:].reshape(part, slotp))
        total += dot_nt(lgw_ref[...], ew_ref[at, :])
        mine_ref[:, at] = total[:side].astype(bf16)
        theirs_ref[:, at] = total[side:].astype(bf16)
        return 0

    lax.fori_loop(0, 4, back, 0)


def down_kernel(s_ref, *refs):
    n2_refs, gd_refs = refs[:8], refs[8:16]
    hid0, hid1, ga0, ga1, gb0, gb1, far_ref, pick0, pick1, lgn0, lgn1, pickn0, pickn1, lgw0, lgw1, ln_ref = refs[16:32]
    down_ref, mida_ref, midb_ref, midn_ref, midl_ref, mide_ref, exa_ref, exb_ref, exn_ref = refs[32:41]
    acc_ref, hold_ref, wide_ref, n2_hold, gd_hold, n2_sems, gd_sems = refs[41:]
    j = pl.program_id(0)
    rank = mida_ref.shape[0]
    piece = n2_refs[0].shape[0]
    here = pl.ds(pl.multiple_of(s_ref[0] * rank, rank), rank)
    main, last = narrow_block(far_ref, 0, far_ref.shape[1] * 2 // 3)
    cut = main.shape[1]
    ring_of = lambda v, w: jnp.concatenate([v[:piece, :], v[2 * piece : 3 * piece, :], w[...]], axis=0)
    rest_of = lambda v: jnp.concatenate([v[piece : 2 * piece, :], v[3 * piece :, :]], axis=0)
    n2_copies = fetch(n2_refs, n2_hold, n2_sems)
    gd_copies = fetch(gd_refs, gd_hold, gd_sems)

    @pl.when(j == 0)
    def _():
        for copy in n2_copies + gd_copies:
            copy.start()
        acc_ref[...] = dot(ring_of(pickn0, pickn1), ln_ref[...])

    hid = ring_of(hid0, hid1)
    acc_ref[:, :cut] += dot(hid, main)
    acc_ref[:, cut:] += dot(hid, last)
    for left0, left1, right0, right1, out_ref, extra_ref in (
        (pick0, pick1, ga0, ga1, mida_ref, exa_ref),
        (pick0, pick1, gb0, gb1, midb_ref, exb_ref),
        (lgn0, lgn1, hid0, hid1, midn_ref, exn_ref),
    ):
        hold_ref[...] = dot_tn(ring_of(left0, left1), ring_of(right0, right1))
        out_ref[...] = hold_ref[here, :].astype(bf16)
        extra_ref[...] = dot_tn(rest_of(left0), rest_of(right0)).astype(bf16)

    @pl.when(j == pl.num_programs(0) - 1)
    def _():
        down_ref[...] = acc_ref[...].astype(bf16)
        for copy in n2_copies + gd_copies:
            copy.wait()
        wide_ref[...] = dot_tn(ring_of(pickn0, pickn1), gd_hold[...])
        midl_ref[...] = wide_ref[here, :].astype(bf16)
        wide_ref[...] = dot_tn(ring_of(lgw0, lgw1), n2_hold[...])
        mide_ref[...] = wide_ref[here, :].astype(bf16)


def outback_kernel(
    main, c_ref, go_ref, w_ref, leave_ref, enter_ref, select_ref, states_ref, branch_ref, slope_ref, dec_ref,
    gg_ref, lg_ref, state_ref, prod_ref, gs_ref,
):
    b = pl.program_id(0)
    q = w_ref.shape[3]

    @pl.when(b == 0)
    def _():
        lg_ref[...] = (dot_nt(go_ref[...], leave_ref[...]) * select_ref[...]).astype(bf16)

    gm = dot_nt(lg_ref[...], enter_ref[...])
    for i in range(4):
        gm += dot_nt(go_ref[:, i * q : (i + 1) * q], tile_of(w_ref, i))
    gg_ref[...] = (slope_ref[...] * (gm * states_ref[...])).astype(bf16)
    gs_ref[...] = gm * branch_ref[...]
    scan_rows_back(dec_ref, gs_ref, state_ref, prod_ref, main)


def geluback_kernel(c_ref, g_ref, w_ref, leave_ref, enter_ref, select_ref, part_ref, lat_ref, lg_ref):
    b = pl.program_id(0)
    q = w_ref.shape[3]

    @pl.when(b == 0)
    def _():
        lat = dot_nt(g_ref[...], leave_ref[...])
        lat_ref[...] = lat
        lg_ref[...] = (lat * select_ref[...]).astype(bf16)

    rows = part_ref.shape[0]
    part = dot_nt(g_ref[:rows, :q], tile_of(w_ref, 0)) + dot_nt(g_ref[:rows, q : 2 * q], tile_of(w_ref, 1))
    part_ref[...] = part + dot_nt(lg_ref[:rows, :], enter_ref[...])


def gateback_kernel(
    c_ref, back_ref, trail_ref, coming_ref, states_ref, entering_ref, conv_ref, sin_ref, sde_ref, dec_ref, mask_ref, rate_ref,
    w_ref, leave_in_ref, leave_de_ref,
    gi_ref, gd_ref, base_ref, lat_ref, hold_ref, gate_ref,
):
    rows = conv_ref.shape[0]
    cols = leave_in_ref.shape[0]
    inner, decay = gate_weights(w_ref, gate_ref)
    retain = mask_ref[:, 0:1]
    hold_ref[7:8, :] = entering_ref[...]
    hold_ref[8:, :] = states_ref[...]
    rate = rate_ref[...]
    sig_in = sin_ref[...]
    sig_de = sde_ref[...]
    conv = conv_ref[...].astype(f32)
    carried = back_ref[...] + trail_ref[...] * coming_ref[...]
    raw = jnp.exp(-8.0 * rate * sig_de)
    grown = 1.0 - raw * raw
    scale = jnp.where(retain > 0.5, jnp.sqrt(jnp.maximum(grown, floor_scale)), 1.0)
    through = carried * conv
    gi = (through * scale * sig_in * (1.0 - sig_in)).astype(bf16)
    grad_grown = jnp.where((grown > floor_scale) & (retain > 0.5), through * sig_in * 0.5 / scale, 0.0)
    grad_log = carried * hold_ref[7 : 7 + rows, :] * dec_ref[...] - 2.0 * raw * raw * grad_grown
    gd = (grad_log * (-8.0 * rate) * sig_de * (1.0 - sig_de)).astype(bf16)
    gi_ref[...] = gi
    gd_ref[...] = gd
    base_ref[...] = carried * sig_in * scale + dot_nt(gi, inner) + dot_nt(gd, decay)

    @pl.when(pl.program_id(0) == 0)
    def _():
        lat_ref[...] = jnp.zeros_like(lat_ref)

    lat_ref[:, :cols] += dot_nt(gi, leave_in_ref[...])
    lat_ref[:, cols:] += dot_nt(gd, leave_de_ref[...])


def fillback_kernel(
    c_ref, base_ref, own_ref, other_ref, hbase_ref, hown_ref, hother_ref, select_ref, mask_ref, taps_ref, enter_in_ref, enter_de_ref, leave_ref,
    w_ref, enter_ref, before_ref,
    gf_ref, lgi_ref, lgd_ref, lat_ref, mine_ref, theirs_ref, gc_ref, hlg_ref, lg_ref, part_ref,
):
    b = pl.program_id(0)
    q = w_ref.shape[3]
    rows, width = base_ref.shape
    main = part_ref.shape[0]
    cols = lgi_ref.shape[1]

    @pl.when(b == 0)
    def _():
        lat = own_ref[...] + other_ref[...]
        hlat = hown_ref[...] + hother_ref[...]
        select = select_ref[:rows, :]
        hselect = select_ref[rows:, :]
        lgi_ref[...] = (lat[:, :cols] * select).astype(bf16)
        lgd_ref[...] = (lat[:, cols:] * select).astype(bf16)
        hlg_ref[:, :cols] = (hlat[:, :cols] * hselect).astype(bf16)
        hlg_ref[:, cols:] = (hlat[:, cols:] * hselect).astype(bf16)
        step = width // 5
        for j in range(5):
            at = slice(j * step, (j + 1) * step)
            ei = enter_in_ref[at, :]
            ed = enter_de_ref[at, :]
            here = base_ref[:, at] + dot_nt(lgi_ref[...], ei) + dot_nt(lgd_ref[...], ed)
            gc_ref[:main, at] = here[:main]
            gc_ref[main : main + HALO, at] = (
                hbase_ref[:, at] + dot_nt(hlg_ref[:, :cols], ei) + dot_nt(hlg_ref[:, cols:], ed)
            )
            gc_ref[main + HALO : rows + HALO, at] = here[main:]
            gc_ref[rows + HALO :, at] = jnp.zeros((HALO, step), f32)
            for lo, hi, to in ((0, main, 0), (main + HALO, rows + HALO, main)):
                total = taps_ref[0:1, at] * gc_ref[lo:hi, at]
                for k in range(1, taps_ref.shape[0]):
                    total = total + taps_ref[k : k + 1, at] * gc_ref[lo + k : hi + k, at] * mask_ref[lo + k : hi + k, k - 1 : k]
                gf_ref[to : to + hi - lo, at] = total.astype(bf16)
        lat = dot_nt(gf_ref[...], leave_ref[...])
        lat_ref[...] = lat
        lg_ref[...] = (lat[:main] * select_ref[:main, :]).astype(bf16)

    part = dot_nt(gf_ref[:main, :q], tile_of(w_ref, 0)) + dot_nt(gf_ref[:main, q : 2 * q], tile_of(w_ref, 1))
    part_ref[...] = before_ref[...] + part + dot_nt(lg_ref[...], enter_ref[...])
    own = mine_ref.shape[0]
    at = pl.multiple_of(c_ref[0] * own, own)
    mine_ref[...] = part_ref[pl.ds(at, own), :]
    theirs_ref[...] = part_ref[pl.ds(pl.multiple_of(own - at, own), own), :].astype(bf16)


def mids_kernel(count, s_ref, *refs):
    out_ref, hold_ref = refs[2 * count :]
    rank = out_ref.shape[0] // count
    here = pl.ds(pl.multiple_of(s_ref[0] * rank, rank), rank)
    for i in range(count):
        hold_ref[...] = dot_tn(refs[2 * i][...], refs[2 * i + 1][...])
        out_ref[i * rank : (i + 1) * rank, :] = hold_ref[here, :].astype(bf16)


def extras_kernel(count, s_ref, *refs):
    enter_ref, leave_ref = refs[4 * count :]
    for i in range(count):
        enter_ref[i] = dot_tn(refs[2 * i][...], refs[2 * i + 1][...]).astype(bf16)
    for i in range(count):
        k = 2 * count + 2 * i
        leave_ref[i] = dot_tn(refs[k][...], refs[k + 1][...]).astype(bf16)


def square_kernel(s_ref, one_ref, own_e_ref, other_e_ref, own_l_ref, other_l_ref, own_me_ref, other_me_ref, own_ml_ref, other_ml_ref, enter_ref, leave_ref):
    size = own_e_ref.shape[1]
    one = one_ref[...]
    for core, e_ref, l_ref, me_ref, ml_ref in (
        (s_ref[0], own_e_ref, own_l_ref, own_me_ref, own_ml_ref),
        (1 - s_ref[0], other_e_ref, other_l_ref, other_me_ref, other_ml_ref),
    ):
        at = pl.ds(pl.multiple_of(core * size, size), size)
        enter_ref[0, at, :] = e_ref[0].astype(f32) + dot_tn(me_ref[...], one)
        leave_ref[0, :, at] = l_ref[0].astype(f32) + dot_tn(one, ml_ref[...])


def unit_parts(one_ref, extra_ref, mid_ref):
    one = one_ref[...]
    return [(extra_ref[m].astype(f32) + dot_tn(one, mid_ref[m])).astype(bf16) for m in range(8)]


def wide_kernel(s_ref, one_ref, spread_ref, extra_ref, mid_ref, out_ref):
    parts = unit_parts(one_ref, extra_ref, mid_ref)
    size = spread_ref.shape[1] // 8
    spread = spread_ref[...]
    done = [
        dot_nt(jnp.concatenate([v[:, p * size : (p + 1) * size] for v in parts], axis=1), spread) for p in range(4)
    ]
    out_ref[...] = jnp.concatenate(done, axis=1)


def enter_kernel(s_ref, one_ref, spread_ref, extra_ref, mid_ref, out_ref):
    parts = unit_parts(one_ref, extra_ref, mid_ref)
    units, size = spread_ref.shape
    size = size // 8
    spread = spread_ref[...]
    for p in range(4):
        some = jnp.concatenate([v[:, p * size : (p + 1) * size] for v in parts], axis=1)
        out_ref[p * units : (p + 1) * units, :] = dot_nt(spread, some)


def shares_kernel(s_ref, one_ref, eye_ref, extra_l_ref, extra_e_ref, mid0_ref, mid1_ref, mid2_ref, leave_ref, enter_ref):
    one = one_ref[...]
    width = leave_ref.shape[1]
    share = extra_l_ref.shape[2]
    start = mid0_ref.shape[2] - 2 * share
    sums = []
    for ref in (mid0_ref, mid1_ref, mid2_ref):
        total = ref[0].astype(f32)
        for m in range(1, 8):
            total = total + ref[m].astype(f32)
        sums.append(total.astype(bf16))
    mid = jnp.concatenate([sums[0][:, start:], sums[1], sums[2]], axis=1)
    leave_ref[...] = dot_tn(one, mid[:, :width])
    enter_ref[...] = dot_tn(mid[:, width : 2 * width], one)
    for m in range(8):
        lo, hi = m * share, min((m + 1) * share, width)
        if lo < hi:
            leave_ref[:, lo:hi] += extra_l_ref[m, :, : hi - lo].astype(f32)
            enter_ref[lo:hi, :] += dot_tn(extra_e_ref[m], eye_ref[...])[: hi - lo]


def linked(former, latter):
    return (former[0] * latter[0], latter[0] * former[1] + latter[1])


def line_carry(value, axis, reverse):
    sign = -1 if reverse else 1
    here = lax.axis_index(axis)
    here = 3 - here if reverse else here
    came = {by: shift4(value, axis, sign * by) for by in (1, 2, 3)}
    unit = (jnp.ones_like(value[0]), jnp.zeros_like(value[0]))

    def take(so_far, by, valid):
        new = linked(so_far, (came[by][0], came[by][1]))
        return tuple(jnp.where(valid, a, b) for a, b in zip(new, so_far))

    enter = unit
    for by in (3, 2, 1):
        enter = take(enter, by, here >= by)
    total = linked(enter, (value[0], value[1]))
    for by in (3, 2, 1):
        total = take(total, by, here < by)
    return enter, jnp.stack(total)


def chips_carry(value, reverse):
    by_y, line = line_carry(value, YAX, reverse)
    by_x, plane = line_carry(line, "x", reverse)
    by_z, _ = line_carry(plane, "z", reverse)
    return linked(linked(by_z, by_x), by_y)[1]


def index_of(place):
    at = 0
    for i, n in zip(place, (4, 4, 4, 2)):
        at = at * n + i
    return at


def scatter_ends(payload, seg_lanes, c):
    reached = {0: [(0, 0, 0)], 1: [(3, 3, 3)]}
    width = payload.shape[1]
    payload = jnp.concatenate([payload, seg_lanes], axis=1)
    for axis in range(3):
        if axis < 2:
            size = payload.shape[0] // 4
            pieces = [payload[k * size : (k + 1) * size] for k in range(4)]
        else:
            size = width // 4
            pieces = [jnp.concatenate([payload[:, k * size : (k + 1) * size], payload[:, width:]], axis=1) for k in range(4)]
        total = jnp.where(c == 0, pieces[0], pieces[3])
        added = {0: [], 1: []}
        for hop in (2, 1, 3):
            pairs = []
            for core in (0, 1):
                for place in reached[core]:
                    to = list(place)
                    to[axis] = hop if core == 0 else 3 - hop
                    added[core].append(tuple(to))
                    pairs.append((index_of((*place, core)), index_of((*to, core))))
            total = total + lax.ppermute(jnp.where(c == 0, pieces[hop], pieces[3 - hop]), AXES, pairs)
        for core in (0, 1):
            reached[core] = reached[core] + added[core]
        payload = total
    return payload


def line_sum(v, axis):
    one, two, three = (shift4(v, axis, by).astype(f32) for by in (1, 2, 3))
    return (v.astype(f32) + two) + (one + three)


def ring_rows(own):
    parts = [own] + [shift4(own, YAX, by) for by in (1, 2, 3)]
    return parts, [swap(part) for part in parts]


def line_back(sums):
    total = sums[0]
    for by in (1, 2, 3):
        total = total + shift4(sums[by].astype(bf16), YAX, -by).astype(f32)
    return total


def per_device(
    block_input,
    cotangent,
    segments,
    adapter_index,
    norm_first,
    norm_second,
    conv_taps,
    decay_rate,
    gelu_proj,
    input_proj,
    inner_gate,
    decay_gate,
    output_proj,
    widen_proj,
    narrow_proj,
    enter_square,
    leave_square,
    enter_widen,
    leave_widen,
    enter_narrow,
    leave_narrow,
):
    c = lax.axis_index("c")
    y = lax.axis_index(YAX)
    member = lax.axis_index(RING)
    plane = lax.axis_index(PLANE)
    chip = lax.axis_index(("z", "x", "v", "u"))
    place = lax.axis_index(AXES)
    toks, width = block_input.shape
    halfw = width // 2
    quarter = width // 4
    heads = HEADS // 2
    head = width // HEADS
    cols = enter_square.shape[-1]
    rank = cols // ADAPTERS
    main = 2 * toks
    per = gelu_proj.shape[0]
    per4 = 4 * per
    ff = widen_proj.shape[1] // 2
    slot = ff // 8
    slotp = slot * 16 // 15
    wide2 = 2 * slotp
    hcol = slotp // 4
    per_n = narrow_proj.shape[0]
    chunk = slotp // 16
    glane = 2 * head // 4

    grad_down_own = cotangent.astype(bf16)
    seg_lanes = jnp.broadcast_to(jnp.tile(segments, 2).astype(bf16)[:, None], (2 * toks, cols))
    payload = jnp.concatenate([block_input.astype(bf16), grad_down_own], axis=0)
    is_end = (place == 0) | (place == 127)
    piece = scatter_ends(jnp.where(is_end, payload, jnp.zeros_like(payload)), jnp.where(is_end, seg_lanes, jnp.zeros_like(seg_lanes)), c)

    gates = jnp.concatenate([inner_gate, decay_gate], axis=1)
    quads = jnp.stack(
        [
            jnp.concatenate(
                [v[:, q * (v.shape[1] // 4) : (q + 1) * (v.shape[1] // 4)] for v in (gelu_proj, input_proj, output_proj, gates)],
                axis=1,
            )
            for q in range(4)
        ]
    )
    lanes = quads.shape[2]
    quads = lax.all_to_all(quads, QUAD, 0, 0, tiled=True).reshape(per4, lanes)
    reach = piece.shape[1]
    stretches = piece.shape[0] // 8
    piece = jnp.concatenate([piece[k * 8 : (k + 1) * 8] for k in range(stretches)], axis=1)
    piece = jnp.pad(piece, ((0, 0), (0, lanes - stretches * reach)))
    quads = jnp.concatenate([quads, piece], axis=0)
    near = lax.all_gather(quads[None], AXES, axis=0, tiled=True).reshape(32, 4, per4 + 8, lanes)

    block_input, segments, widen_proj, narrow_proj = after(quads, block_input, segments, widen_proj, narrow_proj)

    block = 4 * 8 * per_n
    bcols = 4 * 8 * chunk
    at_col = jnp.arange(bcols)
    unit = at_col % (4 * chunk) % chunk
    from_row = at_col % (4 * chunk) // chunk * (8 * per_n) + at_col // (4 * chunk) * per_n + unit
    spread = ((jnp.arange(block)[:, None] == from_row[None, :]) & (unit < per_n)[None, :]).astype(bf16)
    units = 8 * per_n
    at_unit = jnp.arange(8 * chunk)
    spread_one = (jnp.arange(units)[:, None] == (at_unit // chunk * per_n + at_unit % chunk)[None, :]) & (at_unit % chunk < per_n)[None, :]
    spread_one = spread_one.astype(bf16)
    pieces = widen_proj.reshape(per, 8, block).transpose(1, 0, 2).reshape(8 * per, block)
    pieces = dot(pieces, spread).astype(bf16).reshape(8, per, 8, hcol).transpose(2, 1, 0, 3)
    pieces = lax.all_to_all(pieces.reshape(8 * per, wide2), RING, 0, 0, tiled=True)
    rows_n = jnp.pad(narrow_proj, ((0, chunk - per_n), (0, 0)))
    tail_n = rows_n[:, wide2:].reshape(4, chunk // 4, width - wide2).transpose(1, 0, 2).reshape(chunk // 4, wide2)
    shard_far = jnp.concatenate([pieces, rows_n[:, :wide2], tail_n], axis=0)
    far = lax.all_gather(shard_far[None], PLANE, axis=0, tiled=True)

    middle_owner = adapter_index[MIDDLE]
    column_owner = jnp.arange(cols) // rank
    owner_of = jnp.arange(adapter_index.shape[0])
    one_hot = (jnp.arange(cols)[None, :] == (middle_owner * rank + jnp.arange(rank))[:, None]).astype(bf16)
    core_at = c.astype(jnp.int32).reshape(1)
    middle_at = middle_owner.reshape(1)

    def select_of(segs):
        owners = jnp.sum((segs[:, None] == owner_of[None, :]).astype(jnp.int32) * adapter_index[None, :], axis=1)
        return (owners[:, None] == column_owner[None, :]).astype(f32)

    taps = half(conv_taps, c, 1)
    rate = half(decay_rate, c, 0)[None, :]
    enter_half = half(enter_square, c, 1)
    leave_half = half(leave_square, c, 2)
    enter_gates = jnp.concatenate([enter_half[2], enter_half[3]], axis=1)

    rows = 2 * main
    normed_own = norm_apply(block_input, norm_first)
    normed_main = both(normed_own, swap(normed_own), c)
    normed_halo = chip_shift(normed_main[main - HALO :], 1)
    normed_long = jnp.concatenate([normed_halo, normed_main], axis=0)
    seg_main = both(segments, swap(segments), c)
    halo_seg = jnp.broadcast_to(jnp.where(chip > 0, MIDDLE, -1), (HALO,))
    select_main = select_of(seg_main)
    select_halo = jnp.broadcast_to((column_owner == middle_owner).astype(f32)[None, :], (HALO, cols))
    ring_segs = [jnp.concatenate(v) for v in ring_rows(segments)]
    ring_selects = [select_of(v) for v in ring_segs]

    my_spread = lax.dynamic_slice_in_dim(spread, member * hcol, hcol, axis=1)
    leave_wide = leave_widen.reshape(cols, 8, block).transpose(1, 0, 2).reshape(8 * cols, block)
    leave_wide = dot(leave_wide, my_spread).astype(bf16).reshape(8, cols, hcol).transpose(1, 0, 2).reshape(cols, wide2)
    leave_a, leave_b = leave_wide[:, :slotp], leave_wide[:, slotp:]
    enter_down = lax.dot_general(
        my_spread, enter_narrow.reshape(4, block, cols), (((0,), (1,)), ((), ())), preferred_element_type=f32
    )
    enter_down = enter_down.transpose(1, 0, 2).reshape(slotp, cols).astype(bf16)

    near = after((shard_far, normed_long, select_main, ring_selects, leave_a, leave_b, enter_down, enter_gates), near)
    x_extra, normed_extra, down_extra, marks_extra = call(
        functools.partial(ends_kernel, stretches), (1,),
        [pl.BlockSpec((32, 4, 8, lanes), lambda *_: (0, 0, per4 // 8, 0), pipeline_mode=pl.Buffered(1)), fixed((1, width))],
        [(fixed((main, width)), ((main, width), f32)), (fixed((main, width)), ((main, width), bf16)),
         (fixed((main, width)), ((main, width), bf16)), (fixed((main, cols)), ((main, cols), f32))],
        [pltpu.VMEM((main, width), f32)],
        core_at, (near, norm_first[None, :]), 5,
    )
    seg_first = marks_extra[:toks, 0].astype(jnp.int32)
    seg_last = marks_extra[toks:, 0].astype(jnp.int32)
    seg_extra = jnp.concatenate([seg_first, seg_last])
    normed_long = jnp.concatenate([normed_long, normed_extra], axis=0)
    normed = normed_long[HALO:]
    marks = jnp.concatenate([halo_seg, seg_main, seg_first + 100, seg_last + 200])
    same = [(marks[HALO - k : -k] == marks[HALO:]).astype(f32)[:, None] for k in range(1, 4)]
    mask = jnp.concatenate(same + [jnp.zeros((rows, 5), f32)], axis=1)
    mask_long = jnp.concatenate([mask[:main], jnp.ones((HALO, 8), f32), mask[main:], jnp.zeros((HALO, 8), f32)], axis=0)
    select_extra = select_of(seg_extra) * (seg_extra != MIDDLE).astype(f32)[:, None]
    select = jnp.concatenate([select_main, select_extra], axis=0)
    select_long = jnp.concatenate([select_halo, select], axis=0)
    select_after = jnp.concatenate([select, select_halo], axis=0)
    pick_fill = (dot(normed_long, enter_square[1]) * select_long).astype(bf16)
    pick_gelu = (dot(normed, enter_square[0]) * select).astype(bf16)

    col_spec = lambda i: pl.BlockSpec((8, 2, per4, quarter), lambda b, s: (b, s[0], 0, i))
    out_spec = pl.BlockSpec((8, 4, per4, quarter), lambda b, s: (2 * s[0] + b, 0, 0, 2))
    gate_spec = pl.BlockSpec((16, 4, per4, glane), lambda b, s: (s[0], 0, 0, 3 * quarter // glane), pipeline_mode=pl.Buffered(1))
    side_col_spec = lambda i: pl.BlockSpec((32, 1, per4, quarter), lambda b, s: (0, 2 * s[0] + b, 0, i))
    rows_spec = lambda n: pl.BlockSpec((n, quarter), lambda b, s: (0, b))
    head_spec = lambda n: pl.BlockSpec((n, head), lambda h, s: (0, h))
    enter_spec = pl.BlockSpec((quarter, cols), lambda b, s: (b, 0))
    hidden_spec = lambda n: pl.BlockSpec((n, hcol), lambda j, s: (0, j))
    wide_block = (rows, halfw)
    small_block = (rows, cols)
    F = lambda *shape: (fixed(shape), (shape, f32))
    B = lambda *shape: (fixed(shape), (shape, bf16))
    layer = 2 * rows * halfw * width
    mib = 2**20

    gd_rows = ring_rows(grad_down_own)
    long = rows + HALO
    convolved, lat_gates = call(
        fill_kernel, (2,),
        [fixed((long, width)), side_col_spec(1), fixed((long, cols)), rows_spec(cols), fixed((rows, 8)), rows_spec(4),
         pl.BlockSpec((quarter, 2 * cols), lambda b, s: (b, 0))],
        [(rows_spec(rows), (wide_block, bf16)), F(rows, 2 * cols)],
        [pltpu.VMEM((long, quarter), f32)],
        core_at, (normed_long, near, pick_fill, leave_half[1], mask, taps, enter_gates), 12, (shard_far, *gd_rows[0][1:]),
    )
    pick_fill = pick_fill[HALO:]

    sides = lambda v: [half(v, c, 0), half(v, 1 - c, 0)]
    feed_select = [
        jnp.concatenate([ring_selects[0][:toks], sides(select_extra)[0], ring_selects[1][:toks], sides(select_extra)[1]], axis=0),
        jnp.concatenate([ring_selects[0][toks:], ring_selects[1][toks:]], axis=0),
    ]
    sig_in, sig_de, decays, state, prod, pick_in, pick_de = call(
        gates_kernel, (heads,),
        [head_spec(rows), fixed((rows, 2 * cols)), fixed((rows, 2 * cols)), fixed(small_block), gate_spec,
         head_spec(cols), head_spec(cols), fixed((rows, 8)), head_spec(1)],
        [(head_spec(rows), (wide_block, f32))] * 5 + [B(*small_block)] * 2,
        [pltpu.VMEM((rows, head), f32), pltpu.VMEM((halfw, 2 * head), bf16)],
        core_at, (convolved, lat_gates, swap(lat_gates), select, near, leave_half[2], leave_half[3], mask, rate), 12,
    )
    entering = chips_carry(jnp.stack([prod[main - 1], state[main - 1]]), False)[None, :]
    branch, slope = call(
        gelu_kernel, (2,),
        [fixed((rows, width)), side_col_spec(0), fixed(small_block), rows_spec(cols)],
        [(rows_spec(rows), (wide_block, f32))] * 2,
        [],
        core_at, (normed, near, pick_gelu, leave_half[0]), 12,
    )
    states, mixed, lat_out, out_mine, out_send, out_extra = call(
        out_kernel, (2,),
        [rows_spec(rows), rows_spec(rows), rows_spec(1), rows_spec(rows), out_spec, enter_spec, fixed((cols, width)), fixed(small_block)],
        [(rows_spec(rows), (wide_block, f32)), (rows_spec(rows), (wide_block, bf16)), F(*small_block),
         F(toks, width), B(toks + main, width), B(main, width)],
        [pltpu.VMEM((rows, width), f32), pltpu.VMEM((rows, quarter), bf16)],
        core_at, (state, prod, entering, branch, near, enter_half[4], leave_square[4], select), 15,
    )
    got = swap(out_send).astype(f32)
    residual = block_input + out_mine + got[:toks]
    residual_extra = x_extra + (out_extra.astype(f32) + got[toks:])
    n2_extra = norm_apply(residual_extra, norm_second)

    n2_rows = ring_rows(norm_apply(residual, norm_second))
    ring = 8 * toks
    anywhere = pl.BlockSpec(memory_space=pl.ANY)
    far_rows = far.shape[1]

    def feed(n2_pieces, gd_pieces, select, micros, waits=()):
        count = len(n2_pieces) // 2
        n = 2 * count * toks
        return call(
            functools.partial(ffn_kernel, count), (1,),
            [anywhere] * (4 * count)
            + [fixed(far.shape), fixed((cols, slotp)), fixed((cols, slotp)), fixed((slotp, cols)), fixed((width, cols)), fixed((cols, width)),
               fixed((n, cols))],
            [B(n // 2, width)] * 2 + [B(n, slotp)] * 3 + [B(n, cols)] * 4,
            [pltpu.VMEM((n, width), bf16), pltpu.VMEM((n, width), bf16), pltpu.SemaphoreType.DMA((2 * count,)), pltpu.SemaphoreType.DMA((2 * count,))],
            core_at,
            (*n2_pieces, *gd_pieces, far, leave_a, leave_b, enter_down, enter_widen, leave_narrow, select),
            micros, waits,
        )

    mix = lambda rows, extra: [rows[0][0], sides(extra)[0], rows[1][0], sides(extra)[1]]
    mine0, theirs0, *near_parts = feed(mix(n2_rows, n2_extra), mix(gd_rows, down_extra), feed_select[0], 25)
    mine1, theirs1, *far_parts = feed(n2_rows[0][1:] + n2_rows[1][1:], gd_rows[0][1:] + gd_rows[1][1:], feed_select[1], 37, (theirs0,))
    add = lambda a, b: a.astype(f32) + b.astype(f32)
    sums0 = add(mine0, swap(theirs0))

    eighth = main // 8
    extra_mine = sums0[toks:]
    extra_of = lambda k: lax.dynamic_slice_in_dim(extra_mine, jnp.remainder(y - k, 4) * eighth, eighth, axis=0)
    extra_total = line_back([extra_of(k) for k in range(4)]).astype(bf16)
    extra_half = line_order([extra_total] + [shift4(extra_total, YAX, by) for by in (1, 2, 3)], y).reshape(main // 2, -1)
    grad_n2_extra = both(extra_half, swap(extra_half), c).astype(f32)
    lat_side = jnp.concatenate([near_parts[3], near_parts[4]], axis=1)
    lat_sum = to_low(add(lat_side[toks : 2 * toks], swap(lat_side[3 * toks :])))
    lat_sum = line_sum(lat_sum, YAX).astype(bf16)
    lat_extra = both(lat_sum, swap(lat_sum), c)
    lgw_extra = lat_extra[:, :cols]
    pick_n_extra = lat_extra[:, cols:]

    sums1 = add(mine1, swap(theirs1)).astype(bf16)
    sums = [sums0[:toks]] + [sums1[k * toks : (k + 1) * toks] for k in range(3)]
    mid_spec = (pl.BlockSpec((rank, hcol), lambda j, s: (0, j)), ((rank, slotp), bf16))
    extra_spec = (pl.BlockSpec((cols, hcol), lambda j, s: (0, j)), ((cols, slotp), bf16))
    down, mid_a, mid_b, mid_n, mid_l, mid_e, ex_a, ex_b, ex_n = call(
        down_kernel, (4,),
        [anywhere] * 16 + [hidden_spec(4 * toks), hidden_spec(6 * toks)] * 3
        + [pl.BlockSpec((4, far_rows, wide2), lambda j, s: (j, 0, 0))]
        + [fixed((4 * toks, cols)), fixed((6 * toks, cols))] * 4 + [fixed((cols, width))],
        [B(ring, width)] + [mid_spec] * 3 + [B(rank, width)] * 2 + [extra_spec] * 3,
        [pltpu.VMEM((ring, width), f32), pltpu.VMEM((cols, hcol), f32), pltpu.VMEM((cols, width), f32),
         pltpu.VMEM((ring, width), bf16), pltpu.VMEM((ring, width), bf16), pltpu.SemaphoreType.DMA((8,)), pltpu.SemaphoreType.DMA((8,))],
        middle_at,
        (n2_rows[0][0], n2_rows[1][0], *n2_rows[0][1:], *n2_rows[1][1:], gd_rows[0][0], gd_rows[1][0], *gd_rows[0][1:], *gd_rows[1][1:],
         near_parts[2], far_parts[2], near_parts[0], far_parts[0], near_parts[1], far_parts[1], far,
         near_parts[5], far_parts[5], near_parts[6], far_parts[6], near_parts[4], far_parts[4], near_parts[3], far_parts[3], leave_narrow),
        19, (*sums[1:], extra_total),
    )
    ffn_mid = jnp.concatenate([mid_a, mid_b, mid_n, mid_l, mid_e], axis=1)
    mid_shape = ffn_mid.shape
    ffn_mid = lax.all_to_all(ffn_mid.reshape(16, -1, cols), PLANE, 0, 0, tiled=True)
    ffn_mid = to_low(jnp.sum(ffn_mid.astype(f32), axis=0))
    grad_n2 = tied(line_back(sums), ffn_mid)
    ffn_mid = lax.all_to_all(jnp.broadcast_to(ffn_mid[None], (16, *ffn_mid.shape)), PLANE, 0, 0, tiled=True).reshape(mid_shape)

    grad_residual = cotangent + norm_back(residual, norm_second, grad_n2)
    grad_residual_extra = down_extra.astype(f32) + norm_back(residual_extra, norm_second, grad_n2_extra)
    grad_out_own = grad_residual.astype(bf16)
    grad_out = jnp.concatenate([both(grad_out_own, swap(grad_out_own), c), grad_residual_extra.astype(bf16)], axis=0)
    down_mine = jnp.concatenate([down[:toks], down[2 * toks : 5 * toks]], axis=0)
    down_theirs = jnp.concatenate([down[toks : 2 * toks], down[5 * toks :]], axis=0)
    down_total = tied(add(down_mine, swap(down_theirs)), grad_out)
    down_sums = [down_total[k * toks : (k + 1) * toks] for k in range(4)]
    block_output = residual + line_back(down_sums)
    grad_gelu, lg_out, back, trail = call(
        functools.partial(outback_kernel, main), (2,),
        [fixed((rows, width)), out_spec, fixed((cols, width)), enter_spec, fixed(small_block)] + [rows_spec(rows)] * 4,
        [(rows_spec(rows), (wide_block, bf16)), B(*small_block)] + [(rows_spec(rows), (wide_block, f32))] * 2,
        [pltpu.VMEM((rows, quarter), f32)],
        core_at, (grad_out, near, leave_square[4], enter_half[4], select, states, branch, slope, decays), 18,
    )
    coming = chips_carry(jnp.stack([decays[0] * trail[0], decays[0] * back[0]]), True)[None, :]
    gelu_part, lat_gelu = call(
        geluback_kernel, (4,),
        [fixed(wide_block), col_spec(0), fixed((cols, halfw)), enter_spec, fixed(small_block)],
        [(rows_spec(main), ((main, width), f32)), F(*small_block)],
        [pltpu.VMEM(small_block, bf16)],
        core_at, (grad_gelu, near, leave_half[0], enter_square[0], select), 12,
    )

    grad_in, grad_de, base, lat_gates = call(
        gateback_kernel, (heads,),
        [head_spec(rows), head_spec(rows), head_spec(1), head_spec(rows), head_spec(1)] + [head_spec(rows)] * 4
        + [fixed((rows, 8)), head_spec(1), gate_spec, head_spec(cols), head_spec(cols)],
        [(head_spec(rows), (wide_block, bf16))] * 2 + [(head_spec(rows), (wide_block, f32)), F(rows, 2 * cols)],
        [pltpu.VMEM((rows + 8, head), f32), pltpu.VMEM((halfw, 2 * head), bf16)],
        core_at, (back, trail, coming, states, entering, convolved, sig_in, sig_de, decays, mask, rate, near, leave_half[2], leave_half[3]),
        8,
    )

    share = -(-width // 7 // 128) * 128
    share_of = lambda v: lax.dynamic_slice_in_dim(jnp.pad(v, ((0, 0), (0, 8 * share - width))), member * share, share, axis=1)
    lanes_all = 3 * slotp + 2 * share
    (packed,) = call(
        pack_kernel, (1,),
        [fixed((cols, slotp))] * 3 + [fixed((main, cols))] * 2 + [fixed((main, share))] * 2 + [fixed((rank, 3 * slotp + 2 * width))],
        [B(cols + 3 * rank, lanes_all)], [], core_at,
        (ex_a, ex_b, ex_n, pick_n_extra, lgw_extra, share_of(down_extra), share_of(n2_extra), ffn_mid), 3, (base,),
    )
    ffn_all = lax.all_gather(packed, RING, axis=0)

    halo_base = chip_shift(base[:HALO], -1)
    halo_lat = chip_shift(lat_gates[:HALO], -1)
    halo_other = chip_shift(lat_gates[:HALO], -1, cross=True)
    grad_fill, lg_in, lg_de, lat_fill, normed_mine, normed_theirs = call(
        fillback_kernel, (4,),
        [fixed(wide_block), fixed((rows, 2 * cols)), fixed((rows, 2 * cols)), fixed((HALO, halfw)), fixed((HALO, 2 * cols)), fixed((HALO, 2 * cols)),
         fixed((rows + HALO, cols)), fixed((rows + 2 * HALO, 8)), fixed((4, halfw)), fixed((halfw, cols)), fixed((halfw, cols)), fixed((cols, halfw)),
         col_spec(1), enter_spec, rows_spec(main)],
        [B(*wide_block), B(*small_block), B(*small_block), F(*small_block),
         (rows_spec(toks), ((toks, width), f32)), (rows_spec(toks), ((toks, width), bf16))],
        [pltpu.VMEM((rows + 2 * HALO, halfw), f32), pltpu.VMEM((HALO, 2 * cols), bf16), pltpu.VMEM((main, cols), bf16), pltpu.VMEM((main, quarter), f32)],
        core_at,
        (base, lat_gates, swap(lat_gates), halo_base, halo_lat, halo_other, select_after, mask_long, taps, enter_half[2], enter_half[3],
         leave_half[1], near, enter_square[1], gelu_part),
        12,
    )

    lat_all = jnp.concatenate([lat_gelu, lat_fill, lat_out], axis=1)
    lat_all = lat_all + swap(lat_all)
    lg_gelu = (lat_all[:, :cols] * select).astype(bf16)
    lg_fill = (lat_all[:, cols : 2 * cols] * select).astype(bf16)
    pick_out = (lat_all[:, 2 * cols :] * select).astype(bf16)
    normed_half = half(normed, c, 1)
    pairs = [
        (lg_gelu, normed_half), (lg_fill, normed_half), (lg_in, convolved), (lg_de, convolved), (lg_out, mixed),
        (pick_gelu, grad_gelu), (pick_fill, grad_fill), (pick_in, grad_in), (pick_de, grad_de), (pick_out, half(grad_out, c, 1)),
    ]
    part_spec = lambda n, i: pl.BlockSpec((main, n), lambda *_: (i, 0), pipeline_mode=pl.Buffered(1))
    operands = [v for pair in pairs for v in pair]
    (mid,) = call(
        functools.partial(mids_kernel, 10), (1,),
        [part_spec(cols, 0), part_spec(halfw, 0)] * 10,
        [B(10 * rank, halfw)],
        [pltpu.VMEM((cols, halfw), f32)],
        middle_at, operands, 6,
    )
    mid_own = mid
    shape = mid.shape
    mid = lax.all_to_all(mid.reshape(64, -1, cols), CHIPS, 0, 0, tiled=True)
    mid = to_low(jnp.sum(mid.astype(f32), axis=0))
    mid = lax.all_to_all(jnp.broadcast_to(mid[None], (64, *mid.shape)), CHIPS, 0, 0, tiled=True).reshape(shape)

    operands = [*[v for pair in pairs[:5] for v in pair[::-1]], *[v for pair in pairs[5:] for v in pair]]
    enter_extra, leave_extra = call(
        functools.partial(extras_kernel, 5), (1,),
        [part_spec(halfw, 1), part_spec(cols, 1)] * 5 + [part_spec(cols, 1), part_spec(halfw, 1)] * 5,
        [B(5, halfw, cols), B(5, cols, halfw)],
        [],
        core_at, operands, 6, (mid_own,),
    )
    (grad_leave_widen,) = call(
        wide_kernel, (8,),
        [fixed((rank, cols)), fixed((units, 8 * chunk)), pl.BlockSpec((8, cols, hcol), lambda i, s: (0, 0, i)), pl.BlockSpec((8, rank, hcol), lambda i, s: (0, cols // rank, i))],
        [(pl.BlockSpec((cols, block), lambda i, s: (0, i)), ((cols, 2 * ff), f32))],
        [], core_at, (one_hot, spread_one, ffn_all, ffn_all), 12, (mid_own,),
    )
    (grad_enter_narrow,) = call(
        enter_kernel, (4,),
        [fixed((rank, cols)), fixed((units, 8 * chunk)), pl.BlockSpec((8, cols, hcol), lambda i, s: (0, 0, 8 + i)), pl.BlockSpec((8, rank, hcol), lambda i, s: (0, cols // rank, 8 + i))],
        [(pl.BlockSpec((block, cols), lambda i, s: (i, 0)), ((ff, cols), f32))],
        [], core_at, (one_hot, spread_one, ffn_all, ffn_all), 7, (mid_own,),
    )
    grad_normed = normed_mine + swap(normed_theirs).astype(f32)
    input_grad = grad_residual + norm_back(block_input, norm_first, grad_normed)
    eye = jnp.eye(cols, dtype=bf16)
    share_spec = lambda i: pl.BlockSpec((8, cols, share), lambda *_: (0, 0, 3 * slotp // share + i))
    mid_rows = lambda i: pl.BlockSpec((8, rank, lanes_all), lambda *_: (0, cols // rank + i, 0))
    grad_leave_narrow, grad_enter_widen = call(
        shares_kernel, (1,),
        [fixed((rank, cols)), fixed((cols, cols)), share_spec(0), share_spec(1)] + [mid_rows(i) for i in range(3)],
        [F(cols, width), F(width, cols)],
        [], core_at, (one_hot, eye) + (ffn_all,) * 5, 4, (mid_own,),
    )
    per_k = lambda *shape: pl.BlockSpec((1,) + shape, lambda k, s: (k,) + (0,) * len(shape))
    mid_e_spec = pl.BlockSpec((rank, halfw), lambda k, s: (k, 0))
    mid_l_spec = pl.BlockSpec((rank, halfw), lambda k, s: (5 + k, 0))
    mid_other = swap(mid)
    grad_enter_square, grad_leave_square = call(
        square_kernel, (5,),
        [fixed((rank, cols)), per_k(halfw, cols), per_k(halfw, cols), per_k(cols, halfw), per_k(cols, halfw),
         mid_e_spec, mid_e_spec, mid_l_spec, mid_l_spec],
        [(per_k(width, cols), ((5, width, cols), f32)), (per_k(cols, width), ((5, cols, width), f32))],
        [], core_at, (one_hot, enter_extra, swap(enter_extra), leave_extra, swap(leave_extra), mid, mid_other, mid, mid_other), 9,
    )
    return (
        block_output,
        input_grad,
        grad_enter_square,
        grad_leave_square,
        grad_enter_widen,
        grad_leave_widen,
        grad_enter_narrow,
        grad_leave_narrow,
    )


def solution(mesh):
    split = Mesh(mesh.devices.reshape(SIZES), AXES)
    by_row = P(AXES, None)
    return jax.shard_map(
        per_device,
        mesh=split,
        in_specs=(by_row, by_row, P(AXES), P(), P(), P(), P(), P()) + (by_row,) * 7 + (P(),) * 6,
        out_specs=(by_row, by_row, P(), P(), P(), P(), P(), P()),
        check_vma=False,
    )
```

```python
import functools
import jax
import jax.numpy as jnp
from jax import lax
from jax.experimental import pallas as pl
from jax.experimental.pallas import tpu as pltpu
from jax.sharding import Mesh, PartitionSpec as P

HEADS = 10
ADAPTERS = 8
HALO = 16
MIDDLE = 3
AXES = ("z", "x", "v", "u", "c")
SIZES = (4, 4, 2, 2, 2)
YAX = ("v", "u")
RING = ("v", "u", "c")
PLANE = ("z", "x")
QUAD = ("u", "c")
CHIPS = ("z", "x", "v", "u")
VMEM = 56 * 2**20

eps_norm = 1e-06
floor_scale = 0.001
bf16 = jnp.bfloat16
f32 = jnp.float32


def dot(a, b):
    return jnp.dot(a, b, preferred_element_type=f32)


def dot_nt(a, b):
    return lax.dot_general(a, b, (((1,), (1,)), ((), ())), preferred_element_type=f32)


def dot_tn(a, b):
    return lax.dot_general(a, b, (((0,), (0,)), ((), ())), preferred_element_type=f32)


def low(v):
    return lax.reduce_precision(v, 8, 7)


def to_low(v):
    return low(v).astype(bf16)


def norm_scale(values):
    return lax.rsqrt(jnp.mean(values * values, axis=-1, keepdims=True) + eps_norm)


def norm_apply(values, gain):
    return (values * norm_scale(values) * gain).astype(bf16)


def norm_back(values, gain, grad):
    s = norm_scale(values)
    gq = gain * grad
    return s * gq - values * (s * s * s) * jnp.mean(values * gq, axis=-1, keepdims=True)


def sigmoid(v):
    return 1.0 / (1.0 + jnp.exp(-v))


def gelu_parts(a):
    k = 0.7978845608028654
    a2 = a * a
    th = jnp.tanh(k * (a + 0.044715 * a2 * a))
    value = 0.5 * a * (1.0 + th)
    slope = 0.5 * (1.0 + th) + 0.5 * a * (1.0 - th * th) * (k * (1.0 + 3.0 * 0.044715 * a2))
    return value, slope


def swap(v):
    return lax.ppermute(v, "c", [(0, 1), (1, 0)])


def shift4(v, axis, by):
    return lax.ppermute(v, axis, [(i, (i + by) % 4) for i in range(4)])


def chip_shift(v, by, cross=False):
    chips = 64
    pairs = [
        (2 * p + c, 2 * (p + by) + (1 - c if cross else c))
        for p in range(chips)
        for c in range(2)
        if 0 <= p + by < chips
    ]
    return lax.ppermute(v, AXES, pairs)


def both(own, other, c):
    rows = own.shape[0]
    three = jnp.concatenate([own, other, own], axis=0)
    return lax.dynamic_slice_in_dim(three, c * rows, 2 * rows, axis=0)


def half(v, c, axis):
    size = v.shape[axis] // 2
    return lax.dynamic_slice_in_dim(v, c * size, size, axis=axis)


def after(first, *values):
    held = lax.optimization_barrier((first, *values))[1:]
    return held[0] if len(held) == 1 else held


def tied(value, other):
    return value + other[(0,) * other.ndim].astype(f32) * 0.0


def line_order(parts, y):
    back = parts[::-1]
    twice = jnp.stack(back + back)
    return lax.dynamic_slice_in_dim(twice, 3 - y, 4, axis=0)


def call(kernel, grid, ins, outs, scratch, scalars, args, micros, waits=()):
    count = len(args)

    def body(s_ref, *refs):
        kernel(s_ref, *refs[:count], *refs[count + len(waits) :])

    ins = list(ins) + [pl.BlockSpec(memory_space=pl.ANY)] * len(waits)
    args = (*args, *waits)
    return pl.pallas_call(
        body,
        grid_spec=pltpu.PrefetchScalarGridSpec(
            num_scalar_prefetch=1,
            grid=grid,
            in_specs=ins,
            out_specs=[spec for spec, _ in outs],
            scratch_shapes=scratch,
        ),
        out_shape=[jax.ShapeDtypeStruct(*shape) for _, shape in outs],
        compiler_params=pltpu.CompilerParams(vmem_limit_bytes=VMEM),
        cost_estimate=pl.CostEstimate(flops=int(micros * 1e9), bytes_accessed=int(micros * 2e6), transcendentals=0),
    )(scalars, *args)


def fixed(shape):
    return pl.BlockSpec(shape, lambda *_: (0,) * len(shape), pipeline_mode=pl.Buffered(1))


def scan_rows(d_ref, p_ref, s_ref, q_ref):
    rows, width = d_ref.shape
    row = lax.broadcasted_iota(jnp.int32, (8, width), 0)

    def tile(i, carry):
        state, product = carry
        at = pl.ds(pl.multiple_of(i * 8, 8), 8)
        a = d_ref[at, :]
        b = p_ref[at, :]
        for s in (1, 2, 4):
            b = a * jnp.where(row >= s, pltpu.roll(b, s, 0), 0.0) + b
            a = a * jnp.where(row >= s, pltpu.roll(a, s, 0), 1.0)
        value = b + a * state
        through = a * product
        s_ref[at, :] = value
        q_ref[at, :] = through
        return value[7:8, :], through[7:8, :]

    lax.fori_loop(
        0, rows // 8, tile, (jnp.zeros((1, width), f32), jnp.ones((1, width), f32)), unroll=8
    )


def scan_rows_back(d_ref, g_ref, s_ref, q_ref, main):
    rows, width = d_ref.shape
    row = lax.broadcasted_iota(jnp.int32, (8, width), 0)

    def tile(i, carry):
        state, product, after_row = carry
        at = pl.ds(pl.multiple_of(i * 8, 8), 8)
        d = d_ref[at, :]
        b = g_ref[at, :]
        a = jnp.where(row < 7, pltpu.roll(d, 7, 0), after_row)
        for s in (1, 2, 4):
            b = a * jnp.where(row < 8 - s, pltpu.roll(b, 8 - s, 0), 0.0) + b
            a = a * jnp.where(row < 8 - s, pltpu.roll(a, 8 - s, 0), 1.0)
        value = b + a * state
        through = a * product
        s_ref[at, :] = value
        q_ref[at, :] = through
        return value[0:1, :], through[0:1, :], d[0:1, :]

    zero = jnp.zeros((1, width), f32)
    one = jnp.ones((1, width), f32)
    last, cut = rows // 8 - 1, main // 8
    lax.fori_loop(0, last + 1 - cut, lambda k, t: tile(last - k, t), (zero, zero, one), unroll=8)
    lax.fori_loop(0, cut, lambda k, t: tile(cut - 1 - k, t), (zero, one, one), unroll=8)


def tile_of(w, i):
    block = w[:, i]
    return block.reshape(block.shape[0] * block.shape[1], block.shape[2])


def ends_kernel(stretches, s_ref, near_ref, gain_ref, x_ref, normed_ref, down_ref, marks_ref, hold_ref):
    toks = x_ref.shape[0] // 2
    quarter = x_ref.shape[1] // 4
    reach = quarter + marks_ref.shape[1]
    size = 8 * stretches
    for core in range(2):
        for p in range(16):
            for h in range(stretches):
                row = p * size + h * 8
                for y in range(4):
                    block = near_ref[2 * p + y // 2, 2 * (y % 2) + core, :, h * reach : (h + 1) * reach].astype(f32)
                    cols = slice(y * quarter, (y + 1) * quarter)
                    if row < toks:
                        x_ref[core * toks + row : core * toks + row + 8, cols] = block[:, :quarter]
                        if y == 0:
                            marks_ref[core * toks + row : core * toks + row + 8, :] = block[:, quarter:]
                    else:
                        to = core * toks + row - toks
                        hold_ref[to : to + 8, cols] = block[:, :quarter]
    down_ref[...] = hold_ref[...].astype(bf16)
    x = x_ref[...]
    normed_ref[...] = norm_apply(x, gain_ref[...])


def pack_kernel(s_ref, exa_ref, exb_ref, exn_ref, pick_ref, lg_ref, down_ref, n2_ref, mid_ref, out_ref):
    cols, wide = exa_ref.shape
    rank = mid_ref.shape[0]
    lanes = out_ref.shape[1]
    share = down_ref.shape[1]
    for i, ref in enumerate((exa_ref, exb_ref, exn_ref)):
        out_ref[:cols, i * wide : (i + 1) * wide] = ref[...]
    at = 3 * wide
    out_ref[:cols, at : at + share] = dot_tn(pick_ref[...], down_ref[...]).astype(bf16)
    out_ref[:cols, at + share :] = dot_tn(lg_ref[...], n2_ref[...]).astype(bf16)
    total = mid_ref.shape[1]
    for i in range(3):
        lo, hi = i * lanes, min((i + 1) * lanes, total)
        rows = slice(cols + i * rank, cols + (i + 1) * rank)
        out_ref[rows, : hi - lo] = mid_ref[:, lo:hi]
        if hi - lo < lanes:
            out_ref[rows, hi - lo :] = jnp.zeros((rank, lanes - hi + lo), bf16)


def fill_kernel(c_ref, x_ref, w_ref, first_ref, select_ref, leave_ref, mask_ref, taps_ref, enter_ref, conv_ref, lat_ref, pick_ref, acc_ref):
    rows, width = conv_ref.shape

    @pl.when(pl.program_id(0) == 0)
    def _():
        pick_ref[...] = (dot(x_ref[...], first_ref[...]) * select_ref[...]).astype(bf16)

    acc_ref[...] = dot(x_ref[...], tile_of(w_ref, 0)) + dot(pick_ref[...], leave_ref[...])
    step = width // 5
    for j in range(5):
        at = slice(j * step, (j + 1) * step)
        total = taps_ref[0:1, at] * acc_ref[HALO : HALO + rows, at]
        for k in range(1, taps_ref.shape[0]):
            total = total + taps_ref[k : k + 1, at] * acc_ref[HALO - k : HALO - k + rows, at] * mask_ref[:, k - 1 : k]
        conv_ref[:, at] = total.astype(bf16)

    @pl.when(pl.program_id(0) == 0)
    def _():
        lat_ref[...] = jnp.zeros_like(lat_ref)

    lat_ref[...] += dot(conv_ref[...], enter_ref[...])


def gate_weights(w_ref, hold_ref):
    @pl.when(pl.program_id(0) == 0)
    def _():
        wide = w_ref.shape[3]
        for i in range(4):
            hold_ref[:, i * wide : (i + 1) * wide] = tile_of(w_ref, i)

    head = 2 * w_ref.shape[3]
    at = pl.ds(pl.multiple_of(pl.program_id(0) * head, head), head)
    return hold_ref[at, :head], hold_ref[at, head:]


def gates_kernel(
    c_ref, conv_ref, own_ref, other_ref, select_ref, w_ref, leave_in_ref, leave_de_ref, mask_ref, rate_ref,
    sin_ref, sde_ref, dec_ref, state_ref, prod_ref, pick_in_ref, pick_de_ref, push_ref, hold_ref,
):
    cols = select_ref.shape[1]
    inner, decay = gate_weights(w_ref, hold_ref)

    @pl.when(pl.program_id(0) == 0)
    def _():
        lat = own_ref[...] + other_ref[...]
        select = select_ref[...]
        pick_in_ref[...] = (lat[:, :cols] * select).astype(bf16)
        pick_de_ref[...] = (lat[:, cols:] * select).astype(bf16)

    retain = mask_ref[:, 0:1]
    conv = conv_ref[...]
    sig_in = sigmoid(dot(conv, inner) + dot(pick_in_ref[...], leave_in_ref[...]))
    sig_de = sigmoid(dot(conv, decay) + dot(pick_de_ref[...], leave_de_ref[...]))
    raw = jnp.exp(-8.0 * rate_ref[...] * sig_de)
    scale = jnp.where(retain > 0.5, jnp.sqrt(jnp.maximum(1.0 - raw * raw, floor_scale)), 1.0)
    sin_ref[...] = sig_in
    sde_ref[...] = sig_de
    dec_ref[...] = raw * retain
    push_ref[...] = conv.astype(f32) * sig_in * scale
    scan_rows(dec_ref, push_ref, state_ref, prod_ref)


def gelu_kernel(c_ref, x_ref, w_ref, first_ref, select_ref, leave_ref, value_ref, slope_ref, pick_ref):
    @pl.when(pl.program_id(0) == 0)
    def _():
        pick_ref[...] = (dot(x_ref[HALO:, :], first_ref[...]) * select_ref[...]).astype(bf16)

    pre = dot(x_ref[HALO:, :], tile_of(w_ref, 0)) + dot(pick_ref[...], leave_ref[...])
    value, slope = gelu_parts(pre)
    value_ref[...] = value
    slope_ref[...] = slope


def out_kernel(
    c_ref, state_ref, prod_ref, entering_ref, branch_ref, w_ref, enter_ref, leave_ref, select_ref,
    states_ref, mixed_ref, lat_ref, mine_ref, send_ref, extra_ref, acc_ref, hold_ref,
):
    b = pl.program_id(0)
    q = w_ref.shape[3]
    states = state_ref[...] + prod_ref[...] * entering_ref[...]
    states_ref[...] = states
    hold_ref[...] = (branch_ref[...] * states).astype(bf16)
    mixed_ref[...] = hold_ref[...]

    @pl.when(b == 0)
    def _():
        lat_ref[...] = jnp.zeros_like(lat_ref)
        acc_ref[...] = jnp.zeros_like(acc_ref)

    lat_ref[...] += dot(hold_ref[...], enter_ref[...])
    for i in range(4):
        acc_ref[:, i * q : (i + 1) * q] += dot(hold_ref[...], tile_of(w_ref, i))

    @pl.when(b == pl.num_programs(0) - 1)
    def _():
        acc_ref[...] += dot((lat_ref[...] * select_ref[...]).astype(bf16), leave_ref[...])
        rows = mine_ref.shape[0]
        at = pl.multiple_of(c_ref[0] * rows, rows)
        mine_ref[...] = acc_ref[pl.ds(at, rows), :]
        send_ref[:rows, :] = acc_ref[pl.ds(pl.multiple_of(rows - at, rows), rows), :].astype(bf16)
        extra = acc_ref[2 * rows :, :].astype(bf16)
        send_ref[rows:, :] = extra
        extra_ref[...] = extra


def narrow_block(far_ref, j, top):
    wide = far_ref.shape[2]
    tail = wide // 4
    low_rows = (far_ref.shape[1] - top) // 5
    planes = pl.ds(4 * j, 4)
    main = far_ref[planes, top : top + 4 * low_rows, :].reshape(16 * low_rows, wide)
    pieces = []
    for p in range(4):
        rows = far_ref[4 * j + p, top + 4 * low_rows :, :]
        pieces += [rows[:, k * tail : (k + 1) * tail] for k in range(4)]
    return main, jnp.concatenate(pieces, axis=0)


def fetch(refs, hold_ref, sems):
    size = refs[0].shape[0]
    return [pltpu.make_async_copy(r, hold_ref.at[pl.ds(i * size, size), :], sems.at[i]) for i, r in enumerate(refs)]


def ffn_kernel(count, s_ref, *refs):
    n2_refs, gd_refs = refs[:count], refs[count : 2 * count]
    far_hbm, la_ref, lb_ref, en_ref, ew_ref, ln_ref, select_ref = refs[2 * count : 2 * count + 7]
    gn_ref, ga_ref, gb_ref, hid_ref, lgw_ref, pickn_ref, pickw_ref, lgn_ref = refs[2 * count + 7 : 2 * count + 15]
    n2_hold, gd_hold, far_ref, n2_sems, gd_sems, far_sems = refs[2 * count + 15 :]
    width = gn_ref.shape[1]
    slotp = hid_ref.shape[1]
    step = slotp // 4
    wide = far_ref.shape[2]
    top = width // 16

    def far_copies(j):
        at = pl.ds(pl.multiple_of(j * step, step), step)
        at_b = pl.ds(pl.multiple_of(slotp + j * step, step), step)
        planes = pl.ds(4 * j, 4)
        places = [(slice(None), pl.ds(0, top), at), (slice(None), pl.ds(0, top), at_b), (planes, pl.ds(top, far_ref.shape[1] - top), slice(None))]
        return [pltpu.make_async_copy(far_hbm.at[p], far_ref.at[p], far_sems.at[j, i]) for i, p in enumerate(places)]

    n2_copies = fetch(n2_refs, n2_hold, n2_sems)
    gd_copies = fetch(gd_refs, gd_hold, gd_sems)
    for copy in n2_copies + gd_copies:
        copy.start()
    for j in range(4):
        for copy in far_copies(j):
            copy.start()
    for copy in n2_copies + gd_copies:
        copy.wait()
    select = select_ref[...]
    pickw_ref[...] = (dot(n2_hold[...], ew_ref[...]) * select).astype(bf16)
    lgn_ref[...] = (dot_nt(gd_hold[...], ln_ref[...]) * select).astype(bf16)

    def hidden(j, _):
        for copy in far_copies(j):
            copy.wait()
        at = pl.ds(pl.multiple_of(j * step, step), step)
        at_b = pl.ds(pl.multiple_of(slotp + j * step, step), step)
        a = dot(n2_hold[...], far_ref[:, :top, at].reshape(width, step)) + dot(pickw_ref[...], la_ref[:, at])
        up = dot(n2_hold[...], far_ref[:, :top, at_b].reshape(width, step)) + dot(pickw_ref[...], lb_ref[:, at])
        main, last = narrow_block(far_ref, j, top)
        grad = dot_nt(gd_hold[:, :wide], main) + dot_nt(gd_hold[:, wide:], last) + dot_nt(lgn_ref[...], en_ref[at, :])
        act, slope = gelu_parts(a)
        hid_ref[:, at] = (act * up).astype(bf16)
        ga_ref[:, at] = (slope * up * grad).astype(bf16)
        gb_ref[:, at] = (act * grad).astype(bf16)
        return 0

    lax.fori_loop(0, 4, hidden, 0)
    lgw_ref[...] = ((dot_nt(ga_ref[...], la_ref[...]) + dot_nt(gb_ref[...], lb_ref[...])) * select).astype(bf16)
    pickn_ref[...] = (dot(hid_ref[...], en_ref[...]) * select).astype(bf16)
    part = width // 4

    def back(q, _):
        at = pl.ds(pl.multiple_of(q * part, part), part)
        planes = pl.ds(4 * q, 4)
        total = dot_nt(ga_ref[...], far_ref[planes, :top, :slotp].reshape(part, slotp))
        total += dot_nt(gb_ref[...], far_ref[planes, :top, slotp:].reshape(part, slotp))
        gn_ref[:, at] = (total + dot_nt(lgw_ref[...], ew_ref[at, :])).astype(bf16)
        return 0

    lax.fori_loop(0, 4, back, 0)


def down_kernel(s_ref, *refs):
    n2_refs, gd_refs = refs[:8], refs[8:16]
    hid, ga, gb, pick, lgn, pickn, lgw = [refs[16 + 3 * i : 19 + 3 * i] for i in range(7)]
    far_ref, ln_ref = refs[37:39]
    down_ref, mida_ref, midb_ref, midn_ref, midl_ref, mide_ref, exa_ref, exb_ref, exn_ref = refs[39:48]
    acc_ref, hold_ref, wide_ref, n2_hold, gd_hold, n2_sems, gd_sems = refs[48:]
    j = pl.program_id(0)
    rank = mida_ref.shape[0]
    piece = n2_refs[0].shape[0]
    here = pl.ds(pl.multiple_of(s_ref[0] * rank, rank), rank)
    main, last = narrow_block(far_ref, 0, far_ref.shape[1] * 2 // 3)
    cut = main.shape[1]
    ring_of = lambda v: jnp.concatenate([v[0][:piece, :], v[0][2 * piece : 3 * piece, :], v[1][...], v[2][...]], axis=0)
    rest_of = lambda v: jnp.concatenate([v[0][piece : 2 * piece, :], v[0][3 * piece :, :]], axis=0)
    n2_copies = fetch(n2_refs, n2_hold, n2_sems)
    gd_copies = fetch(gd_refs, gd_hold, gd_sems)

    @pl.when(j == 0)
    def _():
        for copy in n2_copies + gd_copies:
            copy.start()
        acc_ref[...] = dot(ring_of(pickn), ln_ref[...])

    hidden = ring_of(hid)
    acc_ref[:, :cut] += dot(hidden, main)
    acc_ref[:, cut:] += dot(hidden, last)
    for left, right, out_ref, extra_ref in ((pick, ga, mida_ref, exa_ref), (pick, gb, midb_ref, exb_ref), (lgn, hid, midn_ref, exn_ref)):
        hold_ref[...] = dot_tn(ring_of(left), ring_of(right))
        out_ref[...] = hold_ref[here, :].astype(bf16)
        extra_ref[...] = dot_tn(rest_of(left), rest_of(right)).astype(bf16)

    @pl.when(j == pl.num_programs(0) - 1)
    def _():
        down_ref[...] = acc_ref[...].astype(bf16)
        for copy in n2_copies + gd_copies:
            copy.wait()
        wide_ref[...] = dot_tn(ring_of(pickn), gd_hold[...])
        midl_ref[...] = wide_ref[here, :].astype(bf16)
        wide_ref[...] = dot_tn(ring_of(lgw), n2_hold[...])
        mide_ref[...] = wide_ref[here, :].astype(bf16)


def outback_kernel(
    main, c_ref, go_ref, w_ref, leave_ref, enter_ref, select_ref, states_ref, branch_ref, slope_ref, dec_ref,
    gg_ref, lg_ref, state_ref, prod_ref, gs_ref,
):
    b = pl.program_id(0)
    q = w_ref.shape[3]

    @pl.when(b == 0)
    def _():
        lg_ref[...] = (dot_nt(go_ref[...], leave_ref[...]) * select_ref[...]).astype(bf16)

    gm = dot_nt(lg_ref[...], enter_ref[...])
    for i in range(4):
        gm += dot_nt(go_ref[:, i * q : (i + 1) * q], tile_of(w_ref, i))
    gg_ref[...] = (slope_ref[...] * (gm * states_ref[...])).astype(bf16)
    gs_ref[...] = gm * branch_ref[...]
    scan_rows_back(dec_ref, gs_ref, state_ref, prod_ref, main)


def geluback_kernel(c_ref, g_ref, w_ref, leave_ref, enter_ref, select_ref, part_ref, lat_ref, lg_ref):
    b = pl.program_id(0)
    q = w_ref.shape[3]

    @pl.when(b == 0)
    def _():
        lat = dot_nt(g_ref[...], leave_ref[...])
        lat_ref[...] = lat
        lg_ref[...] = (lat * select_ref[...]).astype(bf16)

    rows = part_ref.shape[0]
    part = dot_nt(g_ref[:rows, :q], tile_of(w_ref, 0)) + dot_nt(g_ref[:rows, q : 2 * q], tile_of(w_ref, 1))
    part_ref[...] = part + dot_nt(lg_ref[:rows, :], enter_ref[...])


def gateback_kernel(
    c_ref, back_ref, trail_ref, coming_ref, states_ref, entering_ref, conv_ref, sin_ref, sde_ref, dec_ref, mask_ref, rate_ref,
    w_ref, leave_in_ref, leave_de_ref,
    gi_ref, gd_ref, base_ref, lat_ref, hold_ref, gate_ref,
):
    rows = conv_ref.shape[0]
    cols = leave_in_ref.shape[0]
    inner, decay = gate_weights(w_ref, gate_ref)
    retain = mask_ref[:, 0:1]
    hold_ref[7:8, :] = entering_ref[...]
    hold_ref[8:, :] = states_ref[...]
    rate = rate_ref[...]
    sig_in = sin_ref[...]
    sig_de = sde_ref[...]
    conv = conv_ref[...].astype(f32)
    carried = back_ref[...] + trail_ref[...] * coming_ref[...]
    raw = jnp.exp(-8.0 * rate * sig_de)
    grown = 1.0 - raw * raw
    scale = jnp.where(retain > 0.5, jnp.sqrt(jnp.maximum(grown, floor_scale)), 1.0)
    through = carried * conv
    gi = (through * scale * sig_in * (1.0 - sig_in)).astype(bf16)
    grad_grown = jnp.where((grown > floor_scale) & (retain > 0.5), through * sig_in * 0.5 / scale, 0.0)
    grad_log = carried * hold_ref[7 : 7 + rows, :] * dec_ref[...] - 2.0 * raw * raw * grad_grown
    gd = (grad_log * (-8.0 * rate) * sig_de * (1.0 - sig_de)).astype(bf16)
    gi_ref[...] = gi
    gd_ref[...] = gd
    base_ref[...] = carried * sig_in * scale + dot_nt(gi, inner) + dot_nt(gd, decay)

    @pl.when(pl.program_id(0) == 0)
    def _():
        lat_ref[...] = jnp.zeros_like(lat_ref)

    lat_ref[:, :cols] += dot_nt(gi, leave_in_ref[...])
    lat_ref[:, cols:] += dot_nt(gd, leave_de_ref[...])


def fillback_kernel(
    c_ref, base_ref, own_ref, other_ref, hbase_ref, hown_ref, hother_ref, select_ref, mask_ref, taps_ref, enter_in_ref, enter_de_ref, leave_ref,
    w_ref, enter_ref, before_ref,
    gf_ref, lgi_ref, lgd_ref, lat_ref, mine_ref, theirs_ref, gc_ref, hlg_ref, lg_ref, part_ref,
):
    b = pl.program_id(0)
    q = w_ref.shape[3]
    rows, width = base_ref.shape
    main = part_ref.shape[0]
    cols = lgi_ref.shape[1]

    @pl.when(b == 0)
    def _():
        lat = own_ref[...] + other_ref[...]
        hlat = hown_ref[...] + hother_ref[...]
        select = select_ref[:rows, :]
        hselect = select_ref[rows:, :]
        lgi_ref[...] = (lat[:, :cols] * select).astype(bf16)
        lgd_ref[...] = (lat[:, cols:] * select).astype(bf16)
        hlg_ref[:, :cols] = (hlat[:, :cols] * hselect).astype(bf16)
        hlg_ref[:, cols:] = (hlat[:, cols:] * hselect).astype(bf16)
        step = width // 5
        for j in range(5):
            at = slice(j * step, (j + 1) * step)
            ei = enter_in_ref[at, :]
            ed = enter_de_ref[at, :]
            here = base_ref[:, at] + dot_nt(lgi_ref[...], ei) + dot_nt(lgd_ref[...], ed)
            gc_ref[:main, at] = here[:main]
            gc_ref[main : main + HALO, at] = (
                hbase_ref[:, at] + dot_nt(hlg_ref[:, :cols], ei) + dot_nt(hlg_ref[:, cols:], ed)
            )
            gc_ref[main + HALO : rows + HALO, at] = here[main:]
            gc_ref[rows + HALO :, at] = jnp.zeros((HALO, step), f32)
            for lo, hi, to in ((0, main, 0), (main + HALO, rows + HALO, main)):
                total = taps_ref[0:1, at] * gc_ref[lo:hi, at]
                for k in range(1, taps_ref.shape[0]):
                    total = total + taps_ref[k : k + 1, at] * gc_ref[lo + k : hi + k, at] * mask_ref[lo + k : hi + k, k - 1 : k]
                gf_ref[to : to + hi - lo, at] = total.astype(bf16)
        lat = dot_nt(gf_ref[...], leave_ref[...])
        lat_ref[...] = lat
        lg_ref[...] = (lat[:main] * select_ref[:main, :]).astype(bf16)

    part = dot_nt(gf_ref[:main, :q], tile_of(w_ref, 0)) + dot_nt(gf_ref[:main, q : 2 * q], tile_of(w_ref, 1))
    part_ref[...] = before_ref[...] + part + dot_nt(lg_ref[...], enter_ref[...])
    own = mine_ref.shape[0]
    at = pl.multiple_of(c_ref[0] * own, own)
    mine_ref[...] = part_ref[pl.ds(at, own), :]
    theirs_ref[...] = part_ref[pl.ds(pl.multiple_of(own - at, own), own), :].astype(bf16)


def mids_kernel(count, s_ref, *refs):
    out_ref, hold_ref = refs[2 * count :]
    rank = out_ref.shape[0] // count
    here = pl.ds(pl.multiple_of(s_ref[0] * rank, rank), rank)
    for i in range(count):
        hold_ref[...] = dot_tn(refs[2 * i][...], refs[2 * i + 1][...])
        out_ref[i * rank : (i + 1) * rank, :] = hold_ref[here, :].astype(bf16)


def extras_kernel(count, s_ref, *refs):
    enter_ref, leave_ref = refs[4 * count :]
    for i in range(count):
        enter_ref[i] = dot_tn(refs[2 * i][...], refs[2 * i + 1][...]).astype(bf16)
    for i in range(count):
        k = 2 * count + 2 * i
        leave_ref[i] = dot_tn(refs[k][...], refs[k + 1][...]).astype(bf16)


def square_kernel(s_ref, one_ref, own_e_ref, other_e_ref, own_l_ref, other_l_ref, own_me_ref, other_me_ref, own_ml_ref, other_ml_ref, enter_ref, leave_ref):
    size = own_e_ref.shape[1]
    one = one_ref[...]
    for core, e_ref, l_ref, me_ref, ml_ref in (
        (s_ref[0], own_e_ref, own_l_ref, own_me_ref, own_ml_ref),
        (1 - s_ref[0], other_e_ref, other_l_ref, other_me_ref, other_ml_ref),
    ):
        at = pl.ds(pl.multiple_of(core * size, size), size)
        enter_ref[0, at, :] = e_ref[0].astype(f32) + dot_tn(me_ref[...], one)
        leave_ref[0, :, at] = l_ref[0].astype(f32) + dot_tn(one, ml_ref[...])


def unit_parts(one_ref, extra_ref, mid_ref, size):
    count = extra_ref.shape[0]
    cut = lambda ref, p: jnp.concatenate([ref[m, :, p * size : (p + 1) * size] for m in range(count)], axis=1)
    mid = jnp.concatenate([cut(mid_ref, p) for p in range(4)], axis=1)
    placed = dot_tn(one_ref[...], mid).astype(bf16)
    wide = count * size
    return jnp.concatenate([cut(extra_ref, p) + placed[:, p * wide : (p + 1) * wide] for p in range(4)], axis=0)


def wide_kernel(s_ref, one_ref, spread_ref, extra_ref, mid_ref, out_ref):
    cols = out_ref.shape[0]
    done = dot_nt(unit_parts(one_ref, extra_ref, mid_ref, spread_ref.shape[1] // 8), spread_ref[...])
    out_ref[...] = jnp.concatenate([done[p * cols : (p + 1) * cols] for p in range(4)], axis=1)


def enter_kernel(s_ref, one_ref, spread_ref, extra_ref, mid_ref, out_ref):
    units, size = spread_ref.shape
    cols = out_ref.shape[1]
    done = dot_nt(spread_ref[...], unit_parts(one_ref, extra_ref, mid_ref, size // 8))
    for p in range(4):
        out_ref[p * units : (p + 1) * units, :] = done[:, p * cols : (p + 1) * cols]


def shares_kernel(s_ref, one_ref, eye_ref, extra_l_ref, extra_e_ref, mid0_ref, mid1_ref, mid2_ref, leave_ref, enter_ref):
    one = one_ref[...]
    width = leave_ref.shape[1]
    share = extra_l_ref.shape[2]
    start = mid0_ref.shape[2] - 2 * share
    sums = []
    for ref in (mid0_ref, mid1_ref, mid2_ref):
        total = ref[0].astype(f32)
        for m in range(1, 8):
            total = total + ref[m].astype(f32)
        sums.append(total.astype(bf16))
    mid = jnp.concatenate([sums[0][:, start:], sums[1], sums[2]], axis=1)
    leave_ref[...] = dot_tn(one, mid[:, :width])
    enter_ref[...] = dot_tn(mid[:, width : 2 * width], one)
    for m in range(8):
        lo, hi = m * share, min((m + 1) * share, width)
        if lo < hi:
            leave_ref[:, lo:hi] += extra_l_ref[m, :, : hi - lo].astype(f32)
            enter_ref[lo:hi, :] += dot_tn(extra_e_ref[m], eye_ref[...])[: hi - lo]


def linked(former, latter):
    return (former[0] * latter[0], latter[0] * former[1] + latter[1])


def line_carry(value, axis, reverse):
    sign = -1 if reverse else 1
    here = lax.axis_index(axis)
    here = 3 - here if reverse else here
    came = {by: shift4(value, axis, sign * by) for by in (1, 2, 3)}
    unit = (jnp.ones_like(value[0]), jnp.zeros_like(value[0]))

    def take(so_far, by, valid):
        new = linked(so_far, (came[by][0], came[by][1]))
        return tuple(jnp.where(valid, a, b) for a, b in zip(new, so_far))

    enter = unit
    for by in (3, 2, 1):
        enter = take(enter, by, here >= by)
    total = linked(enter, (value[0], value[1]))
    for by in (3, 2, 1):
        total = take(total, by, here < by)
    return enter, jnp.stack(total)


def chips_carry(value, reverse):
    by_y, line = line_carry(value, YAX, reverse)
    by_x, plane = line_carry(line, "x", reverse)
    by_z, _ = line_carry(plane, "z", reverse)
    return linked(linked(by_z, by_x), by_y)[1]


def index_of(place):
    at = 0
    for i, n in zip(place, (4, 4, 4, 2)):
        at = at * n + i
    return at


def scatter_ends(payload, seg_lanes, c):
    reached = {0: [(0, 0, 0)], 1: [(3, 3, 3)]}
    width = payload.shape[1]
    payload = jnp.concatenate([payload, seg_lanes], axis=1)
    for axis in range(3):
        if axis < 2:
            size = payload.shape[0] // 4
            pieces = [payload[k * size : (k + 1) * size] for k in range(4)]
        else:
            size = width // 4
            pieces = [jnp.concatenate([payload[:, k * size : (k + 1) * size], payload[:, width:]], axis=1) for k in range(4)]
        total = jnp.where(c == 0, pieces[0], pieces[3])
        added = {0: [], 1: []}
        for hop in (2, 1, 3):
            pairs = []
            for core in (0, 1):
                for place in reached[core]:
                    to = list(place)
                    to[axis] = hop if core == 0 else 3 - hop
                    added[core].append(tuple(to))
                    pairs.append((index_of((*place, core)), index_of((*to, core))))
            total = total + lax.ppermute(jnp.where(c == 0, pieces[hop], pieces[3 - hop]), AXES, pairs)
        for core in (0, 1):
            reached[core] = reached[core] + added[core]
        payload = total
    return payload


def line_sum(v, axis):
    one, two, three = (shift4(v, axis, by).astype(f32) for by in (1, 2, 3))
    return (v.astype(f32) + two) + (one + three)


def ring_rows(own):
    parts = [own] + [shift4(own, YAX, by) for by in (1, 2, 3)]
    return parts, [swap(part) for part in parts]


def line_back(sums):
    total = sums[0]
    for by in (1, 2, 3):
        total = total + shift4(sums[by].astype(bf16), YAX, -by).astype(f32)
    return total


def per_device(
    block_input,
    cotangent,
    segments,
    adapter_index,
    norm_first,
    norm_second,
    conv_taps,
    decay_rate,
    gelu_proj,
    input_proj,
    inner_gate,
    decay_gate,
    output_proj,
    widen_proj,
    narrow_proj,
    enter_square,
    leave_square,
    enter_widen,
    leave_widen,
    enter_narrow,
    leave_narrow,
):
    c = lax.axis_index("c")
    y = lax.axis_index(YAX)
    member = lax.axis_index(RING)
    plane = lax.axis_index(PLANE)
    chip = lax.axis_index(("z", "x", "v", "u"))
    place = lax.axis_index(AXES)
    toks, width = block_input.shape
    halfw = width // 2
    quarter = width // 4
    heads = HEADS // 2
    head = width // HEADS
    cols = enter_square.shape[-1]
    rank = cols // ADAPTERS
    main = 2 * toks
    per = gelu_proj.shape[0]
    per4 = 4 * per
    ff = widen_proj.shape[1] // 2
    slot = ff // 8
    slotp = slot * 16 // 15
    wide2 = 2 * slotp
    hcol = slotp // 4
    per_n = narrow_proj.shape[0]
    chunk = slotp // 16
    glane = 2 * head // 4

    grad_down_own = cotangent.astype(bf16)
    seg_lanes = jnp.broadcast_to(jnp.tile(segments, 2).astype(bf16)[:, None], (2 * toks, cols))
    payload = jnp.concatenate([block_input.astype(bf16), grad_down_own], axis=0)
    is_end = (place == 0) | (place == 127)
    piece = scatter_ends(jnp.where(is_end, payload, jnp.zeros_like(payload)), jnp.where(is_end, seg_lanes, jnp.zeros_like(seg_lanes)), c)

    gates = jnp.concatenate([inner_gate, decay_gate], axis=1)
    quads = jnp.stack(
        [
            jnp.concatenate(
                [v[:, q * (v.shape[1] // 4) : (q + 1) * (v.shape[1] // 4)] for v in (gelu_proj, input_proj, output_proj, gates)],
                axis=1,
            )
            for q in range(4)
        ]
    )
    lanes = quads.shape[2]
    quads = lax.all_to_all(quads, QUAD, 0, 0, tiled=True).reshape(per4, lanes)
    reach = piece.shape[1]
    stretches = piece.shape[0] // 8
    piece = jnp.concatenate([piece[k * 8 : (k + 1) * 8] for k in range(stretches)], axis=1)
    piece = jnp.pad(piece, ((0, 0), (0, lanes - stretches * reach)))
    quads = jnp.concatenate([quads, piece], axis=0)
    near = lax.all_gather(quads[None], AXES, axis=0, tiled=True).reshape(32, 4, per4 + 8, lanes)

    block_input, segments, widen_proj, narrow_proj = after(quads, block_input, segments, widen_proj, narrow_proj)

    block = 4 * 8 * per_n
    bcols = 4 * 8 * chunk
    at_col = jnp.arange(bcols)
    unit = at_col % (4 * chunk) % chunk
    from_row = at_col % (4 * chunk) // chunk * (8 * per_n) + at_col // (4 * chunk) * per_n + unit
    spread = ((jnp.arange(block)[:, None] == from_row[None, :]) & (unit < per_n)[None, :]).astype(bf16)
    units = 8 * per_n
    at_unit = jnp.arange(8 * chunk)
    spread_one = (jnp.arange(units)[:, None] == (at_unit // chunk * per_n + at_unit % chunk)[None, :]) & (at_unit % chunk < per_n)[None, :]
    spread_one = spread_one.astype(bf16)
    pieces = widen_proj.reshape(per, 8, block).transpose(1, 0, 2).reshape(8 * per, block)
    pieces = dot(pieces, spread).astype(bf16).reshape(8, per, 8, hcol).transpose(2, 1, 0, 3)
    pieces = lax.all_to_all(pieces.reshape(8 * per, wide2), RING, 0, 0, tiled=True)
    rows_n = jnp.pad(narrow_proj, ((0, chunk - per_n), (0, 0)))
    tail_n = rows_n[:, wide2:].reshape(4, chunk // 4, width - wide2).transpose(1, 0, 2).reshape(chunk // 4, wide2)
    shard_far = jnp.concatenate([pieces, rows_n[:, :wide2], tail_n], axis=0)
    far = lax.all_gather(shard_far[None], PLANE, axis=0, tiled=True)

    middle_owner = adapter_index[MIDDLE]
    column_owner = jnp.arange(cols) // rank
    owner_of = jnp.arange(adapter_index.shape[0])
    one_hot = (jnp.arange(cols)[None, :] == (middle_owner * rank + jnp.arange(rank))[:, None]).astype(bf16)
    core_at = c.astype(jnp.int32).reshape(1)
    middle_at = middle_owner.reshape(1)

    def select_of(segs):
        owners = jnp.sum((segs[:, None] == owner_of[None, :]).astype(jnp.int32) * adapter_index[None, :], axis=1)
        return (owners[:, None] == column_owner[None, :]).astype(f32)

    taps = half(conv_taps, c, 1)
    rate = half(decay_rate, c, 0)[None, :]
    enter_half = half(enter_square, c, 1)
    leave_half = half(leave_square, c, 2)
    enter_gates = jnp.concatenate([enter_half[2], enter_half[3]], axis=1)

    rows = 2 * main
    normed_own = norm_apply(block_input, norm_first)
    normed_main = both(normed_own, swap(normed_own), c)
    normed_halo = chip_shift(normed_main[main - HALO :], 1)
    normed_long = jnp.concatenate([normed_halo, normed_main], axis=0)
    seg_main = both(segments, swap(segments), c)
    halo_seg = jnp.broadcast_to(jnp.where(chip > 0, MIDDLE, -1), (HALO,))
    select_main = select_of(seg_main)
    select_halo = jnp.broadcast_to((column_owner == middle_owner).astype(f32)[None, :], (HALO, cols))
    ring_segs = [jnp.concatenate(v) for v in ring_rows(segments)]
    ring_selects = [select_of(v) for v in ring_segs]

    my_spread = lax.dynamic_slice_in_dim(spread, member * hcol, hcol, axis=1)
    leave_wide = leave_widen.reshape(cols, 8, block).transpose(1, 0, 2).reshape(8 * cols, block)
    leave_wide = dot(leave_wide, my_spread).astype(bf16).reshape(8, cols, hcol).transpose(1, 0, 2).reshape(cols, wide2)
    leave_a, leave_b = leave_wide[:, :slotp], leave_wide[:, slotp:]
    enter_down = lax.dot_general(
        my_spread, enter_narrow.reshape(4, block, cols), (((0,), (1,)), ((), ())), preferred_element_type=f32
    )
    enter_down = enter_down.transpose(1, 0, 2).reshape(slotp, cols).astype(bf16)

    near = after((shard_far, normed_long, select_main, ring_selects, leave_a, leave_b, enter_down, enter_gates), near)
    x_extra, normed_extra, down_extra, marks_extra = call(
        functools.partial(ends_kernel, stretches), (1,),
        [pl.BlockSpec((32, 4, 8, lanes), lambda *_: (0, 0, per4 // 8, 0), pipeline_mode=pl.Buffered(1)), fixed((1, width))],
        [(fixed((main, width)), ((main, width), f32)), (fixed((main, width)), ((main, width), bf16)),
         (fixed((main, width)), ((main, width), bf16)), (fixed((main, cols)), ((main, cols), f32))],
        [pltpu.VMEM((main, width), f32)],
        core_at, (near, norm_first[None, :]), 1,
    )
    seg_first = marks_extra[:toks, 0].astype(jnp.int32)
    seg_last = marks_extra[toks:, 0].astype(jnp.int32)
    seg_extra = jnp.concatenate([seg_first, seg_last])
    normed_long = jnp.concatenate([normed_long, normed_extra], axis=0)
    normed = normed_long[HALO:]
    marks = jnp.concatenate([halo_seg, seg_main, seg_first + 100, seg_last + 200])
    same = [(marks[HALO - k : -k] == marks[HALO:]).astype(f32)[:, None] for k in range(1, 4)]
    mask = jnp.concatenate(same + [jnp.zeros((rows, 5), f32)], axis=1)
    mask_long = jnp.concatenate([mask[:main], jnp.ones((HALO, 8), f32), mask[main:], jnp.zeros((HALO, 8), f32)], axis=0)
    select_extra = select_of(seg_extra) * (seg_extra != MIDDLE).astype(f32)[:, None]
    select = jnp.concatenate([select_main, select_extra], axis=0)
    select_long = jnp.concatenate([select_halo, select], axis=0)
    select_after = jnp.concatenate([select, select_halo], axis=0)

    col_spec = lambda i: pl.BlockSpec((8, 2, per4, quarter), lambda b, s: (b, s[0], 0, i))
    out_spec = pl.BlockSpec((8, 4, per4, quarter), lambda b, s: (2 * s[0] + b, 0, 0, 2))
    gate_spec = pl.BlockSpec((16, 4, per4, glane), lambda b, s: (s[0], 0, 0, 3 * quarter // glane), pipeline_mode=pl.Buffered(1))
    side_col_spec = lambda i: pl.BlockSpec((32, 1, per4, quarter), lambda b, s: (0, 2 * s[0] + b, 0, i))
    rows_spec = lambda n: pl.BlockSpec((n, quarter), lambda b, s: (0, b))
    head_spec = lambda n: pl.BlockSpec((n, head), lambda h, s: (0, h))
    enter_spec = pl.BlockSpec((quarter, cols), lambda b, s: (b, 0))
    hidden_spec = lambda n: pl.BlockSpec((n, hcol), lambda j, s: (0, j))
    wide_block = (rows, halfw)
    small_block = (rows, cols)
    F = lambda *shape: (fixed(shape), (shape, f32))
    B = lambda *shape: (fixed(shape), (shape, bf16))
    layer = 2 * rows * halfw * width
    mib = 2**20

    gd_rows = ring_rows(tied(cotangent, near).astype(bf16))
    long = rows + HALO
    convolved, lat_gates, pick_fill = call(
        fill_kernel, (2,),
        [fixed((long, width)), side_col_spec(1), fixed((width, cols)), fixed((long, cols)), rows_spec(cols), fixed((rows, 8)), rows_spec(4),
         pl.BlockSpec((quarter, 2 * cols), lambda b, s: (b, 0))],
        [(rows_spec(rows), (wide_block, bf16)), F(rows, 2 * cols), B(long, cols)],
        [pltpu.VMEM((long, quarter), f32)],
        core_at, (normed_long, near, enter_square[1], select_long, leave_half[1], mask, taps, enter_gates), 1, (shard_far,),
    )
    pick_fill = pick_fill[HALO:]

    sides = lambda v: [v[:toks], v[toks:]]
    feed_select = [
        jnp.concatenate([ring_selects[0][:toks], sides(select_extra)[0], ring_selects[1][:toks], sides(select_extra)[1]], axis=0),
        ring_selects[0][toks:],
        ring_selects[1][toks:],
    ]
    sig_in, sig_de, decays, state, prod, pick_in, pick_de = call(
        gates_kernel, (heads,),
        [head_spec(rows), fixed((rows, 2 * cols)), fixed((rows, 2 * cols)), fixed(small_block), gate_spec,
         head_spec(cols), head_spec(cols), fixed((rows, 8)), head_spec(1)],
        [(head_spec(rows), (wide_block, f32))] * 5 + [B(*small_block)] * 2,
        [pltpu.VMEM((rows, head), f32), pltpu.VMEM((halfw, 2 * head), bf16)],
        core_at, (convolved, lat_gates, swap(lat_gates), select, near, leave_half[2], leave_half[3], mask, rate), 4, tuple(gd_rows[0][1:]),
    )
    entering = chips_carry(jnp.stack([prod[main - 1], state[main - 1]]), False)[None, :]
    branch, slope, pick_gelu = call(
        gelu_kernel, (2,),
        [fixed((long, width)), side_col_spec(0), fixed((width, cols)), fixed(small_block), rows_spec(cols)],
        [(rows_spec(rows), (wide_block, f32))] * 2 + [B(*small_block)],
        [],
        core_at, (normed_long, near, enter_square[0], select, leave_half[0]), 12,
    )
    states, mixed, lat_out, out_mine, out_send, out_extra = call(
        out_kernel, (2,),
        [rows_spec(rows), rows_spec(rows), rows_spec(1), rows_spec(rows), out_spec, enter_spec, fixed((cols, width)), fixed(small_block)],
        [(rows_spec(rows), (wide_block, f32)), (rows_spec(rows), (wide_block, bf16)), F(*small_block),
         F(toks, width), B(toks + main, width), B(main, width)],
        [pltpu.VMEM((rows, width), f32), pltpu.VMEM((rows, quarter), bf16)],
        core_at, (state, prod, entering, branch, near, enter_half[4], leave_square[4], select), 15,
    )
    pick_out = ((lat_out + swap(lat_out)) * select).astype(bf16)
    got = swap(out_send).astype(f32)
    residual = block_input + out_mine + got[:toks]
    residual_extra = x_extra + (out_extra.astype(f32) + got[toks:])
    n2_extra = norm_apply(residual_extra, norm_second)

    n2_rows = ring_rows(norm_apply(residual, norm_second))
    ring = 8 * toks
    anywhere = pl.BlockSpec(memory_space=pl.ANY)
    far_rows = far.shape[1]

    def feed(n2_pieces, gd_pieces, select, micros, waits=()):
        count = len(n2_pieces)
        n = count * toks
        return call(
            functools.partial(ffn_kernel, count), (1,),
            [anywhere] * (2 * count + 1)
            + [fixed((cols, slotp)), fixed((cols, slotp)), fixed((slotp, cols)), fixed((width, cols)), fixed((cols, width)), fixed((n, cols))],
            [B(n, width)] + [B(n, slotp)] * 3 + [B(n, cols)] * 4,
            [pltpu.VMEM((n, width), bf16), pltpu.VMEM((n, width), bf16), pltpu.VMEM(far.shape, bf16),
             pltpu.SemaphoreType.DMA((count,)), pltpu.SemaphoreType.DMA((count,)), pltpu.SemaphoreType.DMA((4, 3))],
            core_at,
            (*n2_pieces, *gd_pieces, far, leave_a, leave_b, enter_down, enter_widen, leave_narrow, select),
            micros, waits,
        )

    mix = lambda rows, extra: [rows[0][0], sides(extra)[0], rows[1][0], sides(extra)[1]]
    gn0, *parts0 = feed(mix(n2_rows, n2_extra), mix(gd_rows, down_extra), feed_select[0], 60)
    gn1, *parts1 = feed(n2_rows[0][1:], gd_rows[0][1:], feed_select[1], 40, (gn0,))
    gn2, *parts2 = feed(n2_rows[1][1:], gd_rows[1][1:], feed_select[2], 60, (gn1,))
    add = lambda a, b: a.astype(f32) + b.astype(f32)

    eighth = main // 8
    side0 = jnp.concatenate([tied(gn0, gn1).astype(bf16), parts0[3], parts0[4]], axis=1)
    extra_part = jnp.concatenate([side0[toks : 2 * toks], side0[3 * toks :]], axis=0)
    extra_total = lax.all_to_all(extra_part, RING, 0, 0, tiled=True).reshape(8, eighth, -1)
    extra_total = to_low(tied(jnp.sum(extra_total.astype(f32), axis=0), gn2))
    extra_all = lax.all_to_all(jnp.broadcast_to(extra_total[None], (8, *extra_total.shape)), RING, 0, 0, tiled=True).reshape(main, -1)
    grad_n2_extra = extra_all[:, :width].astype(f32)
    lat_extra = extra_all[:, width:]
    lgw_extra = lat_extra[:, :cols]
    pick_n_extra = lat_extra[:, cols:]

    sums0 = add(gn0[:toks], swap(gn0[2 * toks : 3 * toks]))
    sums1 = add(gn1, swap(gn2)).astype(bf16)
    sums = [sums0] + [sums1[k * toks : (k + 1) * toks] for k in range(3)]
    mid_spec = (pl.BlockSpec((rank, hcol), lambda j, s: (0, j)), ((rank, slotp), bf16))
    extra_spec = (pl.BlockSpec((cols, hcol), lambda j, s: (0, j)), ((cols, slotp), bf16))
    down, mid_a, mid_b, mid_n, mid_l, mid_e, ex_a, ex_b, ex_n = call(
        down_kernel, (4,),
        [anywhere] * 16 + [hidden_spec(4 * toks), hidden_spec(3 * toks), hidden_spec(3 * toks)] * 3
        + [fixed((4 * toks, cols)), fixed((3 * toks, cols)), fixed((3 * toks, cols))] * 4
        + [pl.BlockSpec((4, far_rows, wide2), lambda j, s: (j, 0, 0)), fixed((cols, width))],
        [B(ring, width)] + [mid_spec] * 3 + [B(rank, width)] * 2 + [extra_spec] * 3,
        [pltpu.VMEM((ring, width), f32), pltpu.VMEM((cols, hcol), f32), pltpu.VMEM((cols, width), f32),
         pltpu.VMEM((ring, width), bf16), pltpu.VMEM((ring, width), bf16), pltpu.SemaphoreType.DMA((8,)), pltpu.SemaphoreType.DMA((8,))],
        middle_at,
        (n2_rows[0][0], n2_rows[1][0], *n2_rows[0][1:], *n2_rows[1][1:], gd_rows[0][0], gd_rows[1][0], *gd_rows[0][1:], *gd_rows[1][1:],
         *[v[i] for i in (2, 0, 1, 5, 6, 4, 3) for v in (parts0, parts1, parts2)], far, leave_narrow),
        60, (*sums[1:], extra_total),
    )
    grad_n2 = tied(tied(line_back(sums), down), extra_all)
    ffn_mid = tied(jnp.concatenate([mid_a, mid_b, mid_n, mid_l, mid_e], axis=1), grad_n2).astype(bf16)
    mid_shape = ffn_mid.shape
    ffn_mid = lax.all_to_all(ffn_mid.reshape(16, -1, cols), PLANE, 0, 0, tiled=True)
    ffn_mid = to_low(jnp.sum(ffn_mid.astype(f32), axis=0))
    ffn_mid = lax.all_to_all(jnp.broadcast_to(ffn_mid[None], (16, *ffn_mid.shape)), PLANE, 0, 0, tiled=True).reshape(mid_shape)

    grad_residual = cotangent + norm_back(residual, norm_second, grad_n2)
    grad_residual_extra = down_extra.astype(f32) + norm_back(residual_extra, norm_second, grad_n2_extra)
    grad_out_own = grad_residual.astype(bf16)
    grad_out = jnp.concatenate([both(grad_out_own, swap(grad_out_own), c), grad_residual_extra.astype(bf16)], axis=0)
    grad_gelu, lg_out, back, trail = call(
        functools.partial(outback_kernel, main), (2,),
        [fixed((rows, width)), out_spec, fixed((cols, width)), enter_spec, fixed(small_block)] + [rows_spec(rows)] * 4,
        [(rows_spec(rows), (wide_block, bf16)), B(*small_block)] + [(rows_spec(rows), (wide_block, f32))] * 2,
        [pltpu.VMEM((rows, quarter), f32)],
        core_at, (grad_out, near, leave_square[4], enter_half[4], select, states, branch, slope, decays), 18,
    )
    coming = chips_carry(jnp.stack([decays[0] * trail[0], decays[0] * back[0]]), True)[None, :]
    gelu_part, lat_gelu = call(
        geluback_kernel, (4,),
        [fixed(wide_block), col_spec(0), fixed((cols, halfw)), enter_spec, fixed(small_block)],
        [(rows_spec(main), ((main, width), f32)), F(*small_block)],
        [pltpu.VMEM(small_block, bf16)],
        core_at, (grad_gelu, near, leave_half[0], enter_square[0], select), 12,
    )

    grad_in, grad_de, base, lat_gates = call(
        gateback_kernel, (heads,),
        [head_spec(rows), head_spec(rows), head_spec(1), head_spec(rows), head_spec(1)] + [head_spec(rows)] * 4
        + [fixed((rows, 8)), head_spec(1), gate_spec, head_spec(cols), head_spec(cols)],
        [(head_spec(rows), (wide_block, bf16))] * 2 + [(head_spec(rows), (wide_block, f32)), F(rows, 2 * cols)],
        [pltpu.VMEM((rows + 8, head), f32), pltpu.VMEM((halfw, 2 * head), bf16)],
        core_at, (back, trail, coming, states, entering, convolved, sig_in, sig_de, decays, mask, rate, near, leave_half[2], leave_half[3]),
        8,
    )

    share = -(-width // 7 // 128) * 128
    share_of = lambda v: lax.dynamic_slice_in_dim(jnp.pad(v, ((0, 0), (0, 8 * share - width))), member * share, share, axis=1)
    lanes_all = 3 * slotp + 2 * share
    (packed,) = call(
        pack_kernel, (1,),
        [fixed((cols, slotp))] * 3 + [fixed((main, cols))] * 2 + [fixed((main, share))] * 2 + [fixed((rank, 3 * slotp + 2 * width))],
        [B(cols + 3 * rank, lanes_all)], [], core_at,
        (ex_a, ex_b, ex_n, pick_n_extra, lgw_extra, share_of(down_extra), share_of(n2_extra), ffn_mid), 3, (base,),
    )
    ffn_all = lax.all_gather(packed, RING, axis=0)

    halo_both = chip_shift(jnp.concatenate([base[:HALO], lat_gates[:HALO]], axis=1), -1)
    halo_base, halo_lat = halo_both[:, :halfw], halo_both[:, halfw:]
    halo_other = chip_shift(lat_gates[:HALO], -1, cross=True)
    grad_fill, lg_in, lg_de, lat_fill, normed_mine, normed_theirs = call(
        fillback_kernel, (4,),
        [fixed(wide_block), fixed((rows, 2 * cols)), fixed((rows, 2 * cols)), fixed((HALO, halfw)), fixed((HALO, 2 * cols)), fixed((HALO, 2 * cols)),
         fixed((rows + HALO, cols)), fixed((rows + 2 * HALO, 8)), fixed((4, halfw)), fixed((halfw, cols)), fixed((halfw, cols)), fixed((cols, halfw)),
         col_spec(1), enter_spec, rows_spec(main)],
        [B(*wide_block), B(*small_block), B(*small_block), F(*small_block),
         (rows_spec(toks), ((toks, width), f32)), (rows_spec(toks), ((toks, width), bf16))],
        [pltpu.VMEM((rows + 2 * HALO, halfw), f32), pltpu.VMEM((HALO, 2 * cols), bf16), pltpu.VMEM((main, cols), bf16), pltpu.VMEM((main, quarter), f32)],
        core_at,
        (base, lat_gates, swap(lat_gates), halo_base, halo_lat, halo_other, select_after, mask_long, taps, enter_half[2], enter_half[3],
         leave_half[1], near, enter_square[1], gelu_part),
        12,
    )

    lg_gelu = ((lat_gelu + swap(lat_gelu)) * select).astype(bf16)
    lg_fill = ((lat_fill + swap(lat_fill)) * select).astype(bf16)
    normed_half = half(normed, c, 1)
    pairs = [
        (lg_gelu, normed_half), (lg_fill, normed_half), (lg_in, convolved), (lg_de, convolved), (lg_out, mixed),
        (pick_gelu, grad_gelu), (pick_fill, grad_fill), (pick_in, grad_in), (pick_de, grad_de), (pick_out, half(grad_out, c, 1)),
    ]
    part_spec = lambda n, i: pl.BlockSpec((main, n), lambda *_: (i, 0), pipeline_mode=pl.Buffered(1))
    operands = [v for pair in pairs for v in pair]
    (mid,) = call(
        functools.partial(mids_kernel, 10), (1,),
        [part_spec(cols, 0), part_spec(halfw, 0)] * 10,
        [B(10 * rank, halfw)],
        [pltpu.VMEM((cols, halfw), f32)],
        middle_at, operands, 6,
    )
    mid_own = mid
    shape = mid.shape
    mid = lax.all_to_all(mid.reshape(64, -1, cols), CHIPS, 0, 0, tiled=True)
    mid = to_low(jnp.sum(mid.astype(f32), axis=0))

    down_mine = jnp.concatenate([down[:toks], down[2 * toks : 5 * toks]], axis=0)
    down_theirs = jnp.concatenate([down[toks : 2 * toks], down[5 * toks :]], axis=0)
    down_total = tied(add(down_mine, swap(down_theirs)), base)
    down_sums = [down_total[k * toks : (k + 1) * toks] for k in range(4)]
    block_output = residual + line_back(down_sums)
    operands = [*[v for pair in pairs[:5] for v in pair[::-1]], *[v for pair in pairs[5:] for v in pair]]
    enter_extra, leave_extra = call(
        functools.partial(extras_kernel, 5), (1,),
        [part_spec(halfw, 1), part_spec(cols, 1)] * 5 + [part_spec(cols, 1), part_spec(halfw, 1)] * 5,
        [B(5, halfw, cols), B(5, cols, halfw)],
        [],
        core_at, operands, 6, (mid_own,),
    )
    (grad_leave_widen,) = call(
        wide_kernel, (8,),
        [fixed((rank, cols)), fixed((units, 8 * chunk)), pl.BlockSpec((8, cols, hcol), lambda i, s: (0, 0, i)), pl.BlockSpec((8, rank, hcol), lambda i, s: (0, cols // rank, i))],
        [(pl.BlockSpec((cols, block), lambda i, s: (0, i)), ((cols, 2 * ff), f32))],
        [], core_at, (one_hot, spread_one, ffn_all, ffn_all), 12, (mid_own,),
    )
    mid = tied(mid, grad_leave_widen).astype(bf16)
    mid = lax.all_to_all(jnp.broadcast_to(mid[None], (64, *mid.shape)), CHIPS, 0, 0, tiled=True).reshape(shape)
    (grad_enter_narrow,) = call(
        enter_kernel, (4,),
        [fixed((rank, cols)), fixed((units, 8 * chunk)), pl.BlockSpec((8, cols, hcol), lambda i, s: (0, 0, 8 + i)), pl.BlockSpec((8, rank, hcol), lambda i, s: (0, cols // rank, 8 + i))],
        [(pl.BlockSpec((block, cols), lambda i, s: (i, 0)), ((ff, cols), f32))],
        [], core_at, (one_hot, spread_one, ffn_all, ffn_all), 7, (mid_own,),
    )
    grad_normed = normed_mine + swap(normed_theirs).astype(f32)
    input_grad = grad_residual + norm_back(block_input, norm_first, grad_normed)
    eye = jnp.eye(cols, dtype=bf16)
    share_spec = lambda i: pl.BlockSpec((8, cols, share), lambda *_: (0, 0, 3 * slotp // share + i))
    mid_rows = lambda i: pl.BlockSpec((8, rank, lanes_all), lambda *_: (0, cols // rank + i, 0))
    grad_leave_narrow, grad_enter_widen = call(
        shares_kernel, (1,),
        [fixed((rank, cols)), fixed((cols, cols)), share_spec(0), share_spec(1)] + [mid_rows(i) for i in range(3)],
        [F(cols, width), F(width, cols)],
        [], core_at, (one_hot, eye) + (ffn_all,) * 5, 4, (mid_own,),
    )
    per_k = lambda *shape: pl.BlockSpec((1,) + shape, lambda k, s: (k,) + (0,) * len(shape))
    mid_e_spec = pl.BlockSpec((rank, halfw), lambda k, s: (k, 0))
    mid_l_spec = pl.BlockSpec((rank, halfw), lambda k, s: (5 + k, 0))
    mid_other = swap(mid)
    grad_enter_square, grad_leave_square = call(
        square_kernel, (5,),
        [fixed((rank, cols)), per_k(halfw, cols), per_k(halfw, cols), per_k(cols, halfw), per_k(cols, halfw),
         mid_e_spec, mid_e_spec, mid_l_spec, mid_l_spec],
        [(per_k(width, cols), ((5, width, cols), f32)), (per_k(cols, width), ((5, cols, width), f32))],
        [], core_at, (one_hot, enter_extra, swap(enter_extra), leave_extra, swap(leave_extra), mid, mid_other, mid, mid_other), 9,
    )
    return (
        block_output,
        input_grad,
        grad_enter_square,
        grad_leave_square,
        grad_enter_widen,
        grad_leave_widen,
        grad_enter_narrow,
        grad_leave_narrow,
    )


def solution(mesh):
    split = Mesh(mesh.devices.reshape(SIZES), AXES)
    by_row = P(AXES, None)
    return jax.shard_map(
        per_device,
        mesh=split,
        in_specs=(by_row, by_row, P(AXES), P(), P(), P(), P(), P()) + (by_row,) * 7 + (P(),) * 6,
        out_specs=(by_row, by_row, P(), P(), P(), P(), P(), P()),
        check_vma=False,
    )
```

```python
import functools
import jax
import jax.numpy as jnp
from jax import lax
from jax.experimental import pallas as pl
from jax.experimental.pallas import tpu as pltpu
from jax.sharding import Mesh, PartitionSpec as P

HEADS = 10
ADAPTERS = 8
HALO = 16
MIDDLE = 3
AXES = ("z", "x", "v", "u", "c")
SIZES = (4, 4, 2, 2, 2)
YAX = ("v", "u")
RING = ("v", "u", "c")
PLANE = ("z", "x")
QUAD = ("u", "c")
CHIPS = ("z", "x", "v", "u")
VMEM = 56 * 2**20

eps_norm = 1e-06
floor_scale = 0.001
bf16 = jnp.bfloat16
f32 = jnp.float32


def dot(a, b):
    return jnp.dot(a, b, preferred_element_type=f32)


def dot_nt(a, b):
    return lax.dot_general(a, b, (((1,), (1,)), ((), ())), preferred_element_type=f32)


def dot_tn(a, b):
    return lax.dot_general(a, b, (((0,), (0,)), ((), ())), preferred_element_type=f32)


def low(v):
    return lax.reduce_precision(v, 8, 7)


def to_low(v):
    return low(v).astype(bf16)


def norm_scale(values):
    return lax.rsqrt(jnp.mean(values * values, axis=-1, keepdims=True) + eps_norm)


def norm_apply(values, gain):
    return (values * norm_scale(values) * gain).astype(bf16)


def norm_back(values, gain, grad):
    s = norm_scale(values)
    gq = gain * grad
    return s * gq - values * (s * s * s) * jnp.mean(values * gq, axis=-1, keepdims=True)


def sigmoid(v):
    return 1.0 / (1.0 + jnp.exp(-v))


def gelu_parts(a):
    k = 0.7978845608028654
    a2 = a * a
    th = jnp.tanh(k * (a + 0.044715 * a2 * a))
    value = 0.5 * a * (1.0 + th)
    slope = 0.5 * (1.0 + th) + 0.5 * a * (1.0 - th * th) * (k * (1.0 + 3.0 * 0.044715 * a2))
    return value, slope


def swap(v):
    return lax.ppermute(v, "c", [(0, 1), (1, 0)])


def shift4(v, axis, by):
    return lax.ppermute(v, axis, [(i, (i + by) % 4) for i in range(4)])


def chip_shift(v, by, cross=False):
    chips = 64
    pairs = [
        (2 * p + c, 2 * (p + by) + (1 - c if cross else c))
        for p in range(chips)
        for c in range(2)
        if 0 <= p + by < chips
    ]
    return lax.ppermute(v, AXES, pairs)


def both(own, other, c):
    rows = own.shape[0]
    three = jnp.concatenate([own, other, own], axis=0)
    return lax.dynamic_slice_in_dim(three, c * rows, 2 * rows, axis=0)


def half(v, c, axis):
    size = v.shape[axis] // 2
    return lax.dynamic_slice_in_dim(v, c * size, size, axis=axis)


def after(first, *values):
    held = lax.optimization_barrier((first, *values))[1:]
    return held[0] if len(held) == 1 else held


def tied(value, other):
    return value + other[(0,) * other.ndim].astype(f32) * 0.0


def line_order(parts, y):
    back = parts[::-1]
    twice = jnp.stack(back + back)
    return lax.dynamic_slice_in_dim(twice, 3 - y, 4, axis=0)


def call(kernel, grid, ins, outs, scratch, scalars, args, micros, waits=()):
    count = len(args)

    def body(s_ref, *refs):
        kernel(s_ref, *refs[:count], *refs[count + len(waits) :])

    ins = list(ins) + [pl.BlockSpec(memory_space=pl.ANY)] * len(waits)
    args = (*args, *waits)
    return pl.pallas_call(
        body,
        grid_spec=pltpu.PrefetchScalarGridSpec(
            num_scalar_prefetch=1,
            grid=grid,
            in_specs=ins,
            out_specs=[spec for spec, _ in outs],
            scratch_shapes=scratch,
        ),
        out_shape=[jax.ShapeDtypeStruct(*shape) for _, shape in outs],
        compiler_params=pltpu.CompilerParams(vmem_limit_bytes=VMEM),
        cost_estimate=pl.CostEstimate(flops=int(micros * 1e9), bytes_accessed=int(micros * 2e6), transcendentals=0),
    )(scalars, *args)


def fixed(shape):
    return pl.BlockSpec(shape, lambda *_: (0,) * len(shape), pipeline_mode=pl.Buffered(1))


def scan_rows(d_ref, p_ref, s_ref, q_ref):
    rows, width = d_ref.shape
    row = lax.broadcasted_iota(jnp.int32, (8, width), 0)

    def tile(i, carry):
        state, product = carry
        at = pl.ds(pl.multiple_of(i * 8, 8), 8)
        a = d_ref[at, :]
        b = p_ref[at, :]
        for s in (1, 2, 4):
            b = a * jnp.where(row >= s, pltpu.roll(b, s, 0), 0.0) + b
            a = a * jnp.where(row >= s, pltpu.roll(a, s, 0), 1.0)
        value = b + a * state
        through = a * product
        s_ref[at, :] = value
        q_ref[at, :] = through
        return value[7:8, :], through[7:8, :]

    lax.fori_loop(
        0, rows // 8, tile, (jnp.zeros((1, width), f32), jnp.ones((1, width), f32)), unroll=8
    )


def scan_rows_back(d_ref, g_ref, s_ref, q_ref, main):
    rows, width = d_ref.shape
    row = lax.broadcasted_iota(jnp.int32, (8, width), 0)

    def tile(i, carry):
        state, product, after_row = carry
        at = pl.ds(pl.multiple_of(i * 8, 8), 8)
        d = d_ref[at, :]
        b = g_ref[at, :]
        a = jnp.where(row < 7, pltpu.roll(d, 7, 0), after_row)
        for s in (1, 2, 4):
            b = a * jnp.where(row < 8 - s, pltpu.roll(b, 8 - s, 0), 0.0) + b
            a = a * jnp.where(row < 8 - s, pltpu.roll(a, 8 - s, 0), 1.0)
        value = b + a * state
        through = a * product
        s_ref[at, :] = value
        q_ref[at, :] = through
        return value[0:1, :], through[0:1, :], d[0:1, :]

    zero = jnp.zeros((1, width), f32)
    one = jnp.ones((1, width), f32)
    last, cut = rows // 8 - 1, main // 8
    lax.fori_loop(0, last + 1 - cut, lambda k, t: tile(last - k, t), (zero, zero, one), unroll=8)
    lax.fori_loop(0, cut, lambda k, t: tile(cut - 1 - k, t), (zero, one, one), unroll=8)


def tile_of(w, i):
    block = w[:, i]
    return block.reshape(block.shape[0] * block.shape[1], block.shape[2])


def ends_kernel(stretches, s_ref, near_ref, gain_ref, x_ref, normed_ref, down_ref, marks_ref, hold_ref):
    toks = x_ref.shape[0] // 2
    quarter = x_ref.shape[1] // 4
    reach = quarter + marks_ref.shape[1]
    size = 8 * stretches
    for core in range(2):
        for p in range(16):
            for h in range(stretches):
                row = p * size + h * 8
                for y in range(4):
                    block = near_ref[2 * p + y // 2, 2 * (y % 2) + core, :, h * reach : (h + 1) * reach].astype(f32)
                    cols = slice(y * quarter, (y + 1) * quarter)
                    if row < toks:
                        x_ref[core * toks + row : core * toks + row + 8, cols] = block[:, :quarter]
                        if y == 0:
                            marks_ref[core * toks + row : core * toks + row + 8, :] = block[:, quarter:]
                    else:
                        to = core * toks + row - toks
                        hold_ref[to : to + 8, cols] = block[:, :quarter]
    down_ref[...] = hold_ref[...].astype(bf16)
    x = x_ref[...]
    normed_ref[...] = norm_apply(x, gain_ref[...])


def pack_kernel(s_ref, exa_ref, exb_ref, exn_ref, pick_ref, lg_ref, down_ref, n2_ref, out_ref):
    wide = exa_ref.shape[1]
    share = down_ref.shape[1]
    for i, ref in enumerate((exa_ref, exb_ref, exn_ref)):
        out_ref[:, i * wide : (i + 1) * wide] = ref[...]
    at = 3 * wide
    out_ref[:, at : at + share] = dot_tn(pick_ref[...], down_ref[...]).astype(bf16)
    out_ref[:, at + share :] = dot_tn(lg_ref[...], n2_ref[...]).astype(bf16)


def fill_kernel(c_ref, x_ref, w_ref, first_ref, select_ref, leave_ref, mask_ref, taps_ref, enter_ref, conv_ref, lat_ref, pick_ref, acc_ref):
    rows, width = conv_ref.shape

    @pl.when(pl.program_id(0) == 0)
    def _():
        pick_ref[...] = (dot(x_ref[...], first_ref[...]) * select_ref[...]).astype(bf16)

    acc_ref[...] = dot(x_ref[...], tile_of(w_ref, 0)) + dot(pick_ref[...], leave_ref[...])
    step = width // 5
    for j in range(5):
        at = slice(j * step, (j + 1) * step)
        total = taps_ref[0:1, at] * acc_ref[HALO : HALO + rows, at]
        for k in range(1, taps_ref.shape[0]):
            total = total + taps_ref[k : k + 1, at] * acc_ref[HALO - k : HALO - k + rows, at] * mask_ref[:, k - 1 : k]
        conv_ref[:, at] = total.astype(bf16)

    @pl.when(pl.program_id(0) == 0)
    def _():
        lat_ref[...] = jnp.zeros_like(lat_ref)

    lat_ref[...] += dot(conv_ref[...], enter_ref[...])


def gate_weights(w_ref, hold_ref):
    @pl.when(pl.program_id(0) == 0)
    def _():
        wide = w_ref.shape[3]
        for i in range(4):
            hold_ref[:, i * wide : (i + 1) * wide] = tile_of(w_ref, i)

    head = 2 * w_ref.shape[3]
    at = pl.ds(pl.multiple_of(pl.program_id(0) * head, head), head)
    return hold_ref[at, :head], hold_ref[at, head:]


def gates_kernel(
    c_ref, conv_ref, own_ref, other_ref, select_ref, w_ref, leave_in_ref, leave_de_ref, mask_ref, rate_ref,
    sin_ref, sde_ref, dec_ref, state_ref, prod_ref, pick_in_ref, pick_de_ref, push_ref, hold_ref,
):
    cols = select_ref.shape[1]
    inner, decay = gate_weights(w_ref, hold_ref)

    @pl.when(pl.program_id(0) == 0)
    def _():
        lat = own_ref[...] + other_ref[...]
        select = select_ref[...]
        pick_in_ref[...] = (lat[:, :cols] * select).astype(bf16)
        pick_de_ref[...] = (lat[:, cols:] * select).astype(bf16)

    retain = mask_ref[:, 0:1]
    conv = conv_ref[...]
    sig_in = sigmoid(dot(conv, inner) + dot(pick_in_ref[...], leave_in_ref[...]))
    sig_de = sigmoid(dot(conv, decay) + dot(pick_de_ref[...], leave_de_ref[...]))
    raw = jnp.exp(-8.0 * rate_ref[...] * sig_de)
    scale = jnp.where(retain > 0.5, jnp.sqrt(jnp.maximum(1.0 - raw * raw, floor_scale)), 1.0)
    sin_ref[...] = sig_in
    sde_ref[...] = sig_de
    dec_ref[...] = raw * retain
    push_ref[...] = conv.astype(f32) * sig_in * scale
    scan_rows(dec_ref, push_ref, state_ref, prod_ref)


def gelu_kernel(c_ref, x_ref, w_ref, first_ref, select_ref, leave_ref, value_ref, slope_ref, pick_ref):
    @pl.when(pl.program_id(0) == 0)
    def _():
        pick_ref[...] = (dot(x_ref[HALO:, :], first_ref[...]) * select_ref[...]).astype(bf16)

    pre = dot(x_ref[HALO:, :], tile_of(w_ref, 0)) + dot(pick_ref[...], leave_ref[...])
    value, slope = gelu_parts(pre)
    value_ref[...] = value
    slope_ref[...] = slope


def out_kernel(
    c_ref, state_ref, prod_ref, entering_ref, branch_ref, w_ref, enter_ref, leave_ref, select_ref,
    states_ref, mixed_ref, lat_ref, mine_ref, send_ref, extra_ref, acc_ref, hold_ref,
):
    b = pl.program_id(0)
    q = w_ref.shape[3]
    states = state_ref[...] + prod_ref[...] * entering_ref[...]
    states_ref[...] = states
    hold_ref[...] = (branch_ref[...] * states).astype(bf16)
    mixed_ref[...] = hold_ref[...]

    @pl.when(b == 0)
    def _():
        lat_ref[...] = jnp.zeros_like(lat_ref)
        acc_ref[...] = jnp.zeros_like(acc_ref)

    lat_ref[...] += dot(hold_ref[...], enter_ref[...])
    for i in range(4):
        acc_ref[:, i * q : (i + 1) * q] += dot(hold_ref[...], tile_of(w_ref, i))

    @pl.when(b == pl.num_programs(0) - 1)
    def _():
        acc_ref[...] += dot((lat_ref[...] * select_ref[...]).astype(bf16), leave_ref[...])
        rows = mine_ref.shape[0]
        at = pl.multiple_of(c_ref[0] * rows, rows)
        mine_ref[...] = acc_ref[pl.ds(at, rows), :]
        send_ref[:rows, :] = acc_ref[pl.ds(pl.multiple_of(rows - at, rows), rows), :].astype(bf16)
        extra = acc_ref[2 * rows :, :].astype(bf16)
        send_ref[rows:, :] = extra
        extra_ref[...] = extra


def narrow_block(far_ref, j, top):
    wide = far_ref.shape[2]
    tail = wide // 4
    low_rows = (far_ref.shape[1] - top) // 5
    planes = pl.ds(4 * j, 4)
    main = far_ref[planes, top : top + 4 * low_rows, :].reshape(16 * low_rows, wide)
    pieces = []
    for p in range(4):
        rows = far_ref[4 * j + p, top + 4 * low_rows :, :]
        pieces += [rows[:, k * tail : (k + 1) * tail] for k in range(4)]
    return main, jnp.concatenate(pieces, axis=0)


def fetch(refs, hold_ref, sems):
    size = refs[0].shape[0]
    return [pltpu.make_async_copy(r, hold_ref.at[pl.ds(i * size, size), :], sems.at[i]) for i, r in enumerate(refs)]


def ffn_kernel(count, s_ref, *refs):
    n2_refs, gd_refs = refs[:count], refs[count : 2 * count]
    far_hbm, la_ref, lb_ref, en_ref, ew_ref, ln_ref, select_ref = refs[2 * count : 2 * count + 7]
    gn_ref, ga_ref, gb_ref, hid_ref, lgw_ref, pickn_ref, pickw_ref, lgn_ref = refs[2 * count + 7 : 2 * count + 15]
    n2_hold, gd_hold, far_ref, n2_sems, gd_sems, far_sems = refs[2 * count + 15 :]
    width = gn_ref.shape[1]
    slotp = hid_ref.shape[1]
    step = slotp // 4
    wide = far_ref.shape[2]
    top = width // 16

    def far_copies(j):
        at = pl.ds(pl.multiple_of(j * step, step), step)
        at_b = pl.ds(pl.multiple_of(slotp + j * step, step), step)
        planes = pl.ds(4 * j, 4)
        places = [(slice(None), pl.ds(0, top), at), (slice(None), pl.ds(0, top), at_b), (planes, pl.ds(top, far_ref.shape[1] - top), slice(None))]
        return [pltpu.make_async_copy(far_hbm.at[p], far_ref.at[p], far_sems.at[j, i]) for i, p in enumerate(places)]

    n2_copies = fetch(n2_refs, n2_hold, n2_sems)
    gd_copies = fetch(gd_refs, gd_hold, gd_sems)
    for copy in n2_copies + gd_copies:
        copy.start()
    for j in range(4):
        for copy in far_copies(j):
            copy.start()
    for copy in n2_copies + gd_copies:
        copy.wait()
    select = select_ref[...]
    pickw_ref[...] = (dot(n2_hold[...], ew_ref[...]) * select).astype(bf16)
    lgn_ref[...] = (dot_nt(gd_hold[...], ln_ref[...]) * select).astype(bf16)

    def hidden(j, _):
        for copy in far_copies(j):
            copy.wait()
        at = pl.ds(pl.multiple_of(j * step, step), step)
        at_b = pl.ds(pl.multiple_of(slotp + j * step, step), step)
        a = dot(n2_hold[...], far_ref[:, :top, at].reshape(width, step)) + dot(pickw_ref[...], la_ref[:, at])
        up = dot(n2_hold[...], far_ref[:, :top, at_b].reshape(width, step)) + dot(pickw_ref[...], lb_ref[:, at])
        main, last = narrow_block(far_ref, j, top)
        grad = dot_nt(gd_hold[:, :wide], main) + dot_nt(gd_hold[:, wide:], last) + dot_nt(lgn_ref[...], en_ref[at, :])
        act, slope = gelu_parts(a)
        hid_ref[:, at] = (act * up).astype(bf16)
        ga_ref[:, at] = (slope * up * grad).astype(bf16)
        gb_ref[:, at] = (act * grad).astype(bf16)
        return 0

    lax.fori_loop(0, 4, hidden, 0)
    lgw_ref[...] = ((dot_nt(ga_ref[...], la_ref[...]) + dot_nt(gb_ref[...], lb_ref[...])) * select).astype(bf16)
    pickn_ref[...] = (dot(hid_ref[...], en_ref[...]) * select).astype(bf16)
    part = width // 4

    def back(q, _):
        at = pl.ds(pl.multiple_of(q * part, part), part)
        planes = pl.ds(4 * q, 4)
        total = dot_nt(ga_ref[...], far_ref[planes, :top, :slotp].reshape(part, slotp))
        total += dot_nt(gb_ref[...], far_ref[planes, :top, slotp:].reshape(part, slotp))
        gn_ref[:, at] = (total + dot_nt(lgw_ref[...], ew_ref[at, :])).astype(bf16)
        return 0

    lax.fori_loop(0, 4, back, 0)


def down_kernel(s_ref, *refs):
    n2_refs, gd_refs = refs[:8], refs[8:16]
    hid, ga, gb, pick, lgn, pickn, lgw = [refs[16 + 3 * i : 19 + 3 * i] for i in range(7)]
    far_ref, ln_ref = refs[37:39]
    down_ref, mida_ref, midb_ref, midn_ref, midl_ref, mide_ref, exa_ref, exb_ref, exn_ref = refs[39:48]
    acc_ref, hold_ref, wide_ref, n2_hold, gd_hold, n2_sems, gd_sems = refs[48:]
    j = pl.program_id(0)
    rank = mida_ref.shape[0]
    piece = n2_refs[0].shape[0]
    here = pl.ds(pl.multiple_of(s_ref[0] * rank, rank), rank)
    main, last = narrow_block(far_ref, 0, far_ref.shape[1] * 2 // 3)
    cut = main.shape[1]
    ring_of = lambda v: jnp.concatenate([v[0][:piece, :], v[0][2 * piece : 3 * piece, :], v[1][...], v[2][...]], axis=0)
    rest_of = lambda v: jnp.concatenate([v[0][piece : 2 * piece, :], v[0][3 * piece :, :]], axis=0)
    n2_copies = fetch(n2_refs, n2_hold, n2_sems)
    gd_copies = fetch(gd_refs, gd_hold, gd_sems)

    @pl.when(j == 0)
    def _():
        for copy in n2_copies + gd_copies:
            copy.start()
        acc_ref[...] = dot(ring_of(pickn), ln_ref[...])

    hidden = ring_of(hid)
    acc_ref[:, :cut] += dot(hidden, main)
    acc_ref[:, cut:] += dot(hidden, last)
    for left, right, out_ref, extra_ref in ((pick, ga, mida_ref, exa_ref), (pick, gb, midb_ref, exb_ref), (lgn, hid, midn_ref, exn_ref)):
        hold_ref[...] = dot_tn(ring_of(left), ring_of(right))
        out_ref[...] = hold_ref[here, :].astype(bf16)
        extra_ref[...] = dot_tn(rest_of(left), rest_of(right)).astype(bf16)

    @pl.when(j == pl.num_programs(0) - 1)
    def _():
        down_ref[...] = acc_ref[...].astype(bf16)
        for copy in n2_copies + gd_copies:
            copy.wait()
        wide_ref[...] = dot_tn(ring_of(pickn), gd_hold[...])
        midl_ref[...] = wide_ref[here, :].astype(bf16)
        wide_ref[...] = dot_tn(ring_of(lgw), n2_hold[...])
        mide_ref[...] = wide_ref[here, :].astype(bf16)


def outback_kernel(
    main, c_ref, go_ref, w_ref, leave_ref, enter_ref, select_ref, states_ref, branch_ref, slope_ref, dec_ref,
    gg_ref, lg_ref, state_ref, prod_ref, gs_ref,
):
    b = pl.program_id(0)
    q = w_ref.shape[3]

    @pl.when(b == 0)
    def _():
        lg_ref[...] = (dot_nt(go_ref[...], leave_ref[...]) * select_ref[...]).astype(bf16)

    gm = dot_nt(lg_ref[...], enter_ref[...])
    for i in range(4):
        gm += dot_nt(go_ref[:, i * q : (i + 1) * q], tile_of(w_ref, i))
    gg_ref[...] = (slope_ref[...] * (gm * states_ref[...])).astype(bf16)
    gs_ref[...] = gm * branch_ref[...]
    scan_rows_back(dec_ref, gs_ref, state_ref, prod_ref, main)


def geluback_kernel(c_ref, g_ref, w_ref, leave_ref, enter_ref, select_ref, part_ref, lat_ref, lg_ref):
    b = pl.program_id(0)
    q = w_ref.shape[3]

    @pl.when(b == 0)
    def _():
        lat = dot_nt(g_ref[...], leave_ref[...])
        lat_ref[...] = lat
        lg_ref[...] = (lat * select_ref[...]).astype(bf16)

    rows = part_ref.shape[0]
    part = dot_nt(g_ref[:rows, :q], tile_of(w_ref, 0)) + dot_nt(g_ref[:rows, q : 2 * q], tile_of(w_ref, 1))
    part_ref[...] = part + dot_nt(lg_ref[:rows, :], enter_ref[...])


def gateback_kernel(
    c_ref, back_ref, trail_ref, coming_ref, states_ref, entering_ref, conv_ref, sin_ref, sde_ref, dec_ref, mask_ref, rate_ref,
    w_ref, leave_in_ref, leave_de_ref,
    gi_ref, gd_ref, base_ref, lat_ref, hold_ref, gate_ref,
):
    rows = conv_ref.shape[0]
    cols = leave_in_ref.shape[0]
    inner, decay = gate_weights(w_ref, gate_ref)
    retain = mask_ref[:, 0:1]
    hold_ref[7:8, :] = entering_ref[...]
    hold_ref[8:, :] = states_ref[...]
    rate = rate_ref[...]
    sig_in = sin_ref[...]
    sig_de = sde_ref[...]
    conv = conv_ref[...].astype(f32)
    carried = back_ref[...] + trail_ref[...] * coming_ref[...]
    raw = jnp.exp(-8.0 * rate * sig_de)
    grown = 1.0 - raw * raw
    scale = jnp.where(retain > 0.5, jnp.sqrt(jnp.maximum(grown, floor_scale)), 1.0)
    through = carried * conv
    gi = (through * scale * sig_in * (1.0 - sig_in)).astype(bf16)
    grad_grown = jnp.where((grown > floor_scale) & (retain > 0.5), through * sig_in * 0.5 / scale, 0.0)
    grad_log = carried * hold_ref[7 : 7 + rows, :] * dec_ref[...] - 2.0 * raw * raw * grad_grown
    gd = (grad_log * (-8.0 * rate) * sig_de * (1.0 - sig_de)).astype(bf16)
    gi_ref[...] = gi
    gd_ref[...] = gd
    base_ref[...] = carried * sig_in * scale + dot_nt(gi, inner) + dot_nt(gd, decay)

    @pl.when(pl.program_id(0) == 0)
    def _():
        lat_ref[...] = jnp.zeros_like(lat_ref)

    lat_ref[:, :cols] += dot_nt(gi, leave_in_ref[...])
    lat_ref[:, cols:] += dot_nt(gd, leave_de_ref[...])


def fillback_kernel(
    c_ref, base_ref, own_ref, other_ref, hbase_ref, hown_ref, hother_ref, select_ref, mask_ref, taps_ref, enter_in_ref, enter_de_ref, leave_ref,
    w_ref, enter_ref, before_ref,
    gf_ref, lgi_ref, lgd_ref, lat_ref, mine_ref, theirs_ref, gc_ref, hlg_ref, lg_ref, part_ref,
):
    b = pl.program_id(0)
    q = w_ref.shape[3]
    rows, width = base_ref.shape
    main = part_ref.shape[0]
    cols = lgi_ref.shape[1]

    @pl.when(b == 0)
    def _():
        lat = own_ref[...] + other_ref[...]
        hlat = hown_ref[...] + hother_ref[...]
        select = select_ref[:rows, :]
        hselect = select_ref[rows:, :]
        lgi_ref[...] = (lat[:, :cols] * select).astype(bf16)
        lgd_ref[...] = (lat[:, cols:] * select).astype(bf16)
        hlg_ref[:, :cols] = (hlat[:, :cols] * hselect).astype(bf16)
        hlg_ref[:, cols:] = (hlat[:, cols:] * hselect).astype(bf16)
        step = width // 5
        for j in range(5):
            at = slice(j * step, (j + 1) * step)
            ei = enter_in_ref[at, :]
            ed = enter_de_ref[at, :]
            here = base_ref[:, at] + dot_nt(lgi_ref[...], ei) + dot_nt(lgd_ref[...], ed)
            gc_ref[:main, at] = here[:main]
            gc_ref[main : main + HALO, at] = (
                hbase_ref[:, at] + dot_nt(hlg_ref[:, :cols], ei) + dot_nt(hlg_ref[:, cols:], ed)
            )
            gc_ref[main + HALO : rows + HALO, at] = here[main:]
            gc_ref[rows + HALO :, at] = jnp.zeros((HALO, step), f32)
            for lo, hi, to in ((0, main, 0), (main + HALO, rows + HALO, main)):
                total = taps_ref[0:1, at] * gc_ref[lo:hi, at]
                for k in range(1, taps_ref.shape[0]):
                    total = total + taps_ref[k : k + 1, at] * gc_ref[lo + k : hi + k, at] * mask_ref[lo + k : hi + k, k - 1 : k]
                gf_ref[to : to + hi - lo, at] = total.astype(bf16)
        lat = dot_nt(gf_ref[...], leave_ref[...])
        lat_ref[...] = lat
        lg_ref[...] = (lat[:main] * select_ref[:main, :]).astype(bf16)

    part = dot_nt(gf_ref[:main, :q], tile_of(w_ref, 0)) + dot_nt(gf_ref[:main, q : 2 * q], tile_of(w_ref, 1))
    part_ref[...] = before_ref[...] + part + dot_nt(lg_ref[...], enter_ref[...])
    own = mine_ref.shape[0]
    at = pl.multiple_of(c_ref[0] * own, own)
    mine_ref[...] = part_ref[pl.ds(at, own), :]
    theirs_ref[...] = part_ref[pl.ds(pl.multiple_of(own - at, own), own), :].astype(bf16)


def mids_kernel(count, s_ref, *refs):
    out_ref, hold_ref = refs[2 * count :]
    rank = out_ref.shape[0] // count
    here = pl.ds(pl.multiple_of(s_ref[0] * rank, rank), rank)
    for i in range(count):
        hold_ref[...] = dot_tn(refs[2 * i][...], refs[2 * i + 1][...])
        out_ref[i * rank : (i + 1) * rank, :] = hold_ref[here, :].astype(bf16)


def extras_kernel(count, s_ref, *refs):
    enter_ref, leave_ref = refs[4 * count :]
    for i in range(count):
        enter_ref[i] = dot_tn(refs[2 * i][...], refs[2 * i + 1][...]).astype(bf16)
    for i in range(count):
        k = 2 * count + 2 * i
        leave_ref[i] = dot_tn(refs[k][...], refs[k + 1][...]).astype(bf16)


def square_kernel(s_ref, one_ref, own_e_ref, other_e_ref, own_l_ref, other_l_ref, own_me_ref, other_me_ref, own_ml_ref, other_ml_ref, enter_ref, leave_ref):
    size = own_e_ref.shape[1]
    one = one_ref[...]
    for core, e_ref, l_ref, me_ref, ml_ref in (
        (s_ref[0], own_e_ref, own_l_ref, own_me_ref, own_ml_ref),
        (1 - s_ref[0], other_e_ref, other_l_ref, other_me_ref, other_ml_ref),
    ):
        at = pl.ds(pl.multiple_of(core * size, size), size)
        enter_ref[0, at, :] = e_ref[0].astype(f32) + dot_tn(me_ref[...], one)
        leave_ref[0, :, at] = l_ref[0].astype(f32) + dot_tn(one, ml_ref[...])


def unit_parts(one_ref, extra_ref, mid_ref, size):
    count = extra_ref.shape[0]
    cut = lambda ref, p: jnp.concatenate([ref[m, :, p * size : (p + 1) * size] for m in range(count)], axis=1)
    mid = jnp.concatenate([mid_ref[0, m, :, p * size : (p + 1) * size] for p in range(4) for m in range(count)], axis=1)
    placed = dot_tn(one_ref[...], mid).astype(bf16)
    wide = count * size
    return jnp.concatenate([cut(extra_ref, p) + placed[:, p * wide : (p + 1) * wide] for p in range(4)], axis=0)


def wide_kernel(s_ref, one_ref, spread_ref, extra_ref, mid_ref, out_ref):
    cols = out_ref.shape[0]
    done = dot_nt(unit_parts(one_ref, extra_ref, mid_ref, spread_ref.shape[1] // 8), spread_ref[...])
    out_ref[...] = jnp.concatenate([done[p * cols : (p + 1) * cols] for p in range(4)], axis=1)


def enter_kernel(s_ref, one_ref, spread_ref, extra_ref, mid_ref, out_ref):
    units, size = spread_ref.shape
    cols = out_ref.shape[1]
    done = dot_nt(spread_ref[...], unit_parts(one_ref, extra_ref, mid_ref, size // 8))
    for p in range(4):
        out_ref[p * units : (p + 1) * units, :] = done[:, p * cols : (p + 1) * cols]


def shares_kernel(s_ref, one_ref, eye_ref, extra_l_ref, extra_e_ref, mid_ref, leave_ref, enter_ref):
    one = one_ref[...]
    width = leave_ref.shape[1]
    share = extra_l_ref.shape[2]
    per = mid_ref.shape[3]
    sums = []
    for p in range(16 - 2 * width // per, 16):
        total = mid_ref[p, 0].astype(f32)
        for m in range(1, 8):
            total = total + mid_ref[p, m].astype(f32)
        sums.append(total.astype(bf16))
    mid = jnp.concatenate(sums, axis=1)
    leave_ref[...] = dot_tn(one, mid[:, :width])
    enter_ref[...] = dot_tn(mid[:, width : 2 * width], one)
    for m in range(8):
        lo, hi = m * share, min((m + 1) * share, width)
        if lo < hi:
            leave_ref[:, lo:hi] += extra_l_ref[m, :, : hi - lo].astype(f32)
            enter_ref[lo:hi, :] += dot_tn(extra_e_ref[m], eye_ref[...])[: hi - lo]


def linked(former, latter):
    return (former[0] * latter[0], latter[0] * former[1] + latter[1])


def line_carry(value, axis, reverse):
    sign = -1 if reverse else 1
    here = lax.axis_index(axis)
    here = 3 - here if reverse else here
    came = {by: shift4(value, axis, sign * by) for by in (1, 2, 3)}
    unit = (jnp.ones_like(value[0]), jnp.zeros_like(value[0]))

    def take(so_far, by, valid):
        new = linked(so_far, (came[by][0], came[by][1]))
        return tuple(jnp.where(valid, a, b) for a, b in zip(new, so_far))

    enter = unit
    for by in (3, 2, 1):
        enter = take(enter, by, here >= by)
    total = linked(enter, (value[0], value[1]))
    for by in (3, 2, 1):
        total = take(total, by, here < by)
    return enter, jnp.stack(total)


def chips_carry(value, reverse):
    by_y, line = line_carry(value, YAX, reverse)
    by_x, plane = line_carry(line, "x", reverse)
    by_z, _ = line_carry(plane, "z", reverse)
    return linked(linked(by_z, by_x), by_y)[1]


def index_of(place):
    at = 0
    for i, n in zip(place, (4, 4, 4, 2)):
        at = at * n + i
    return at


def scatter_ends(payload, seg_lanes, c):
    reached = {0: [(0, 0, 0)], 1: [(3, 3, 3)]}
    width = payload.shape[1]
    payload = jnp.concatenate([payload, seg_lanes], axis=1)
    for axis in range(3):
        if axis < 2:
            size = payload.shape[0] // 4
            pieces = [payload[k * size : (k + 1) * size] for k in range(4)]
        else:
            size = width // 4
            pieces = [jnp.concatenate([payload[:, k * size : (k + 1) * size], payload[:, width:]], axis=1) for k in range(4)]
        total = jnp.where(c == 0, pieces[0], pieces[3])
        added = {0: [], 1: []}
        for hop in (2, 1, 3):
            pairs = []
            for core in (0, 1):
                for place in reached[core]:
                    to = list(place)
                    to[axis] = hop if core == 0 else 3 - hop
                    added[core].append(tuple(to))
                    pairs.append((index_of((*place, core)), index_of((*to, core))))
            total = total + lax.ppermute(jnp.where(c == 0, pieces[hop], pieces[3 - hop]), AXES, pairs)
        for core in (0, 1):
            reached[core] = reached[core] + added[core]
        payload = total
    return payload


def line_sum(v, axis):
    one, two, three = (shift4(v, axis, by).astype(f32) for by in (1, 2, 3))
    return (v.astype(f32) + two) + (one + three)


def ring_rows(own):
    parts = [own] + [shift4(own, YAX, by) for by in (1, 2, 3)]
    return parts, [swap(part) for part in parts]


def line_back(sums):
    total = sums[0]
    for by in (1, 2, 3):
        total = total + shift4(sums[by].astype(bf16), YAX, -by).astype(f32)
    return total


def per_device(
    block_input,
    cotangent,
    segments,
    adapter_index,
    norm_first,
    norm_second,
    conv_taps,
    decay_rate,
    gelu_proj,
    input_proj,
    inner_gate,
    decay_gate,
    output_proj,
    widen_proj,
    narrow_proj,
    enter_square,
    leave_square,
    enter_widen,
    leave_widen,
    enter_narrow,
    leave_narrow,
):
    c = lax.axis_index("c")
    y = lax.axis_index(YAX)
    member = lax.axis_index(RING)
    plane = lax.axis_index(PLANE)
    chip = lax.axis_index(("z", "x", "v", "u"))
    place = lax.axis_index(AXES)
    toks, width = block_input.shape
    halfw = width // 2
    quarter = width // 4
    heads = HEADS // 2
    head = width // HEADS
    cols = enter_square.shape[-1]
    rank = cols // ADAPTERS
    main = 2 * toks
    per = gelu_proj.shape[0]
    per4 = 4 * per
    ff = widen_proj.shape[1] // 2
    slot = ff // 8
    slotp = slot * 16 // 15
    wide2 = 2 * slotp
    hcol = slotp // 4
    per_n = narrow_proj.shape[0]
    chunk = slotp // 16
    glane = 2 * head // 4

    grad_down_own = cotangent.astype(bf16)
    seg_lanes = jnp.broadcast_to(jnp.tile(segments, 2).astype(bf16)[:, None], (2 * toks, cols))
    payload = jnp.concatenate([block_input.astype(bf16), grad_down_own], axis=0)
    is_end = (place == 0) | (place == 127)
    piece = scatter_ends(jnp.where(is_end, payload, jnp.zeros_like(payload)), jnp.where(is_end, seg_lanes, jnp.zeros_like(seg_lanes)), c)

    gates = jnp.concatenate([inner_gate, decay_gate], axis=1)
    quads = jnp.stack(
        [
            jnp.concatenate(
                [v[:, q * (v.shape[1] // 4) : (q + 1) * (v.shape[1] // 4)] for v in (gelu_proj, input_proj, output_proj, gates)],
                axis=1,
            )
            for q in range(4)
        ]
    )
    lanes = quads.shape[2]
    quads = lax.all_to_all(quads, QUAD, 0, 0, tiled=True).reshape(per4, lanes)
    reach = piece.shape[1]
    stretches = piece.shape[0] // 8
    piece = jnp.concatenate([piece[k * 8 : (k + 1) * 8] for k in range(stretches)], axis=1)
    piece = jnp.pad(piece, ((0, 0), (0, lanes - stretches * reach)))
    quads = jnp.concatenate([quads, piece], axis=0)
    near = lax.all_gather(quads[None], AXES, axis=0, tiled=True).reshape(32, 4, per4 + 8, lanes)

    block_input, segments, widen_proj, narrow_proj = after(quads, block_input, segments, widen_proj, narrow_proj)

    block = 4 * 8 * per_n
    bcols = 4 * 8 * chunk
    at_col = jnp.arange(bcols)
    unit = at_col % (4 * chunk) % chunk
    from_row = at_col % (4 * chunk) // chunk * (8 * per_n) + at_col // (4 * chunk) * per_n + unit
    spread = ((jnp.arange(block)[:, None] == from_row[None, :]) & (unit < per_n)[None, :]).astype(bf16)
    units = 8 * per_n
    at_unit = jnp.arange(8 * chunk)
    spread_one = (jnp.arange(units)[:, None] == (at_unit // chunk * per_n + at_unit % chunk)[None, :]) & (at_unit % chunk < per_n)[None, :]
    spread_one = spread_one.astype(bf16)
    pieces = widen_proj.reshape(per, 8, block).transpose(1, 0, 2).reshape(8 * per, block)
    pieces = dot(pieces, spread).astype(bf16).reshape(8, per, 8, hcol).transpose(2, 1, 0, 3)
    pieces = lax.all_to_all(pieces.reshape(8 * per, wide2), RING, 0, 0, tiled=True)
    rows_n = jnp.pad(narrow_proj, ((0, chunk - per_n), (0, 0)))
    tail_n = rows_n[:, wide2:].reshape(4, chunk // 4, width - wide2).transpose(1, 0, 2).reshape(chunk // 4, wide2)
    shard_far = jnp.concatenate([pieces, rows_n[:, :wide2], tail_n], axis=0)
    far = lax.all_gather(shard_far[None], PLANE, axis=0, tiled=True)

    middle_owner = adapter_index[MIDDLE]
    column_owner = jnp.arange(cols) // rank
    owner_of = jnp.arange(adapter_index.shape[0])
    one_hot = (jnp.arange(cols)[None, :] == (middle_owner * rank + jnp.arange(rank))[:, None]).astype(bf16)
    core_at = c.astype(jnp.int32).reshape(1)
    middle_at = middle_owner.reshape(1)

    def select_of(segs):
        owners = jnp.sum((segs[:, None] == owner_of[None, :]).astype(jnp.int32) * adapter_index[None, :], axis=1)
        return (owners[:, None] == column_owner[None, :]).astype(f32)

    taps = half(conv_taps, c, 1)
    rate = half(decay_rate, c, 0)[None, :]
    enter_half = half(enter_square, c, 1)
    leave_half = half(leave_square, c, 2)
    enter_gates = jnp.concatenate([enter_half[2], enter_half[3]], axis=1)

    rows = 2 * main
    normed_own = norm_apply(block_input, norm_first)
    normed_main = both(normed_own, swap(normed_own), c)
    normed_halo = chip_shift(normed_main[main - HALO :], 1)
    normed_long = jnp.concatenate([normed_halo, normed_main], axis=0)
    seg_main = both(segments, swap(segments), c)
    halo_seg = jnp.broadcast_to(jnp.where(chip > 0, MIDDLE, -1), (HALO,))
    select_main = select_of(seg_main)
    select_halo = jnp.broadcast_to((column_owner == middle_owner).astype(f32)[None, :], (HALO, cols))
    ring_segs = [jnp.concatenate(v) for v in ring_rows(segments)]
    ring_selects = [select_of(v) for v in ring_segs]

    my_spread = lax.dynamic_slice_in_dim(spread, member * hcol, hcol, axis=1)
    leave_wide = leave_widen.reshape(cols, 8, block).transpose(1, 0, 2).reshape(8 * cols, block)
    leave_wide = dot(leave_wide, my_spread).astype(bf16).reshape(8, cols, hcol).transpose(1, 0, 2).reshape(cols, wide2)
    leave_a, leave_b = leave_wide[:, :slotp], leave_wide[:, slotp:]
    enter_down = lax.dot_general(
        my_spread, enter_narrow.reshape(4, block, cols), (((0,), (1,)), ((), ())), preferred_element_type=f32
    )
    enter_down = enter_down.transpose(1, 0, 2).reshape(slotp, cols).astype(bf16)

    near = after((shard_far, normed_long, select_main, ring_selects, leave_a, leave_b, enter_down, enter_gates), near)
    x_extra, normed_extra, down_extra, marks_extra = call(
        functools.partial(ends_kernel, stretches), (1,),
        [pl.BlockSpec((32, 4, 8, lanes), lambda *_: (0, 0, per4 // 8, 0), pipeline_mode=pl.Buffered(1)), fixed((1, width))],
        [(fixed((main, width)), ((main, width), f32)), (fixed((main, width)), ((main, width), bf16)),
         (fixed((main, width)), ((main, width), bf16)), (fixed((main, cols)), ((main, cols), f32))],
        [pltpu.VMEM((main, width), f32)],
        core_at, (near, norm_first[None, :]), 1,
    )
    seg_first = marks_extra[:toks, 0].astype(jnp.int32)
    seg_last = marks_extra[toks:, 0].astype(jnp.int32)
    seg_extra = jnp.concatenate([seg_first, seg_last])
    normed_long = jnp.concatenate([normed_long, normed_extra], axis=0)
    normed = normed_long[HALO:]
    marks = jnp.concatenate([halo_seg, seg_main, seg_first + 100, seg_last + 200])
    same = [(marks[HALO - k : -k] == marks[HALO:]).astype(f32)[:, None] for k in range(1, 4)]
    mask = jnp.concatenate(same + [jnp.zeros((rows, 5), f32)], axis=1)
    mask_long = jnp.concatenate([mask[:main], jnp.ones((HALO, 8), f32), mask[main:], jnp.zeros((HALO, 8), f32)], axis=0)
    select_extra = select_of(seg_extra) * (seg_extra != MIDDLE).astype(f32)[:, None]
    select = jnp.concatenate([select_main, select_extra], axis=0)
    select_long = jnp.concatenate([select_halo, select], axis=0)
    select_after = jnp.concatenate([select, select_halo], axis=0)

    col_spec = lambda i: pl.BlockSpec((8, 2, per4, quarter), lambda b, s: (b, s[0], 0, i))
    out_spec = pl.BlockSpec((8, 4, per4, quarter), lambda b, s: (2 * s[0] + b, 0, 0, 2))
    gate_spec = pl.BlockSpec((16, 4, per4, glane), lambda b, s: (s[0], 0, 0, 3 * quarter // glane), pipeline_mode=pl.Buffered(1))
    side_col_spec = lambda i: pl.BlockSpec((32, 1, per4, quarter), lambda b, s: (0, 2 * s[0] + b, 0, i))
    rows_spec = lambda n: pl.BlockSpec((n, quarter), lambda b, s: (0, b))
    head_spec = lambda n: pl.BlockSpec((n, head), lambda h, s: (0, h))
    enter_spec = pl.BlockSpec((quarter, cols), lambda b, s: (b, 0))
    hidden_spec = lambda n: pl.BlockSpec((n, hcol), lambda j, s: (0, j))
    wide_block = (rows, halfw)
    small_block = (rows, cols)
    F = lambda *shape: (fixed(shape), (shape, f32))
    B = lambda *shape: (fixed(shape), (shape, bf16))
    layer = 2 * rows * halfw * width
    mib = 2**20

    gd_rows = ring_rows(tied(cotangent, near).astype(bf16))
    long = rows + HALO
    convolved, lat_gates, pick_fill = call(
        fill_kernel, (2,),
        [fixed((long, width)), side_col_spec(1), fixed((width, cols)), fixed((long, cols)), rows_spec(cols), fixed((rows, 8)), rows_spec(4),
         pl.BlockSpec((quarter, 2 * cols), lambda b, s: (b, 0))],
        [(rows_spec(rows), (wide_block, bf16)), F(rows, 2 * cols), B(long, cols)],
        [pltpu.VMEM((long, quarter), f32)],
        core_at, (normed_long, near, enter_square[1], select_long, leave_half[1], mask, taps, enter_gates), 1, (shard_far,),
    )
    pick_fill = pick_fill[HALO:]

    sides = lambda v: [v[:toks], v[toks:]]
    feed_select = [
        jnp.concatenate([ring_selects[0][:toks], sides(select_extra)[0], ring_selects[1][:toks], sides(select_extra)[1]], axis=0),
        ring_selects[0][toks:],
        ring_selects[1][toks:],
    ]
    sig_in, sig_de, decays, state, prod, pick_in, pick_de = call(
        gates_kernel, (heads,),
        [head_spec(rows), fixed((rows, 2 * cols)), fixed((rows, 2 * cols)), fixed(small_block), gate_spec,
         head_spec(cols), head_spec(cols), fixed((rows, 8)), head_spec(1)],
        [(head_spec(rows), (wide_block, f32))] * 5 + [B(*small_block)] * 2,
        [pltpu.VMEM((rows, head), f32), pltpu.VMEM((halfw, 2 * head), bf16)],
        core_at, (convolved, lat_gates, swap(lat_gates), select, near, leave_half[2], leave_half[3], mask, rate), 4, tuple(gd_rows[0][1:]),
    )
    entering = chips_carry(jnp.stack([prod[main - 1], state[main - 1]]), False)[None, :]
    branch, slope, pick_gelu = call(
        gelu_kernel, (2,),
        [fixed((long, width)), side_col_spec(0), fixed((width, cols)), fixed(small_block), rows_spec(cols)],
        [(rows_spec(rows), (wide_block, f32))] * 2 + [B(*small_block)],
        [],
        core_at, (normed_long, near, enter_square[0], select, leave_half[0]), 12,
    )
    states, mixed, lat_out, out_mine, out_send, out_extra = call(
        out_kernel, (2,),
        [rows_spec(rows), rows_spec(rows), rows_spec(1), rows_spec(rows), out_spec, enter_spec, fixed((cols, width)), fixed(small_block)],
        [(rows_spec(rows), (wide_block, f32)), (rows_spec(rows), (wide_block, bf16)), F(*small_block),
         F(toks, width), B(toks + main, width), B(main, width)],
        [pltpu.VMEM((rows, width), f32), pltpu.VMEM((rows, quarter), bf16)],
        core_at, (state, prod, entering, branch, near, enter_half[4], leave_square[4], select), 15,
    )
    pick_out = ((lat_out + swap(lat_out)) * select).astype(bf16)
    got = swap(out_send).astype(f32)
    residual = block_input + out_mine + got[:toks]
    residual_extra = x_extra + (out_extra.astype(f32) + got[toks:])
    n2_extra = norm_apply(residual_extra, norm_second)

    n2_rows = ring_rows(norm_apply(residual, norm_second))
    ring = 8 * toks
    anywhere = pl.BlockSpec(memory_space=pl.ANY)
    far_rows = far.shape[1]

    def feed(n2_pieces, gd_pieces, select, micros, waits=()):
        count = len(n2_pieces)
        n = count * toks
        return call(
            functools.partial(ffn_kernel, count), (1,),
            [anywhere] * (2 * count + 1)
            + [fixed((cols, slotp)), fixed((cols, slotp)), fixed((slotp, cols)), fixed((width, cols)), fixed((cols, width)), fixed((n, cols))],
            [B(n, width)] + [B(n, slotp)] * 3 + [B(n, cols)] * 4,
            [pltpu.VMEM((n, width), bf16), pltpu.VMEM((n, width), bf16), pltpu.VMEM(far.shape, bf16),
             pltpu.SemaphoreType.DMA((count,)), pltpu.SemaphoreType.DMA((count,)), pltpu.SemaphoreType.DMA((4, 3))],
            core_at,
            (*n2_pieces, *gd_pieces, far, leave_a, leave_b, enter_down, enter_widen, leave_narrow, select),
            micros, waits,
        )

    mix = lambda rows, extra: [rows[0][0], sides(extra)[0], rows[1][0], sides(extra)[1]]
    gn0, *parts0 = feed(mix(n2_rows, n2_extra), mix(gd_rows, down_extra), feed_select[0], 60)
    gn1, *parts1 = feed(n2_rows[0][1:], gd_rows[0][1:], feed_select[1], 40, (gn0,))
    gn2, *parts2 = feed(n2_rows[1][1:], gd_rows[1][1:], feed_select[2], 60, (gn1,))
    add = lambda a, b: a.astype(f32) + b.astype(f32)

    eighth = main // 8
    side0 = jnp.concatenate([tied(gn0, gn1).astype(bf16), parts0[3], parts0[4]], axis=1)
    extra_part = jnp.concatenate([side0[toks : 2 * toks], side0[3 * toks :]], axis=0)
    extra_total = lax.all_to_all(extra_part, RING, 0, 0, tiled=True).reshape(8, eighth, -1)
    extra_total = to_low(tied(jnp.sum(extra_total.astype(f32), axis=0), gn2))
    extra_all = lax.all_to_all(jnp.broadcast_to(extra_total[None], (8, *extra_total.shape)), RING, 0, 0, tiled=True).reshape(main, -1)
    sums0 = add(gn0[:toks], swap(gn0[2 * toks : 3 * toks]))
    sums1 = add(gn1, swap(gn2)).astype(bf16)
    sums = [sums0] + [sums1[k * toks : (k + 1) * toks] for k in range(3)]
    mid_spec = (pl.BlockSpec((rank, hcol), lambda j, s: (0, j)), ((rank, slotp), bf16))
    extra_spec = (pl.BlockSpec((cols, hcol), lambda j, s: (0, j)), ((cols, slotp), bf16))
    down, mid_a, mid_b, mid_n, mid_l, mid_e, ex_a, ex_b, ex_n = call(
        down_kernel, (4,),
        [anywhere] * 16 + [hidden_spec(4 * toks), hidden_spec(3 * toks), hidden_spec(3 * toks)] * 3
        + [fixed((4 * toks, cols)), fixed((3 * toks, cols)), fixed((3 * toks, cols))] * 4
        + [pl.BlockSpec((4, far_rows, wide2), lambda j, s: (j, 0, 0)), fixed((cols, width))],
        [B(ring, width)] + [mid_spec] * 3 + [B(rank, width)] * 2 + [extra_spec] * 3,
        [pltpu.VMEM((ring, width), f32), pltpu.VMEM((cols, hcol), f32), pltpu.VMEM((cols, width), f32),
         pltpu.VMEM((ring, width), bf16), pltpu.VMEM((ring, width), bf16), pltpu.SemaphoreType.DMA((8,)), pltpu.SemaphoreType.DMA((8,))],
        middle_at,
        (n2_rows[0][0], n2_rows[1][0], *n2_rows[0][1:], *n2_rows[1][1:], gd_rows[0][0], gd_rows[1][0], *gd_rows[0][1:], *gd_rows[1][1:],
         *[v[i] for i in (2, 0, 1, 5, 6, 4, 3) for v in (parts0, parts1, parts2)], far, leave_narrow),
        60, (*sums[1:], extra_total),
    )
    grad_n2 = tied(line_back(sums), down)
    grad_n2_extra = tied(extra_all[:, :width].astype(f32), down)
    lat_extra = extra_all[:, width:]
    lgw_extra = lat_extra[:, :cols]
    pick_n_extra = lat_extra[:, cols:]
    ffn_mid = tied(jnp.concatenate([mid_a, mid_b, mid_n, mid_l, mid_e], axis=1), grad_n2).astype(bf16)
    ffn_mid = lax.all_to_all(ffn_mid.reshape(rank, 16, -1).transpose(1, 0, 2), PLANE, 0, 0, tiled=True)
    ffn_mid = to_low(jnp.sum(ffn_mid.astype(f32), axis=0))
    ffn_mid = lax.all_gather(ffn_mid[None], AXES, axis=0, tiled=True).reshape(16, 8, rank, -1)

    grad_residual = cotangent + norm_back(residual, norm_second, grad_n2)
    grad_residual_extra = down_extra.astype(f32) + norm_back(residual_extra, norm_second, grad_n2_extra)
    grad_out_own = grad_residual.astype(bf16)
    grad_out = jnp.concatenate([both(grad_out_own, swap(grad_out_own), c), grad_residual_extra.astype(bf16)], axis=0)
    grad_gelu, lg_out, back, trail = call(
        functools.partial(outback_kernel, main), (2,),
        [fixed((rows, width)), out_spec, fixed((cols, width)), enter_spec, fixed(small_block)] + [rows_spec(rows)] * 4,
        [(rows_spec(rows), (wide_block, bf16)), B(*small_block)] + [(rows_spec(rows), (wide_block, f32))] * 2,
        [pltpu.VMEM((rows, quarter), f32)],
        core_at, (grad_out, near, leave_square[4], enter_half[4], select, states, branch, slope, decays), 18,
    )
    coming = chips_carry(jnp.stack([decays[0] * trail[0], decays[0] * back[0]]), True)[None, :]
    down_mine = jnp.concatenate([down[:toks], down[2 * toks : 5 * toks]], axis=0)
    down_theirs = jnp.concatenate([down[toks : 2 * toks], down[5 * toks :]], axis=0)
    down_total = tied(add(down_mine, swap(down_theirs)), coming)
    down_sums = [down_total[k * toks : (k + 1) * toks] for k in range(4)]
    block_output = residual + line_back(down_sums)
    gelu_part, lat_gelu = call(
        geluback_kernel, (4,),
        [fixed(wide_block), col_spec(0), fixed((cols, halfw)), enter_spec, fixed(small_block)],
        [(rows_spec(main), ((main, width), f32)), F(*small_block)],
        [pltpu.VMEM(small_block, bf16)],
        core_at, (grad_gelu, near, leave_half[0], enter_square[0], select), 1,
    )

    grad_in, grad_de, base, lat_gates = call(
        gateback_kernel, (heads,),
        [head_spec(rows), head_spec(rows), head_spec(1), head_spec(rows), head_spec(1)] + [head_spec(rows)] * 4
        + [fixed((rows, 8)), head_spec(1), gate_spec, head_spec(cols), head_spec(cols)],
        [(head_spec(rows), (wide_block, bf16))] * 2 + [(head_spec(rows), (wide_block, f32)), F(rows, 2 * cols)],
        [pltpu.VMEM((rows + 8, head), f32), pltpu.VMEM((halfw, 2 * head), bf16)],
        core_at, (back, trail, coming, states, entering, convolved, sig_in, sig_de, decays, mask, rate, near, leave_half[2], leave_half[3]),
        8,
    )

    share = -(-width // 7 // 128) * 128
    share_of = lambda v: lax.dynamic_slice_in_dim(jnp.pad(v, ((0, 0), (0, 8 * share - width))), member * share, share, axis=1)
    lanes_all = 3 * slotp + 2 * share
    (packed,) = call(
        pack_kernel, (1,),
        [fixed((cols, slotp))] * 3 + [fixed((main, cols))] * 2 + [fixed((main, share))] * 2,
        [B(cols, lanes_all)], [], core_at,
        (ex_a, ex_b, ex_n, pick_n_extra, lgw_extra, share_of(down_extra), share_of(n2_extra)), 3, (base,),
    )
    ffn_all = lax.all_gather(packed, RING, axis=0)

    halo_both = chip_shift(jnp.concatenate([base[:HALO], lat_gates[:HALO]], axis=1), -1)
    halo_base, halo_lat = halo_both[:, :halfw], halo_both[:, halfw:]
    halo_other = chip_shift(lat_gates[:HALO], -1, cross=True)
    grad_fill, lg_in, lg_de, lat_fill, normed_mine, normed_theirs = call(
        fillback_kernel, (4,),
        [fixed(wide_block), fixed((rows, 2 * cols)), fixed((rows, 2 * cols)), fixed((HALO, halfw)), fixed((HALO, 2 * cols)), fixed((HALO, 2 * cols)),
         fixed((rows + HALO, cols)), fixed((rows + 2 * HALO, 8)), fixed((4, halfw)), fixed((halfw, cols)), fixed((halfw, cols)), fixed((cols, halfw)),
         col_spec(1), enter_spec, rows_spec(main)],
        [B(*wide_block), B(*small_block), B(*small_block), F(*small_block),
         (rows_spec(toks), ((toks, width), f32)), (rows_spec(toks), ((toks, width), bf16))],
        [pltpu.VMEM((rows + 2 * HALO, halfw), f32), pltpu.VMEM((HALO, 2 * cols), bf16), pltpu.VMEM((main, cols), bf16), pltpu.VMEM((main, quarter), f32)],
        core_at,
        (base, lat_gates, swap(lat_gates), halo_base, halo_lat, halo_other, select_after, mask_long, taps, enter_half[2], enter_half[3],
         leave_half[1], near, enter_square[1], gelu_part),
        1,
    )

    lg_gelu = ((lat_gelu + swap(lat_gelu)) * select).astype(bf16)
    lg_fill = ((lat_fill + swap(lat_fill)) * select).astype(bf16)
    normed_half = half(normed, c, 1)
    pairs = [
        (lg_gelu, normed_half), (lg_fill, normed_half), (lg_in, convolved), (lg_de, convolved), (lg_out, mixed),
        (pick_gelu, grad_gelu), (pick_fill, grad_fill), (pick_in, grad_in), (pick_de, grad_de), (pick_out, half(grad_out, c, 1)),
    ]
    part_spec = lambda n, i: pl.BlockSpec((main, n), lambda *_: (i, 0), pipeline_mode=pl.Buffered(1))
    operands = [v for pair in pairs for v in pair]
    (mid,) = call(
        functools.partial(mids_kernel, 10), (1,),
        [part_spec(cols, 0), part_spec(halfw, 0)] * 10,
        [B(10 * rank, halfw)],
        [pltpu.VMEM((cols, halfw), f32)],
        middle_at, operands, 6, (block_output,),
    )
    mid_own = mid
    shape = mid.shape
    mid = lax.all_to_all(mid.reshape(64, -1, cols), CHIPS, 0, 0, tiled=True)
    mid = to_low(jnp.sum(mid.astype(f32), axis=0))

    operands = [*[v for pair in pairs[:5] for v in pair[::-1]], *[v for pair in pairs[5:] for v in pair]]
    enter_extra, leave_extra = call(
        functools.partial(extras_kernel, 5), (1,),
        [part_spec(halfw, 1), part_spec(cols, 1)] * 5 + [part_spec(cols, 1), part_spec(halfw, 1)] * 5,
        [B(5, halfw, cols), B(5, cols, halfw)],
        [],
        core_at, operands, 6, (mid_own,),
    )
    (grad_leave_widen,) = call(
        wide_kernel, (8,),
        [fixed((rank, cols)), fixed((units, 8 * chunk)), pl.BlockSpec((8, cols, hcol), lambda i, s: (0, 0, i)), pl.BlockSpec((1, 8, rank, hcol), lambda i, s: (i // 2, 0, 0, i % 2))],
        [(pl.BlockSpec((cols, block), lambda i, s: (0, i)), ((cols, 2 * ff), f32))],
        [], core_at, (one_hot, spread_one, ffn_all, ffn_mid), 12, (mid_own,),
    )
    mid = tied(mid, grad_leave_widen).astype(bf16)
    mid = lax.all_to_all(jnp.broadcast_to(mid[None], (64, *mid.shape)), CHIPS, 0, 0, tiled=True).reshape(shape)
    (grad_enter_narrow,) = call(
        enter_kernel, (4,),
        [fixed((rank, cols)), fixed((units, 8 * chunk)), pl.BlockSpec((8, cols, hcol), lambda i, s: (0, 0, 8 + i)), pl.BlockSpec((1, 8, rank, hcol), lambda i, s: (4 + i // 2, 0, 0, i % 2))],
        [(pl.BlockSpec((block, cols), lambda i, s: (i, 0)), ((ff, cols), f32))],
        [], core_at, (one_hot, spread_one, ffn_all, ffn_mid), 7, (mid_own,),
    )
    grad_normed = normed_mine + swap(normed_theirs).astype(f32)
    input_grad = grad_residual + norm_back(block_input, norm_first, grad_normed)
    eye = jnp.eye(cols, dtype=bf16)
    share_spec = lambda i: pl.BlockSpec((8, cols, share), lambda *_: (0, 0, 3 * slotp // share + i))
    grad_leave_narrow, grad_enter_widen = call(
        shares_kernel, (1,),
        [fixed((rank, cols)), fixed((cols, cols)), share_spec(0), share_spec(1), fixed(ffn_mid.shape)],
        [F(cols, width), F(width, cols)],
        [], core_at, (one_hot, eye, ffn_all, ffn_all, ffn_mid), 4, (mid_own,),
    )
    per_k = lambda *shape: pl.BlockSpec((1,) + shape, lambda k, s: (k,) + (0,) * len(shape))
    mid_e_spec = pl.BlockSpec((rank, halfw), lambda k, s: (k, 0))
    mid_l_spec = pl.BlockSpec((rank, halfw), lambda k, s: (5 + k, 0))
    mid = tied(tied(mid, grad_enter_narrow), grad_leave_narrow).astype(bf16)
    mid_other = swap(mid)
    grad_enter_square, grad_leave_square = call(
        square_kernel, (5,),
        [fixed((rank, cols)), per_k(halfw, cols), per_k(halfw, cols), per_k(cols, halfw), per_k(cols, halfw),
         mid_e_spec, mid_e_spec, mid_l_spec, mid_l_spec],
        [(per_k(width, cols), ((5, width, cols), f32)), (per_k(cols, width), ((5, cols, width), f32))],
        [], core_at, (one_hot, enter_extra, swap(enter_extra), leave_extra, swap(leave_extra), mid, mid_other, mid, mid_other), 9,
    )
    return (
        block_output,
        input_grad,
        grad_enter_square,
        grad_leave_square,
        grad_enter_widen,
        grad_leave_widen,
        grad_enter_narrow,
        grad_leave_narrow,
    )


def solution(mesh):
    split = Mesh(mesh.devices.reshape(SIZES), AXES)
    by_row = P(AXES, None)
    return jax.shard_map(
        per_device,
        mesh=split,
        in_specs=(by_row, by_row, P(AXES), P(), P(), P(), P(), P()) + (by_row,) * 7 + (P(),) * 6,
        out_specs=(by_row, by_row, P(), P(), P(), P(), P(), P()),
        check_vma=False,
    )
```

```python
import functools
import jax
import jax.numpy as jnp
from jax import lax
from jax.experimental import pallas as pl
from jax.experimental.pallas import tpu as pltpu
from jax.sharding import Mesh, PartitionSpec as P

HEADS = 10
ADAPTERS = 8
HALO = 16
MIDDLE = 3
AXES = ("z", "x", "v", "u", "c")
SIZES = (4, 4, 2, 2, 2)
YAX = ("v", "u")
RING = ("v", "u", "c")
PLANE = ("z", "x")
QUAD = ("u", "c")
CHIPS = ("z", "x", "v", "u")
VMEM = 56 * 2**20

eps_norm = 1e-06
floor_scale = 0.001
bf16 = jnp.bfloat16
f32 = jnp.float32


def dot(a, b):
    return jnp.dot(a, b, preferred_element_type=f32)


def dot_nt(a, b):
    return lax.dot_general(a, b, (((1,), (1,)), ((), ())), preferred_element_type=f32)


def dot_tn(a, b):
    return lax.dot_general(a, b, (((0,), (0,)), ((), ())), preferred_element_type=f32)


def low(v):
    return lax.reduce_precision(v, 8, 7)


def to_low(v):
    return low(v).astype(bf16)


def norm_scale(values):
    return lax.rsqrt(jnp.mean(values * values, axis=-1, keepdims=True) + eps_norm)


def norm_apply(values, gain):
    return (values * norm_scale(values) * gain).astype(bf16)


def norm_back(values, gain, grad):
    s = norm_scale(values)
    gq = gain * grad
    return s * gq - values * (s * s * s) * jnp.mean(values * gq, axis=-1, keepdims=True)


def sigmoid(v):
    return 1.0 / (1.0 + jnp.exp(-v))


def gelu_parts(a):
    k = 0.7978845608028654
    a2 = a * a
    th = jnp.tanh(k * (a + 0.044715 * a2 * a))
    value = 0.5 * a * (1.0 + th)
    slope = 0.5 * (1.0 + th) + 0.5 * a * (1.0 - th * th) * (k * (1.0 + 3.0 * 0.044715 * a2))
    return value, slope


def swap(v):
    return lax.ppermute(v, "c", [(0, 1), (1, 0)])


def shift4(v, axis, by):
    return lax.ppermute(v, axis, [(i, (i + by) % 4) for i in range(4)])


def chip_shift(v, by, cross=False):
    chips = 64
    pairs = [
        (2 * p + c, 2 * (p + by) + (1 - c if cross else c))
        for p in range(chips)
        for c in range(2)
        if 0 <= p + by < chips
    ]
    return lax.ppermute(v, AXES, pairs)


def both(own, other, c):
    rows = own.shape[0]
    three = jnp.concatenate([own, other, own], axis=0)
    return lax.dynamic_slice_in_dim(three, c * rows, 2 * rows, axis=0)


def half(v, c, axis):
    size = v.shape[axis] // 2
    return lax.dynamic_slice_in_dim(v, c * size, size, axis=axis)


def after(first, *values):
    held = lax.optimization_barrier((first, *values))[1:]
    return held[0] if len(held) == 1 else held


def tied(value, other):
    return value + other[(0,) * other.ndim].astype(f32) * 0.0


def line_order(parts, y):
    back = parts[::-1]
    twice = jnp.stack(back + back)
    return lax.dynamic_slice_in_dim(twice, 3 - y, 4, axis=0)


def call(kernel, grid, ins, outs, scratch, scalars, args, micros, waits=()):
    count = len(args)

    def body(s_ref, *refs):
        kernel(s_ref, *refs[:count], *refs[count + len(waits) :])

    ins = list(ins) + [pl.BlockSpec(memory_space=pl.ANY)] * len(waits)
    args = (*args, *waits)
    return pl.pallas_call(
        body,
        grid_spec=pltpu.PrefetchScalarGridSpec(
            num_scalar_prefetch=1,
            grid=grid,
            in_specs=ins,
            out_specs=[spec for spec, _ in outs],
            scratch_shapes=scratch,
        ),
        out_shape=[jax.ShapeDtypeStruct(*shape) for _, shape in outs],
        compiler_params=pltpu.CompilerParams(vmem_limit_bytes=VMEM),
        cost_estimate=pl.CostEstimate(flops=int(micros * 1e9), bytes_accessed=int(micros * 2e6), transcendentals=0),
    )(scalars, *args)


def fixed(shape):
    return pl.BlockSpec(shape, lambda *_: (0,) * len(shape), pipeline_mode=pl.Buffered(1))


def scan_rows(d_ref, p_ref, s_ref, q_ref):
    rows, width = d_ref.shape
    row = lax.broadcasted_iota(jnp.int32, (8, width), 0)

    def tile(i, carry):
        state, product = carry
        at = pl.ds(pl.multiple_of(i * 8, 8), 8)
        a = d_ref[at, :]
        b = p_ref[at, :]
        for s in (1, 2, 4):
            b = a * jnp.where(row >= s, pltpu.roll(b, s, 0), 0.0) + b
            a = a * jnp.where(row >= s, pltpu.roll(a, s, 0), 1.0)
        value = b + a * state
        through = a * product
        s_ref[at, :] = value
        q_ref[at, :] = through
        return value[7:8, :], through[7:8, :]

    lax.fori_loop(
        0, rows // 8, tile, (jnp.zeros((1, width), f32), jnp.ones((1, width), f32)), unroll=8
    )


def scan_rows_back(d_ref, g_ref, s_ref, q_ref, main):
    rows, width = d_ref.shape
    row = lax.broadcasted_iota(jnp.int32, (8, width), 0)

    def tile(i, carry):
        state, product, after_row = carry
        at = pl.ds(pl.multiple_of(i * 8, 8), 8)
        d = d_ref[at, :]
        b = g_ref[at, :]
        a = jnp.where(row < 7, pltpu.roll(d, 7, 0), after_row)
        for s in (1, 2, 4):
            b = a * jnp.where(row < 8 - s, pltpu.roll(b, 8 - s, 0), 0.0) + b
            a = a * jnp.where(row < 8 - s, pltpu.roll(a, 8 - s, 0), 1.0)
        value = b + a * state
        through = a * product
        s_ref[at, :] = value
        q_ref[at, :] = through
        return value[0:1, :], through[0:1, :], d[0:1, :]

    zero = jnp.zeros((1, width), f32)
    one = jnp.ones((1, width), f32)
    last, cut = rows // 8 - 1, main // 8
    lax.fori_loop(0, last + 1 - cut, lambda k, t: tile(last - k, t), (zero, zero, one), unroll=8)
    lax.fori_loop(0, cut, lambda k, t: tile(cut - 1 - k, t), (zero, one, one), unroll=8)


def tile_of(w, i):
    block = w[:, i]
    return block.reshape(block.shape[0] * block.shape[1], block.shape[2])


def ends_kernel(stretches, s_ref, near_ref, gain_ref, x_ref, normed_ref, down_ref, marks_ref, hold_ref):
    toks = x_ref.shape[0] // 2
    quarter = x_ref.shape[1] // 4
    reach = quarter + marks_ref.shape[1]
    size = 8 * stretches
    for core in range(2):
        for p in range(16):
            for h in range(stretches):
                row = p * size + h * 8
                for y in range(4):
                    block = near_ref[2 * p + y // 2, 2 * (y % 2) + core, :, h * reach : (h + 1) * reach].astype(f32)
                    cols = slice(y * quarter, (y + 1) * quarter)
                    if row < toks:
                        x_ref[core * toks + row : core * toks + row + 8, cols] = block[:, :quarter]
                        if y == 0:
                            marks_ref[core * toks + row : core * toks + row + 8, :] = block[:, quarter:]
                    else:
                        to = core * toks + row - toks
                        hold_ref[to : to + 8, cols] = block[:, :quarter]
    down_ref[...] = hold_ref[...].astype(bf16)
    x = x_ref[...]
    normed_ref[...] = norm_apply(x, gain_ref[...])


def pack_kernel(s_ref, exa_ref, exb_ref, exn_ref, pick_ref, lg_ref, down_ref, n2_ref, out_ref):
    wide = exa_ref.shape[1]
    share = down_ref.shape[1]
    for i, ref in enumerate((exa_ref, exb_ref, exn_ref)):
        out_ref[:, i * wide : (i + 1) * wide] = ref[...]
    at = 3 * wide
    out_ref[:, at : at + share] = dot_tn(pick_ref[...], down_ref[...]).astype(bf16)
    out_ref[:, at + share :] = dot_tn(lg_ref[...], n2_ref[...]).astype(bf16)


def fill_kernel(c_ref, x_ref, w_ref, first_ref, select_ref, leave_ref, mask_ref, taps_ref, enter_ref, conv_ref, lat_ref, pick_ref, acc_ref):
    rows, width = conv_ref.shape

    @pl.when(pl.program_id(0) == 0)
    def _():
        pick_ref[...] = (dot(x_ref[...], first_ref[...]) * select_ref[...]).astype(bf16)

    acc_ref[...] = dot(x_ref[...], tile_of(w_ref, 0)) + dot(pick_ref[...], leave_ref[...])
    step = width // 5
    for j in range(5):
        at = slice(j * step, (j + 1) * step)
        total = taps_ref[0:1, at] * acc_ref[HALO : HALO + rows, at]
        for k in range(1, taps_ref.shape[0]):
            total = total + taps_ref[k : k + 1, at] * acc_ref[HALO - k : HALO - k + rows, at] * mask_ref[:, k - 1 : k]
        conv_ref[:, at] = total.astype(bf16)

    @pl.when(pl.program_id(0) == 0)
    def _():
        lat_ref[...] = jnp.zeros_like(lat_ref)

    lat_ref[...] += dot(conv_ref[...], enter_ref[...])


def gate_weights(w_ref, hold_ref):
    @pl.when(pl.program_id(0) == 0)
    def _():
        wide = w_ref.shape[3]
        for i in range(4):
            hold_ref[:, i * wide : (i + 1) * wide] = tile_of(w_ref, i)

    head = 2 * w_ref.shape[3]
    at = pl.ds(pl.multiple_of(pl.program_id(0) * head, head), head)
    return hold_ref[at, :head], hold_ref[at, head:]


def gates_kernel(
    c_ref, conv_ref, own_ref, other_ref, select_ref, w_ref, leave_in_ref, leave_de_ref, mask_ref, rate_ref,
    sin_ref, sde_ref, dec_ref, state_ref, prod_ref, pick_in_ref, pick_de_ref, push_ref, hold_ref,
):
    cols = select_ref.shape[1]
    inner, decay = gate_weights(w_ref, hold_ref)

    @pl.when(pl.program_id(0) == 0)
    def _():
        lat = own_ref[...] + other_ref[...]
        select = select_ref[...]
        pick_in_ref[...] = (lat[:, :cols] * select).astype(bf16)
        pick_de_ref[...] = (lat[:, cols:] * select).astype(bf16)

    retain = mask_ref[:, 0:1]
    conv = conv_ref[...]
    sig_in = sigmoid(dot(conv, inner) + dot(pick_in_ref[...], leave_in_ref[...]))
    sig_de = sigmoid(dot(conv, decay) + dot(pick_de_ref[...], leave_de_ref[...]))
    raw = jnp.exp(-8.0 * rate_ref[...] * sig_de)
    scale = jnp.where(retain > 0.5, jnp.sqrt(jnp.maximum(1.0 - raw * raw, floor_scale)), 1.0)
    sin_ref[...] = sig_in
    sde_ref[...] = sig_de
    dec_ref[...] = raw * retain
    push_ref[...] = conv.astype(f32) * sig_in * scale
    scan_rows(dec_ref, push_ref, state_ref, prod_ref)


def gelu_kernel(c_ref, x_ref, w_ref, first_ref, select_ref, leave_ref, value_ref, slope_ref, pick_ref):
    @pl.when(pl.program_id(0) == 0)
    def _():
        pick_ref[...] = (dot(x_ref[HALO:, :], first_ref[...]) * select_ref[...]).astype(bf16)

    pre = dot(x_ref[HALO:, :], tile_of(w_ref, 0)) + dot(pick_ref[...], leave_ref[...])
    value, slope = gelu_parts(pre)
    value_ref[...] = value
    slope_ref[...] = slope


def out_kernel(
    c_ref, state_ref, prod_ref, entering_ref, branch_ref, w_ref, enter_ref, leave_ref, select_ref,
    states_ref, mixed_ref, lat_ref, mine_ref, send_ref, extra_ref, acc_ref, hold_ref,
):
    b = pl.program_id(0)
    q = w_ref.shape[3]
    states = state_ref[...] + prod_ref[...] * entering_ref[...]
    states_ref[...] = states
    hold_ref[...] = (branch_ref[...] * states).astype(bf16)
    mixed_ref[...] = hold_ref[...]

    @pl.when(b == 0)
    def _():
        lat_ref[...] = jnp.zeros_like(lat_ref)
        acc_ref[...] = jnp.zeros_like(acc_ref)

    lat_ref[...] += dot(hold_ref[...], enter_ref[...])
    for i in range(4):
        acc_ref[:, i * q : (i + 1) * q] += dot(hold_ref[...], tile_of(w_ref, i))

    @pl.when(b == pl.num_programs(0) - 1)
    def _():
        acc_ref[...] += dot((lat_ref[...] * select_ref[...]).astype(bf16), leave_ref[...])
        rows = mine_ref.shape[0]
        at = pl.multiple_of(c_ref[0] * rows, rows)
        mine_ref[...] = acc_ref[pl.ds(at, rows), :]
        send_ref[:rows, :] = acc_ref[pl.ds(pl.multiple_of(rows - at, rows), rows), :].astype(bf16)
        extra = acc_ref[2 * rows :, :].astype(bf16)
        send_ref[rows:, :] = extra
        extra_ref[...] = extra


def narrow_block(far_ref, j, top):
    wide = far_ref.shape[2]
    tail = wide // 4
    low_rows = (far_ref.shape[1] - top) // 5
    planes = pl.ds(4 * j, 4)
    main = far_ref[planes, top : top + 4 * low_rows, :].reshape(16 * low_rows, wide)
    pieces = []
    for p in range(4):
        rows = far_ref[4 * j + p, top + 4 * low_rows :, :]
        pieces += [rows[:, k * tail : (k + 1) * tail] for k in range(4)]
    return main, jnp.concatenate(pieces, axis=0)


def fetch(refs, hold_ref, sems):
    size = refs[0].shape[0]
    return [pltpu.make_async_copy(r, hold_ref.at[pl.ds(i * size, size), :], sems.at[i]) for i, r in enumerate(refs)]


def ffn_kernel(count, s_ref, *refs):
    n2_refs, gd_refs = refs[:count], refs[count : 2 * count]
    far_hbm, la_ref, lb_ref, en_ref, ew_ref, ln_ref, select_ref = refs[2 * count : 2 * count + 7]
    gn_ref, ga_ref, gb_ref, hid_ref, lgw_ref, pickn_ref, pickw_ref, lgn_ref = refs[2 * count + 7 : 2 * count + 15]
    n2_hold, gd_hold, far_ref, n2_sems, gd_sems, far_sems = refs[2 * count + 15 :]
    width = gn_ref.shape[1]
    slotp = hid_ref.shape[1]
    step = slotp // 4
    wide = far_ref.shape[2]
    top = width // 16

    def far_copies(j):
        at = pl.ds(pl.multiple_of(j * step, step), step)
        at_b = pl.ds(pl.multiple_of(slotp + j * step, step), step)
        planes = pl.ds(4 * j, 4)
        places = [(slice(None), pl.ds(0, top), at), (slice(None), pl.ds(0, top), at_b), (planes, pl.ds(top, far_ref.shape[1] - top), slice(None))]
        return [pltpu.make_async_copy(far_hbm.at[p], far_ref.at[p], far_sems.at[j, i]) for i, p in enumerate(places)]

    n2_copies = fetch(n2_refs, n2_hold, n2_sems)
    gd_copies = fetch(gd_refs, gd_hold, gd_sems)
    for copy in n2_copies + gd_copies:
        copy.start()
    for j in range(4):
        for copy in far_copies(j):
            copy.start()
    for copy in n2_copies + gd_copies:
        copy.wait()
    select = select_ref[...]
    pickw_ref[...] = (dot(n2_hold[...], ew_ref[...]) * select).astype(bf16)
    lgn_ref[...] = (dot_nt(gd_hold[...], ln_ref[...]) * select).astype(bf16)

    def hidden(j, _):
        for copy in far_copies(j):
            copy.wait()
        at = pl.ds(pl.multiple_of(j * step, step), step)
        at_b = pl.ds(pl.multiple_of(slotp + j * step, step), step)
        a = dot(n2_hold[...], far_ref[:, :top, at].reshape(width, step)) + dot(pickw_ref[...], la_ref[:, at])
        up = dot(n2_hold[...], far_ref[:, :top, at_b].reshape(width, step)) + dot(pickw_ref[...], lb_ref[:, at])
        main, last = narrow_block(far_ref, j, top)
        grad = dot_nt(gd_hold[:, :wide], main) + dot_nt(gd_hold[:, wide:], last) + dot_nt(lgn_ref[...], en_ref[at, :])
        act, slope = gelu_parts(a)
        hid_ref[:, at] = (act * up).astype(bf16)
        ga_ref[:, at] = (slope * up * grad).astype(bf16)
        gb_ref[:, at] = (act * grad).astype(bf16)
        return 0

    lax.fori_loop(0, 4, hidden, 0)
    lgw_ref[...] = ((dot_nt(ga_ref[...], la_ref[...]) + dot_nt(gb_ref[...], lb_ref[...])) * select).astype(bf16)
    pickn_ref[...] = (dot(hid_ref[...], en_ref[...]) * select).astype(bf16)
    part = width // 4

    def back(q, _):
        at = pl.ds(pl.multiple_of(q * part, part), part)
        planes = pl.ds(4 * q, 4)
        total = dot_nt(ga_ref[...], far_ref[planes, :top, :slotp].reshape(part, slotp))
        total += dot_nt(gb_ref[...], far_ref[planes, :top, slotp:].reshape(part, slotp))
        gn_ref[:, at] = (total + dot_nt(lgw_ref[...], ew_ref[at, :])).astype(bf16)
        return 0

    lax.fori_loop(0, 4, back, 0)


def down_kernel(s_ref, *refs):
    n2_refs, gd_refs = refs[:8], refs[8:16]
    hid, ga, gb, pick, lgn, pickn, lgw = [refs[16 + 3 * i : 19 + 3 * i] for i in range(7)]
    far_ref, ln_ref = refs[37:39]
    mine_ref, theirs_ref, mida_ref, midb_ref, midn_ref, midl_ref, mide_ref, exa_ref, exb_ref, exn_ref = refs[39:49]
    acc_ref, hold_ref, wide_ref, n2_hold, gd_hold, n2_sems, gd_sems = refs[49:]
    j = pl.program_id(0)
    rank = mida_ref.shape[0]
    piece = n2_refs[0].shape[0]
    here = pl.ds(pl.multiple_of(s_ref[0] * rank, rank), rank)
    main, last = narrow_block(far_ref, 0, far_ref.shape[1] * 2 // 3)
    cut = main.shape[1]
    ring_of = lambda v: jnp.concatenate([v[0][:piece, :], v[0][2 * piece : 3 * piece, :], v[1][...], v[2][...]], axis=0)
    rest_of = lambda v: jnp.concatenate([v[0][piece : 2 * piece, :], v[0][3 * piece :, :]], axis=0)
    n2_copies = fetch(n2_refs, n2_hold, n2_sems)
    gd_copies = fetch(gd_refs, gd_hold, gd_sems)

    @pl.when(j == 0)
    def _():
        for copy in n2_copies + gd_copies:
            copy.start()
        acc_ref[...] = dot(ring_of(pickn), ln_ref[...])

    hidden = ring_of(hid)
    acc_ref[:, :cut] += dot(hidden, main)
    acc_ref[:, cut:] += dot(hidden, last)
    for left, right, out_ref, extra_ref in ((pick, ga, mida_ref, exa_ref), (pick, gb, midb_ref, exb_ref), (lgn, hid, midn_ref, exn_ref)):
        hold_ref[...] = dot_tn(ring_of(left), ring_of(right))
        out_ref[...] = hold_ref[here, :].astype(bf16)
        extra_ref[...] = dot_tn(rest_of(left), rest_of(right)).astype(bf16)

    @pl.when(j == pl.num_programs(0) - 1)
    def _():
        for k in range(4):
            to = pl.ds(pl.multiple_of(lax.rem(s_ref[1] - k + 4, 4) * piece, piece), piece)
            own, other = (0, 1) if k == 0 else (k + 1, k + 4)
            mine_ref[to, :] = acc_ref[own * piece : (own + 1) * piece, :].astype(bf16)
            theirs_ref[to, :] = acc_ref[other * piece : (other + 1) * piece, :].astype(bf16)
        for copy in n2_copies + gd_copies:
            copy.wait()
        wide_ref[...] = dot_tn(ring_of(pickn), gd_hold[...])
        midl_ref[...] = wide_ref[here, :].astype(bf16)
        wide_ref[...] = dot_tn(ring_of(lgw), n2_hold[...])
        mide_ref[...] = wide_ref[here, :].astype(bf16)


def outback_kernel(
    main, c_ref, go_ref, w_ref, leave_ref, enter_ref, select_ref, states_ref, branch_ref, slope_ref, dec_ref,
    gg_ref, lg_ref, state_ref, prod_ref, gs_ref,
):
    b = pl.program_id(0)
    q = w_ref.shape[3]

    @pl.when(b == 0)
    def _():
        lg_ref[...] = (dot_nt(go_ref[...], leave_ref[...]) * select_ref[...]).astype(bf16)

    gm = dot_nt(lg_ref[...], enter_ref[...])
    for i in range(4):
        gm += dot_nt(go_ref[:, i * q : (i + 1) * q], tile_of(w_ref, i))
    gg_ref[...] = (slope_ref[...] * (gm * states_ref[...])).astype(bf16)
    gs_ref[...] = gm * branch_ref[...]
    scan_rows_back(dec_ref, gs_ref, state_ref, prod_ref, main)


def geluback_kernel(c_ref, g_ref, w_ref, leave_ref, enter_ref, select_ref, part_ref, lat_ref, lg_ref):
    b = pl.program_id(0)
    q = w_ref.shape[3]

    @pl.when(b == 0)
    def _():
        lat = dot_nt(g_ref[...], leave_ref[...])
        lat_ref[...] = lat
        lg_ref[...] = (lat * select_ref[...]).astype(bf16)

    rows = part_ref.shape[0]
    part = dot_nt(g_ref[:rows, :q], tile_of(w_ref, 0)) + dot_nt(g_ref[:rows, q : 2 * q], tile_of(w_ref, 1))
    part_ref[...] = part + dot_nt(lg_ref[:rows, :], enter_ref[...])


def gateback_kernel(
    c_ref, back_ref, trail_ref, coming_ref, states_ref, entering_ref, conv_ref, sin_ref, sde_ref, dec_ref, mask_ref, rate_ref,
    w_ref, leave_in_ref, leave_de_ref,
    gi_ref, gd_ref, base_ref, lat_ref, hold_ref, gate_ref,
):
    rows = conv_ref.shape[0]
    cols = leave_in_ref.shape[0]
    inner, decay = gate_weights(w_ref, gate_ref)
    retain = mask_ref[:, 0:1]
    hold_ref[7:8, :] = entering_ref[...]
    hold_ref[8:, :] = states_ref[...]
    rate = rate_ref[...]
    sig_in = sin_ref[...]
    sig_de = sde_ref[...]
    conv = conv_ref[...].astype(f32)
    carried = back_ref[...] + trail_ref[...] * coming_ref[...]
    raw = jnp.exp(-8.0 * rate * sig_de)
    grown = 1.0 - raw * raw
    scale = jnp.where(retain > 0.5, jnp.sqrt(jnp.maximum(grown, floor_scale)), 1.0)
    through = carried * conv
    gi = (through * scale * sig_in * (1.0 - sig_in)).astype(bf16)
    grad_grown = jnp.where((grown > floor_scale) & (retain > 0.5), through * sig_in * 0.5 / scale, 0.0)
    grad_log = carried * hold_ref[7 : 7 + rows, :] * dec_ref[...] - 2.0 * raw * raw * grad_grown
    gd = (grad_log * (-8.0 * rate) * sig_de * (1.0 - sig_de)).astype(bf16)
    gi_ref[...] = gi
    gd_ref[...] = gd
    base_ref[...] = carried * sig_in * scale + dot_nt(gi, inner) + dot_nt(gd, decay)

    @pl.when(pl.program_id(0) == 0)
    def _():
        lat_ref[...] = jnp.zeros_like(lat_ref)

    lat_ref[:, :cols] += dot_nt(gi, leave_in_ref[...])
    lat_ref[:, cols:] += dot_nt(gd, leave_de_ref[...])


def fillback_kernel(
    c_ref, base_ref, own_ref, other_ref, hbase_ref, hown_ref, hother_ref, select_ref, mask_ref, taps_ref, enter_in_ref, enter_de_ref, leave_ref,
    w_ref, enter_ref, before_ref,
    gf_ref, lgi_ref, lgd_ref, lat_ref, mine_ref, theirs_ref, gc_ref, hlg_ref, lg_ref, part_ref,
):
    b = pl.program_id(0)
    q = w_ref.shape[3]
    rows, width = base_ref.shape
    main = part_ref.shape[0]
    cols = lgi_ref.shape[1]

    @pl.when(b == 0)
    def _():
        lat = own_ref[...] + other_ref[...]
        hlat = hown_ref[...] + hother_ref[...]
        select = select_ref[:rows, :]
        hselect = select_ref[rows:, :]
        lgi_ref[...] = (lat[:, :cols] * select).astype(bf16)
        lgd_ref[...] = (lat[:, cols:] * select).astype(bf16)
        hlg_ref[:, :cols] = (hlat[:, :cols] * hselect).astype(bf16)
        hlg_ref[:, cols:] = (hlat[:, cols:] * hselect).astype(bf16)
        step = width // 5
        for j in range(5):
            at = slice(j * step, (j + 1) * step)
            ei = enter_in_ref[at, :]
            ed = enter_de_ref[at, :]
            here = base_ref[:, at] + dot_nt(lgi_ref[...], ei) + dot_nt(lgd_ref[...], ed)
            gc_ref[:main, at] = here[:main]
            gc_ref[main : main + HALO, at] = (
                hbase_ref[:, at] + dot_nt(hlg_ref[:, :cols], ei) + dot_nt(hlg_ref[:, cols:], ed)
            )
            gc_ref[main + HALO : rows + HALO, at] = here[main:]
            gc_ref[rows + HALO :, at] = jnp.zeros((HALO, step), f32)
            for lo, hi, to in ((0, main, 0), (main + HALO, rows + HALO, main)):
                total = taps_ref[0:1, at] * gc_ref[lo:hi, at]
                for k in range(1, taps_ref.shape[0]):
                    total = total + taps_ref[k : k + 1, at] * gc_ref[lo + k : hi + k, at] * mask_ref[lo + k : hi + k, k - 1 : k]
                gf_ref[to : to + hi - lo, at] = total.astype(bf16)
        lat = dot_nt(gf_ref[...], leave_ref[...])
        lat_ref[...] = lat
        lg_ref[...] = (lat[:main] * select_ref[:main, :]).astype(bf16)

    part = dot_nt(gf_ref[:main, :q], tile_of(w_ref, 0)) + dot_nt(gf_ref[:main, q : 2 * q], tile_of(w_ref, 1))
    part_ref[...] = before_ref[...] + part + dot_nt(lg_ref[...], enter_ref[...])
    own = mine_ref.shape[0]
    at = pl.multiple_of(c_ref[0] * own, own)
    mine_ref[...] = part_ref[pl.ds(at, own), :]
    theirs_ref[...] = part_ref[pl.ds(pl.multiple_of(own - at, own), own), :].astype(bf16)


def mids_kernel(count, rank, s_ref, *refs):
    out_ref, hold_ref = refs[2 * count :]
    here = pl.ds(pl.multiple_of(s_ref[0] * rank, rank), rank)
    lanes = out_ref.shape[1]
    parts = hold_ref.shape[1] // lanes
    for i in range(count):
        hold_ref[...] = dot_tn(refs[2 * i][...], refs[2 * i + 1][...])
        for j in range(parts):
            at = (i * parts + j) * rank
            out_ref[at : at + rank, :] = hold_ref[here, j * lanes : (j + 1) * lanes].astype(bf16)
    filled = count * parts * rank
    out_ref[filled:, :] = jnp.zeros((out_ref.shape[0] - filled, lanes), bf16)


def extras_kernel(count, s_ref, *refs):
    enter_ref, leave_ref = refs[4 * count :]
    for i in range(count):
        enter_ref[i] = dot_tn(refs[2 * i][...], refs[2 * i + 1][...]).astype(bf16)
    for i in range(count):
        k = 2 * count + 2 * i
        leave_ref[i] = dot_tn(refs[k][...], refs[k + 1][...]).astype(bf16)


def square_kernel(s_ref, one_ref, own_e_ref, other_e_ref, own_l_ref, other_l_ref, own_me_ref, other_me_ref, own_ml_ref, other_ml_ref, enter_ref, leave_ref):
    size = own_e_ref.shape[1]
    one = one_ref[...]
    rank = one.shape[0]
    whole = lambda ref: jnp.concatenate([ref[j * rank : (j + 1) * rank, :] for j in range(ref.shape[0] // rank)], axis=1)
    for core, e_ref, l_ref, me_ref, ml_ref in (
        (s_ref[0], own_e_ref, own_l_ref, own_me_ref, own_ml_ref),
        (1 - s_ref[0], other_e_ref, other_l_ref, other_me_ref, other_ml_ref),
    ):
        at = pl.ds(pl.multiple_of(core * size, size), size)
        enter_ref[0, at, :] = e_ref[0].astype(f32) + dot_tn(whole(me_ref), one)
        leave_ref[0, :, at] = l_ref[0].astype(f32) + dot_tn(one, whole(ml_ref))


def unit_parts(one_ref, extra_ref, mid_ref, size):
    count = extra_ref.shape[0]
    cut = lambda ref, p: jnp.concatenate([ref[m, :, p * size : (p + 1) * size] for m in range(count)], axis=1)
    mid = jnp.concatenate([mid_ref[0, m, :, p * size : (p + 1) * size] for p in range(4) for m in range(count)], axis=1)
    placed = dot_tn(one_ref[...], mid).astype(bf16)
    wide = count * size
    return jnp.concatenate([cut(extra_ref, p) + placed[:, p * wide : (p + 1) * wide] for p in range(4)], axis=0)


def wide_kernel(s_ref, one_ref, spread_ref, extra_ref, mid_ref, out_ref):
    cols = out_ref.shape[0]
    done = dot_nt(unit_parts(one_ref, extra_ref, mid_ref, spread_ref.shape[1] // 8), spread_ref[...])
    out_ref[...] = jnp.concatenate([done[p * cols : (p + 1) * cols] for p in range(4)], axis=1)


def enter_kernel(s_ref, one_ref, spread_ref, extra_ref, mid_ref, out_ref):
    units, size = spread_ref.shape
    cols = out_ref.shape[1]
    done = dot_nt(spread_ref[...], unit_parts(one_ref, extra_ref, mid_ref, size // 8))
    for p in range(4):
        out_ref[p * units : (p + 1) * units, :] = done[:, p * cols : (p + 1) * cols]


def shares_kernel(s_ref, one_ref, eye_ref, extra_l_ref, extra_e_ref, mid_ref, leave_ref, enter_ref):
    one = one_ref[...]
    width = leave_ref.shape[1]
    share = extra_l_ref.shape[2]
    per = mid_ref.shape[3]
    sums = []
    for p in range(16 - 2 * width // per, 16):
        total = mid_ref[p, 0].astype(f32)
        for m in range(1, 8):
            total = total + mid_ref[p, m].astype(f32)
        sums.append(total.astype(bf16))
    mid = jnp.concatenate(sums, axis=1)
    leave_ref[...] = dot_tn(one, mid[:, :width])
    enter_ref[...] = dot_tn(mid[:, width : 2 * width], one)
    for m in range(8):
        lo, hi = m * share, min((m + 1) * share, width)
        if lo < hi:
            leave_ref[:, lo:hi] += extra_l_ref[m, :, : hi - lo].astype(f32)
            enter_ref[lo:hi, :] += dot_tn(extra_e_ref[m], eye_ref[...])[: hi - lo]


def linked(former, latter):
    return (former[0] * latter[0], latter[0] * former[1] + latter[1])


def line_carry(value, axis, reverse):
    sign = -1 if reverse else 1
    here = lax.axis_index(axis)
    here = 3 - here if reverse else here
    came = {by: shift4(value, axis, sign * by) for by in (1, 2, 3)}
    unit = (jnp.ones_like(value[0]), jnp.zeros_like(value[0]))

    def take(so_far, by, valid):
        new = linked(so_far, (came[by][0], came[by][1]))
        return tuple(jnp.where(valid, a, b) for a, b in zip(new, so_far))

    enter = unit
    for by in (3, 2, 1):
        enter = take(enter, by, here >= by)
    total = linked(enter, (value[0], value[1]))
    for by in (3, 2, 1):
        total = take(total, by, here < by)
    return enter, jnp.stack(total)


def chips_carry(value, reverse):
    by_y, line = line_carry(value, YAX, reverse)
    by_x, plane = line_carry(line, "x", reverse)
    by_z, _ = line_carry(plane, "z", reverse)
    return linked(linked(by_z, by_x), by_y)[1]


def index_of(place):
    at = 0
    for i, n in zip(place, (4, 4, 4, 2)):
        at = at * n + i
    return at


def scatter_ends(payload, seg_lanes, c):
    reached = {0: [(0, 0, 0)], 1: [(3, 3, 3)]}
    width = payload.shape[1]
    payload = jnp.concatenate([payload, seg_lanes], axis=1)
    for axis in range(3):
        if axis < 2:
            size = payload.shape[0] // 4
            pieces = [payload[k * size : (k + 1) * size] for k in range(4)]
        else:
            size = width // 4
            pieces = [jnp.concatenate([payload[:, k * size : (k + 1) * size], payload[:, width:]], axis=1) for k in range(4)]
        total = jnp.where(c == 0, pieces[0], pieces[3])
        added = {0: [], 1: []}
        for hop in (2, 1, 3):
            pairs = []
            for core in (0, 1):
                for place in reached[core]:
                    to = list(place)
                    to[axis] = hop if core == 0 else 3 - hop
                    added[core].append(tuple(to))
                    pairs.append((index_of((*place, core)), index_of((*to, core))))
            total = total + lax.ppermute(jnp.where(c == 0, pieces[hop], pieces[3 - hop]), AXES, pairs)
        for core in (0, 1):
            reached[core] = reached[core] + added[core]
        payload = total
    return payload


def line_sum(v, axis):
    one, two, three = (shift4(v, axis, by).astype(f32) for by in (1, 2, 3))
    return (v.astype(f32) + two) + (one + three)


def ring_rows(own):
    parts = [own] + [shift4(own, YAX, by) for by in (1, 2, 3)]
    return parts, [swap(part) for part in parts]


def line_back(sums):
    total = sums[0]
    for by in (1, 2, 3):
        total = total + shift4(sums[by].astype(bf16), YAX, -by).astype(f32)
    return total


def per_device(
    block_input,
    cotangent,
    segments,
    adapter_index,
    norm_first,
    norm_second,
    conv_taps,
    decay_rate,
    gelu_proj,
    input_proj,
    inner_gate,
    decay_gate,
    output_proj,
    widen_proj,
    narrow_proj,
    enter_square,
    leave_square,
    enter_widen,
    leave_widen,
    enter_narrow,
    leave_narrow,
):
    c = lax.axis_index("c")
    y = lax.axis_index(YAX)
    member = lax.axis_index(RING)
    plane = lax.axis_index(PLANE)
    chip = lax.axis_index(("z", "x", "v", "u"))
    place = lax.axis_index(AXES)
    toks, width = block_input.shape
    halfw = width // 2
    quarter = width // 4
    heads = HEADS // 2
    head = width // HEADS
    cols = enter_square.shape[-1]
    rank = cols // ADAPTERS
    main = 2 * toks
    per = gelu_proj.shape[0]
    per4 = 4 * per
    ff = widen_proj.shape[1] // 2
    slot = ff // 8
    slotp = slot * 16 // 15
    wide2 = 2 * slotp
    hcol = slotp // 4
    per_n = narrow_proj.shape[0]
    chunk = slotp // 16
    glane = 2 * head // 4

    grad_down_own = cotangent.astype(bf16)
    seg_lanes = jnp.broadcast_to(jnp.tile(segments, 2).astype(bf16)[:, None], (2 * toks, cols))
    payload = jnp.concatenate([block_input.astype(bf16), grad_down_own], axis=0)
    is_end = (place == 0) | (place == 127)
    piece = scatter_ends(jnp.where(is_end, payload, jnp.zeros_like(payload)), jnp.where(is_end, seg_lanes, jnp.zeros_like(seg_lanes)), c)

    gates = jnp.concatenate([inner_gate, decay_gate], axis=1)
    quads = jnp.stack(
        [
            jnp.concatenate(
                [v[:, q * (v.shape[1] // 4) : (q + 1) * (v.shape[1] // 4)] for v in (gelu_proj, input_proj, output_proj, gates)],
                axis=1,
            )
            for q in range(4)
        ]
    )
    lanes = quads.shape[2]
    quads = lax.all_to_all(quads, QUAD, 0, 0, tiled=True).reshape(per4, lanes)
    reach = piece.shape[1]
    stretches = piece.shape[0] // 8
    piece = jnp.concatenate([piece[k * 8 : (k + 1) * 8] for k in range(stretches)], axis=1)
    piece = jnp.pad(piece, ((0, 0), (0, lanes - stretches * reach)))
    quads = jnp.concatenate([quads, piece], axis=0)
    near = lax.all_gather(quads[None], AXES, axis=0, tiled=True).reshape(32, 4, per4 + 8, lanes)

    block_input, segments, widen_proj, narrow_proj = after(quads, block_input, segments, widen_proj, narrow_proj)

    block = 4 * 8 * per_n
    bcols = 4 * 8 * chunk
    at_col = jnp.arange(bcols)
    unit = at_col % (4 * chunk) % chunk
    from_row = at_col % (4 * chunk) // chunk * (8 * per_n) + at_col // (4 * chunk) * per_n + unit
    spread = ((jnp.arange(block)[:, None] == from_row[None, :]) & (unit < per_n)[None, :]).astype(bf16)
    units = 8 * per_n
    at_unit = jnp.arange(8 * chunk)
    spread_one = (jnp.arange(units)[:, None] == (at_unit // chunk * per_n + at_unit % chunk)[None, :]) & (at_unit % chunk < per_n)[None, :]
    spread_one = spread_one.astype(bf16)
    pieces = widen_proj.reshape(per, 8, block).transpose(1, 0, 2).reshape(8 * per, block)
    pieces = dot(pieces, spread).astype(bf16).reshape(8, per, 8, hcol).transpose(2, 1, 0, 3)
    pieces = lax.all_to_all(pieces.reshape(8 * per, wide2), RING, 0, 0, tiled=True)
    rows_n = jnp.pad(narrow_proj, ((0, chunk - per_n), (0, 0)))
    tail_n = rows_n[:, wide2:].reshape(4, chunk // 4, width - wide2).transpose(1, 0, 2).reshape(chunk // 4, wide2)
    shard_far = jnp.concatenate([pieces, rows_n[:, :wide2], tail_n], axis=0)
    far = lax.all_gather(shard_far[None], PLANE, axis=0, tiled=True)

    middle_owner = adapter_index[MIDDLE]
    column_owner = jnp.arange(cols) // rank
    owner_of = jnp.arange(adapter_index.shape[0])
    one_hot = (jnp.arange(cols)[None, :] == (middle_owner * rank + jnp.arange(rank))[:, None]).astype(bf16)
    core_at = c.astype(jnp.int32).reshape(1)
    middle_at = middle_owner.reshape(1)

    def select_of(segs):
        owners = jnp.sum((segs[:, None] == owner_of[None, :]).astype(jnp.int32) * adapter_index[None, :], axis=1)
        return (owners[:, None] == column_owner[None, :]).astype(f32)

    taps = half(conv_taps, c, 1)
    rate = half(decay_rate, c, 0)[None, :]
    enter_half = half(enter_square, c, 1)
    leave_half = half(leave_square, c, 2)
    enter_gates = jnp.concatenate([enter_half[2], enter_half[3]], axis=1)

    rows = 2 * main
    normed_own = norm_apply(block_input, norm_first)
    normed_main = both(normed_own, swap(normed_own), c)
    normed_halo = chip_shift(normed_main[main - HALO :], 1)
    normed_long = jnp.concatenate([normed_halo, normed_main], axis=0)
    seg_main = both(segments, swap(segments), c)
    halo_seg = jnp.broadcast_to(jnp.where(chip > 0, MIDDLE, -1), (HALO,))
    select_main = select_of(seg_main)
    select_halo = jnp.broadcast_to((column_owner == middle_owner).astype(f32)[None, :], (HALO, cols))
    ring_segs = [jnp.concatenate(v) for v in ring_rows(segments)]
    ring_selects = [select_of(v) for v in ring_segs]

    my_spread = lax.dynamic_slice_in_dim(spread, member * hcol, hcol, axis=1)
    leave_wide = leave_widen.reshape(cols, 8, block).transpose(1, 0, 2).reshape(8 * cols, block)
    leave_wide = dot(leave_wide, my_spread).astype(bf16).reshape(8, cols, hcol).transpose(1, 0, 2).reshape(cols, wide2)
    leave_a, leave_b = leave_wide[:, :slotp], leave_wide[:, slotp:]
    enter_down = lax.dot_general(
        my_spread, enter_narrow.reshape(4, block, cols), (((0,), (1,)), ((), ())), preferred_element_type=f32
    )
    enter_down = enter_down.transpose(1, 0, 2).reshape(slotp, cols).astype(bf16)

    near = after((shard_far, normed_long, select_main, ring_selects, leave_a, leave_b, enter_down, enter_gates), near)
    x_extra, normed_extra, down_extra, marks_extra = call(
        functools.partial(ends_kernel, stretches), (1,),
        [pl.BlockSpec((32, 4, 8, lanes), lambda *_: (0, 0, per4 // 8, 0), pipeline_mode=pl.Buffered(1)), fixed((1, width))],
        [(fixed((main, width)), ((main, width), f32)), (fixed((main, width)), ((main, width), bf16)),
         (fixed((main, width)), ((main, width), bf16)), (fixed((main, cols)), ((main, cols), f32))],
        [pltpu.VMEM((main, width), f32)],
        core_at, (near, norm_first[None, :]), 1,
    )
    seg_first = marks_extra[:toks, 0].astype(jnp.int32)
    seg_last = marks_extra[toks:, 0].astype(jnp.int32)
    seg_extra = jnp.concatenate([seg_first, seg_last])
    normed_long = jnp.concatenate([normed_long, normed_extra], axis=0)
    normed = normed_long[HALO:]
    marks = jnp.concatenate([halo_seg, seg_main, seg_first + 100, seg_last + 200])
    same = [(marks[HALO - k : -k] == marks[HALO:]).astype(f32)[:, None] for k in range(1, 4)]
    mask = jnp.concatenate(same + [jnp.zeros((rows, 5), f32)], axis=1)
    mask_long = jnp.concatenate([mask[:main], jnp.ones((HALO, 8), f32), mask[main:], jnp.zeros((HALO, 8), f32)], axis=0)
    select_extra = select_of(seg_extra) * (seg_extra != MIDDLE).astype(f32)[:, None]
    select = jnp.concatenate([select_main, select_extra], axis=0)
    select_long = jnp.concatenate([select_halo, select], axis=0)
    select_after = jnp.concatenate([select, select_halo], axis=0)

    col_spec = lambda i: pl.BlockSpec((8, 2, per4, quarter), lambda b, s: (b, s[0], 0, i))
    out_spec = pl.BlockSpec((8, 4, per4, quarter), lambda b, s: (2 * s[0] + b, 0, 0, 2))
    gate_spec = pl.BlockSpec((16, 4, per4, glane), lambda b, s: (s[0], 0, 0, 3 * quarter // glane), pipeline_mode=pl.Buffered(1))
    side_col_spec = lambda i: pl.BlockSpec((32, 1, per4, quarter), lambda b, s: (0, 2 * s[0] + b, 0, i))
    rows_spec = lambda n: pl.BlockSpec((n, quarter), lambda b, s: (0, b))
    head_spec = lambda n: pl.BlockSpec((n, head), lambda h, s: (0, h))
    enter_spec = pl.BlockSpec((quarter, cols), lambda b, s: (b, 0))
    hidden_spec = lambda n: pl.BlockSpec((n, hcol), lambda j, s: (0, j))
    wide_block = (rows, halfw)
    small_block = (rows, cols)
    F = lambda *shape: (fixed(shape), (shape, f32))
    B = lambda *shape: (fixed(shape), (shape, bf16))
    layer = 2 * rows * halfw * width
    mib = 2**20

    gd_rows = ring_rows(tied(cotangent, near).astype(bf16))
    long = rows + HALO
    convolved, lat_gates, pick_fill = call(
        fill_kernel, (2,),
        [fixed((long, width)), side_col_spec(1), fixed((width, cols)), fixed((long, cols)), rows_spec(cols), fixed((rows, 8)), rows_spec(4),
         pl.BlockSpec((quarter, 2 * cols), lambda b, s: (b, 0))],
        [(rows_spec(rows), (wide_block, bf16)), F(rows, 2 * cols), B(long, cols)],
        [pltpu.VMEM((long, quarter), f32)],
        core_at, (normed_long, near, enter_square[1], select_long, leave_half[1], mask, taps, enter_gates), 1, (shard_far,),
    )
    pick_fill = pick_fill[HALO:]

    sides = lambda v: [v[:toks], v[toks:]]
    feed_select = [
        jnp.concatenate([ring_selects[0][:toks], sides(select_extra)[0], ring_selects[1][:toks], sides(select_extra)[1]], axis=0),
        ring_selects[0][toks:],
        ring_selects[1][toks:],
    ]
    sig_in, sig_de, decays, state, prod, pick_in, pick_de = call(
        gates_kernel, (heads,),
        [head_spec(rows), fixed((rows, 2 * cols)), fixed((rows, 2 * cols)), fixed(small_block), gate_spec,
         head_spec(cols), head_spec(cols), fixed((rows, 8)), head_spec(1)],
        [(head_spec(rows), (wide_block, f32))] * 5 + [B(*small_block)] * 2,
        [pltpu.VMEM((rows, head), f32), pltpu.VMEM((halfw, 2 * head), bf16)],
        core_at, (convolved, lat_gates, swap(lat_gates), select, near, leave_half[2], leave_half[3], mask, rate), 4, tuple(gd_rows[0][1:]),
    )
    entering = chips_carry(jnp.stack([prod[main - 1], state[main - 1]]), False)[None, :]
    normed_half = half(normed, c, 1)
    share = -(-width // 7 // 128) * 128
    share_of = lambda v: lax.dynamic_slice_in_dim(jnp.pad(v, ((0, 0), (0, 8 * share - width))), member * share, share, axis=1)
    down_share = share_of(down_extra)
    branch, slope, pick_gelu = call(
        gelu_kernel, (2,),
        [fixed((long, width)), side_col_spec(0), fixed((width, cols)), fixed(small_block), rows_spec(cols)],
        [(rows_spec(rows), (wide_block, f32))] * 2 + [B(*small_block)],
        [],
        core_at, (normed_long, near, enter_square[0], select, leave_half[0]), 12, (normed_half, down_share),
    )
    states, mixed, lat_out, out_mine, out_send, out_extra = call(
        out_kernel, (2,),
        [rows_spec(rows), rows_spec(rows), rows_spec(1), rows_spec(rows), out_spec, enter_spec, fixed((cols, width)), fixed(small_block)],
        [(rows_spec(rows), (wide_block, f32)), (rows_spec(rows), (wide_block, bf16)), F(*small_block),
         F(toks, width), B(toks + main, width), B(main, width)],
        [pltpu.VMEM((rows, width), f32), pltpu.VMEM((rows, quarter), bf16)],
        core_at, (state, prod, entering, branch, near, enter_half[4], leave_square[4], select), 15,
    )
    pick_out = ((lat_out + swap(lat_out)) * select).astype(bf16)
    got = swap(out_send).astype(f32)
    residual = block_input + out_mine + got[:toks]
    residual_extra = x_extra + (out_extra.astype(f32) + got[toks:])
    n2_extra = norm_apply(residual_extra, norm_second)

    n2_rows = ring_rows(norm_apply(residual, norm_second))
    ring = 8 * toks
    anywhere = pl.BlockSpec(memory_space=pl.ANY)
    far_rows = far.shape[1]

    def feed(n2_pieces, gd_pieces, select, micros, waits=()):
        count = len(n2_pieces)
        n = count * toks
        return call(
            functools.partial(ffn_kernel, count), (1,),
            [anywhere] * (2 * count + 1)
            + [fixed((cols, slotp)), fixed((cols, slotp)), fixed((slotp, cols)), fixed((width, cols)), fixed((cols, width)), fixed((n, cols))],
            [B(n, width)] + [B(n, slotp)] * 3 + [B(n, cols)] * 4,
            [pltpu.VMEM((n, width), bf16), pltpu.VMEM((n, width), bf16), pltpu.VMEM(far.shape, bf16),
             pltpu.SemaphoreType.DMA((count,)), pltpu.SemaphoreType.DMA((count,)), pltpu.SemaphoreType.DMA((4, 3))],
            core_at,
            (*n2_pieces, *gd_pieces, far, leave_a, leave_b, enter_down, enter_widen, leave_narrow, select),
            micros, waits,
        )

    mix = lambda rows, extra: [rows[0][0], sides(extra)[0], rows[1][0], sides(extra)[1]]
    gn0, *parts0 = feed(mix(n2_rows, n2_extra), mix(gd_rows, down_extra), feed_select[0], 60)
    gn1, *parts1 = feed(n2_rows[0][1:], gd_rows[0][1:], feed_select[1], 40, (gn0,))
    gn2, *parts2 = feed(n2_rows[1][1:], gd_rows[1][1:], feed_select[2], 60, (gn1,))
    add = lambda a, b: a.astype(f32) + b.astype(f32)

    eighth = main // 8
    side0 = jnp.concatenate([tied(gn0, gn1).astype(bf16), parts0[3], parts0[4]], axis=1)
    extra_part = jnp.concatenate([side0[toks : 2 * toks], side0[3 * toks :]], axis=0)
    extra_total = lax.all_to_all(extra_part, RING, 0, 0, tiled=True).reshape(8, eighth, -1)
    extra_total = to_low(tied(jnp.sum(extra_total.astype(f32), axis=0), gn2))
    extra_all = lax.all_to_all(jnp.broadcast_to(extra_total[None], (8, *extra_total.shape)), RING, 0, 0, tiled=True).reshape(main, -1)
    sums0 = add(gn0[:toks], swap(gn0[2 * toks : 3 * toks]))
    sums1 = add(gn1, swap(gn2)).astype(bf16)
    sums = [sums0] + [sums1[k * toks : (k + 1) * toks] for k in range(3)]
    mid_spec = (pl.BlockSpec((rank, hcol), lambda j, s: (0, j)), ((rank, slotp), bf16))
    extra_spec = (pl.BlockSpec((cols, hcol), lambda j, s: (0, j)), ((cols, slotp), bf16))
    down_mine, down_theirs, mid_a, mid_b, mid_n, mid_l, mid_e, ex_a, ex_b, ex_n = call(
        down_kernel, (4,),
        [anywhere] * 16 + [hidden_spec(4 * toks), hidden_spec(3 * toks), hidden_spec(3 * toks)] * 3
        + [fixed((4 * toks, cols)), fixed((3 * toks, cols)), fixed((3 * toks, cols))] * 4
        + [pl.BlockSpec((4, far_rows, wide2), lambda j, s: (j, 0, 0)), fixed((cols, width))],
        [B(ring // 2, width)] * 2 + [mid_spec] * 3 + [B(rank, width)] * 2 + [extra_spec] * 3,
        [pltpu.VMEM((ring, width), f32), pltpu.VMEM((cols, hcol), f32), pltpu.VMEM((cols, width), f32),
         pltpu.VMEM((ring, width), bf16), pltpu.VMEM((ring, width), bf16), pltpu.SemaphoreType.DMA((8,)), pltpu.SemaphoreType.DMA((8,))],
        jnp.concatenate([middle_at, y.astype(jnp.int32).reshape(1)]),
        (n2_rows[0][0], n2_rows[1][0], *n2_rows[0][1:], *n2_rows[1][1:], gd_rows[0][0], gd_rows[1][0], *gd_rows[0][1:], *gd_rows[1][1:],
         *[v[i] for i in (2, 0, 1, 5, 6, 4, 3) for v in (parts0, parts1, parts2)], far, leave_narrow),
        60, (*sums[1:], extra_total),
    )
    grad_n2 = tied(line_back(sums), mid_l)
    grad_n2_extra = tied(extra_all[:, :width].astype(f32), mid_l)
    lat_extra = extra_all[:, width:]
    lgw_extra = lat_extra[:, :cols]
    pick_n_extra = lat_extra[:, cols:]
    ffn_mid = tied(jnp.concatenate([mid_a, mid_b, mid_n, mid_l, mid_e], axis=1), grad_n2).astype(bf16)
    ffn_mid = lax.all_to_all(ffn_mid.reshape(rank, 16, -1).transpose(1, 0, 2), PLANE, 0, 0, tiled=True)
    ffn_mid = to_low(jnp.sum(ffn_mid.astype(f32), axis=0))
    ffn_mid = lax.all_gather(ffn_mid[None], AXES, axis=0, tiled=True).reshape(16, 8, rank, -1)

    grad_residual = cotangent + norm_back(residual, norm_second, grad_n2)
    grad_residual_extra = down_extra.astype(f32) + norm_back(residual_extra, norm_second, grad_n2_extra)
    grad_out_own = grad_residual.astype(bf16)
    grad_out = jnp.concatenate([both(grad_out_own, swap(grad_out_own), c), grad_residual_extra.astype(bf16)], axis=0)
    grad_gelu, lg_out, back, trail = call(
        functools.partial(outback_kernel, main), (2,),
        [fixed((rows, width)), out_spec, fixed((cols, width)), enter_spec, fixed(small_block)] + [rows_spec(rows)] * 4,
        [(rows_spec(rows), (wide_block, bf16)), B(*small_block)] + [(rows_spec(rows), (wide_block, f32))] * 2,
        [pltpu.VMEM((rows, quarter), f32)],
        core_at, (grad_out, near, leave_square[4], enter_half[4], select, states, branch, slope, decays), 18,
    )
    coming = chips_carry(jnp.stack([decays[0] * trail[0], decays[0] * back[0]]), True)[None, :]
    down_total = tied(add(down_mine, swap(down_theirs)), coming).astype(bf16)
    down_total = lax.all_to_all(down_total, YAX, 0, 0, tiled=True).reshape(4, toks, width)
    block_output = residual + jnp.sum(down_total.astype(f32), axis=0)
    gelu_part, lat_gelu = call(
        geluback_kernel, (4,),
        [fixed(wide_block), col_spec(0), fixed((cols, halfw)), enter_spec, fixed(small_block)],
        [(rows_spec(main), ((main, width), f32)), F(*small_block)],
        [pltpu.VMEM(small_block, bf16)],
        core_at, (grad_gelu, near, leave_half[0], enter_square[0], select), 12,
    )

    grad_in, grad_de, base, lat_gates = call(
        gateback_kernel, (heads,),
        [head_spec(rows), head_spec(rows), head_spec(1), head_spec(rows), head_spec(1)] + [head_spec(rows)] * 4
        + [fixed((rows, 8)), head_spec(1), gate_spec, head_spec(cols), head_spec(cols)],
        [(head_spec(rows), (wide_block, bf16))] * 2 + [(head_spec(rows), (wide_block, f32)), F(rows, 2 * cols)],
        [pltpu.VMEM((rows + 8, head), f32), pltpu.VMEM((halfw, 2 * head), bf16)],
        core_at, (back, trail, coming, states, entering, convolved, sig_in, sig_de, decays, mask, rate, near, leave_half[2], leave_half[3]),
        8,
    )

    lanes_all = 3 * slotp + 2 * share
    (packed,) = call(
        pack_kernel, (1,),
        [fixed((cols, slotp))] * 3 + [fixed((main, cols))] * 2 + [fixed((main, share))] * 2,
        [B(cols, lanes_all)], [], core_at,
        (ex_a, ex_b, ex_n, pick_n_extra, lgw_extra, down_share, share_of(n2_extra)), 3, (base,),
    )
    ffn_all = lax.all_gather(packed, RING, axis=0)

    halo_both = chip_shift(jnp.concatenate([base[:HALO], lat_gates[:HALO]], axis=1), -1)
    halo_base, halo_lat = halo_both[:, :halfw], halo_both[:, halfw:]
    halo_other = chip_shift(lat_gates[:HALO], -1, cross=True)
    grad_fill, lg_in, lg_de, lat_fill, normed_mine, normed_theirs = call(
        fillback_kernel, (4,),
        [fixed(wide_block), fixed((rows, 2 * cols)), fixed((rows, 2 * cols)), fixed((HALO, halfw)), fixed((HALO, 2 * cols)), fixed((HALO, 2 * cols)),
         fixed((rows + HALO, cols)), fixed((rows + 2 * HALO, 8)), fixed((4, halfw)), fixed((halfw, cols)), fixed((halfw, cols)), fixed((cols, halfw)),
         col_spec(1), enter_spec, rows_spec(main)],
        [B(*wide_block), B(*small_block), B(*small_block), F(*small_block),
         (rows_spec(toks), ((toks, width), f32)), (rows_spec(toks), ((toks, width), bf16))],
        [pltpu.VMEM((rows + 2 * HALO, halfw), f32), pltpu.VMEM((HALO, 2 * cols), bf16), pltpu.VMEM((main, cols), bf16), pltpu.VMEM((main, quarter), f32)],
        core_at,
        (base, lat_gates, swap(lat_gates), halo_base, halo_lat, halo_other, select_after, mask_long, taps, enter_half[2], enter_half[3],
         leave_half[1], near, enter_square[1], gelu_part),
        12,
    )

    lg_gelu = ((lat_gelu + swap(lat_gelu)) * select).astype(bf16)
    lg_fill = ((lat_fill + swap(lat_fill)) * select).astype(bf16)
    pairs = [
        (lg_gelu, normed_half), (lg_fill, normed_half), (lg_in, convolved), (lg_de, convolved), (lg_out, mixed),
        (pick_gelu, grad_gelu), (pick_fill, grad_fill), (pick_in, grad_in), (pick_de, grad_de), (pick_out, half(grad_out, c, 1)),
    ]
    part_spec = lambda n, i: pl.BlockSpec((main, n), lambda *_: (i, 0), pipeline_mode=pl.Buffered(1))
    operands = [v for pair in pairs for v in pair]
    mid_rows = -(-10 * rank * halfw // cols // 64 // 16) * 16
    (mid,) = call(
        functools.partial(mids_kernel, 10, rank), (1,),
        [part_spec(cols, 0), part_spec(halfw, 0)] * 10,
        [B(64 * mid_rows, cols)],
        [pltpu.VMEM((cols, halfw), f32)],
        middle_at, operands, 6,
    )
    mid_own = mid
    mid = lax.all_to_all(mid, CHIPS, 0, 0, tiled=True).reshape(64, mid_rows, cols)
    mid = to_low(jnp.sum(mid.astype(f32), axis=0))

    operands = [*[v for pair in pairs[:5] for v in pair[::-1]], *[v for pair in pairs[5:] for v in pair]]
    enter_extra, leave_extra = call(
        functools.partial(extras_kernel, 5), (1,),
        [part_spec(halfw, 1), part_spec(cols, 1)] * 5 + [part_spec(cols, 1), part_spec(halfw, 1)] * 5,
        [B(5, halfw, cols), B(5, cols, halfw)],
        [],
        core_at, operands, 6, (mid_own,),
    )
    (grad_leave_widen,) = call(
        wide_kernel, (8,),
        [fixed((rank, cols)), fixed((units, 8 * chunk)), pl.BlockSpec((8, cols, hcol), lambda i, s: (0, 0, i)), pl.BlockSpec((1, 8, rank, hcol), lambda i, s: (i // 2, 0, 0, i % 2))],
        [(pl.BlockSpec((cols, block), lambda i, s: (0, i)), ((cols, 2 * ff), f32))],
        [], core_at, (one_hot, spread_one, ffn_all, ffn_mid), 12, (mid_own,),
    )
    mid = tied(mid, grad_leave_widen).astype(bf16)
    mid = lax.all_to_all(jnp.broadcast_to(mid[None], (64, *mid.shape)).reshape(-1, cols), CHIPS, 0, 0, tiled=True)
    (grad_enter_narrow,) = call(
        enter_kernel, (4,),
        [fixed((rank, cols)), fixed((units, 8 * chunk)), pl.BlockSpec((8, cols, hcol), lambda i, s: (0, 0, 8 + i)), pl.BlockSpec((1, 8, rank, hcol), lambda i, s: (4 + i // 2, 0, 0, i % 2))],
        [(pl.BlockSpec((block, cols), lambda i, s: (i, 0)), ((ff, cols), f32))],
        [], core_at, (one_hot, spread_one, ffn_all, ffn_mid), 7, (mid_own,),
    )
    grad_normed = normed_mine + swap(normed_theirs).astype(f32)
    input_grad = grad_residual + norm_back(block_input, norm_first, grad_normed)
    eye = jnp.eye(cols, dtype=bf16)
    share_spec = lambda i: pl.BlockSpec((8, cols, share), lambda *_: (0, 0, 3 * slotp // share + i))
    grad_leave_narrow, grad_enter_widen = call(
        shares_kernel, (1,),
        [fixed((rank, cols)), fixed((cols, cols)), share_spec(0), share_spec(1), fixed(ffn_mid.shape)],
        [F(cols, width), F(width, cols)],
        [], core_at, (one_hot, eye, ffn_all, ffn_all, ffn_mid), 4, (mid_own,),
    )
    per_k = lambda *shape: pl.BlockSpec((1,) + shape, lambda k, s: (k,) + (0,) * len(shape))
    mid_e_spec = pl.BlockSpec((rank * halfw // cols, cols), lambda k, s: (k, 0))
    mid_l_spec = pl.BlockSpec((rank * halfw // cols, cols), lambda k, s: (5 + k, 0))
    mid = tied(tied(mid, grad_enter_narrow), grad_leave_narrow).astype(bf16)
    mid_other = swap(mid)
    grad_enter_square, grad_leave_square = call(
        square_kernel, (5,),
        [fixed((rank, cols)), per_k(halfw, cols), per_k(halfw, cols), per_k(cols, halfw), per_k(cols, halfw),
         mid_e_spec, mid_e_spec, mid_l_spec, mid_l_spec],
        [(per_k(width, cols), ((5, width, cols), f32)), (per_k(cols, width), ((5, cols, width), f32))],
        [], core_at, (one_hot, enter_extra, swap(enter_extra), leave_extra, swap(leave_extra), mid, mid_other, mid, mid_other), 9,
    )
    return (
        block_output,
        input_grad,
        grad_enter_square,
        grad_leave_square,
        grad_enter_widen,
        grad_leave_widen,
        grad_enter_narrow,
        grad_leave_narrow,
    )


def solution(mesh):
    split = Mesh(mesh.devices.reshape(SIZES), AXES)
    by_row = P(AXES, None)
    return jax.shard_map(
        per_device,
        mesh=split,
        in_specs=(by_row, by_row, P(AXES), P(), P(), P(), P(), P()) + (by_row,) * 7 + (P(),) * 6,
        out_specs=(by_row, by_row, P(), P(), P(), P(), P(), P()),
        check_vma=False,
    )
```

```python
import functools
import jax
import jax.numpy as jnp
from jax import lax
from jax.experimental import pallas as pl
from jax.experimental.pallas import tpu as pltpu
from jax.sharding import Mesh, PartitionSpec as P

HEADS = 10
ADAPTERS = 8
HALO = 16
MIDDLE = 3
AXES = ("z", "x", "v", "u", "c")
SIZES = (4, 4, 2, 2, 2)
YAX = ("v", "u")
RING = ("v", "u", "c")
PLANE = ("z", "x")
QUAD = ("u", "c")
CHIPS = ("z", "x", "v", "u")
VMEM = 56 * 2**20

eps_norm = 1e-06
floor_scale = 0.001
bf16 = jnp.bfloat16
f32 = jnp.float32


def dot(a, b):
    return jnp.dot(a, b, preferred_element_type=f32)


def dot_nt(a, b):
    return lax.dot_general(a, b, (((1,), (1,)), ((), ())), preferred_element_type=f32)


def dot_tn(a, b):
    return lax.dot_general(a, b, (((0,), (0,)), ((), ())), preferred_element_type=f32)


def low(v):
    return lax.reduce_precision(v, 8, 7)


def to_low(v):
    return low(v).astype(bf16)


def norm_scale(values):
    return lax.rsqrt(jnp.mean(values * values, axis=-1, keepdims=True) + eps_norm)


def norm_apply(values, gain):
    return (values * norm_scale(values) * gain).astype(bf16)


def norm_back(values, gain, grad):
    s = norm_scale(values)
    gq = gain * grad
    return s * gq - values * (s * s * s) * jnp.mean(values * gq, axis=-1, keepdims=True)


def sigmoid(v):
    return 1.0 / (1.0 + jnp.exp(-v))


def gelu_parts(a):
    k = 0.7978845608028654
    a2 = a * a
    th = jnp.tanh(k * (a + 0.044715 * a2 * a))
    value = 0.5 * a * (1.0 + th)
    slope = 0.5 * (1.0 + th) + 0.5 * a * (1.0 - th * th) * (k * (1.0 + 3.0 * 0.044715 * a2))
    return value, slope


def swap(v):
    return lax.ppermute(v, "c", [(0, 1), (1, 0)])


def shift4(v, axis, by):
    return lax.ppermute(v, axis, [(i, (i + by) % 4) for i in range(4)])


def chip_shift(v, by, cross=False):
    chips = 64
    pairs = [
        (2 * p + c, 2 * (p + by) + (1 - c if cross else c))
        for p in range(chips)
        for c in range(2)
        if 0 <= p + by < chips
    ]
    return lax.ppermute(v, AXES, pairs)


def both(own, other, c):
    rows = own.shape[0]
    three = jnp.concatenate([own, other, own], axis=0)
    return lax.dynamic_slice_in_dim(three, c * rows, 2 * rows, axis=0)


def half(v, c, axis):
    size = v.shape[axis] // 2
    return lax.dynamic_slice_in_dim(v, c * size, size, axis=axis)


def after(first, *values):
    held = lax.optimization_barrier((first, *values))[1:]
    return held[0] if len(held) == 1 else held


def tied(value, other):
    return value + other[(0,) * other.ndim].astype(f32) * 0.0


def line_order(parts, y):
    back = parts[::-1]
    twice = jnp.stack(back + back)
    return lax.dynamic_slice_in_dim(twice, 3 - y, 4, axis=0)


def call(kernel, grid, ins, outs, scratch, scalars, args, micros, waits=()):
    count = len(args)

    def body(s_ref, *refs):
        kernel(s_ref, *refs[:count], *refs[count + len(waits) :])

    ins = list(ins) + [pl.BlockSpec(memory_space=pl.ANY)] * len(waits)
    args = (*args, *waits)
    return pl.pallas_call(
        body,
        grid_spec=pltpu.PrefetchScalarGridSpec(
            num_scalar_prefetch=1,
            grid=grid,
            in_specs=ins,
            out_specs=[spec for spec, _ in outs],
            scratch_shapes=scratch,
        ),
        out_shape=[jax.ShapeDtypeStruct(*shape) for _, shape in outs],
        compiler_params=pltpu.CompilerParams(vmem_limit_bytes=VMEM),
        cost_estimate=pl.CostEstimate(flops=int(micros * 1e9), bytes_accessed=int(micros * 2e6), transcendentals=0),
    )(scalars, *args)


def fixed(shape):
    return pl.BlockSpec(shape, lambda *_: (0,) * len(shape), pipeline_mode=pl.Buffered(1))


def scan_rows(d_ref, p_ref, s_ref, q_ref):
    rows, width = d_ref.shape
    row = lax.broadcasted_iota(jnp.int32, (8, width), 0)

    def tile(i, carry):
        state, product = carry
        at = pl.ds(pl.multiple_of(i * 8, 8), 8)
        a = d_ref[at, :]
        b = p_ref[at, :]
        for s in (1, 2, 4):
            b = a * jnp.where(row >= s, pltpu.roll(b, s, 0), 0.0) + b
            a = a * jnp.where(row >= s, pltpu.roll(a, s, 0), 1.0)
        value = b + a * state
        through = a * product
        s_ref[at, :] = value
        q_ref[at, :] = through
        return value[7:8, :], through[7:8, :]

    lax.fori_loop(
        0, rows // 8, tile, (jnp.zeros((1, width), f32), jnp.ones((1, width), f32)), unroll=8
    )


def scan_rows_back(d_ref, g_ref, s_ref, q_ref, main):
    rows, width = d_ref.shape
    row = lax.broadcasted_iota(jnp.int32, (8, width), 0)

    def tile(i, carry):
        state, product, after_row = carry
        at = pl.ds(pl.multiple_of(i * 8, 8), 8)
        d = d_ref[at, :]
        b = g_ref[at, :]
        a = jnp.where(row < 7, pltpu.roll(d, 7, 0), after_row)
        for s in (1, 2, 4):
            b = a * jnp.where(row < 8 - s, pltpu.roll(b, 8 - s, 0), 0.0) + b
            a = a * jnp.where(row < 8 - s, pltpu.roll(a, 8 - s, 0), 1.0)
        value = b + a * state
        through = a * product
        s_ref[at, :] = value
        q_ref[at, :] = through
        return value[0:1, :], through[0:1, :], d[0:1, :]

    zero = jnp.zeros((1, width), f32)
    one = jnp.ones((1, width), f32)
    last, cut = rows // 8 - 1, main // 8
    lax.fori_loop(0, last + 1 - cut, lambda k, t: tile(last - k, t), (zero, zero, one), unroll=8)
    lax.fori_loop(0, cut, lambda k, t: tile(cut - 1 - k, t), (zero, one, one), unroll=8)


def tile_of(w, i):
    block = w[:, i]
    return block.reshape(block.shape[0] * block.shape[1], block.shape[2])


def ends_kernel(stretches, s_ref, near_ref, gain_ref, x_ref, normed_ref, down_ref, marks_ref, hold_ref):
    toks = x_ref.shape[0] // 2
    quarter = x_ref.shape[1] // 4
    reach = quarter + marks_ref.shape[1]
    size = 8 * stretches
    for core in range(2):
        for p in range(16):
            for h in range(stretches):
                row = p * size + h * 8
                for y in range(4):
                    block = near_ref[2 * p + y // 2, 2 * (y % 2) + core, :, h * reach : (h + 1) * reach].astype(f32)
                    cols = slice(y * quarter, (y + 1) * quarter)
                    if row < toks:
                        x_ref[core * toks + row : core * toks + row + 8, cols] = block[:, :quarter]
                        if y == 0:
                            marks_ref[core * toks + row : core * toks + row + 8, :] = block[:, quarter:]
                    else:
                        to = core * toks + row - toks
                        hold_ref[to : to + 8, cols] = block[:, :quarter]
    down_ref[...] = hold_ref[...].astype(bf16)
    x = x_ref[...]
    normed_ref[...] = norm_apply(x, gain_ref[...])


def pack_kernel(s_ref, exa_ref, exb_ref, exn_ref, pick_ref, lg_ref, down_ref, n2_ref, out_ref):
    wide = exa_ref.shape[1]
    share = down_ref.shape[1]
    for i, ref in enumerate((exa_ref, exb_ref, exn_ref)):
        out_ref[:, i * wide : (i + 1) * wide] = ref[...]
    at = 3 * wide
    out_ref[:, at : at + share] = dot_tn(pick_ref[...], down_ref[...]).astype(bf16)
    out_ref[:, at + share :] = dot_tn(lg_ref[...], n2_ref[...]).astype(bf16)


def fill_kernel(c_ref, x_ref, w_ref, first_ref, select_ref, leave_ref, mask_ref, taps_ref, enter_ref, conv_ref, lat_ref, pick_ref, acc_ref):
    rows, width = conv_ref.shape

    @pl.when(pl.program_id(0) == 0)
    def _():
        pick_ref[...] = (dot(x_ref[...], first_ref[...]) * select_ref[...]).astype(bf16)

    acc_ref[...] = dot(x_ref[...], tile_of(w_ref, 0)) + dot(pick_ref[...], leave_ref[...])
    step = width // 5
    for j in range(5):
        at = slice(j * step, (j + 1) * step)
        total = taps_ref[0:1, at] * acc_ref[HALO : HALO + rows, at]
        for k in range(1, taps_ref.shape[0]):
            total = total + taps_ref[k : k + 1, at] * acc_ref[HALO - k : HALO - k + rows, at] * mask_ref[:, k - 1 : k]
        conv_ref[:, at] = total.astype(bf16)

    @pl.when(pl.program_id(0) == 0)
    def _():
        lat_ref[...] = jnp.zeros_like(lat_ref)

    lat_ref[...] += dot(conv_ref[...], enter_ref[...])


def gate_weights(w_ref, hold_ref):
    @pl.when(pl.program_id(0) == 0)
    def _():
        wide = w_ref.shape[3]
        for i in range(4):
            hold_ref[:, i * wide : (i + 1) * wide] = tile_of(w_ref, i)

    head = 2 * w_ref.shape[3]
    at = pl.ds(pl.multiple_of(pl.program_id(0) * head, head), head)
    return hold_ref[at, :head], hold_ref[at, head:]


def gates_kernel(
    c_ref, conv_ref, own_ref, other_ref, select_ref, w_ref, leave_in_ref, leave_de_ref, mask_ref, rate_ref,
    sin_ref, sde_ref, dec_ref, state_ref, prod_ref, pick_in_ref, pick_de_ref, push_ref, hold_ref,
):
    cols = select_ref.shape[1]
    inner, decay = gate_weights(w_ref, hold_ref)

    @pl.when(pl.program_id(0) == 0)
    def _():
        lat = own_ref[...] + other_ref[...]
        select = select_ref[...]
        pick_in_ref[...] = (lat[:, :cols] * select).astype(bf16)
        pick_de_ref[...] = (lat[:, cols:] * select).astype(bf16)

    retain = mask_ref[:, 0:1]
    conv = conv_ref[...]
    sig_in = sigmoid(dot(conv, inner) + dot(pick_in_ref[...], leave_in_ref[...]))
    sig_de = sigmoid(dot(conv, decay) + dot(pick_de_ref[...], leave_de_ref[...]))
    raw = jnp.exp(-8.0 * rate_ref[...] * sig_de)
    scale = jnp.where(retain > 0.5, jnp.sqrt(jnp.maximum(1.0 - raw * raw, floor_scale)), 1.0)
    sin_ref[...] = sig_in
    sde_ref[...] = sig_de
    dec_ref[...] = raw * retain
    push_ref[...] = conv.astype(f32) * sig_in * scale
    scan_rows(dec_ref, push_ref, state_ref, prod_ref)


def gelu_kernel(c_ref, x_ref, w_ref, first_ref, select_ref, leave_ref, value_ref, slope_ref, pick_ref):
    @pl.when(pl.program_id(0) == 0)
    def _():
        pick_ref[...] = (dot(x_ref[HALO:, :], first_ref[...]) * select_ref[...]).astype(bf16)

    pre = dot(x_ref[HALO:, :], tile_of(w_ref, 0)) + dot(pick_ref[...], leave_ref[...])
    value, slope = gelu_parts(pre)
    value_ref[...] = value
    slope_ref[...] = slope


def out_kernel(
    c_ref, state_ref, prod_ref, entering_ref, branch_ref, w_ref, enter_ref, leave_ref, select_ref,
    states_ref, mixed_ref, lat_ref, mine_ref, send_ref, extra_ref, acc_ref, hold_ref,
):
    b = pl.program_id(0)
    q = w_ref.shape[3]
    states = state_ref[...] + prod_ref[...] * entering_ref[...]
    states_ref[...] = states
    hold_ref[...] = (branch_ref[...] * states).astype(bf16)
    mixed_ref[...] = hold_ref[...]

    @pl.when(b == 0)
    def _():
        lat_ref[...] = jnp.zeros_like(lat_ref)
        acc_ref[...] = jnp.zeros_like(acc_ref)

    lat_ref[...] += dot(hold_ref[...], enter_ref[...])
    for i in range(4):
        acc_ref[:, i * q : (i + 1) * q] += dot(hold_ref[...], tile_of(w_ref, i))

    @pl.when(b == pl.num_programs(0) - 1)
    def _():
        acc_ref[...] += dot((lat_ref[...] * select_ref[...]).astype(bf16), leave_ref[...])
        rows = mine_ref.shape[0]
        at = pl.multiple_of(c_ref[0] * rows, rows)
        mine_ref[...] = acc_ref[pl.ds(at, rows), :]
        send_ref[:rows, :] = acc_ref[pl.ds(pl.multiple_of(rows - at, rows), rows), :].astype(bf16)
        extra = acc_ref[2 * rows :, :].astype(bf16)
        send_ref[rows:, :] = extra
        extra_ref[...] = extra


def narrow_block(far_ref, j, top):
    wide = far_ref.shape[2]
    tail = wide // 4
    low_rows = (far_ref.shape[1] - top) // 5
    planes = pl.ds(4 * j, 4)
    main = far_ref[planes, top : top + 4 * low_rows, :].reshape(16 * low_rows, wide)
    pieces = []
    for p in range(4):
        rows = far_ref[4 * j + p, top + 4 * low_rows :, :]
        pieces += [rows[:, k * tail : (k + 1) * tail] for k in range(4)]
    return main, jnp.concatenate(pieces, axis=0)


def fetch(refs, hold_ref, sems):
    size = refs[0].shape[0]
    return [pltpu.make_async_copy(r, hold_ref.at[pl.ds(i * size, size), :], sems.at[i]) for i, r in enumerate(refs)]


def ffn_kernel(count, s_ref, *refs):
    n2_refs, gd_refs = refs[:count], refs[count : 2 * count]
    far_hbm, la_ref, lb_ref, en_ref, ew_ref, ln_ref, select_ref = refs[2 * count : 2 * count + 7]
    gn_ref, ga_ref, gb_ref, hid_ref, lgw_ref, pickn_ref, pickw_ref, lgn_ref = refs[2 * count + 7 : 2 * count + 15]
    n2_hold, gd_hold, far_ref, n2_sems, gd_sems, far_sems = refs[2 * count + 15 :]
    width = gn_ref.shape[1]
    slotp = hid_ref.shape[1]
    step = slotp // 4
    wide = far_ref.shape[2]
    top = width // 16

    def far_copies(j):
        at = pl.ds(pl.multiple_of(j * step, step), step)
        at_b = pl.ds(pl.multiple_of(slotp + j * step, step), step)
        planes = pl.ds(4 * j, 4)
        places = [(slice(None), pl.ds(0, top), at), (slice(None), pl.ds(0, top), at_b), (planes, pl.ds(top, far_ref.shape[1] - top), slice(None))]
        return [pltpu.make_async_copy(far_hbm.at[p], far_ref.at[p], far_sems.at[j, i]) for i, p in enumerate(places)]

    n2_copies = fetch(n2_refs, n2_hold, n2_sems)
    gd_copies = fetch(gd_refs, gd_hold, gd_sems)
    for copy in n2_copies + gd_copies:
        copy.start()
    for j in range(4):
        for copy in far_copies(j):
            copy.start()
    for copy in n2_copies + gd_copies:
        copy.wait()
    select = select_ref[...]
    pickw_ref[...] = (dot(n2_hold[...], ew_ref[...]) * select).astype(bf16)
    lgn_ref[...] = (dot_nt(gd_hold[...], ln_ref[...]) * select).astype(bf16)

    def hidden(j, _):
        for copy in far_copies(j):
            copy.wait()
        at = pl.ds(pl.multiple_of(j * step, step), step)
        at_b = pl.ds(pl.multiple_of(slotp + j * step, step), step)
        a = dot(n2_hold[...], far_ref[:, :top, at].reshape(width, step)) + dot(pickw_ref[...], la_ref[:, at])
        up = dot(n2_hold[...], far_ref[:, :top, at_b].reshape(width, step)) + dot(pickw_ref[...], lb_ref[:, at])
        main, last = narrow_block(far_ref, j, top)
        grad = dot_nt(gd_hold[:, :wide], main) + dot_nt(gd_hold[:, wide:], last) + dot_nt(lgn_ref[...], en_ref[at, :])
        act, slope = gelu_parts(a)
        hid_ref[:, at] = (act * up).astype(bf16)
        ga_ref[:, at] = (slope * up * grad).astype(bf16)
        gb_ref[:, at] = (act * grad).astype(bf16)
        return 0

    lax.fori_loop(0, 4, hidden, 0)
    lgw_ref[...] = ((dot_nt(ga_ref[...], la_ref[...]) + dot_nt(gb_ref[...], lb_ref[...])) * select).astype(bf16)
    pickn_ref[...] = (dot(hid_ref[...], en_ref[...]) * select).astype(bf16)
    part = width // 4

    def back(q, _):
        at = pl.ds(pl.multiple_of(q * part, part), part)
        planes = pl.ds(4 * q, 4)
        total = dot_nt(ga_ref[...], far_ref[planes, :top, :slotp].reshape(part, slotp))
        total += dot_nt(gb_ref[...], far_ref[planes, :top, slotp:].reshape(part, slotp))
        gn_ref[:, at] = (total + dot_nt(lgw_ref[...], ew_ref[at, :])).astype(bf16)
        return 0

    lax.fori_loop(0, 4, back, 0)


def down_kernel(s_ref, *refs):
    n2_refs, gd_refs = refs[:8], refs[8:16]
    hid, ga, gb, pick, lgn, pickn, lgw = [refs[16 + 3 * i : 19 + 3 * i] for i in range(7)]
    far_ref, ln_ref = refs[37:39]
    mine_ref, theirs_ref, mida_ref, midb_ref, midn_ref, midl_ref, mide_ref, exa_ref, exb_ref, exn_ref = refs[39:49]
    acc_ref, hold_ref, wide_ref, n2_hold, gd_hold, n2_sems, gd_sems = refs[49:]
    j = pl.program_id(0)
    rank = mida_ref.shape[0]
    piece = n2_refs[0].shape[0]
    here = pl.ds(pl.multiple_of(s_ref[0] * rank, rank), rank)
    main, last = narrow_block(far_ref, 0, far_ref.shape[1] * 2 // 3)
    cut = main.shape[1]
    ring_of = lambda v: jnp.concatenate([v[0][:piece, :], v[0][2 * piece : 3 * piece, :], v[1][...], v[2][...]], axis=0)
    rest_of = lambda v: jnp.concatenate([v[0][piece : 2 * piece, :], v[0][3 * piece :, :]], axis=0)
    n2_copies = fetch(n2_refs, n2_hold, n2_sems)
    gd_copies = fetch(gd_refs, gd_hold, gd_sems)

    @pl.when(j == 0)
    def _():
        for copy in n2_copies + gd_copies:
            copy.start()
        acc_ref[...] = dot(ring_of(pickn), ln_ref[...])

    hidden = ring_of(hid)
    acc_ref[:, :cut] += dot(hidden, main)
    acc_ref[:, cut:] += dot(hidden, last)
    for left, right, out_ref, extra_ref in ((pick, ga, mida_ref, exa_ref), (pick, gb, midb_ref, exb_ref), (lgn, hid, midn_ref, exn_ref)):
        hold_ref[...] = dot_tn(ring_of(left), ring_of(right))
        out_ref[...] = hold_ref[here, :].astype(bf16)
        extra_ref[...] = dot_tn(rest_of(left), rest_of(right)).astype(bf16)

    @pl.when(j == pl.num_programs(0) - 1)
    def _():
        for k in range(4):
            to = pl.ds(pl.multiple_of(lax.rem(s_ref[1] - k + 4, 4) * piece, piece), piece)
            own, other = (0, 1) if k == 0 else (k + 1, k + 4)
            mine_ref[to, :] = acc_ref[own * piece : (own + 1) * piece, :].astype(bf16)
            theirs_ref[to, :] = acc_ref[other * piece : (other + 1) * piece, :].astype(bf16)
        for copy in n2_copies + gd_copies:
            copy.wait()
        wide_ref[...] = dot_tn(ring_of(pickn), gd_hold[...])
        midl_ref[...] = wide_ref[here, :].astype(bf16)
        wide_ref[...] = dot_tn(ring_of(lgw), n2_hold[...])
        mide_ref[...] = wide_ref[here, :].astype(bf16)


def outback_kernel(
    main, c_ref, go_ref, w_ref, leave_ref, enter_ref, select_ref, states_ref, branch_ref, slope_ref, dec_ref,
    gg_ref, lg_ref, state_ref, prod_ref, gs_ref,
):
    b = pl.program_id(0)
    q = w_ref.shape[3]

    @pl.when(b == 0)
    def _():
        lg_ref[...] = (dot_nt(go_ref[...], leave_ref[...]) * select_ref[...]).astype(bf16)

    gm = dot_nt(lg_ref[...], enter_ref[...])
    for i in range(4):
        gm += dot_nt(go_ref[:, i * q : (i + 1) * q], tile_of(w_ref, i))
    gg_ref[...] = (slope_ref[...] * (gm * states_ref[...])).astype(bf16)
    gs_ref[...] = gm * branch_ref[...]
    scan_rows_back(dec_ref, gs_ref, state_ref, prod_ref, main)


def geluback_kernel(c_ref, g_ref, w_ref, leave_ref, enter_ref, select_ref, part_ref, lat_ref, lg_ref):
    b = pl.program_id(0)
    q = w_ref.shape[3]

    @pl.when(b == 0)
    def _():
        lat = dot_nt(g_ref[...], leave_ref[...])
        lat_ref[...] = lat
        lg_ref[...] = (lat * select_ref[...]).astype(bf16)

    rows = part_ref.shape[0]
    part = dot_nt(g_ref[:rows, :q], tile_of(w_ref, 0)) + dot_nt(g_ref[:rows, q : 2 * q], tile_of(w_ref, 1))
    part_ref[...] = part + dot_nt(lg_ref[:rows, :], enter_ref[...])


def gateback_kernel(
    c_ref, back_ref, trail_ref, coming_ref, states_ref, entering_ref, conv_ref, sin_ref, sde_ref, dec_ref, mask_ref, rate_ref,
    w_ref, leave_in_ref, leave_de_ref,
    gi_ref, gd_ref, base_ref, lat_ref, hold_ref, gate_ref,
):
    rows = conv_ref.shape[0]
    cols = leave_in_ref.shape[0]
    inner, decay = gate_weights(w_ref, gate_ref)
    retain = mask_ref[:, 0:1]
    hold_ref[7:8, :] = entering_ref[...]
    hold_ref[8:, :] = states_ref[...]
    rate = rate_ref[...]
    sig_in = sin_ref[...]
    sig_de = sde_ref[...]
    conv = conv_ref[...].astype(f32)
    carried = back_ref[...] + trail_ref[...] * coming_ref[...]
    raw = jnp.exp(-8.0 * rate * sig_de)
    grown = 1.0 - raw * raw
    scale = jnp.where(retain > 0.5, jnp.sqrt(jnp.maximum(grown, floor_scale)), 1.0)
    through = carried * conv
    gi = (through * scale * sig_in * (1.0 - sig_in)).astype(bf16)
    grad_grown = jnp.where((grown > floor_scale) & (retain > 0.5), through * sig_in * 0.5 / scale, 0.0)
    grad_log = carried * hold_ref[7 : 7 + rows, :] * dec_ref[...] - 2.0 * raw * raw * grad_grown
    gd = (grad_log * (-8.0 * rate) * sig_de * (1.0 - sig_de)).astype(bf16)
    gi_ref[...] = gi
    gd_ref[...] = gd
    base_ref[...] = carried * sig_in * scale + dot_nt(gi, inner) + dot_nt(gd, decay)

    @pl.when(pl.program_id(0) == 0)
    def _():
        lat_ref[...] = jnp.zeros_like(lat_ref)

    lat_ref[:, :cols] += dot_nt(gi, leave_in_ref[...])
    lat_ref[:, cols:] += dot_nt(gd, leave_de_ref[...])


def fillback_kernel(
    c_ref, base_ref, own_ref, other_ref, hbase_ref, hown_ref, hother_ref, select_ref, mask_ref, taps_ref, enter_in_ref, enter_de_ref, leave_ref,
    w_ref, enter_ref, before_ref,
    gf_ref, lgi_ref, lgd_ref, lat_ref, mine_ref, theirs_ref, gc_ref, hlg_ref, lg_ref, part_ref,
):
    b = pl.program_id(0)
    q = w_ref.shape[3]
    rows, width = base_ref.shape
    main = part_ref.shape[0]
    cols = lgi_ref.shape[1]

    @pl.when(b == 0)
    def _():
        lat = own_ref[...] + other_ref[...]
        hlat = hown_ref[...] + hother_ref[...]
        select = select_ref[:rows, :]
        hselect = select_ref[rows:, :]
        lgi_ref[...] = (lat[:, :cols] * select).astype(bf16)
        lgd_ref[...] = (lat[:, cols:] * select).astype(bf16)
        hlg_ref[:, :cols] = (hlat[:, :cols] * hselect).astype(bf16)
        hlg_ref[:, cols:] = (hlat[:, cols:] * hselect).astype(bf16)
        step = width // 5
        for j in range(5):
            at = slice(j * step, (j + 1) * step)
            ei = enter_in_ref[at, :]
            ed = enter_de_ref[at, :]
            here = base_ref[:, at] + dot_nt(lgi_ref[...], ei) + dot_nt(lgd_ref[...], ed)
            gc_ref[:main, at] = here[:main]
            gc_ref[main : main + HALO, at] = (
                hbase_ref[:, at] + dot_nt(hlg_ref[:, :cols], ei) + dot_nt(hlg_ref[:, cols:], ed)
            )
            gc_ref[main + HALO : rows + HALO, at] = here[main:]
            gc_ref[rows + HALO :, at] = jnp.zeros((HALO, step), f32)
            for lo, hi, to in ((0, main, 0), (main + HALO, rows + HALO, main)):
                total = taps_ref[0:1, at] * gc_ref[lo:hi, at]
                for k in range(1, taps_ref.shape[0]):
                    total = total + taps_ref[k : k + 1, at] * gc_ref[lo + k : hi + k, at] * mask_ref[lo + k : hi + k, k - 1 : k]
                gf_ref[to : to + hi - lo, at] = total.astype(bf16)
        lat = dot_nt(gf_ref[...], leave_ref[...])
        lat_ref[...] = lat
        lg_ref[...] = (lat[:main] * select_ref[:main, :]).astype(bf16)

    part = dot_nt(gf_ref[:main, :q], tile_of(w_ref, 0)) + dot_nt(gf_ref[:main, q : 2 * q], tile_of(w_ref, 1))
    part_ref[...] = before_ref[...] + part + dot_nt(lg_ref[...], enter_ref[...])
    own = mine_ref.shape[0]
    at = pl.multiple_of(c_ref[0] * own, own)
    mine_ref[...] = part_ref[pl.ds(at, own), :]
    theirs_ref[...] = part_ref[pl.ds(pl.multiple_of(own - at, own), own), :].astype(bf16)


def mids_kernel(count, rank, s_ref, *refs):
    out_ref, hold_ref = refs[2 * count :]
    here = pl.ds(pl.multiple_of(s_ref[0] * rank, rank), rank)
    lanes = out_ref.shape[1]
    parts = hold_ref.shape[1] // lanes
    for i in range(count):
        hold_ref[...] = dot_tn(refs[2 * i][...], refs[2 * i + 1][...])
        for j in range(parts):
            at = (i * parts + j) * rank
            out_ref[at : at + rank, :] = hold_ref[here, j * lanes : (j + 1) * lanes].astype(bf16)
    filled = count * parts * rank
    out_ref[filled:, :] = jnp.zeros((out_ref.shape[0] - filled, lanes), bf16)


def extras_kernel(count, s_ref, *refs):
    enter_ref, leave_ref = refs[4 * count :]
    for i in range(count):
        enter_ref[i] = dot_tn(refs[2 * i][...], refs[2 * i + 1][...]).astype(bf16)
    for i in range(count):
        k = 2 * count + 2 * i
        leave_ref[i] = dot_tn(refs[k][...], refs[k + 1][...]).astype(bf16)


def square_kernel(s_ref, one_ref, own_e_ref, other_e_ref, own_l_ref, other_l_ref, own_me_ref, other_me_ref, own_ml_ref, other_ml_ref, enter_ref, leave_ref):
    size = own_e_ref.shape[1]
    one = one_ref[...]
    rank = one.shape[0]
    whole = lambda ref: jnp.concatenate([ref[j * rank : (j + 1) * rank, :] for j in range(ref.shape[0] // rank)], axis=1)
    for core, e_ref, l_ref, me_ref, ml_ref in (
        (s_ref[0], own_e_ref, own_l_ref, own_me_ref, own_ml_ref),
        (1 - s_ref[0], other_e_ref, other_l_ref, other_me_ref, other_ml_ref),
    ):
        at = pl.ds(pl.multiple_of(core * size, size), size)
        enter_ref[0, at, :] = e_ref[0].astype(f32) + dot_tn(whole(me_ref), one)
        leave_ref[0, :, at] = l_ref[0].astype(f32) + dot_tn(one, whole(ml_ref))


def unit_parts(one_ref, extra_ref, mid_ref, size):
    count = extra_ref.shape[0]
    cut = lambda ref, p: jnp.concatenate([ref[m, :, p * size : (p + 1) * size] for m in range(count)], axis=1)
    mid = jnp.concatenate([mid_ref[0, m, :, p * size : (p + 1) * size] for p in range(4) for m in range(count)], axis=1)
    placed = dot_tn(one_ref[...], mid).astype(bf16)
    wide = count * size
    return jnp.concatenate([cut(extra_ref, p) + placed[:, p * wide : (p + 1) * wide] for p in range(4)], axis=0)


def wide_kernel(s_ref, one_ref, spread_ref, extra_ref, mid_ref, out_ref):
    cols = out_ref.shape[0]
    done = dot_nt(unit_parts(one_ref, extra_ref, mid_ref, spread_ref.shape[1] // 8), spread_ref[...])
    out_ref[...] = jnp.concatenate([done[p * cols : (p + 1) * cols] for p in range(4)], axis=1)


def enter_kernel(s_ref, one_ref, spread_ref, extra_ref, mid_ref, out_ref):
    units, size = spread_ref.shape
    cols = out_ref.shape[1]
    done = dot_nt(spread_ref[...], unit_parts(one_ref, extra_ref, mid_ref, size // 8))
    for p in range(4):
        out_ref[p * units : (p + 1) * units, :] = done[:, p * cols : (p + 1) * cols]


def shares_kernel(s_ref, one_ref, eye_ref, extra_l_ref, extra_e_ref, mid_ref, leave_ref, enter_ref):
    one = one_ref[...]
    width = leave_ref.shape[1]
    share = extra_l_ref.shape[2]
    per = mid_ref.shape[3]
    sums = []
    for p in range(16 - 2 * width // per, 16):
        total = mid_ref[p, 0].astype(f32)
        for m in range(1, 8):
            total = total + mid_ref[p, m].astype(f32)
        sums.append(total.astype(bf16))
    mid = jnp.concatenate(sums, axis=1)
    leave_ref[...] = dot_tn(one, mid[:, :width])
    enter_ref[...] = dot_tn(mid[:, width : 2 * width], one)
    for m in range(8):
        lo, hi = m * share, min((m + 1) * share, width)
        if lo < hi:
            leave_ref[:, lo:hi] += extra_l_ref[m, :, : hi - lo].astype(f32)
            enter_ref[lo:hi, :] += dot_tn(extra_e_ref[m], eye_ref[...])[: hi - lo]


def linked(former, latter):
    return (former[0] * latter[0], latter[0] * former[1] + latter[1])


def line_carry(value, axis, reverse):
    sign = -1 if reverse else 1
    here = lax.axis_index(axis)
    here = 3 - here if reverse else here
    came = {by: shift4(value, axis, sign * by) for by in (1, 2, 3)}
    unit = (jnp.ones_like(value[0]), jnp.zeros_like(value[0]))

    def take(so_far, by, valid):
        new = linked(so_far, (came[by][0], came[by][1]))
        return tuple(jnp.where(valid, a, b) for a, b in zip(new, so_far))

    enter = unit
    for by in (3, 2, 1):
        enter = take(enter, by, here >= by)
    total = linked(enter, (value[0], value[1]))
    for by in (3, 2, 1):
        total = take(total, by, here < by)
    return enter, jnp.stack(total)


def chips_carry(value, reverse):
    by_y, line = line_carry(value, YAX, reverse)
    by_x, plane = line_carry(line, "x", reverse)
    by_z, _ = line_carry(plane, "z", reverse)
    return linked(linked(by_z, by_x), by_y)[1]


def index_of(place):
    at = 0
    for i, n in zip(place, (4, 4, 4, 2)):
        at = at * n + i
    return at


def scatter_ends(payload, seg_lanes, c):
    reached = {0: [(0, 0, 0)], 1: [(3, 3, 3)]}
    width = payload.shape[1]
    payload = jnp.concatenate([payload, seg_lanes], axis=1)
    for axis in range(3):
        if axis < 2:
            size = payload.shape[0] // 4
            pieces = [payload[k * size : (k + 1) * size] for k in range(4)]
        else:
            size = width // 4
            pieces = [jnp.concatenate([payload[:, k * size : (k + 1) * size], payload[:, width:]], axis=1) for k in range(4)]
        total = jnp.where(c == 0, pieces[0], pieces[3])
        added = {0: [], 1: []}
        for hop in (2, 1, 3):
            pairs = []
            for core in (0, 1):
                for place in reached[core]:
                    to = list(place)
                    to[axis] = hop if core == 0 else 3 - hop
                    added[core].append(tuple(to))
                    pairs.append((index_of((*place, core)), index_of((*to, core))))
            total = total + lax.ppermute(jnp.where(c == 0, pieces[hop], pieces[3 - hop]), AXES, pairs)
        for core in (0, 1):
            reached[core] = reached[core] + added[core]
        payload = total
    return payload


def line_sum(v, axis):
    one, two, three = (shift4(v, axis, by).astype(f32) for by in (1, 2, 3))
    return (v.astype(f32) + two) + (one + three)


def ring_rows(own):
    parts = [own] + [shift4(own, YAX, by) for by in (1, 2, 3)]
    return parts, [swap(part) for part in parts]


def line_back(sums):
    total = sums[0]
    for by in (1, 2, 3):
        total = total + shift4(sums[by].astype(bf16), YAX, -by).astype(f32)
    return total


def per_device(
    block_input,
    cotangent,
    segments,
    adapter_index,
    norm_first,
    norm_second,
    conv_taps,
    decay_rate,
    gelu_proj,
    input_proj,
    inner_gate,
    decay_gate,
    output_proj,
    widen_proj,
    narrow_proj,
    enter_square,
    leave_square,
    enter_widen,
    leave_widen,
    enter_narrow,
    leave_narrow,
):
    c = lax.axis_index("c")
    y = lax.axis_index(YAX)
    member = lax.axis_index(RING)
    plane = lax.axis_index(PLANE)
    chip = lax.axis_index(("z", "x", "v", "u"))
    place = lax.axis_index(AXES)
    toks, width = block_input.shape
    halfw = width // 2
    quarter = width // 4
    heads = HEADS // 2
    head = width // HEADS
    cols = enter_square.shape[-1]
    rank = cols // ADAPTERS
    main = 2 * toks
    per = gelu_proj.shape[0]
    per4 = 4 * per
    ff = widen_proj.shape[1] // 2
    slot = ff // 8
    slotp = slot * 16 // 15
    wide2 = 2 * slotp
    hcol = slotp // 4
    per_n = narrow_proj.shape[0]
    chunk = slotp // 16
    glane = 2 * head // 4

    grad_down_own = cotangent.astype(bf16)
    seg_lanes = jnp.broadcast_to(jnp.tile(segments, 2).astype(bf16)[:, None], (2 * toks, cols))
    payload = jnp.concatenate([block_input.astype(bf16), grad_down_own], axis=0)
    is_end = (place == 0) | (place == 127)
    piece = scatter_ends(jnp.where(is_end, payload, jnp.zeros_like(payload)), jnp.where(is_end, seg_lanes, jnp.zeros_like(seg_lanes)), c)

    gates = jnp.concatenate([inner_gate, decay_gate], axis=1)
    quads = jnp.stack(
        [
            jnp.concatenate(
                [v[:, q * (v.shape[1] // 4) : (q + 1) * (v.shape[1] // 4)] for v in (gelu_proj, input_proj, output_proj, gates)],
                axis=1,
            )
            for q in range(4)
        ]
    )
    lanes = quads.shape[2]
    quads = lax.all_to_all(quads, QUAD, 0, 0, tiled=True).reshape(per4, lanes)
    reach = piece.shape[1]
    stretches = piece.shape[0] // 8
    piece = jnp.concatenate([piece[k * 8 : (k + 1) * 8] for k in range(stretches)], axis=1)
    piece = jnp.pad(piece, ((0, 0), (0, lanes - stretches * reach)))
    quads = jnp.concatenate([quads, piece], axis=0)
    near = lax.all_gather(quads[None], AXES, axis=0, tiled=True).reshape(32, 4, per4 + 8, lanes)

    block_input, segments, widen_proj, narrow_proj = after(quads, block_input, segments, widen_proj, narrow_proj)

    block = 4 * 8 * per_n
    bcols = 4 * 8 * chunk
    at_col = jnp.arange(bcols)
    unit = at_col % (4 * chunk) % chunk
    from_row = at_col % (4 * chunk) // chunk * (8 * per_n) + at_col // (4 * chunk) * per_n + unit
    spread = ((jnp.arange(block)[:, None] == from_row[None, :]) & (unit < per_n)[None, :]).astype(bf16)
    units = 8 * per_n
    at_unit = jnp.arange(8 * chunk)
    spread_one = (jnp.arange(units)[:, None] == (at_unit // chunk * per_n + at_unit % chunk)[None, :]) & (at_unit % chunk < per_n)[None, :]
    spread_one = spread_one.astype(bf16)
    pieces = widen_proj.reshape(per, 8, block).transpose(1, 0, 2).reshape(8 * per, block)
    pieces = dot(pieces, spread).astype(bf16).reshape(8, per, 8, hcol).transpose(2, 1, 0, 3)
    pieces = lax.all_to_all(pieces.reshape(8 * per, wide2), RING, 0, 0, tiled=True)
    rows_n = jnp.pad(narrow_proj, ((0, chunk - per_n), (0, 0)))
    tail_n = rows_n[:, wide2:].reshape(4, chunk // 4, width - wide2).transpose(1, 0, 2).reshape(chunk // 4, wide2)
    shard_far = jnp.concatenate([pieces, rows_n[:, :wide2], tail_n], axis=0)
    far = lax.all_gather(shard_far[None], PLANE, axis=0, tiled=True)

    middle_owner = adapter_index[MIDDLE]
    column_owner = jnp.arange(cols) // rank
    owner_of = jnp.arange(adapter_index.shape[0])
    one_hot = (jnp.arange(cols)[None, :] == (middle_owner * rank + jnp.arange(rank))[:, None]).astype(bf16)
    core_at = c.astype(jnp.int32).reshape(1)
    middle_at = middle_owner.reshape(1)

    def select_of(segs):
        owners = jnp.sum((segs[:, None] == owner_of[None, :]).astype(jnp.int32) * adapter_index[None, :], axis=1)
        return (owners[:, None] == column_owner[None, :]).astype(f32)

    taps = half(conv_taps, c, 1)
    rate = half(decay_rate, c, 0)[None, :]
    enter_half = half(enter_square, c, 1)
    leave_half = half(leave_square, c, 2)
    enter_gates = jnp.concatenate([enter_half[2], enter_half[3]], axis=1)

    rows = 2 * main
    normed_own = norm_apply(block_input, norm_first)
    normed_main = both(normed_own, swap(normed_own), c)
    normed_halo = chip_shift(normed_main[main - HALO :], 1)
    normed_long = jnp.concatenate([normed_halo, normed_main], axis=0)
    seg_main = both(segments, swap(segments), c)
    halo_seg = jnp.broadcast_to(jnp.where(chip > 0, MIDDLE, -1), (HALO,))
    select_main = select_of(seg_main)
    select_halo = jnp.broadcast_to((column_owner == middle_owner).astype(f32)[None, :], (HALO, cols))
    ring_segs = [jnp.concatenate(v) for v in ring_rows(segments)]
    ring_selects = [select_of(v) for v in ring_segs]

    my_spread = lax.dynamic_slice_in_dim(spread, member * hcol, hcol, axis=1)
    leave_wide = leave_widen.reshape(cols, 8, block).transpose(1, 0, 2).reshape(8 * cols, block)
    leave_wide = dot(leave_wide, my_spread).astype(bf16).reshape(8, cols, hcol).transpose(1, 0, 2).reshape(cols, wide2)
    leave_a, leave_b = leave_wide[:, :slotp], leave_wide[:, slotp:]
    enter_down = lax.dot_general(
        my_spread, enter_narrow.reshape(4, block, cols), (((0,), (1,)), ((), ())), preferred_element_type=f32
    )
    enter_down = enter_down.transpose(1, 0, 2).reshape(slotp, cols).astype(bf16)

    near = after((shard_far, normed_long, select_main, ring_selects, leave_a, leave_b, enter_down, enter_gates), near)
    x_extra, normed_extra, down_extra, marks_extra = call(
        functools.partial(ends_kernel, stretches), (1,),
        [pl.BlockSpec((32, 4, 8, lanes), lambda *_: (0, 0, per4 // 8, 0), pipeline_mode=pl.Buffered(1)), fixed((1, width))],
        [(fixed((main, width)), ((main, width), f32)), (fixed((main, width)), ((main, width), bf16)),
         (fixed((main, width)), ((main, width), bf16)), (fixed((main, cols)), ((main, cols), f32))],
        [pltpu.VMEM((main, width), f32)],
        core_at, (near, norm_first[None, :]), 1,
    )
    seg_first = marks_extra[:toks, 0].astype(jnp.int32)
    seg_last = marks_extra[toks:, 0].astype(jnp.int32)
    seg_extra = jnp.concatenate([seg_first, seg_last])
    normed_long = jnp.concatenate([normed_long, normed_extra], axis=0)
    normed = normed_long[HALO:]
    marks = jnp.concatenate([halo_seg, seg_main, seg_first + 100, seg_last + 200])
    same = [(marks[HALO - k : -k] == marks[HALO:]).astype(f32)[:, None] for k in range(1, 4)]
    mask = jnp.concatenate(same + [jnp.zeros((rows, 5), f32)], axis=1)
    mask_long = jnp.concatenate([mask[:main], jnp.ones((HALO, 8), f32), mask[main:], jnp.zeros((HALO, 8), f32)], axis=0)
    select_extra = select_of(seg_extra) * (seg_extra != MIDDLE).astype(f32)[:, None]
    select = jnp.concatenate([select_main, select_extra], axis=0)
    select_long = jnp.concatenate([select_halo, select], axis=0)
    select_after = jnp.concatenate([select, select_halo], axis=0)

    col_spec = lambda i: pl.BlockSpec((8, 2, per4, quarter), lambda b, s: (b, s[0], 0, i))
    out_spec = pl.BlockSpec((8, 4, per4, quarter), lambda b, s: (2 * s[0] + b, 0, 0, 2))
    gate_spec = pl.BlockSpec((16, 4, per4, glane), lambda b, s: (s[0], 0, 0, 3 * quarter // glane), pipeline_mode=pl.Buffered(1))
    side_col_spec = lambda i: pl.BlockSpec((32, 1, per4, quarter), lambda b, s: (0, 2 * s[0] + b, 0, i))
    rows_spec = lambda n: pl.BlockSpec((n, quarter), lambda b, s: (0, b))
    head_spec = lambda n: pl.BlockSpec((n, head), lambda h, s: (0, h))
    enter_spec = pl.BlockSpec((quarter, cols), lambda b, s: (b, 0))
    hidden_spec = lambda n: pl.BlockSpec((n, hcol), lambda j, s: (0, j))
    wide_block = (rows, halfw)
    small_block = (rows, cols)
    F = lambda *shape: (fixed(shape), (shape, f32))
    B = lambda *shape: (fixed(shape), (shape, bf16))
    layer = 2 * rows * halfw * width
    mib = 2**20

    gd_rows = ring_rows(tied(cotangent, near).astype(bf16))
    long = rows + HALO
    convolved, lat_gates, pick_fill = call(
        fill_kernel, (2,),
        [fixed((long, width)), side_col_spec(1), fixed((width, cols)), fixed((long, cols)), rows_spec(cols), fixed((rows, 8)), rows_spec(4),
         pl.BlockSpec((quarter, 2 * cols), lambda b, s: (b, 0))],
        [(rows_spec(rows), (wide_block, bf16)), F(rows, 2 * cols), B(long, cols)],
        [pltpu.VMEM((long, quarter), f32)],
        core_at, (normed_long, near, enter_square[1], select_long, leave_half[1], mask, taps, enter_gates), 1, (shard_far,),
    )
    pick_fill = pick_fill[HALO:]

    sides = lambda v: [v[:toks], v[toks:]]
    feed_select = [
        jnp.concatenate([ring_selects[0][:toks], sides(select_extra)[0], ring_selects[1][:toks], sides(select_extra)[1]], axis=0),
        ring_selects[0][toks:],
        ring_selects[1][toks:],
    ]
    sig_in, sig_de, decays, state, prod, pick_in, pick_de = call(
        gates_kernel, (heads,),
        [head_spec(rows), fixed((rows, 2 * cols)), fixed((rows, 2 * cols)), fixed(small_block), gate_spec,
         head_spec(cols), head_spec(cols), fixed((rows, 8)), head_spec(1)],
        [(head_spec(rows), (wide_block, f32))] * 5 + [B(*small_block)] * 2,
        [pltpu.VMEM((rows, head), f32), pltpu.VMEM((halfw, 2 * head), bf16)],
        core_at, (convolved, lat_gates, swap(lat_gates), select, near, leave_half[2], leave_half[3], mask, rate), 4, tuple(gd_rows[0][1:]),
    )
    entering = chips_carry(jnp.stack([prod[main - 1], state[main - 1]]), False)[None, :]
    normed_half = half(normed, c, 1)
    share = -(-width // 7 // 128) * 128
    share_of = lambda v: lax.dynamic_slice_in_dim(jnp.pad(v, ((0, 0), (0, 8 * share - width))), member * share, share, axis=1)
    down_share = share_of(down_extra)
    branch, slope, pick_gelu = call(
        gelu_kernel, (2,),
        [fixed((long, width)), side_col_spec(0), fixed((width, cols)), fixed(small_block), rows_spec(cols)],
        [(rows_spec(rows), (wide_block, f32))] * 2 + [B(*small_block)],
        [],
        core_at, (normed_long, near, enter_square[0], select, leave_half[0]), 12, (normed_half, down_share),
    )
    states, mixed, lat_out, out_mine, out_send, out_extra = call(
        out_kernel, (2,),
        [rows_spec(rows), rows_spec(rows), rows_spec(1), rows_spec(rows), out_spec, enter_spec, fixed((cols, width)), fixed(small_block)],
        [(rows_spec(rows), (wide_block, f32)), (rows_spec(rows), (wide_block, bf16)), F(*small_block),
         F(toks, width), B(toks + main, width), B(main, width)],
        [pltpu.VMEM((rows, width), f32), pltpu.VMEM((rows, quarter), bf16)],
        core_at, (state, prod, entering, branch, near, enter_half[4], leave_square[4], select), 15,
    )
    pick_out = ((lat_out + swap(lat_out)) * select).astype(bf16)
    got = swap(out_send).astype(f32)
    residual = block_input + out_mine + got[:toks]
    residual_extra = x_extra + (out_extra.astype(f32) + got[toks:])
    n2_extra = norm_apply(residual_extra, norm_second)

    n2_rows = ring_rows(norm_apply(residual, norm_second))
    ring = 8 * toks
    anywhere = pl.BlockSpec(memory_space=pl.ANY)
    far_rows = far.shape[1]

    def feed(n2_pieces, gd_pieces, select, micros, waits=()):
        count = len(n2_pieces)
        n = count * toks
        return call(
            functools.partial(ffn_kernel, count), (1,),
            [anywhere] * (2 * count + 1)
            + [fixed((cols, slotp)), fixed((cols, slotp)), fixed((slotp, cols)), fixed((width, cols)), fixed((cols, width)), fixed((n, cols))],
            [B(n, width)] + [B(n, slotp)] * 3 + [B(n, cols)] * 4,
            [pltpu.VMEM((n, width), bf16), pltpu.VMEM((n, width), bf16), pltpu.VMEM(far.shape, bf16),
             pltpu.SemaphoreType.DMA((count,)), pltpu.SemaphoreType.DMA((count,)), pltpu.SemaphoreType.DMA((4, 3))],
            core_at,
            (*n2_pieces, *gd_pieces, far, leave_a, leave_b, enter_down, enter_widen, leave_narrow, select),
            micros, waits,
        )

    mix = lambda rows, extra: [rows[0][0], sides(extra)[0], rows[1][0], sides(extra)[1]]
    gn0, *parts0 = feed(mix(n2_rows, n2_extra), mix(gd_rows, down_extra), feed_select[0], 60)
    gn1, *parts1 = feed(n2_rows[0][1:], gd_rows[0][1:], feed_select[1], 40, (gn0,))
    gn2, *parts2 = feed(n2_rows[1][1:], gd_rows[1][1:], feed_select[2], 60, (gn1,))
    add = lambda a, b: a.astype(f32) + b.astype(f32)

    eighth = main // 8
    side0 = jnp.concatenate([tied(gn0, gn1).astype(bf16), parts0[3], parts0[4]], axis=1)
    extra_part = jnp.concatenate([side0[toks : 2 * toks], side0[3 * toks :]], axis=0)
    extra_total = lax.all_to_all(extra_part, RING, 0, 0, tiled=True).reshape(8, eighth, -1)
    extra_total = to_low(tied(jnp.sum(extra_total.astype(f32), axis=0), gn2))
    extra_all = lax.all_to_all(jnp.broadcast_to(extra_total[None], (8, *extra_total.shape)), RING, 0, 0, tiled=True).reshape(main, -1)
    sums0 = add(gn0[:toks], swap(gn0[2 * toks : 3 * toks]))
    sums1 = add(gn1, swap(gn2)).astype(bf16)
    sums = [sums0] + [sums1[k * toks : (k + 1) * toks] for k in range(3)]
    mid_spec = (pl.BlockSpec((rank, hcol), lambda j, s: (0, j)), ((rank, slotp), bf16))
    extra_spec = (pl.BlockSpec((cols, hcol), lambda j, s: (0, j)), ((cols, slotp), bf16))
    down_mine, down_theirs, mid_a, mid_b, mid_n, mid_l, mid_e, ex_a, ex_b, ex_n = call(
        down_kernel, (4,),
        [anywhere] * 16 + [hidden_spec(4 * toks), hidden_spec(3 * toks), hidden_spec(3 * toks)] * 3
        + [fixed((4 * toks, cols)), fixed((3 * toks, cols)), fixed((3 * toks, cols))] * 4
        + [pl.BlockSpec((4, far_rows, wide2), lambda j, s: (j, 0, 0)), fixed((cols, width))],
        [B(ring // 2, width)] * 2 + [mid_spec] * 3 + [B(rank, width)] * 2 + [extra_spec] * 3,
        [pltpu.VMEM((ring, width), f32), pltpu.VMEM((cols, hcol), f32), pltpu.VMEM((cols, width), f32),
         pltpu.VMEM((ring, width), bf16), pltpu.VMEM((ring, width), bf16), pltpu.SemaphoreType.DMA((8,)), pltpu.SemaphoreType.DMA((8,))],
        jnp.concatenate([middle_at, y.astype(jnp.int32).reshape(1)]),
        (n2_rows[0][0], n2_rows[1][0], *n2_rows[0][1:], *n2_rows[1][1:], gd_rows[0][0], gd_rows[1][0], *gd_rows[0][1:], *gd_rows[1][1:],
         *[v[i] for i in (2, 0, 1, 5, 6, 4, 3) for v in (parts0, parts1, parts2)], far, leave_narrow),
        60, (*sums[1:], extra_total),
    )
    grad_n2 = tied(line_back(sums), mid_l)
    grad_n2_extra = tied(extra_all[:, :width].astype(f32), mid_l)
    lat_extra = extra_all[:, width:]
    lgw_extra = lat_extra[:, :cols]
    pick_n_extra = lat_extra[:, cols:]
    ffn_mid = tied(jnp.concatenate([mid_a, mid_b, mid_n, mid_l, mid_e], axis=1), grad_n2).astype(bf16)
    ffn_mid = lax.all_to_all(ffn_mid.reshape(rank, 16, -1).transpose(1, 0, 2), PLANE, 0, 0, tiled=True)
    ffn_mid = to_low(jnp.sum(ffn_mid.astype(f32), axis=0))
    ffn_mid = lax.all_gather(ffn_mid[None], AXES, axis=0, tiled=True).reshape(16, 8, rank, -1)

    grad_residual = cotangent + norm_back(residual, norm_second, grad_n2)
    grad_residual_extra = down_extra.astype(f32) + norm_back(residual_extra, norm_second, grad_n2_extra)
    grad_out_own = grad_residual.astype(bf16)
    grad_out = jnp.concatenate([both(grad_out_own, swap(grad_out_own), c), grad_residual_extra.astype(bf16)], axis=0)
    grad_gelu, lg_out, back, trail = call(
        functools.partial(outback_kernel, main), (2,),
        [fixed((rows, width)), out_spec, fixed((cols, width)), enter_spec, fixed(small_block)] + [rows_spec(rows)] * 4,
        [(rows_spec(rows), (wide_block, bf16)), B(*small_block)] + [(rows_spec(rows), (wide_block, f32))] * 2,
        [pltpu.VMEM((rows, quarter), f32)],
        core_at, (grad_out, near, leave_square[4], enter_half[4], select, states, branch, slope, decays), 18,
    )
    coming = chips_carry(jnp.stack([decays[0] * trail[0], decays[0] * back[0]]), True)[None, :]
    down_total = tied(add(down_mine, swap(down_theirs)), coming).astype(bf16)
    down_total = lax.all_to_all(down_total, YAX, 0, 0, tiled=True).reshape(4, toks, width)
    gelu_part, lat_gelu = call(
        geluback_kernel, (4,),
        [fixed(wide_block), col_spec(0), fixed((cols, halfw)), enter_spec, fixed(small_block)],
        [(rows_spec(main), ((main, width), f32)), F(*small_block)],
        [pltpu.VMEM(small_block, bf16)],
        core_at, (grad_gelu, near, leave_half[0], enter_square[0], select), 12,
    )

    grad_in, grad_de, base, lat_gates = call(
        gateback_kernel, (heads,),
        [head_spec(rows), head_spec(rows), head_spec(1), head_spec(rows), head_spec(1)] + [head_spec(rows)] * 4
        + [fixed((rows, 8)), head_spec(1), gate_spec, head_spec(cols), head_spec(cols)],
        [(head_spec(rows), (wide_block, bf16))] * 2 + [(head_spec(rows), (wide_block, f32)), F(rows, 2 * cols)],
        [pltpu.VMEM((rows + 8, head), f32), pltpu.VMEM((halfw, 2 * head), bf16)],
        core_at, (back, trail, coming, states, entering, convolved, sig_in, sig_de, decays, mask, rate, near, leave_half[2], leave_half[3]),
        8,
    )

    lanes_all = 3 * slotp + 2 * share
    (packed,) = call(
        pack_kernel, (1,),
        [fixed((cols, slotp))] * 3 + [fixed((main, cols))] * 2 + [fixed((main, share))] * 2,
        [B(cols, lanes_all)], [], core_at,
        (ex_a, ex_b, ex_n, pick_n_extra, lgw_extra, down_share, share_of(n2_extra)), 3, (base,),
    )
    ffn_all = lax.all_gather(packed, RING, axis=0)

    halo_both = chip_shift(jnp.concatenate([base[:HALO], lat_gates[:HALO]], axis=1), -1)
    halo_base, halo_lat = halo_both[:, :halfw], halo_both[:, halfw:]
    halo_other = chip_shift(lat_gates[:HALO], -1, cross=True)
    grad_fill, lg_in, lg_de, lat_fill, normed_mine, normed_theirs = call(
        fillback_kernel, (4,),
        [fixed(wide_block), fixed((rows, 2 * cols)), fixed((rows, 2 * cols)), fixed((HALO, halfw)), fixed((HALO, 2 * cols)), fixed((HALO, 2 * cols)),
         fixed((rows + HALO, cols)), fixed((rows + 2 * HALO, 8)), fixed((4, halfw)), fixed((halfw, cols)), fixed((halfw, cols)), fixed((cols, halfw)),
         col_spec(1), enter_spec, rows_spec(main)],
        [B(*wide_block), B(*small_block), B(*small_block), F(*small_block),
         (rows_spec(toks), ((toks, width), f32)), (rows_spec(toks), ((toks, width), bf16))],
        [pltpu.VMEM((rows + 2 * HALO, halfw), f32), pltpu.VMEM((HALO, 2 * cols), bf16), pltpu.VMEM((main, cols), bf16), pltpu.VMEM((main, quarter), f32)],
        core_at,
        (base, lat_gates, swap(lat_gates), halo_base, halo_lat, halo_other, select_after, mask_long, taps, enter_half[2], enter_half[3],
         leave_half[1], near, enter_square[1], gelu_part),
        12,
    )

    lg_gelu = ((lat_gelu + swap(lat_gelu)) * select).astype(bf16)
    lg_fill = ((lat_fill + swap(lat_fill)) * select).astype(bf16)
    pairs = [
        (lg_gelu, normed_half), (lg_fill, normed_half), (lg_in, convolved), (lg_de, convolved), (lg_out, mixed),
        (pick_gelu, grad_gelu), (pick_fill, grad_fill), (pick_in, grad_in), (pick_de, grad_de), (pick_out, half(grad_out, c, 1)),
    ]
    part_spec = lambda n, i: pl.BlockSpec((main, n), lambda *_: (i, 0), pipeline_mode=pl.Buffered(1))
    operands = [v for pair in pairs for v in pair]
    mid_rows = -(-10 * rank * halfw // cols // 64 // 16) * 16
    (mid,) = call(
        functools.partial(mids_kernel, 10, rank), (1,),
        [part_spec(cols, 0), part_spec(halfw, 0)] * 10,
        [B(64 * mid_rows, cols)],
        [pltpu.VMEM((cols, halfw), f32)],
        middle_at, operands, 6,
    )
    mid_own = mid
    mid = lax.all_to_all(mid, CHIPS, 0, 0, tiled=True).reshape(64, mid_rows, cols)
    mid = to_low(jnp.sum(mid.astype(f32), axis=0))

    operands = [*[v for pair in pairs[:5] for v in pair[::-1]], *[v for pair in pairs[5:] for v in pair]]
    enter_extra, leave_extra = call(
        functools.partial(extras_kernel, 5), (1,),
        [part_spec(halfw, 1), part_spec(cols, 1)] * 5 + [part_spec(cols, 1), part_spec(halfw, 1)] * 5,
        [B(5, halfw, cols), B(5, cols, halfw)],
        [],
        core_at, operands, 6, (mid_own,),
    )
    (grad_leave_widen,) = call(
        wide_kernel, (8,),
        [fixed((rank, cols)), fixed((units, 8 * chunk)), pl.BlockSpec((8, cols, hcol), lambda i, s: (0, 0, i)), pl.BlockSpec((1, 8, rank, hcol), lambda i, s: (i // 2, 0, 0, i % 2))],
        [(pl.BlockSpec((cols, block), lambda i, s: (0, i)), ((cols, 2 * ff), f32))],
        [], core_at, (one_hot, spread_one, ffn_all, ffn_mid), 12, (mid_own,),
    )
    mid = tied(mid, grad_leave_widen).astype(bf16)
    mid = lax.all_to_all(jnp.broadcast_to(mid[None], (64, *mid.shape)).reshape(-1, cols), CHIPS, 0, 0, tiled=True)
    (grad_enter_narrow,) = call(
        enter_kernel, (4,),
        [fixed((rank, cols)), fixed((units, 8 * chunk)), pl.BlockSpec((8, cols, hcol), lambda i, s: (0, 0, 8 + i)), pl.BlockSpec((1, 8, rank, hcol), lambda i, s: (4 + i // 2, 0, 0, i % 2))],
        [(pl.BlockSpec((block, cols), lambda i, s: (i, 0)), ((ff, cols), f32))],
        [], core_at, (one_hot, spread_one, ffn_all, ffn_mid), 7, (mid_own,),
    )
    grad_normed = normed_mine + swap(normed_theirs).astype(f32)
    input_grad = grad_residual + norm_back(block_input, norm_first, grad_normed)
    eye = jnp.eye(cols, dtype=bf16)
    share_spec = lambda i: pl.BlockSpec((8, cols, share), lambda *_: (0, 0, 3 * slotp // share + i))
    grad_leave_narrow, grad_enter_widen = call(
        shares_kernel, (1,),
        [fixed((rank, cols)), fixed((cols, cols)), share_spec(0), share_spec(1), fixed(ffn_mid.shape)],
        [F(cols, width), F(width, cols)],
        [], core_at, (one_hot, eye, ffn_all, ffn_all, ffn_mid), 4, (mid_own,),
    )
    per_k = lambda *shape: pl.BlockSpec((1,) + shape, lambda k, s: (k,) + (0,) * len(shape))
    mid_e_spec = pl.BlockSpec((rank * halfw // cols, cols), lambda k, s: (k, 0))
    mid_l_spec = pl.BlockSpec((rank * halfw // cols, cols), lambda k, s: (5 + k, 0))
    mid_other = swap(mid)
    grad_enter_square, grad_leave_square = call(
        square_kernel, (5,),
        [fixed((rank, cols)), per_k(halfw, cols), per_k(halfw, cols), per_k(cols, halfw), per_k(cols, halfw),
         mid_e_spec, mid_e_spec, mid_l_spec, mid_l_spec],
        [(per_k(width, cols), ((5, width, cols), f32)), (per_k(cols, width), ((5, cols, width), f32))],
        [], core_at, (one_hot, enter_extra, swap(enter_extra), leave_extra, swap(leave_extra), mid, mid_other, mid, mid_other), 9, (grad_enter_narrow, grad_leave_narrow),
    )
    block_output = tied(residual + jnp.sum(down_total.astype(f32), axis=0), grad_leave_square)
    return (
        block_output,
        input_grad,
        grad_enter_square,
        grad_leave_square,
        grad_enter_widen,
        grad_leave_widen,
        grad_enter_narrow,
        grad_leave_narrow,
    )


def solution(mesh):
    split = Mesh(mesh.devices.reshape(SIZES), AXES)
    by_row = P(AXES, None)
    return jax.shard_map(
        per_device,
        mesh=split,
        in_specs=(by_row, by_row, P(AXES), P(), P(), P(), P(), P()) + (by_row,) * 7 + (P(),) * 6,
        out_specs=(by_row, by_row, P(), P(), P(), P(), P(), P()),
        check_vma=False,
    )
```

```python
import functools
import jax
import jax.numpy as jnp
from jax import lax
from jax.experimental import pallas as pl
from jax.experimental.pallas import tpu as pltpu
from jax.sharding import Mesh, PartitionSpec as P

HEADS = 10
ADAPTERS = 8
HALO = 16
MIDDLE = 3
AXES = ("z", "x", "v", "u", "c")
SIZES = (4, 4, 2, 2, 2)
YAX = ("v", "u")
RING = ("v", "u", "c")
PLANE = ("z", "x")
QUAD = ("u", "c")
CHIPS = ("z", "x", "v", "u")
VMEM = 56 * 2**20

eps_norm = 1e-06
floor_scale = 0.001
bf16 = jnp.bfloat16
f32 = jnp.float32


def dot(a, b):
    return jnp.dot(a, b, preferred_element_type=f32)


def dot_nt(a, b):
    return lax.dot_general(a, b, (((1,), (1,)), ((), ())), preferred_element_type=f32)


def dot_tn(a, b):
    return lax.dot_general(a, b, (((0,), (0,)), ((), ())), preferred_element_type=f32)


def low(v):
    return lax.reduce_precision(v, 8, 7)


def to_low(v):
    return low(v).astype(bf16)


def norm_scale(values):
    return lax.rsqrt(jnp.mean(values * values, axis=-1, keepdims=True) + eps_norm)


def norm_apply(values, gain):
    return (values * norm_scale(values) * gain).astype(bf16)


def norm_back(values, gain, grad):
    s = norm_scale(values)
    gq = gain * grad
    return s * gq - values * (s * s * s) * jnp.mean(values * gq, axis=-1, keepdims=True)


def sigmoid(v):
    return 1.0 / (1.0 + jnp.exp(-v))


def gelu_parts(a):
    k = 0.7978845608028654
    a2 = a * a
    th = jnp.tanh(k * (a + 0.044715 * a2 * a))
    value = 0.5 * a * (1.0 + th)
    slope = 0.5 * (1.0 + th) + 0.5 * a * (1.0 - th * th) * (k * (1.0 + 3.0 * 0.044715 * a2))
    return value, slope


def swap(v):
    return lax.ppermute(v, "c", [(0, 1), (1, 0)])


def shift4(v, axis, by):
    return lax.ppermute(v, axis, [(i, (i + by) % 4) for i in range(4)])


def chip_shift(v, by, cross=False):
    chips = 64
    pairs = [
        (2 * p + c, 2 * (p + by) + (1 - c if cross else c))
        for p in range(chips)
        for c in range(2)
        if 0 <= p + by < chips
    ]
    return lax.ppermute(v, AXES, pairs)


def both(own, other, c):
    rows = own.shape[0]
    three = jnp.concatenate([own, other, own], axis=0)
    return lax.dynamic_slice_in_dim(three, c * rows, 2 * rows, axis=0)


def half(v, c, axis):
    size = v.shape[axis] // 2
    return lax.dynamic_slice_in_dim(v, c * size, size, axis=axis)


def after(first, *values):
    held = lax.optimization_barrier((first, *values))[1:]
    return held[0] if len(held) == 1 else held


def tied(value, other):
    return value + other[(0,) * other.ndim].astype(f32) * 0.0


def line_order(parts, y):
    back = parts[::-1]
    twice = jnp.stack(back + back)
    return lax.dynamic_slice_in_dim(twice, 3 - y, 4, axis=0)


def call(kernel, grid, ins, outs, scratch, scalars, args, micros, waits=()):
    count = len(args)

    def body(s_ref, *refs):
        kernel(s_ref, *refs[:count], *refs[count + len(waits) :])

    ins = list(ins) + [pl.BlockSpec(memory_space=pl.ANY)] * len(waits)
    args = (*args, *waits)
    return pl.pallas_call(
        body,
        grid_spec=pltpu.PrefetchScalarGridSpec(
            num_scalar_prefetch=1,
            grid=grid,
            in_specs=ins,
            out_specs=[spec for spec, _ in outs],
            scratch_shapes=scratch,
        ),
        out_shape=[jax.ShapeDtypeStruct(*shape) for _, shape in outs],
        compiler_params=pltpu.CompilerParams(vmem_limit_bytes=VMEM),
        cost_estimate=pl.CostEstimate(flops=int(micros * 1e9), bytes_accessed=int(micros * 2e6), transcendentals=0),
    )(scalars, *args)


def fixed(shape):
    return pl.BlockSpec(shape, lambda *_: (0,) * len(shape), pipeline_mode=pl.Buffered(1))


def scan_rows(d_ref, p_ref, s_ref, q_ref):
    rows, width = d_ref.shape
    row = lax.broadcasted_iota(jnp.int32, (8, width), 0)

    def tile(i, carry):
        state, product = carry
        at = pl.ds(pl.multiple_of(i * 8, 8), 8)
        a = d_ref[at, :]
        b = p_ref[at, :]
        for s in (1, 2, 4):
            b = a * jnp.where(row >= s, pltpu.roll(b, s, 0), 0.0) + b
            a = a * jnp.where(row >= s, pltpu.roll(a, s, 0), 1.0)
        value = b + a * state
        through = a * product
        s_ref[at, :] = value
        q_ref[at, :] = through
        return value[7:8, :], through[7:8, :]

    lax.fori_loop(
        0, rows // 8, tile, (jnp.zeros((1, width), f32), jnp.ones((1, width), f32)), unroll=8
    )


def scan_rows_back(d_ref, g_ref, s_ref, q_ref, main):
    rows, width = d_ref.shape
    row = lax.broadcasted_iota(jnp.int32, (8, width), 0)

    def tile(i, carry):
        state, product, after_row = carry
        at = pl.ds(pl.multiple_of(i * 8, 8), 8)
        d = d_ref[at, :]
        b = g_ref[at, :]
        a = jnp.where(row < 7, pltpu.roll(d, 7, 0), after_row)
        for s in (1, 2, 4):
            b = a * jnp.where(row < 8 - s, pltpu.roll(b, 8 - s, 0), 0.0) + b
            a = a * jnp.where(row < 8 - s, pltpu.roll(a, 8 - s, 0), 1.0)
        value = b + a * state
        through = a * product
        s_ref[at, :] = value
        q_ref[at, :] = through
        return value[0:1, :], through[0:1, :], d[0:1, :]

    zero = jnp.zeros((1, width), f32)
    one = jnp.ones((1, width), f32)
    last, cut = rows // 8 - 1, main // 8
    lax.fori_loop(0, last + 1 - cut, lambda k, t: tile(last - k, t), (zero, zero, one), unroll=8)
    lax.fori_loop(0, cut, lambda k, t: tile(cut - 1 - k, t), (zero, one, one), unroll=8)


def tile_of(w, i):
    block = w[:, i]
    return block.reshape(block.shape[0] * block.shape[1], block.shape[2])


def ends_kernel(stretches, s_ref, near_ref, gain_ref, x_ref, normed_ref, down_ref, marks_ref, hold_ref):
    toks = x_ref.shape[0] // 2
    quarter = x_ref.shape[1] // 4
    reach = quarter + marks_ref.shape[1]
    size = 8 * stretches
    for core in range(2):
        for p in range(16):
            for h in range(stretches):
                row = p * size + h * 8
                for y in range(4):
                    block = near_ref[2 * p + y // 2, 2 * (y % 2) + core, :, h * reach : (h + 1) * reach].astype(f32)
                    cols = slice(y * quarter, (y + 1) * quarter)
                    if row < toks:
                        x_ref[core * toks + row : core * toks + row + 8, cols] = block[:, :quarter]
                        if y == 0:
                            marks_ref[core * toks + row : core * toks + row + 8, :] = block[:, quarter:]
                    else:
                        to = core * toks + row - toks
                        hold_ref[to : to + 8, cols] = block[:, :quarter]
    down_ref[...] = hold_ref[...].astype(bf16)
    x = x_ref[...]
    normed_ref[...] = norm_apply(x, gain_ref[...])


def pack_kernel(s_ref, exa_ref, exb_ref, exn_ref, pick_ref, lg_ref, down_ref, n2_ref, out_ref):
    wide = exa_ref.shape[1]
    share = down_ref.shape[1]
    for i, ref in enumerate((exa_ref, exb_ref, exn_ref)):
        out_ref[:, i * wide : (i + 1) * wide] = ref[...]
    at = 3 * wide
    out_ref[:, at : at + share] = dot_tn(pick_ref[...], down_ref[...]).astype(bf16)
    out_ref[:, at + share :] = dot_tn(lg_ref[...], n2_ref[...]).astype(bf16)


def fill_kernel(c_ref, x_ref, w_ref, first_ref, select_ref, leave_ref, mask_ref, taps_ref, enter_ref, conv_ref, lat_ref, pick_ref, acc_ref):
    rows, width = conv_ref.shape

    @pl.when(pl.program_id(0) == 0)
    def _():
        pick_ref[...] = (dot(x_ref[...], first_ref[...]) * select_ref[...]).astype(bf16)

    acc_ref[...] = dot(x_ref[...], tile_of(w_ref, 0)) + dot(pick_ref[...], leave_ref[...])
    step = width // 5
    for j in range(5):
        at = slice(j * step, (j + 1) * step)
        total = taps_ref[0:1, at] * acc_ref[HALO : HALO + rows, at]
        for k in range(1, taps_ref.shape[0]):
            total = total + taps_ref[k : k + 1, at] * acc_ref[HALO - k : HALO - k + rows, at] * mask_ref[:, k - 1 : k]
        conv_ref[:, at] = total.astype(bf16)

    @pl.when(pl.program_id(0) == 0)
    def _():
        lat_ref[...] = jnp.zeros_like(lat_ref)

    lat_ref[...] += dot(conv_ref[...], enter_ref[...])


def gate_weights(w_ref, hold_ref):
    @pl.when(pl.program_id(0) == 0)
    def _():
        wide = w_ref.shape[3]
        for i in range(4):
            hold_ref[:, i * wide : (i + 1) * wide] = tile_of(w_ref, i)

    head = 2 * w_ref.shape[3]
    at = pl.ds(pl.multiple_of(pl.program_id(0) * head, head), head)
    return hold_ref[at, :head], hold_ref[at, head:]


def gates_kernel(
    c_ref, conv_ref, own_ref, other_ref, select_ref, w_ref, leave_in_ref, leave_de_ref, mask_ref, rate_ref,
    sin_ref, sde_ref, dec_ref, state_ref, prod_ref, pick_in_ref, pick_de_ref, push_ref, hold_ref,
):
    cols = select_ref.shape[1]
    inner, decay = gate_weights(w_ref, hold_ref)

    @pl.when(pl.program_id(0) == 0)
    def _():
        lat = own_ref[...] + other_ref[...]
        select = select_ref[...]
        pick_in_ref[...] = (lat[:, :cols] * select).astype(bf16)
        pick_de_ref[...] = (lat[:, cols:] * select).astype(bf16)

    retain = mask_ref[:, 0:1]
    conv = conv_ref[...]
    sig_in = sigmoid(dot(conv, inner) + dot(pick_in_ref[...], leave_in_ref[...]))
    sig_de = sigmoid(dot(conv, decay) + dot(pick_de_ref[...], leave_de_ref[...]))
    raw = jnp.exp(-8.0 * rate_ref[...] * sig_de)
    scale = jnp.where(retain > 0.5, jnp.sqrt(jnp.maximum(1.0 - raw * raw, floor_scale)), 1.0)
    sin_ref[...] = sig_in
    sde_ref[...] = sig_de
    dec_ref[...] = raw * retain
    push_ref[...] = conv.astype(f32) * sig_in * scale
    scan_rows(dec_ref, push_ref, state_ref, prod_ref)


def gelu_kernel(c_ref, x_ref, w_ref, first_ref, select_ref, leave_ref, value_ref, slope_ref, pick_ref):
    @pl.when(pl.program_id(0) == 0)
    def _():
        pick_ref[...] = (dot(x_ref[HALO:, :], first_ref[...]) * select_ref[...]).astype(bf16)

    pre = dot(x_ref[HALO:, :], tile_of(w_ref, 0)) + dot(pick_ref[...], leave_ref[...])
    value, slope = gelu_parts(pre)
    value_ref[...] = value
    slope_ref[...] = slope


def out_kernel(
    c_ref, state_ref, prod_ref, entering_ref, branch_ref, w_ref, enter_ref, leave_ref, select_ref,
    states_ref, mixed_ref, lat_ref, mine_ref, send_ref, extra_ref, acc_ref, hold_ref,
):
    b = pl.program_id(0)
    q = w_ref.shape[3]
    states = state_ref[...] + prod_ref[...] * entering_ref[...]
    states_ref[...] = states
    hold_ref[...] = (branch_ref[...] * states).astype(bf16)
    mixed_ref[...] = hold_ref[...]

    @pl.when(b == 0)
    def _():
        lat_ref[...] = jnp.zeros_like(lat_ref)
        acc_ref[...] = jnp.zeros_like(acc_ref)

    lat_ref[...] += dot(hold_ref[...], enter_ref[...])
    for i in range(4):
        acc_ref[:, i * q : (i + 1) * q] += dot(hold_ref[...], tile_of(w_ref, i))

    @pl.when(b == pl.num_programs(0) - 1)
    def _():
        acc_ref[...] += dot((lat_ref[...] * select_ref[...]).astype(bf16), leave_ref[...])
        rows = mine_ref.shape[0]
        at = pl.multiple_of(c_ref[0] * rows, rows)
        mine_ref[...] = acc_ref[pl.ds(at, rows), :]
        send_ref[:rows, :] = acc_ref[pl.ds(pl.multiple_of(rows - at, rows), rows), :].astype(bf16)
        extra = acc_ref[2 * rows :, :].astype(bf16)
        send_ref[rows:, :] = extra
        extra_ref[...] = extra


def narrow_block(far_ref, j, top):
    wide = far_ref.shape[2]
    tail = wide // 4
    low_rows = (far_ref.shape[1] - top) // 5
    planes = pl.ds(4 * j, 4)
    main = far_ref[planes, top : top + 4 * low_rows, :].reshape(16 * low_rows, wide)
    pieces = []
    for p in range(4):
        rows = far_ref[4 * j + p, top + 4 * low_rows :, :]
        pieces += [rows[:, k * tail : (k + 1) * tail] for k in range(4)]
    return main, jnp.concatenate(pieces, axis=0)


def fetch(refs, hold_ref, sems):
    size = refs[0].shape[0]
    return [pltpu.make_async_copy(r, hold_ref.at[pl.ds(i * size, size), :], sems.at[i]) for i, r in enumerate(refs)]


def ffn_kernel(count, s_ref, *refs):
    n2_refs, gd_refs = refs[:count], refs[count : 2 * count]
    far_hbm, la_ref, lb_ref, en_ref, ew_ref, ln_ref, select_ref = refs[2 * count : 2 * count + 7]
    gn_ref, ga_ref, gb_ref, hid_ref, lgw_ref, pickn_ref, pickw_ref, lgn_ref = refs[2 * count + 7 : 2 * count + 15]
    n2_hold, gd_hold, far_ref, n2_sems, gd_sems, far_sems = refs[2 * count + 15 :]
    width = gn_ref.shape[1]
    slotp = hid_ref.shape[1]
    step = slotp // 4
    wide = far_ref.shape[2]
    top = width // 16

    def far_copies(j):
        at = pl.ds(pl.multiple_of(j * step, step), step)
        at_b = pl.ds(pl.multiple_of(slotp + j * step, step), step)
        planes = pl.ds(4 * j, 4)
        places = [(slice(None), pl.ds(0, top), at), (slice(None), pl.ds(0, top), at_b), (planes, pl.ds(top, far_ref.shape[1] - top), slice(None))]
        return [pltpu.make_async_copy(far_hbm.at[p], far_ref.at[p], far_sems.at[j, i]) for i, p in enumerate(places)]

    n2_copies = fetch(n2_refs, n2_hold, n2_sems)
    gd_copies = fetch(gd_refs, gd_hold, gd_sems)
    for copy in n2_copies + gd_copies:
        copy.start()
    for j in range(4):
        for copy in far_copies(j):
            copy.start()
    for copy in n2_copies + gd_copies:
        copy.wait()
    select = select_ref[...]
    pickw_ref[...] = (dot(n2_hold[...], ew_ref[...]) * select).astype(bf16)
    lgn_ref[...] = (dot_nt(gd_hold[...], ln_ref[...]) * select).astype(bf16)

    def hidden(j, _):
        for copy in far_copies(j):
            copy.wait()
        at = pl.ds(pl.multiple_of(j * step, step), step)
        at_b = pl.ds(pl.multiple_of(slotp + j * step, step), step)
        a = dot(n2_hold[...], far_ref[:, :top, at].reshape(width, step)) + dot(pickw_ref[...], la_ref[:, at])
        up = dot(n2_hold[...], far_ref[:, :top, at_b].reshape(width, step)) + dot(pickw_ref[...], lb_ref[:, at])
        main, last = narrow_block(far_ref, j, top)
        grad = dot_nt(gd_hold[:, :wide], main) + dot_nt(gd_hold[:, wide:], last) + dot_nt(lgn_ref[...], en_ref[at, :])
        act, slope = gelu_parts(a)
        hid_ref[:, at] = (act * up).astype(bf16)
        ga_ref[:, at] = (slope * up * grad).astype(bf16)
        gb_ref[:, at] = (act * grad).astype(bf16)
        return 0

    lax.fori_loop(0, 4, hidden, 0)
    lgw_ref[...] = ((dot_nt(ga_ref[...], la_ref[...]) + dot_nt(gb_ref[...], lb_ref[...])) * select).astype(bf16)
    pickn_ref[...] = (dot(hid_ref[...], en_ref[...]) * select).astype(bf16)
    part = width // 4

    def back(q, _):
        at = pl.ds(pl.multiple_of(q * part, part), part)
        planes = pl.ds(4 * q, 4)
        total = dot_nt(ga_ref[...], far_ref[planes, :top, :slotp].reshape(part, slotp))
        total += dot_nt(gb_ref[...], far_ref[planes, :top, slotp:].reshape(part, slotp))
        gn_ref[:, at] = (total + dot_nt(lgw_ref[...], ew_ref[at, :])).astype(bf16)
        return 0

    lax.fori_loop(0, 4, back, 0)


def down_kernel(s_ref, *refs):
    n2_refs, gd_refs = refs[:8], refs[8:16]
    hid, ga, gb, pick, lgn, pickn, lgw = [refs[16 + 3 * i : 19 + 3 * i] for i in range(7)]
    far_ref, ln_ref = refs[37:39]
    mine_ref, theirs_ref, mida_ref, midb_ref, midn_ref, midl_ref, mide_ref, exa_ref, exb_ref, exn_ref = refs[39:49]
    acc_ref, hold_ref, wide_ref, n2_hold, gd_hold, n2_sems, gd_sems = refs[49:]
    j = pl.program_id(0)
    rank = mida_ref.shape[0]
    piece = n2_refs[0].shape[0]
    here = pl.ds(pl.multiple_of(s_ref[0] * rank, rank), rank)
    main, last = narrow_block(far_ref, 0, far_ref.shape[1] * 2 // 3)
    cut = main.shape[1]
    ring_of = lambda v: jnp.concatenate([v[0][:piece, :], v[0][2 * piece : 3 * piece, :], v[1][...], v[2][...]], axis=0)
    rest_of = lambda v: jnp.concatenate([v[0][piece : 2 * piece, :], v[0][3 * piece :, :]], axis=0)
    n2_copies = fetch(n2_refs, n2_hold, n2_sems)
    gd_copies = fetch(gd_refs, gd_hold, gd_sems)

    @pl.when(j == 0)
    def _():
        for copy in n2_copies + gd_copies:
            copy.start()
        acc_ref[...] = dot(ring_of(pickn), ln_ref[...])

    hidden = ring_of(hid)
    acc_ref[:, :cut] += dot(hidden, main)
    acc_ref[:, cut:] += dot(hidden, last)
    for left, right, out_ref, extra_ref in ((pick, ga, mida_ref, exa_ref), (pick, gb, midb_ref, exb_ref), (lgn, hid, midn_ref, exn_ref)):
        hold_ref[...] = dot_tn(ring_of(left), ring_of(right))
        out_ref[...] = hold_ref[here, :].astype(bf16)
        extra_ref[...] = dot_tn(rest_of(left), rest_of(right)).astype(bf16)

    @pl.when(j == pl.num_programs(0) - 1)
    def _():
        for k in range(4):
            to = pl.ds(pl.multiple_of(lax.rem(s_ref[1] - k + 4, 4) * piece, piece), piece)
            own, other = (0, 1) if k == 0 else (k + 1, k + 4)
            mine_ref[to, :] = acc_ref[own * piece : (own + 1) * piece, :].astype(bf16)
            theirs_ref[to, :] = acc_ref[other * piece : (other + 1) * piece, :].astype(bf16)
        for copy in n2_copies + gd_copies:
            copy.wait()
        wide_ref[...] = dot_tn(ring_of(pickn), gd_hold[...])
        midl_ref[...] = wide_ref[here, :].astype(bf16)
        wide_ref[...] = dot_tn(ring_of(lgw), n2_hold[...])
        mide_ref[...] = wide_ref[here, :].astype(bf16)


def outback_kernel(
    main, c_ref, go_ref, w_ref, leave_ref, enter_ref, select_ref, states_ref, branch_ref, slope_ref, dec_ref,
    gg_ref, lg_ref, state_ref, prod_ref, gs_ref,
):
    b = pl.program_id(0)
    q = w_ref.shape[3]

    @pl.when(b == 0)
    def _():
        lg_ref[...] = (dot_nt(go_ref[...], leave_ref[...]) * select_ref[...]).astype(bf16)

    gm = dot_nt(lg_ref[...], enter_ref[...])
    for i in range(4):
        gm += dot_nt(go_ref[:, i * q : (i + 1) * q], tile_of(w_ref, i))
    gg_ref[...] = (slope_ref[...] * (gm * states_ref[...])).astype(bf16)
    gs_ref[...] = gm * branch_ref[...]
    scan_rows_back(dec_ref, gs_ref, state_ref, prod_ref, main)


def geluback_kernel(c_ref, g_ref, w_ref, leave_ref, enter_ref, select_ref, part_ref, lat_ref, lg_ref):
    b = pl.program_id(0)
    q = w_ref.shape[3]

    @pl.when(b == 0)
    def _():
        lat = dot_nt(g_ref[...], leave_ref[...])
        lat_ref[...] = lat
        lg_ref[...] = (lat * select_ref[...]).astype(bf16)

    rows = part_ref.shape[0]
    part = dot_nt(g_ref[:rows, :q], tile_of(w_ref, 0)) + dot_nt(g_ref[:rows, q : 2 * q], tile_of(w_ref, 1))
    part_ref[...] = part + dot_nt(lg_ref[:rows, :], enter_ref[...])


def gateback_kernel(
    c_ref, back_ref, trail_ref, coming_ref, states_ref, entering_ref, conv_ref, sin_ref, sde_ref, dec_ref, mask_ref, rate_ref,
    w_ref, leave_in_ref, leave_de_ref,
    gi_ref, gd_ref, base_ref, lat_ref, hold_ref, gate_ref,
):
    rows = conv_ref.shape[0]
    cols = leave_in_ref.shape[0]
    inner, decay = gate_weights(w_ref, gate_ref)
    retain = mask_ref[:, 0:1]
    hold_ref[7:8, :] = entering_ref[...]
    hold_ref[8:, :] = states_ref[...]
    rate = rate_ref[...]
    sig_in = sin_ref[...]
    sig_de = sde_ref[...]
    conv = conv_ref[...].astype(f32)
    carried = back_ref[...] + trail_ref[...] * coming_ref[...]
    raw = jnp.exp(-8.0 * rate * sig_de)
    grown = 1.0 - raw * raw
    scale = jnp.where(retain > 0.5, jnp.sqrt(jnp.maximum(grown, floor_scale)), 1.0)
    through = carried * conv
    gi = (through * scale * sig_in * (1.0 - sig_in)).astype(bf16)
    grad_grown = jnp.where((grown > floor_scale) & (retain > 0.5), through * sig_in * 0.5 / scale, 0.0)
    grad_log = carried * hold_ref[7 : 7 + rows, :] * dec_ref[...] - 2.0 * raw * raw * grad_grown
    gd = (grad_log * (-8.0 * rate) * sig_de * (1.0 - sig_de)).astype(bf16)
    gi_ref[...] = gi
    gd_ref[...] = gd
    base_ref[...] = carried * sig_in * scale + dot_nt(gi, inner) + dot_nt(gd, decay)

    @pl.when(pl.program_id(0) == 0)
    def _():
        lat_ref[...] = jnp.zeros_like(lat_ref)

    lat_ref[:, :cols] += dot_nt(gi, leave_in_ref[...])
    lat_ref[:, cols:] += dot_nt(gd, leave_de_ref[...])


def fillback_kernel(
    c_ref, base_ref, own_ref, other_ref, hbase_ref, hown_ref, hother_ref, select_ref, mask_ref, taps_ref, enter_in_ref, enter_de_ref, leave_ref,
    w_ref, enter_ref, before_ref,
    gf_ref, lgi_ref, lgd_ref, lat_ref, mine_ref, theirs_ref, gc_ref, hlg_ref, lg_ref, part_ref,
):
    b = pl.program_id(0)
    q = w_ref.shape[3]
    rows, width = base_ref.shape
    main = part_ref.shape[0]
    cols = lgi_ref.shape[1]

    @pl.when(b == 0)
    def _():
        lat = own_ref[...] + other_ref[...]
        hlat = hown_ref[...] + hother_ref[...]
        select = select_ref[:rows, :]
        hselect = select_ref[rows:, :]
        lgi_ref[...] = (lat[:, :cols] * select).astype(bf16)
        lgd_ref[...] = (lat[:, cols:] * select).astype(bf16)
        hlg_ref[:, :cols] = (hlat[:, :cols] * hselect).astype(bf16)
        hlg_ref[:, cols:] = (hlat[:, cols:] * hselect).astype(bf16)
        step = width // 5
        for j in range(5):
            at = slice(j * step, (j + 1) * step)
            ei = enter_in_ref[at, :]
            ed = enter_de_ref[at, :]
            here = base_ref[:, at] + dot_nt(lgi_ref[...], ei) + dot_nt(lgd_ref[...], ed)
            gc_ref[:main, at] = here[:main]
            gc_ref[main : main + HALO, at] = (
                hbase_ref[:, at] + dot_nt(hlg_ref[:, :cols], ei) + dot_nt(hlg_ref[:, cols:], ed)
            )
            gc_ref[main + HALO : rows + HALO, at] = here[main:]
            gc_ref[rows + HALO :, at] = jnp.zeros((HALO, step), f32)
            for lo, hi, to in ((0, main, 0), (main + HALO, rows + HALO, main)):
                total = taps_ref[0:1, at] * gc_ref[lo:hi, at]
                for k in range(1, taps_ref.shape[0]):
                    total = total + taps_ref[k : k + 1, at] * gc_ref[lo + k : hi + k, at] * mask_ref[lo + k : hi + k, k - 1 : k]
                gf_ref[to : to + hi - lo, at] = total.astype(bf16)
        lat = dot_nt(gf_ref[...], leave_ref[...])
        lat_ref[...] = lat
        lg_ref[...] = (lat[:main] * select_ref[:main, :]).astype(bf16)

    part = dot_nt(gf_ref[:main, :q], tile_of(w_ref, 0)) + dot_nt(gf_ref[:main, q : 2 * q], tile_of(w_ref, 1))
    part_ref[...] = before_ref[...] + part + dot_nt(lg_ref[...], enter_ref[...])
    own = mine_ref.shape[0]
    at = pl.multiple_of(c_ref[0] * own, own)
    mine_ref[...] = part_ref[pl.ds(at, own), :]
    theirs_ref[...] = part_ref[pl.ds(pl.multiple_of(own - at, own), own), :].astype(bf16)


def mids_kernel(count, rank, s_ref, *refs):
    out_ref, hold_ref = refs[2 * count :]
    here = pl.ds(pl.multiple_of(s_ref[0] * rank, rank), rank)
    lanes = out_ref.shape[1]
    parts = hold_ref.shape[1] // lanes
    for i in range(count):
        hold_ref[...] = dot_tn(refs[2 * i][...], refs[2 * i + 1][...])
        for j in range(parts):
            at = (i * parts + j) * rank
            out_ref[at : at + rank, :] = hold_ref[here, j * lanes : (j + 1) * lanes].astype(bf16)
    filled = count * parts * rank
    out_ref[filled:, :] = jnp.zeros((out_ref.shape[0] - filled, lanes), bf16)


def extras_kernel(count, s_ref, *refs):
    enter_ref, leave_ref = refs[4 * count :]
    for i in range(count):
        enter_ref[i] = dot_tn(refs[2 * i][...], refs[2 * i + 1][...]).astype(bf16)
    for i in range(count):
        k = 2 * count + 2 * i
        leave_ref[i] = dot_tn(refs[k][...], refs[k + 1][...]).astype(bf16)


def square_kernel(s_ref, one_ref, own_e_ref, other_e_ref, own_l_ref, other_l_ref, own_me_ref, other_me_ref, own_ml_ref, other_ml_ref, enter_ref, leave_ref):
    size = own_e_ref.shape[1]
    one = one_ref[...]
    rank = one.shape[0]
    whole = lambda ref: jnp.concatenate([ref[j * rank : (j + 1) * rank, :] for j in range(ref.shape[0] // rank)], axis=1)
    for core, e_ref, l_ref, me_ref, ml_ref in (
        (s_ref[0], own_e_ref, own_l_ref, own_me_ref, own_ml_ref),
        (1 - s_ref[0], other_e_ref, other_l_ref, other_me_ref, other_ml_ref),
    ):
        at = pl.ds(pl.multiple_of(core * size, size), size)
        enter_ref[0, at, :] = e_ref[0].astype(f32) + dot_tn(whole(me_ref), one)
        leave_ref[0, :, at] = l_ref[0].astype(f32) + dot_tn(one, whole(ml_ref))


def unit_parts(one_ref, extra_ref, mid_ref, size):
    count = extra_ref.shape[0]
    cut = lambda ref, p: jnp.concatenate([ref[m, :, p * size : (p + 1) * size] for m in range(count)], axis=1)
    mid = jnp.concatenate([mid_ref[0, m, :, p * size : (p + 1) * size] for p in range(4) for m in range(count)], axis=1)
    placed = dot_tn(one_ref[...], mid).astype(bf16)
    wide = count * size
    return jnp.concatenate([cut(extra_ref, p) + placed[:, p * wide : (p + 1) * wide] for p in range(4)], axis=0)


def wide_kernel(s_ref, one_ref, spread_ref, extra_ref, mid_ref, out_ref):
    cols = out_ref.shape[0]
    done = dot_nt(unit_parts(one_ref, extra_ref, mid_ref, spread_ref.shape[1] // 8), spread_ref[...])
    out_ref[...] = jnp.concatenate([done[p * cols : (p + 1) * cols] for p in range(4)], axis=1)


def enter_kernel(s_ref, one_ref, spread_ref, extra_ref, mid_ref, out_ref):
    units, size = spread_ref.shape
    cols = out_ref.shape[1]
    done = dot_nt(spread_ref[...], unit_parts(one_ref, extra_ref, mid_ref, size // 8))
    for p in range(4):
        out_ref[p * units : (p + 1) * units, :] = done[:, p * cols : (p + 1) * cols]


def shares_kernel(s_ref, one_ref, eye_ref, extra_l_ref, extra_e_ref, mid_ref, leave_ref, enter_ref):
    one = one_ref[...]
    width = leave_ref.shape[1]
    share = extra_l_ref.shape[2]
    per = mid_ref.shape[3]
    sums = []
    for p in range(16 - 2 * width // per, 16):
        total = mid_ref[p, 0].astype(f32)
        for m in range(1, 8):
            total = total + mid_ref[p, m].astype(f32)
        sums.append(total.astype(bf16))
    mid = jnp.concatenate(sums, axis=1)
    leave_ref[...] = dot_tn(one, mid[:, :width])
    enter_ref[...] = dot_tn(mid[:, width : 2 * width], one)
    for m in range(8):
        lo, hi = m * share, min((m + 1) * share, width)
        if lo < hi:
            leave_ref[:, lo:hi] += extra_l_ref[m, :, : hi - lo].astype(f32)
            enter_ref[lo:hi, :] += dot_tn(extra_e_ref[m], eye_ref[...])[: hi - lo]


def linked(former, latter):
    return (former[0] * latter[0], latter[0] * former[1] + latter[1])


def line_carry(value, axis, reverse):
    sign = -1 if reverse else 1
    here = lax.axis_index(axis)
    here = 3 - here if reverse else here
    came = {by: shift4(value, axis, sign * by) for by in (1, 2, 3)}
    unit = (jnp.ones_like(value[0]), jnp.zeros_like(value[0]))

    def take(so_far, by, valid):
        new = linked(so_far, (came[by][0], came[by][1]))
        return tuple(jnp.where(valid, a, b) for a, b in zip(new, so_far))

    enter = unit
    for by in (3, 2, 1):
        enter = take(enter, by, here >= by)
    total = linked(enter, (value[0], value[1]))
    for by in (3, 2, 1):
        total = take(total, by, here < by)
    return enter, jnp.stack(total)


def chips_carry(value, reverse):
    by_y, line = line_carry(value, YAX, reverse)
    by_x, plane = line_carry(line, "x", reverse)
    by_z, _ = line_carry(plane, "z", reverse)
    return linked(linked(by_z, by_x), by_y)[1]


def index_of(place):
    at = 0
    for i, n in zip(place, (4, 4, 4, 2)):
        at = at * n + i
    return at


def scatter_ends(payload, seg_lanes, c):
    reached = {0: [(0, 0, 0)], 1: [(3, 3, 3)]}
    width = payload.shape[1]
    payload = jnp.concatenate([payload, seg_lanes], axis=1)
    for axis in range(3):
        if axis < 2:
            size = payload.shape[0] // 4
            pieces = [payload[k * size : (k + 1) * size] for k in range(4)]
        else:
            size = width // 4
            pieces = [jnp.concatenate([payload[:, k * size : (k + 1) * size], payload[:, width:]], axis=1) for k in range(4)]
        total = jnp.where(c == 0, pieces[0], pieces[3])
        added = {0: [], 1: []}
        for hop in (2, 1, 3):
            pairs = []
            for core in (0, 1):
                for place in reached[core]:
                    to = list(place)
                    to[axis] = hop if core == 0 else 3 - hop
                    added[core].append(tuple(to))
                    pairs.append((index_of((*place, core)), index_of((*to, core))))
            total = total + lax.ppermute(jnp.where(c == 0, pieces[hop], pieces[3 - hop]), AXES, pairs)
        for core in (0, 1):
            reached[core] = reached[core] + added[core]
        payload = total
    return payload


def line_sum(v, axis):
    one, two, three = (shift4(v, axis, by).astype(f32) for by in (1, 2, 3))
    return (v.astype(f32) + two) + (one + three)


def ring_rows(own):
    parts = [own] + [shift4(own, YAX, by) for by in (1, 2, 3)]
    return parts, [swap(part) for part in parts]


def line_back(sums):
    total = sums[0]
    for by in (1, 2, 3):
        total = total + shift4(sums[by].astype(bf16), YAX, -by).astype(f32)
    return total


def per_device(
    block_input,
    cotangent,
    segments,
    adapter_index,
    norm_first,
    norm_second,
    conv_taps,
    decay_rate,
    gelu_proj,
    input_proj,
    inner_gate,
    decay_gate,
    output_proj,
    widen_proj,
    narrow_proj,
    enter_square,
    leave_square,
    enter_widen,
    leave_widen,
    enter_narrow,
    leave_narrow,
):
    c = lax.axis_index("c")
    y = lax.axis_index(YAX)
    member = lax.axis_index(RING)
    plane = lax.axis_index(PLANE)
    chip = lax.axis_index(("z", "x", "v", "u"))
    place = lax.axis_index(AXES)
    toks, width = block_input.shape
    halfw = width // 2
    quarter = width // 4
    heads = HEADS // 2
    head = width // HEADS
    cols = enter_square.shape[-1]
    rank = cols // ADAPTERS
    main = 2 * toks
    per = gelu_proj.shape[0]
    per4 = 4 * per
    ff = widen_proj.shape[1] // 2
    slot = ff // 8
    slotp = slot * 16 // 15
    wide2 = 2 * slotp
    hcol = slotp // 4
    per_n = narrow_proj.shape[0]
    chunk = slotp // 16
    glane = 2 * head // 4

    grad_down_own = cotangent.astype(bf16)
    seg_lanes = jnp.broadcast_to(jnp.tile(segments, 2).astype(bf16)[:, None], (2 * toks, cols))
    payload = jnp.concatenate([block_input.astype(bf16), grad_down_own], axis=0)
    is_end = (place == 0) | (place == 127)
    piece = scatter_ends(jnp.where(is_end, payload, jnp.zeros_like(payload)), jnp.where(is_end, seg_lanes, jnp.zeros_like(seg_lanes)), c)

    gates = jnp.concatenate([inner_gate, decay_gate], axis=1)
    quads = jnp.stack(
        [
            jnp.concatenate(
                [v[:, q * (v.shape[1] // 4) : (q + 1) * (v.shape[1] // 4)] for v in (gelu_proj, input_proj, output_proj, gates)],
                axis=1,
            )
            for q in range(4)
        ]
    )
    lanes = quads.shape[2]
    quads = lax.all_to_all(quads, QUAD, 0, 0, tiled=True).reshape(per4, lanes)
    reach = piece.shape[1]
    stretches = piece.shape[0] // 8
    piece = jnp.concatenate([piece[k * 8 : (k + 1) * 8] for k in range(stretches)], axis=1)
    piece = jnp.pad(piece, ((0, 0), (0, lanes - stretches * reach)))
    quads = jnp.concatenate([quads, piece], axis=0)
    near = lax.all_gather(quads[None], AXES, axis=0, tiled=True).reshape(32, 4, per4 + 8, lanes)

    block_input, segments, widen_proj, narrow_proj = after(quads, block_input, segments, widen_proj, narrow_proj)

    block = 4 * 8 * per_n
    bcols = 4 * 8 * chunk
    at_col = jnp.arange(bcols)
    unit = at_col % (4 * chunk) % chunk
    from_row = at_col % (4 * chunk) // chunk * (8 * per_n) + at_col // (4 * chunk) * per_n + unit
    spread = ((jnp.arange(block)[:, None] == from_row[None, :]) & (unit < per_n)[None, :]).astype(bf16)
    units = 8 * per_n
    at_unit = jnp.arange(8 * chunk)
    spread_one = (jnp.arange(units)[:, None] == (at_unit // chunk * per_n + at_unit % chunk)[None, :]) & (at_unit % chunk < per_n)[None, :]
    spread_one = spread_one.astype(bf16)
    pieces = widen_proj.reshape(per, 8, block).transpose(1, 0, 2).reshape(8 * per, block)
    pieces = dot(pieces, spread).astype(bf16).reshape(8, per, 8, hcol).transpose(2, 1, 0, 3)
    pieces = lax.all_to_all(pieces.reshape(8 * per, wide2), RING, 0, 0, tiled=True)
    rows_n = jnp.pad(narrow_proj, ((0, chunk - per_n), (0, 0)))
    tail_n = rows_n[:, wide2:].reshape(4, chunk // 4, width - wide2).transpose(1, 0, 2).reshape(chunk // 4, wide2)
    shard_far = jnp.concatenate([pieces, rows_n[:, :wide2], tail_n], axis=0)
    far = lax.all_gather(shard_far[None], PLANE, axis=0, tiled=True)

    middle_owner = adapter_index[MIDDLE]
    column_owner = jnp.arange(cols) // rank
    owner_of = jnp.arange(adapter_index.shape[0])
    one_hot = (jnp.arange(cols)[None, :] == (middle_owner * rank + jnp.arange(rank))[:, None]).astype(bf16)
    core_at = c.astype(jnp.int32).reshape(1)
    middle_at = middle_owner.reshape(1)

    def select_of(segs):
        owners = jnp.sum((segs[:, None] == owner_of[None, :]).astype(jnp.int32) * adapter_index[None, :], axis=1)
        return (owners[:, None] == column_owner[None, :]).astype(f32)

    taps = half(conv_taps, c, 1)
    rate = half(decay_rate, c, 0)[None, :]
    enter_half = half(enter_square, c, 1)
    leave_half = half(leave_square, c, 2)
    enter_gates = jnp.concatenate([enter_half[2], enter_half[3]], axis=1)

    rows = 2 * main
    normed_own = norm_apply(block_input, norm_first)
    normed_main = both(normed_own, swap(normed_own), c)
    normed_halo = chip_shift(normed_main[main - HALO :], 1)
    normed_long = jnp.concatenate([normed_halo, normed_main], axis=0)
    seg_main = both(segments, swap(segments), c)
    halo_seg = jnp.broadcast_to(jnp.where(chip > 0, MIDDLE, -1), (HALO,))
    select_main = select_of(seg_main)
    select_halo = jnp.broadcast_to((column_owner == middle_owner).astype(f32)[None, :], (HALO, cols))
    ring_segs = [jnp.concatenate(v) for v in ring_rows(segments)]
    ring_selects = [select_of(v) for v in ring_segs]

    my_spread = lax.dynamic_slice_in_dim(spread, member * hcol, hcol, axis=1)
    leave_wide = leave_widen.reshape(cols, 8, block).transpose(1, 0, 2).reshape(8 * cols, block)
    leave_wide = dot(leave_wide, my_spread).astype(bf16).reshape(8, cols, hcol).transpose(1, 0, 2).reshape(cols, wide2)
    leave_a, leave_b = leave_wide[:, :slotp], leave_wide[:, slotp:]
    enter_down = lax.dot_general(
        my_spread, enter_narrow.reshape(4, block, cols), (((0,), (1,)), ((), ())), preferred_element_type=f32
    )
    enter_down = enter_down.transpose(1, 0, 2).reshape(slotp, cols).astype(bf16)

    near = after((shard_far, normed_long, select_main, ring_selects, leave_a, leave_b, enter_down, enter_gates), near)
    x_extra, normed_extra, down_extra, marks_extra = call(
        functools.partial(ends_kernel, stretches), (1,),
        [pl.BlockSpec((32, 4, 8, lanes), lambda *_: (0, 0, per4 // 8, 0), pipeline_mode=pl.Buffered(1)), fixed((1, width))],
        [(fixed((main, width)), ((main, width), f32)), (fixed((main, width)), ((main, width), bf16)),
         (fixed((main, width)), ((main, width), bf16)), (fixed((main, cols)), ((main, cols), f32))],
        [pltpu.VMEM((main, width), f32)],
        core_at, (near, norm_first[None, :]), 1,
    )
    seg_first = marks_extra[:toks, 0].astype(jnp.int32)
    seg_last = marks_extra[toks:, 0].astype(jnp.int32)
    seg_extra = jnp.concatenate([seg_first, seg_last])
    normed_long = jnp.concatenate([normed_long, normed_extra], axis=0)
    normed = normed_long[HALO:]
    marks = jnp.concatenate([halo_seg, seg_main, seg_first + 100, seg_last + 200])
    same = [(marks[HALO - k : -k] == marks[HALO:]).astype(f32)[:, None] for k in range(1, 4)]
    mask = jnp.concatenate(same + [jnp.zeros((rows, 5), f32)], axis=1)
    mask_long = jnp.concatenate([mask[:main], jnp.ones((HALO, 8), f32), mask[main:], jnp.zeros((HALO, 8), f32)], axis=0)
    select_extra = select_of(seg_extra) * (seg_extra != MIDDLE).astype(f32)[:, None]
    select = jnp.concatenate([select_main, select_extra], axis=0)
    select_long = jnp.concatenate([select_halo, select], axis=0)
    select_after = jnp.concatenate([select, select_halo], axis=0)

    col_spec = lambda i: pl.BlockSpec((8, 2, per4, quarter), lambda b, s: (b, s[0], 0, i))
    out_spec = pl.BlockSpec((8, 4, per4, quarter), lambda b, s: (2 * s[0] + b, 0, 0, 2))
    gate_spec = pl.BlockSpec((16, 4, per4, glane), lambda b, s: (s[0], 0, 0, 3 * quarter // glane), pipeline_mode=pl.Buffered(1))
    side_col_spec = lambda i: pl.BlockSpec((32, 1, per4, quarter), lambda b, s: (0, 2 * s[0] + b, 0, i))
    rows_spec = lambda n: pl.BlockSpec((n, quarter), lambda b, s: (0, b))
    head_spec = lambda n: pl.BlockSpec((n, head), lambda h, s: (0, h))
    enter_spec = pl.BlockSpec((quarter, cols), lambda b, s: (b, 0))
    hidden_spec = lambda n: pl.BlockSpec((n, hcol), lambda j, s: (0, j))
    wide_block = (rows, halfw)
    small_block = (rows, cols)
    F = lambda *shape: (fixed(shape), (shape, f32))
    B = lambda *shape: (fixed(shape), (shape, bf16))
    layer = 2 * rows * halfw * width
    mib = 2**20

    gd_rows = ring_rows(tied(cotangent, near).astype(bf16))
    long = rows + HALO
    convolved, lat_gates, pick_fill = call(
        fill_kernel, (2,),
        [fixed((long, width)), side_col_spec(1), fixed((width, cols)), fixed((long, cols)), rows_spec(cols), fixed((rows, 8)), rows_spec(4),
         pl.BlockSpec((quarter, 2 * cols), lambda b, s: (b, 0))],
        [(rows_spec(rows), (wide_block, bf16)), F(rows, 2 * cols), B(long, cols)],
        [pltpu.VMEM((long, quarter), f32)],
        core_at, (normed_long, near, enter_square[1], select_long, leave_half[1], mask, taps, enter_gates), 1, (shard_far,),
    )
    pick_fill = pick_fill[HALO:]

    sides = lambda v: [v[:toks], v[toks:]]
    feed_select = [
        jnp.concatenate([ring_selects[0][:toks], sides(select_extra)[0], ring_selects[1][:toks], sides(select_extra)[1]], axis=0),
        ring_selects[0][toks:],
        ring_selects[1][toks:],
    ]
    sig_in, sig_de, decays, state, prod, pick_in, pick_de = call(
        gates_kernel, (heads,),
        [head_spec(rows), fixed((rows, 2 * cols)), fixed((rows, 2 * cols)), fixed(small_block), gate_spec,
         head_spec(cols), head_spec(cols), fixed((rows, 8)), head_spec(1)],
        [(head_spec(rows), (wide_block, f32))] * 5 + [B(*small_block)] * 2,
        [pltpu.VMEM((rows, head), f32), pltpu.VMEM((halfw, 2 * head), bf16)],
        core_at, (convolved, lat_gates, swap(lat_gates), select, near, leave_half[2], leave_half[3], mask, rate), 4, tuple(gd_rows[0][1:]),
    )
    entering = chips_carry(jnp.stack([prod[main - 1], state[main - 1]]), False)[None, :]
    normed_half = half(normed, c, 1)
    share = -(-width // 7 // 128) * 128
    share_of = lambda v: lax.dynamic_slice_in_dim(jnp.pad(v, ((0, 0), (0, 8 * share - width))), member * share, share, axis=1)
    down_share = share_of(down_extra)
    branch, slope, pick_gelu = call(
        gelu_kernel, (2,),
        [fixed((long, width)), side_col_spec(0), fixed((width, cols)), fixed(small_block), rows_spec(cols)],
        [(rows_spec(rows), (wide_block, f32))] * 2 + [B(*small_block)],
        [],
        core_at, (normed_long, near, enter_square[0], select, leave_half[0]), 12, (normed_half, down_share),
    )
    states, mixed, lat_out, out_mine, out_send, out_extra = call(
        out_kernel, (2,),
        [rows_spec(rows), rows_spec(rows), rows_spec(1), rows_spec(rows), out_spec, enter_spec, fixed((cols, width)), fixed(small_block)],
        [(rows_spec(rows), (wide_block, f32)), (rows_spec(rows), (wide_block, bf16)), F(*small_block),
         F(toks, width), B(toks + main, width), B(main, width)],
        [pltpu.VMEM((rows, width), f32), pltpu.VMEM((rows, quarter), bf16)],
        core_at, (state, prod, entering, branch, near, enter_half[4], leave_square[4], select), 15,
    )
    pick_out = ((lat_out + swap(lat_out)) * select).astype(bf16)
    got = swap(out_send).astype(f32)
    residual = block_input + out_mine + got[:toks]
    residual_extra = x_extra + (out_extra.astype(f32) + got[toks:])
    n2_extra = norm_apply(residual_extra, norm_second)

    n2_rows = ring_rows(norm_apply(residual, norm_second))
    ring = 8 * toks
    anywhere = pl.BlockSpec(memory_space=pl.ANY)
    far_rows = far.shape[1]

    def feed(n2_pieces, gd_pieces, select, micros, waits=()):
        count = len(n2_pieces)
        n = count * toks
        return call(
            functools.partial(ffn_kernel, count), (1,),
            [anywhere] * (2 * count + 1)
            + [fixed((cols, slotp)), fixed((cols, slotp)), fixed((slotp, cols)), fixed((width, cols)), fixed((cols, width)), fixed((n, cols))],
            [B(n, width)] + [B(n, slotp)] * 3 + [B(n, cols)] * 4,
            [pltpu.VMEM((n, width), bf16), pltpu.VMEM((n, width), bf16), pltpu.VMEM(far.shape, bf16),
             pltpu.SemaphoreType.DMA((count,)), pltpu.SemaphoreType.DMA((count,)), pltpu.SemaphoreType.DMA((4, 3))],
            core_at,
            (*n2_pieces, *gd_pieces, far, leave_a, leave_b, enter_down, enter_widen, leave_narrow, select),
            micros, waits,
        )

    mix = lambda rows, extra: [rows[0][0], sides(extra)[0], rows[1][0], sides(extra)[1]]
    gn0, *parts0 = feed(mix(n2_rows, n2_extra), mix(gd_rows, down_extra), feed_select[0], 60)
    gn1, *parts1 = feed(n2_rows[0][1:], gd_rows[0][1:], feed_select[1], 40, (gn0,))
    gn2, *parts2 = feed(n2_rows[1][1:], gd_rows[1][1:], feed_select[2], 60, (gn1,))
    add = lambda a, b: a.astype(f32) + b.astype(f32)

    eighth = main // 8
    side0 = jnp.concatenate([tied(gn0, gn1).astype(bf16), parts0[3], parts0[4]], axis=1)
    extra_part = jnp.concatenate([side0[toks : 2 * toks], side0[3 * toks :]], axis=0)
    extra_total = lax.all_to_all(extra_part, RING, 0, 0, tiled=True).reshape(8, eighth, -1)
    extra_total = to_low(tied(jnp.sum(extra_total.astype(f32), axis=0), gn2))
    extra_all = lax.all_to_all(jnp.broadcast_to(extra_total[None], (8, *extra_total.shape)), RING, 0, 0, tiled=True).reshape(main, -1)
    sums0 = add(gn0[:toks], swap(gn0[2 * toks : 3 * toks]))
    sums1 = add(gn1, swap(gn2)).astype(bf16)
    sums = [sums0] + [sums1[k * toks : (k + 1) * toks] for k in range(3)]
    mid_spec = (pl.BlockSpec((rank, hcol), lambda j, s: (0, j)), ((rank, slotp), bf16))
    extra_spec = (pl.BlockSpec((cols, hcol), lambda j, s: (0, j)), ((cols, slotp), bf16))
    down_mine, down_theirs, mid_a, mid_b, mid_n, mid_l, mid_e, ex_a, ex_b, ex_n = call(
        down_kernel, (4,),
        [anywhere] * 16 + [hidden_spec(4 * toks), hidden_spec(3 * toks), hidden_spec(3 * toks)] * 3
        + [fixed((4 * toks, cols)), fixed((3 * toks, cols)), fixed((3 * toks, cols))] * 4
        + [pl.BlockSpec((4, far_rows, wide2), lambda j, s: (j, 0, 0)), fixed((cols, width))],
        [B(ring // 2, width)] * 2 + [mid_spec] * 3 + [B(rank, width)] * 2 + [extra_spec] * 3,
        [pltpu.VMEM((ring, width), f32), pltpu.VMEM((cols, hcol), f32), pltpu.VMEM((cols, width), f32),
         pltpu.VMEM((ring, width), bf16), pltpu.VMEM((ring, width), bf16), pltpu.SemaphoreType.DMA((8,)), pltpu.SemaphoreType.DMA((8,))],
        jnp.concatenate([middle_at, y.astype(jnp.int32).reshape(1)]),
        (n2_rows[0][0], n2_rows[1][0], *n2_rows[0][1:], *n2_rows[1][1:], gd_rows[0][0], gd_rows[1][0], *gd_rows[0][1:], *gd_rows[1][1:],
         *[v[i] for i in (2, 0, 1, 5, 6, 4, 3) for v in (parts0, parts1, parts2)], far, leave_narrow),
        60, (*sums[1:], extra_total),
    )
    grad_n2 = tied(line_back(sums), mid_l)
    grad_n2_extra = tied(extra_all[:, :width].astype(f32), mid_l)
    lat_extra = extra_all[:, width:]
    lgw_extra = lat_extra[:, :cols]
    pick_n_extra = lat_extra[:, cols:]
    ffn_mid = tied(jnp.concatenate([mid_a, mid_b, mid_n, mid_l, mid_e], axis=1), grad_n2).astype(bf16)
    ffn_mid = lax.all_to_all(ffn_mid.reshape(rank, 16, -1).transpose(1, 0, 2), PLANE, 0, 0, tiled=True)
    ffn_mid = to_low(jnp.sum(ffn_mid.astype(f32), axis=0))
    ffn_mid = lax.all_gather(ffn_mid[None], AXES, axis=0, tiled=True).reshape(16, 8, rank, -1)

    grad_residual = cotangent + norm_back(residual, norm_second, grad_n2)
    grad_residual_extra = down_extra.astype(f32) + norm_back(residual_extra, norm_second, grad_n2_extra)
    grad_out_own = grad_residual.astype(bf16)
    grad_out = jnp.concatenate([both(grad_out_own, swap(grad_out_own), c), grad_residual_extra.astype(bf16)], axis=0)
    grad_gelu, lg_out, back, trail = call(
        functools.partial(outback_kernel, main), (2,),
        [fixed((rows, width)), out_spec, fixed((cols, width)), enter_spec, fixed(small_block)] + [rows_spec(rows)] * 4,
        [(rows_spec(rows), (wide_block, bf16)), B(*small_block)] + [(rows_spec(rows), (wide_block, f32))] * 2,
        [pltpu.VMEM((rows, quarter), f32)],
        core_at, (grad_out, near, leave_square[4], enter_half[4], select, states, branch, slope, decays), 18,
    )
    coming = chips_carry(jnp.stack([decays[0] * trail[0], decays[0] * back[0]]), True)[None, :]
    down_total = tied(add(down_mine, swap(down_theirs)), coming).astype(bf16)
    down_total = lax.all_to_all(down_total, YAX, 0, 0, tiled=True).reshape(4, toks, width)
    gelu_part, lat_gelu = call(
        geluback_kernel, (4,),
        [fixed(wide_block), col_spec(0), fixed((cols, halfw)), enter_spec, fixed(small_block)],
        [(rows_spec(main), ((main, width), f32)), F(*small_block)],
        [pltpu.VMEM(small_block, bf16)],
        core_at, (grad_gelu, near, leave_half[0], enter_square[0], select), 2,
    )

    grad_in, grad_de, base, lat_gates = call(
        gateback_kernel, (heads,),
        [head_spec(rows), head_spec(rows), head_spec(1), head_spec(rows), head_spec(1)] + [head_spec(rows)] * 4
        + [fixed((rows, 8)), head_spec(1), gate_spec, head_spec(cols), head_spec(cols)],
        [(head_spec(rows), (wide_block, bf16))] * 2 + [(head_spec(rows), (wide_block, f32)), F(rows, 2 * cols)],
        [pltpu.VMEM((rows + 8, head), f32), pltpu.VMEM((halfw, 2 * head), bf16)],
        core_at, (back, trail, coming, states, entering, convolved, sig_in, sig_de, decays, mask, rate, near, leave_half[2], leave_half[3]),
        60,
    )

    lanes_all = 3 * slotp + 2 * share
    (packed,) = call(
        pack_kernel, (1,),
        [fixed((cols, slotp))] * 3 + [fixed((main, cols))] * 2 + [fixed((main, share))] * 2,
        [B(cols, lanes_all)], [], core_at,
        (ex_a, ex_b, ex_n, pick_n_extra, lgw_extra, down_share, share_of(n2_extra)), 3, (base,),
    )
    ffn_all = lax.all_gather(packed, RING, axis=0)

    halo_both = chip_shift(jnp.concatenate([base[:HALO], lat_gates[:HALO]], axis=1), -1)
    halo_base, halo_lat = halo_both[:, :halfw], halo_both[:, halfw:]
    halo_other = chip_shift(lat_gates[:HALO], -1, cross=True)
    grad_fill, lg_in, lg_de, lat_fill, normed_mine, normed_theirs = call(
        fillback_kernel, (4,),
        [fixed(wide_block), fixed((rows, 2 * cols)), fixed((rows, 2 * cols)), fixed((HALO, halfw)), fixed((HALO, 2 * cols)), fixed((HALO, 2 * cols)),
         fixed((rows + HALO, cols)), fixed((rows + 2 * HALO, 8)), fixed((4, halfw)), fixed((halfw, cols)), fixed((halfw, cols)), fixed((cols, halfw)),
         col_spec(1), enter_spec, rows_spec(main)],
        [B(*wide_block), B(*small_block), B(*small_block), F(*small_block),
         (rows_spec(toks), ((toks, width), f32)), (rows_spec(toks), ((toks, width), bf16))],
        [pltpu.VMEM((rows + 2 * HALO, halfw), f32), pltpu.VMEM((HALO, 2 * cols), bf16), pltpu.VMEM((main, cols), bf16), pltpu.VMEM((main, quarter), f32)],
        core_at,
        (base, lat_gates, swap(lat_gates), halo_base, halo_lat, halo_other, select_after, mask_long, taps, enter_half[2], enter_half[3],
         leave_half[1], near, enter_square[1], gelu_part),
        2,
    )

    lg_gelu = ((lat_gelu + swap(lat_gelu)) * select).astype(bf16)
    lg_fill = ((lat_fill + swap(lat_fill)) * select).astype(bf16)
    pairs = [
        (lg_gelu, normed_half), (lg_fill, normed_half), (lg_in, convolved), (lg_de, convolved), (lg_out, mixed),
        (pick_gelu, grad_gelu), (pick_fill, grad_fill), (pick_in, grad_in), (pick_de, grad_de), (pick_out, half(grad_out, c, 1)),
    ]
    part_spec = lambda n, i: pl.BlockSpec((main, n), lambda *_: (i, 0), pipeline_mode=pl.Buffered(1))
    operands = [v for pair in pairs for v in pair]
    mid_rows = -(-10 * rank * halfw // cols // 64 // 16) * 16
    (mid,) = call(
        functools.partial(mids_kernel, 10, rank), (1,),
        [part_spec(cols, 0), part_spec(halfw, 0)] * 10,
        [B(64 * mid_rows, cols)],
        [pltpu.VMEM((cols, halfw), f32)],
        middle_at, operands, 6, (down_total,),
    )
    mid_own = mid
    mid = lax.all_to_all(mid, CHIPS, 0, 0, tiled=True).reshape(64, mid_rows, cols)
    mid = to_low(jnp.sum(mid.astype(f32), axis=0))

    operands = [*[v for pair in pairs[:5] for v in pair[::-1]], *[v for pair in pairs[5:] for v in pair]]
    enter_extra, leave_extra = call(
        functools.partial(extras_kernel, 5), (1,),
        [part_spec(halfw, 1), part_spec(cols, 1)] * 5 + [part_spec(cols, 1), part_spec(halfw, 1)] * 5,
        [B(5, halfw, cols), B(5, cols, halfw)],
        [],
        core_at, operands, 6, (mid_own,),
    )
    (grad_leave_widen,) = call(
        wide_kernel, (8,),
        [fixed((rank, cols)), fixed((units, 8 * chunk)), pl.BlockSpec((8, cols, hcol), lambda i, s: (0, 0, i)), pl.BlockSpec((1, 8, rank, hcol), lambda i, s: (i // 2, 0, 0, i % 2))],
        [(pl.BlockSpec((cols, block), lambda i, s: (0, i)), ((cols, 2 * ff), f32))],
        [], core_at, (one_hot, spread_one, ffn_all, ffn_mid), 12, (mid_own,),
    )
    mid = tied(mid, grad_leave_widen).astype(bf16)
    mid = lax.all_to_all(jnp.broadcast_to(mid[None], (64, *mid.shape)).reshape(-1, cols), CHIPS, 0, 0, tiled=True)
    (grad_enter_narrow,) = call(
        enter_kernel, (4,),
        [fixed((rank, cols)), fixed((units, 8 * chunk)), pl.BlockSpec((8, cols, hcol), lambda i, s: (0, 0, 8 + i)), pl.BlockSpec((1, 8, rank, hcol), lambda i, s: (4 + i // 2, 0, 0, i % 2))],
        [(pl.BlockSpec((block, cols), lambda i, s: (i, 0)), ((ff, cols), f32))],
        [], core_at, (one_hot, spread_one, ffn_all, ffn_mid), 7, (mid_own,),
    )
    grad_normed = normed_mine + swap(normed_theirs).astype(f32)
    input_grad = grad_residual + norm_back(block_input, norm_first, grad_normed)
    eye = jnp.eye(cols, dtype=bf16)
    share_spec = lambda i: pl.BlockSpec((8, cols, share), lambda *_: (0, 0, 3 * slotp // share + i))
    grad_leave_narrow, grad_enter_widen = call(
        shares_kernel, (1,),
        [fixed((rank, cols)), fixed((cols, cols)), share_spec(0), share_spec(1), fixed(ffn_mid.shape)],
        [F(cols, width), F(width, cols)],
        [], core_at, (one_hot, eye, ffn_all, ffn_all, ffn_mid), 4, (mid_own,),
    )
    per_k = lambda *shape: pl.BlockSpec((1,) + shape, lambda k, s: (k,) + (0,) * len(shape))
    mid_e_spec = pl.BlockSpec((rank * halfw // cols, cols), lambda k, s: (k, 0))
    mid_l_spec = pl.BlockSpec((rank * halfw // cols, cols), lambda k, s: (5 + k, 0))
    mid_other = swap(mid)
    grad_enter_square, grad_leave_square = call(
        square_kernel, (5,),
        [fixed((rank, cols)), per_k(halfw, cols), per_k(halfw, cols), per_k(cols, halfw), per_k(cols, halfw),
         mid_e_spec, mid_e_spec, mid_l_spec, mid_l_spec],
        [(per_k(width, cols), ((5, width, cols), f32)), (per_k(cols, width), ((5, cols, width), f32))],
        [], core_at, (one_hot, enter_extra, swap(enter_extra), leave_extra, swap(leave_extra), mid, mid_other, mid, mid_other), 9, (grad_enter_narrow, grad_leave_narrow),
    )
    block_output = tied(residual + jnp.sum(down_total.astype(f32), axis=0), grad_leave_square)
    return (
        block_output,
        input_grad,
        grad_enter_square,
        grad_leave_square,
        grad_enter_widen,
        grad_leave_widen,
        grad_enter_narrow,
        grad_leave_narrow,
    )


def solution(mesh):
    split = Mesh(mesh.devices.reshape(SIZES), AXES)
    by_row = P(AXES, None)
    return jax.shard_map(
        per_device,
        mesh=split,
        in_specs=(by_row, by_row, P(AXES), P(), P(), P(), P(), P()) + (by_row,) * 7 + (P(),) * 6,
        out_specs=(by_row, by_row, P(), P(), P(), P(), P(), P()),
        check_vma=False,
    )
```
